32 devices in a mesh: img: 4 (over z), row: 8 (over y, x, core).
Axes of the slice: x: 2, y: 2, z: 4, core: 2. Of those that a mesh axis runs over, the one named last changes fastest.
Arguments:
- flat_params: float32 [286720], P(('img', 'row')), may hold values from -1.5 to 1.5, as said below
- first_moment: float32 [286720], P(('img', 'row')), may hold values from -0.001 to 0.001
- second_moment: float32 [286720], P(('img', 'row')), may hold values from 1e-10 to 1e-06, as said below
- pixels: bfloat16 [64, 64, 7, 3, 1024], P('img', 'row'), may hold values from -6 to 6, as said below
- extents: int32 [64, 2], P('img'), may hold values from 32 to 256, as said below
- labels: int32 [64], P('img'), may hold values from 0 to 999
- teacher: float32 [64, 1000], P('img'), may hold values from -18 to 18
Outputs:
- new_params: float32 [286720], P(('img', 'row'))
- moment_one: float32 [286720], P(('img', 'row'))
- moment_two: float32 [286720], P(('img', 'row'))
- grad_norm: float32 [], replicated
- loss_value: float32 [], replicated
The draws below stay inside these ranges and needn't reach their ends.
Inputs may be any that keep to these rules, and one draw needn't show every extreme that they name: `extents`: both entries are multiples of 8; in every group of 16 images one image, which one drawn from the seed, fills the canvas; the last image of all has the smallest allowed rows and columns. pixels[n, r, a] is pixel row 4 r + a - 3 of image n, zero outside its 256 rows; entries of different token rows that name the same pixel row are equal. `flat_params`: layout of the steps; matrices scaled by their fan-in, gains near one. `second_moment`: Positive.
All inputs are finite; a program needn't handle non-finite values.
Results may differ from the reference program's by a relative error of at most 0.0018.
The reference program's roundings to bfloat16 on the way count: a program that leaves them out, or rounds other values in their place, can miss the bound.
Values may be sent and summed in bfloat16 or wider, within the bound.
No kernel may reach another device: no remote copies, remote signals or barrier semaphores. Data moves between devices by JAX's collectives and lax.ppermute only.
A program may use at most 704 MiB of HBM per device.

```python
import math
import jax
import jax.numpy as jnp
import numpy as np
from jax import lax

DIM = 96
MLP = 384
CLASSES = 1000
PATCH = 7
ROWS = 8
STEP = 7
IMG_DEV = 16
CANVAS_W = 256
CANVAS_H = 64
IMAGES = 64
NUSED = 286312
NPAR = 286720


def scale_layout():
    patch_in = 3 * PATCH * PATCH
    entries_list = []
    entries_list.append((patch_in * DIM, patch_in ** (-0.5), 0.0))
    entries_list.append((3 * DIM * DIM, DIM ** (-0.5), 0.0))
    entries_list.append((DIM * DIM, DIM ** (-0.5), 0.0))
    entries_list.append((DIM * MLP, DIM ** (-0.5), 0.0))
    entries_list.append((MLP * DIM, MLP ** (-0.5), 0.0))
    entries_list.append((DIM * CLASSES, DIM ** (-0.5), 0.0))
    entries_list.append(((2 * CANVAS_H - 8) * DIM, 0.1, 0.0))
    entries_list.append(((2 * CANVAS_W - 8) * DIM, 0.1, 0.0))
    entries_list.append((27 * DIM, 1.0 / 3.0, 0.0))
    for vec_row in range(15):
        if vec_row in (1, 3, 5, 7, 10, 13):
            entries_list.append((DIM, 0.1, 1.0))
        else:
            entries_list.append((DIM, 0.1, 0.0))
    entries_list.append((3 * DIM, 0.1, 0.0))
    entries_list.append((MLP, 0.1, 0.0))
    entries_list.append((CLASSES, 0.1, 0.0))
    entries_list.append((NPAR - NUSED, 0.02, 0.0))
    scales = jnp.concatenate([jnp.full((count_one,), spread, jnp.float32) for count_one, spread, centre in entries_list])
    offsets = jnp.concatenate([jnp.full((count_one,), centre, jnp.float32) for count_one, spread, centre in entries_list])
    return (scales, offsets)


def draw_flat_params(key, part):
    scales, offsets = scale_layout()
    noise_vals = jax.random.truncated_normal(jax.random.fold_in(key, 11), -3.0, 3.0, (NPAR,), jnp.float32)
    return noise_vals * scales + offsets


def draw_first_moment(key, part):
    base_size = 2.0 * 0.02 / math.sqrt(NUSED)
    noise_vals = jax.random.truncated_normal(jax.random.fold_in(key, 12), -3.0, 3.0, (NPAR,), jnp.float32)
    return noise_vals * base_size


def draw_second_moment(key, part):
    base_size = 2.0 * 0.02 / math.sqrt(NUSED)
    spread = jax.random.uniform(jax.random.fold_in(key, 13), (NPAR,), jnp.float32, math.log(0.5), math.log(8.0))
    return jnp.exp(spread) * (base_size * base_size)


def draw_pixels(key, part):
    pixel_key = jax.random.fold_in(key, 31)
    full_shape = (IMAGES, 4 * CANVAS_H, 3, 4 * CANVAS_W)
    base = jax.random.truncated_normal(pixel_key, -6.0, 6.0, full_shape, jnp.float32)
    framed = jnp.pad(base, ((0, 0), (3, 3), (0, 0), (0, 0)))
    row_index = 4 * jnp.arange(CANVAS_H)[:, None] + jnp.arange(PATCH)[None, :]
    return framed[:, row_index].astype(jnp.bfloat16)


def draw_extents(key, part):
    key_first = jax.random.fold_in(key, 21)
    key_second = jax.random.fold_in(key, 22)
    key_third = jax.random.fold_in(key, 23)
    rows_drawn = 8 * jax.random.randint(key_first, (IMAGES,), CANVAS_H // 16, CANVAS_H // 8 + 1)
    cols_drawn = 8 * jax.random.randint(key_second, (IMAGES,), CANVAS_W // 16, CANVAS_W // 8 + 1)
    full_slot = jax.random.randint(key_third, (IMAGES // IMG_DEV,), 0, IMG_DEV - 1)
    image_ids = jnp.arange(IMAGES)
    leading = image_ids % IMG_DEV == full_slot[image_ids // IMG_DEV]
    trailing = image_ids == IMAGES - 1
    rows_drawn = jnp.where(leading, CANVAS_H, jnp.where(trailing, 8 * (CANVAS_H // 16), rows_drawn))
    cols_drawn = jnp.where(leading, CANVAS_W, jnp.where(trailing, 8 * (CANVAS_W // 16), cols_drawn))
    return jnp.stack([rows_drawn, cols_drawn], axis=1).astype(jnp.int32)


def plant(array, rng, low, high):
    longest = array.shape.index(max(array.shape))
    spots = []
    for shift in (0, 1):
        where = [jax.random.randint(jax.random.fold_in(rng, axis), (), 0, length) for axis, length in enumerate(array.shape)]
        where[longest] = (where[longest] + shift) % array.shape[longest]
        spots.append(tuple(where))
    return array.at[spots[0]].set(low).at[spots[1]].set(high)


def level_of(own_key, shape, split, least, high):
    gain, own = 1.0, jax.random.fold_in(own_key, 6)
    for dim, parts in split:
        draws = jnp.exp(jax.random.uniform(jax.random.fold_in(own, dim), (parts,), jnp.float32, least / len(split), high / len(split)))
        gain = gain * jnp.repeat(draws, shape[dim] // parts).reshape([-1 if axis == dim else 1 for axis in range(len(shape))])
    return gain


def scatter_about(own_key, dims, deviation, most, shards=(), kind=jnp.bfloat16):
    values = deviation * jax.random.normal(own_key, dims, jnp.float32)
    if shards:
        values = values * level_of(own_key, dims, shards, -0.22, 0.18)
    return jnp.clip(values, -most, most).astype(kind)


def setup_inputs(seed: int = 0) -> dict:
    key_list = jax.random.split(jax.random.key(seed), 8)
    return {
        "flat_params": draw_flat_params(jax.random.fold_in(key_list[7], 71), 0),
        "first_moment": draw_first_moment(jax.random.fold_in(key_list[7], 71), 0),
        "second_moment": draw_second_moment(jax.random.fold_in(key_list[7], 71), 0),
        "pixels": draw_pixels(jax.random.fold_in(key_list[7], 71), 0),
        "extents": draw_extents(jax.random.fold_in(key_list[7], 71), 0),
        "labels": plant(jax.random.randint(key_list[5], (IMAGES,), 0, CLASSES), jax.random.fold_in(key_list[5], 1), 0, CLASSES - 1).astype(jnp.int32),
        "teacher": scatter_about(key_list[6], (IMAGES, CLASSES), 3.0, 18.0, ((0, 4),), jnp.float32),
    }


HIGHEST_PREC = lax.Precision.HIGHEST
CLIP_NORM = 0.02
LEARN_RATE = 0.05
WEIGHT_DECAY = 0.05
BETA_FIRST = 0.5
BETA_SECOND = 0.5
ADAM_EPS = 1e-08
NORM_EPS = 1e-06
NEG_FILL = -1e+30

@jax.custom_vjp
def low(v):
    return lax.optimization_barrier(v.astype(jnp.bfloat16)).astype(jnp.float32)

@jax.custom_vjp
def low_back(v):
    return v

def low_keep(v):
    return (low(v), None)

def low_pass(kept, grad):
    return (grad,)

def back_keep(v):
    return (v, None)

def back_low(kept, grad):
    return (low(grad),)
low.defvjp(low_keep, low_pass)
low_back.defvjp(back_keep, back_low)

def segment_list(canvas_rows, canvas_cols):
    return [('w_patch', (3 * PATCH * PATCH, DIM)), ('w_qkv', (DIM, 3 * DIM)), ('w_proj', (DIM, DIM)), ('w_fc1', (DIM, MLP)), ('w_fc2', (MLP, DIM)), ('w_head', (DIM, CLASSES)), ('rel_rows', (2 * canvas_rows - 8, DIM)), ('rel_cols', (2 * canvas_cols - 8, DIM)), ('kernels', (3, 9, DIM)), ('vectors', (15, DIM)), ('b_qkv', (3 * DIM,)), ('b_fc1', (MLP,)), ('b_head', (CLASSES,))]

def unpack(flat_vec, segments):
    pieces = {}
    position = 0
    for seg_name, seg_shape in segments:
        entries = int(np.prod(seg_shape))
        pieces[seg_name] = flat_vec[position:position + entries].reshape(seg_shape)
        position += entries
    return pieces

def layer_norm(values, gain_vec, shift_vec):
    mean_part = lax.optimization_barrier(jnp.mean(values, axis=-1, keepdims=True))
    centered = values - mean_part
    variance = lax.optimization_barrier(jnp.mean(centered * centered, axis=-1, keepdims=True))
    return centered * lax.rsqrt(variance + NORM_EPS) * gain_vec + shift_vec

def image_loss(pooled, head_w, head_b, teacher, labels, image_total):
    logits = jnp.dot(pooled, head_w, precision=HIGHEST_PREC) + head_b
    log_student = jax.nn.log_softmax(logits, axis=-1)
    log_teacher = jax.nn.log_softmax(teacher, axis=-1)
    onehot = (jnp.arange(CLASSES)[None, :] == labels[:, None]).astype(jnp.float32)
    per_image = lax.optimization_barrier(jnp.sum(jnp.exp(log_teacher) * (log_teacher - log_student), axis=-1)) - lax.optimization_barrier(jnp.sum(onehot * log_student, axis=-1))
    return jnp.sum(per_image) / image_total

def image_features(weights, pixel_img, extent):
    height = extent[0]
    breadth = extent[1]
    key_rows = CANVAS_H // ROWS
    key_cols = CANVAS_W // ROWS
    vectors = weights['vectors']
    kernels = weights['kernels']
    framed = jnp.pad(pixel_img, ((0, 0), (0, 0), (0, 0), (3, 3)))
    columns = []
    for tap_row in range(PATCH):
        for tap_col in range(PATCH):
            pix_piece = framed[:, tap_row, :, tap_col:tap_col + 4 * CANVAS_W:4]
            columns.append(jnp.transpose(pix_piece, (0, 2, 1)))
    patches = jnp.concatenate(columns, axis=-1)
    row_ids = jnp.arange(CANVAS_H)
    col_ids = jnp.arange(CANVAS_W)
    token_mask = ((row_ids[:, None] < height) & (col_ids[None, :] < breadth)).astype(jnp.float32)[:, :, None]
    key_valid = (jnp.arange(key_rows)[:, None] < height // ROWS) & (jnp.arange(key_cols)[None, :] < breadth // ROWS)
    x_zero = (jnp.einsum('rwk,kc->rwc', patches, weights['w_patch'], precision=HIGHEST_PREC) + vectors[0]) * token_mask
    normed_one = low(layer_norm(x_zero, vectors[1], vectors[2]))
    proj_qkv = low(low_back(jnp.einsum('rwc,ce->rwe', normed_one, weights['w_qkv'], precision=HIGHEST_PREC) + weights['b_qkv']))
    framed_q = jnp.pad(proj_qkv[:, :, :DIM], ((1, 1), (1, 1), (0, 0)))
    pooled_q = jnp.zeros((CANVAS_H, CANVAS_W, DIM), jnp.float32)
    for tap_row in range(3):
        for tap_col in range(3):
            pooled_q = pooled_q + framed_q[tap_row:tap_row + CANVAS_H, tap_col:tap_col + CANVAS_W] * kernels[0, tap_row * 3 + tap_col]
    query_n = low(layer_norm(pooled_q, vectors[3], vectors[4]))
    pooled_kv = []
    for member in range(2):
        framed_kv = jnp.pad(proj_qkv[:, :, (member + 1) * DIM:(member + 2) * DIM], ((1, 1), (1, 1), (0, 0)))
        pooled_one = jnp.zeros((key_rows, key_cols, DIM), jnp.float32)
        for tap_row in range(3):
            for tap_col in range(3):
                tap_vals = framed_kv[tap_row:tap_row + ROWS * (key_rows - 1) + 1:ROWS, tap_col:tap_col + ROWS * (key_cols - 1) + 1:ROWS]
                pooled_one = pooled_one + tap_vals * kernels[1 + member, tap_row * 3 + tap_col]
        pooled_kv.append(low(layer_norm(pooled_one, vectors[5 + 2 * member], vectors[6 + 2 * member])))
    key_n = pooled_kv[0]
    value_n = pooled_kv[1]
    row_table = np.arange(CANVAS_H)[:, None] - ROWS * np.arange(key_rows)[None, :] + CANVAS_H - ROWS
    col_table = np.arange(CANVAS_W)[:, None] - ROWS * np.arange(key_cols)[None, :] + CANVAS_W - ROWS
    scores = jnp.einsum('rwc,akc->rwak', query_n, key_n, precision=HIGHEST_PREC) * DIM ** (-0.5)
    rel_r = jnp.einsum('rwc,rac->rwa', query_n, weights['rel_rows'][row_table], precision=HIGHEST_PREC)
    rel_c = jnp.einsum('rwc,wkc->rwk', query_n, weights['rel_cols'][col_table], precision=HIGHEST_PREC)
    scores = low_back(scores + rel_r[:, :, :, None] + rel_c[:, :, None, :])
    masked = jnp.where(key_valid[None, None], scores, NEG_FILL)
    row_max = lax.optimization_barrier(jnp.max(masked, axis=(2, 3), keepdims=True))
    exp_scores = jnp.exp(masked - row_max)
    attn_probs = low(exp_scores / lax.optimization_barrier(jnp.sum(exp_scores, axis=(2, 3), keepdims=True)))
    attention_output = low_back(jnp.einsum('rwak,akc->rwc', attn_probs, value_n, precision=HIGHEST_PREC))
    attended = low(attention_output + query_n)
    proj_out = low_back(jnp.einsum('rwc,cd->rwd', attended, weights['w_proj'], precision=HIGHEST_PREC) + vectors[9])
    x_one = x_zero + proj_out
    normed_two = low(layer_norm(x_one, vectors[10], vectors[11]))
    hidden_pre = low_back(jnp.einsum('rwc,ch->rwh', normed_two, weights['w_fc1'], precision=HIGHEST_PREC) + weights['b_fc1'])
    activated = low(jax.nn.gelu(hidden_pre, approximate=False))
    mlp_out = low_back(jnp.einsum('rwh,hc->rwc', activated, weights['w_fc2'], precision=HIGHEST_PREC) + vectors[12])
    x_two = x_one + mlp_out
    normed_three = layer_norm(x_two, vectors[13], vectors[14])
    return lax.optimization_barrier(jnp.sum(normed_three * token_mask, axis=(0, 1))) / (height * breadth).astype(jnp.float32)

def forward(params_now, pixels_f, extents, labels, teacher):
    weights = unpack(low(params_now), segment_list(CANVAS_H, CANVAS_W))

    def one_image(image_item):
        return image_features(weights, image_item[0], image_item[1])
    pooled = lax.map(jax.checkpoint(one_image), (pixels_f, extents))
    return image_loss(pooled, weights['w_head'], weights['b_head'], teacher, labels, IMAGES * 1.0)

def adam_update(params_now, first_moment, second_moment, grads, grad_norm):
    clip_factor = jnp.minimum(1.0, CLIP_NORM / (grad_norm + 1e-06))
    clipped = grads * clip_factor
    moment_one = BETA_FIRST * first_moment + (1.0 - BETA_FIRST) * clipped
    moment_two = BETA_SECOND * second_moment + (1.0 - BETA_SECOND) * clipped * clipped
    fix_one = 1.0 - BETA_FIRST ** STEP
    fix_two = 1.0 - BETA_SECOND ** STEP
    update = moment_one / fix_one / (jnp.sqrt(moment_two / fix_two) + ADAM_EPS) + WEIGHT_DECAY * params_now
    return (params_now - LEARN_RATE * update, moment_one, moment_two)

def reference(flat_params, first_moment, second_moment, pixels, extents, labels, teacher):
    pixels_f = pixels.astype(jnp.float32)

    def loss_of(params_now):
        return forward(params_now, pixels_f, extents, labels, teacher)
    loss_value, pullback = jax.vjp(loss_of, flat_params)
    grads = pullback(jnp.ones_like(loss_value))[0]
    grad_norm = jnp.sqrt(jnp.sum(grads * grads))
    new_params, moment_one, moment_two = adam_update(flat_params, first_moment, second_moment, grads, grad_norm)
    return (new_params, moment_one, moment_two, grad_norm, loss_value)
```

```python
import functools

import jax
import jax.numpy as jnp
import numpy as np
from jax import lax
from jax.experimental import pallas as pl
from jax.experimental.pallas import tpu as pltpu
from jax.sharding import PartitionSpec as P

DIM = 96
MLP = 384
CLASSES = 1000
PATCH = 7
ROWS = 8
STEP = 7
CANVAS_W = 256

HIGHEST_PREC = lax.Precision.HIGHEST
CLIP_NORM = 0.02
LEARN_RATE = 0.05
WEIGHT_DECAY = 0.05
BETA_FIRST = 0.5
BETA_SECOND = 0.5
ADAM_EPS = 1e-08
NORM_EPS = 1e-06
NEG_FILL = -1e30

F32 = jnp.float32
BF16 = jnp.bfloat16
SCALE = DIM ** (-0.5)
EXP2_SCALE = SCALE * 1.4426950408889634

TOKENS = ROWS * CANVAS_W
PAIR = 512
PAIRS = TOKENS // PAIR
TILES = CANVAS_W // 32
PADDED = TOKENS + 512
WIN = 40
PATCH_ROWS = 224
VMEM_BYTES = 56 * 1024 * 1024


def deinterleave_matrix():
    out = np.zeros((4, 128, 4, 4, 32), np.float32)
    for row in range(4):
        for phase in range(4):
            for col in range(32):
                out[row, 4 * col + phase, phase, row, col] = 1.0
    return out.reshape(512, 512)


def tap_matrix():
    out = np.zeros((CANVAS_W, 128), np.float32)
    for tap in range(3):
        for key in range(32):
            col = 8 * key + tap - 1
            if col >= 0:
                out[col, tap * 32 + key] = 1.0
    return out


def dot(a, b):
    return jnp.dot(a, b, preferred_element_type=F32)


def dot_nt(a, b):
    return lax.dot_general(a, b, (((1,), (1,)), ((), ())), preferred_element_type=F32)


def normalized(x):
    mean = jnp.sum(x, axis=0, keepdims=True) * (1.0 / DIM)
    centered = x - mean
    var = jnp.sum(centered * centered, axis=0, keepdims=True) * (1.0 / DIM)
    rstd = lax.rsqrt(var + NORM_EPS)
    return centered * rstd, rstd


def norm_back(grad, hat, rstd, gain):
    inner = grad * gain
    mean_one = jnp.sum(inner, axis=0, keepdims=True) * (1.0 / DIM)
    mean_two = jnp.sum(inner * hat, axis=0, keepdims=True) * (1.0 / DIM)
    return rstd * (inner - mean_one - hat * mean_two)


def fold_lanes(x):
    total = x[:, 0:128]
    for k in range(1, x.shape[1] // 128):
        total = total + x[:, 128 * k : 128 * k + 128]
    return total


def column(vec_ref, index):
    place = index + 27 if index < 15 else index - 15 if index < 42 else index
    return vec_ref[:, place : place + 1]


def lane_ids(width, rows=1):
    return lax.broadcasted_iota(jnp.int32, (rows, width), 1)


def pair_mask(pair, breadth, row_ok):
    lane = lane_ids(PAIR)
    col = pair * 64 + (lane >> 8) * 32 + (lane & 31)
    return jnp.where((col < breadth) & row_ok, 1.0, 0.0).astype(F32)


def pair_lanes(pair, base=0):
    return pl.ds(pl.multiple_of(pair * PAIR + base, 128), PAIR)


def pair_count(breadth):
    return jnp.minimum((breadth >> 6) + 1, PAIRS)


def col_shifts(window, base):
    lane = lane_ids(128, DIM)
    here = window[:, base : base + 128]
    before = window[:, base - 256 : base - 128]
    after = window[:, base + 256 : base + 384]
    left = jnp.where((lane & 31) == 0, pltpu.roll(before, 97, 1), pltpu.roll(here, 1, 1))
    right = jnp.where((lane & 31) == 31, pltpu.roll(after, 31, 1), pltpu.roll(here, 127, 1))
    return left, here, right


def rows_down(first, second, entering):
    lane = lane_ids(128, DIM)
    a, b = pltpu.roll(first, 32, 1), pltpu.roll(second, 32, 1)
    return jnp.where(lane < 32, entering, a), jnp.where(lane < 32, a, b), b


def rows_up(first, second, entering):
    lane = lane_ids(128, DIM)
    a, b = pltpu.roll(first, 96, 1), pltpu.roll(second, 96, 1)
    return jnp.where(lane >= 96, b, a), jnp.where(lane >= 96, entering, b), a


def spread_halo(dst_ref, halo, target):
    for tile in range(TILES):
        block = halo[:, 128 * (tile // 4) : 128 * (tile // 4) + 128]
        shift = (target - 32 * (tile % 4)) % 128
        dst_ref[:, 128 * tile : 128 * tile + 128] = pltpu.roll(block, shift, 1) if shift else block


def gather_halo(src_ref, target):
    lane = lane_ids(128, DIM)
    blocks = []
    for half in range(2):
        total = None
        for k in range(4):
            tile = 4 * half + k
            block = src_ref[:, 128 * tile : 128 * tile + 128]
            shift = (32 * k - target) % 128
            block = pltpu.roll(block, shift, 1) if shift else block
            total = block if total is None else jnp.where((lane >> 5) == k, block, total)
        blocks.append(total)
    return jnp.concatenate(blocks, axis=1)


def reverse_bits(value, count):
    result = 0
    for bit in range(count.bit_length() - 1):
        result = result * 2 + ((value >> bit) & 1)
    return result


def key_tables(kv_ref, row_index, key_rows, height, breadth, ka_ref, kn_ref):
    keys = [None] * key_rows
    for i in range(key_rows):
        slot = reverse_bits(jnp.bitwise_xor(row_index, i), key_rows)
        keys[i] = kv_ref[slot, 0].astype(F32)
    both = jnp.concatenate(keys, axis=1)
    total = key_rows * 32
    more = aug_rows(key_rows)
    rank = lax.broadcasted_iota(jnp.int32, (more, total), 0)
    key = lax.broadcasted_iota(jnp.int32, (more, total), 1)
    key_r, key_c = key >> 5, key & 31
    half = key_rows + 32
    low = rank >= half
    rank_in = jnp.where(low, rank - half, rank)
    hit = rank_in == jnp.where(rank_in < key_rows, key_r, key_c + key_rows)
    invalid = (key_r * ROWS >= height) | (key_c * ROWS >= breadth)
    table = jnp.where(rank < 2 * half, jnp.where(hit, 1.0, 0.0), 0.0)
    table = jnp.where((rank == 2 * half) & invalid, NEG_FILL, table)
    full = jnp.concatenate([both[:DIM], table, jnp.zeros((256 - DIM - more, total), F32)], axis=0)
    ka_ref[...] = full[: DIM + more].astype(BF16)
    kn_ref[...] = jnp.transpose(full).astype(BF16)
    return both[DIM:]


def aug_rows(key_rows):
    return 2 * key_rows + 64 + 16


def embed_kernel(ext_ref, row_ref, pix_ref, tail_ref, perm_ref, tap_ref, wp_ref, wqkv_ref, vec_ref, bkv_ref, kexp_ref,
                 patch_ref, x0_ref, q_ref, first_ref, last_ref, nsel_ref, kvt_ref, below_ref, own_ref, s_ref, n_ref, *, offset):
    image = pl.program_id(0)
    height = ext_ref[offset + image, 0]
    breadth = ext_ref[offset + image, 1]
    row_ok = row_ref[0] * ROWS < height

    @pl.when(image == 0)
    def _():
        s_ref[...] = jnp.zeros_like(s_ref)

    for r in range(ROWS):
        for a in range(4):
            s_ref[16 * r + 4 * a : 16 * r + 4 * a + 3, :] = pix_ref[0, r, a].astype(F32)
    for a in range(3):
        s_ref[128 + 4 * a : 128 + 4 * a + 3, :] = tail_ref[0, 0, a].astype(F32)
    lane = lane_ids(1024, 144)
    for shifted in range(2):
        rows = s_ref[...]
        if shifted:
            rows = jnp.where(lane < 4, 0.0, pltpu.roll(rows, 4, 1))
        rows = rows.astype(BF16)
        stack = []
        for start in (0, 4, 1, 5):
            for tile in range(TILES):
                stack.append(jnp.concatenate(
                    [rows[16 * (start + k) : 16 * (start + k) + 16, 128 * tile : 128 * tile + 128] for k in range(4)], axis=1))
        out = dot(jnp.concatenate(stack, axis=0), perm_ref[...]).astype(BF16)
        for which, start in enumerate((0, 4, 1, 5)):
            half, side = which // 2, which % 2
            for tile in range(TILES):
                block = out[128 * which + 16 * tile : 128 * which + 16 * tile + 16]
                for phase in range(shifted, 4):
                    top = 64 * half + 16 * phase if not shifted else 128 + 48 * half + 16 * (phase - 1)
                    patch_ref[0, top : top + 16, 256 * tile + 128 * side : 256 * tile + 128 * side + 128] = block[
                        :, 128 * phase : 128 * phase + 128]

    count = pair_count(breadth)

    def active(pair, carry):
        lanes = pair_lanes(pair)
        x0 = (dot(wp_ref[...], patch_ref[0, :, lanes]) + column(vec_ref, 0)) * pair_mask(pair, breadth, row_ok)
        x0_ref[0, :, lanes] = x0
        hat, _ = normalized(x0)
        normed = (hat * column(vec_ref, 1) + column(vec_ref, 2)).astype(BF16)
        n_ref[:, lanes] = normed.astype(F32)
        q_ref[0, :, pair_lanes(pair, 256)] = (dot(wqkv_ref[0:DIM, :], normed) + column(vec_ref, 42)).astype(BF16)
        return carry

    def idle(pair, carry):
        n_ref[:, pair_lanes(pair)] = jnp.zeros((DIM, PAIR), F32)
        q_ref[0, :, pair_lanes(pair, 256)] = jnp.zeros((DIM, PAIR), BF16)
        return carry

    lax.fori_loop(0, count, active, 0)
    lax.fori_loop(count, PAIRS, idle, 0)
    q_ref[0, :, 0:256] = jnp.zeros((DIM, 256), BF16)
    q_ref[0, :, 256 + TOKENS : 512 + TOKENS] = jnp.zeros((DIM, 256), BF16)

    rows = []
    for start in (224, 0, 32):
        rows.append(jnp.concatenate([n_ref[:, 256 * t + start : 256 * t + start + 32] for t in range(TILES)], axis=1).astype(BF16))
    last_ref[0] = (dot(wqkv_ref[0:DIM, :], rows[0]) + column(vec_ref, 42)).astype(BF16)
    first_ref[0] = (dot(wqkv_ref[0:DIM, :], rows[1]) + column(vec_ref, 42)).astype(BF16)
    nsel = jnp.concatenate([dot(row, tap_ref[...]) for row in rows], axis=1).astype(BF16)
    nsel_ref[0] = nsel
    taps = (dot(wqkv_ref[DIM : 3 * DIM, :], nsel) + bkv_ref[...]).astype(BF16)
    kvt_ref[0] = taps
    product = taps.astype(F32) * kexp_ref[...]
    sums = []
    for k in range(3):
        part = product[:, 128 * k : 128 * k + 128]
        sums.append((part + pltpu.roll(part, 96, 1) + pltpu.roll(part, 64, 1))[:, 0:32])
    below_ref[0] = sums[0]
    own_ref[0] = sums[1] + sums[2]


def call_embed(ext, row, pixels, consts, wts, images, offset):
    whole = lambda *shape: pl.BlockSpec(shape, lambda i, *_: (0,) * len(shape))
    per = lambda *shape: pl.BlockSpec((1,) + shape, lambda i, *_: (i,) + (0,) * len(shape))
    shapes = [
        ((PATCH_ROWS, TOKENS), BF16), ((DIM, TOKENS), F32), ((DIM, PADDED), BF16), ((DIM, CANVAS_W), BF16),
        ((DIM, CANVAS_W), BF16), ((DIM, 384), BF16), ((2 * DIM, 384), BF16), ((2 * DIM, 32), F32), ((2 * DIM, 32), F32)]
    return pl.pallas_call(
        functools.partial(embed_kernel, offset=offset),
        grid_spec=pltpu.PrefetchScalarGridSpec(
            num_scalar_prefetch=2, grid=(images,),
            in_specs=[
                pl.BlockSpec((1, ROWS, 4, 3, 1024), lambda i, *_: (i + offset, 0, 0, 0, 0)),
                pl.BlockSpec((1, 1, 4, 3, 1024), lambda i, *_: (i + offset, ROWS - 1, 1, 0, 0)),
                whole(512, 512), whole(CANVAS_W, 128), whole(DIM, PATCH_ROWS), whole(3 * DIM, DIM), whole(DIM, 64),
                whole(2 * DIM, 1), whole(2 * DIM, 384)],
            out_specs=[per(*s) for s, _ in shapes],
            scratch_shapes=[pltpu.VMEM((144, 1024), F32), pltpu.VMEM((DIM, TOKENS), F32)]),
        out_shape=[jax.ShapeDtypeStruct((images,) + s, t) for s, t in shapes],
        compiler_params=pltpu.CompilerParams(vmem_limit_bytes=VMEM_BYTES),
        cost_estimate=pl.CostEstimate(flops=images * 2_000_000_000, bytes_accessed=images * 4_000_000, transcendentals=0),
        name="embed",
    )(ext, row, pixels, pixels, consts["perm"], consts["tap"], wts["wp"], wts["wqkv_t"], wts["vec"], wts["b_kv"], wts["kexp"])


def pool_norm_kernel(own_ref, got_ref, vec_ref, kv_ref):
    for member in range(2):
        part = slice(member * DIM, member * DIM + DIM)
        for image in range(own_ref.shape[0]):
            hat, _ = normalized(own_ref[image, part] + got_ref[image, part])
            kv_ref[image, part] = (hat * column(vec_ref, 5 + 2 * member) + column(vec_ref, 6 + 2 * member)).astype(BF16)


def call_pool_norm(own, got, vec):
    return pl.pallas_call(
        pool_norm_kernel, out_shape=jax.ShapeDtypeStruct(own.shape, BF16), name="pool_norm",
        cost_estimate=pl.CostEstimate(flops=own.size * 10, bytes_accessed=own.size * 10, transcendentals=0))(own, got, vec)


def pool_back_kernel(own_ref, got_ref, grad_ref, vec_ref, pre_ref, sums_ref):
    for member in range(2):
        part = slice(member * DIM, member * DIM + DIM)
        gain = jnp.zeros((DIM, 32), F32)
        shift = jnp.zeros((DIM, 32), F32)
        for image in range(own_ref.shape[0]):
            hat, rstd = normalized(own_ref[image, part] + got_ref[image, part])
            grad = grad_ref[image, part]
            gain = gain + grad * hat
            shift = shift + grad
            pre_ref[image, part] = norm_back(grad, hat, rstd, column(vec_ref, 5 + 2 * member))
        sums_ref[2 * member] = gain
        sums_ref[2 * member + 1] = shift


def call_pool_back(own, got, grad, vec):
    return pl.pallas_call(
        pool_back_kernel,
        out_shape=[jax.ShapeDtypeStruct(own.shape, F32), jax.ShapeDtypeStruct((4, DIM, 32), F32)], name="pool_back",
        cost_estimate=pl.CostEstimate(flops=own.size * 20, bytes_accessed=own.size * 16, transcendentals=0))(own, got, grad, vec)


def lane_bit(lane, bit):
    return (lane & bit) != 0


def relative_terms(products, key_rows):
    lane = lane_ids(PAIR, WIN)
    parts = [products[WIN * s : WIN * s + WIN] for s in range(8)]
    for bit in (1, 2, 4):
        chosen = lane_bit(lane, bit)
        parts = [jnp.where(chosen, parts[2 * k + 1], parts[2 * k]) for k in range(len(parts) // 2)]
    by_col = parts[0]
    for bit, step in ((8, 1), (16, 2), (256, 4)):
        by_col = jnp.where(lane_bit(lane, bit), by_col, pltpu.roll(by_col, WIN - step, 0))
    lane = lane_ids(PAIR, key_rows)
    rows = products[8 * WIN :]
    parts = [rows[key_rows * r : key_rows * r + key_rows] for r in range(8)]
    for bit in (32, 64, 128):
        chosen = lane_bit(lane, bit)
        parts = [jnp.where(chosen, parts[2 * k + 1], parts[2 * k]) for k in range(len(parts) // 2)]
    return jnp.concatenate([parts[0], by_col[0:32]], axis=0)


def relative_spread(grad_terms, key_rows):
    lane = lane_ids(PAIR, WIN)
    by_row = grad_terms[:key_rows]
    by_col = jnp.concatenate([grad_terms[key_rows:], jnp.zeros((WIN - 32, grad_terms.shape[1]), F32)], axis=0)
    for bit, step in ((8, 1), (16, 2), (256, 4)):
        by_col = jnp.where(lane_bit(lane, bit), by_col, pltpu.roll(by_col, step, 0))
    parts = [jnp.where((lane & 7) == s, by_col, 0.0) for s in range(8)]
    lane = lane_ids(PAIR, key_rows)
    parts += [jnp.where(((lane >> 5) & 7) == r, by_row, 0.0) for r in range(8)]
    return jnp.concatenate(parts, axis=0).astype(BF16)


def mlp_forward(x1, vec_ref, w1t_ref, b1_ref, w2t_ref):
    hat_two, rstd_two = normalized(x1)
    normed = (hat_two * column(vec_ref, 10) + column(vec_ref, 11)).astype(BF16)
    hidden = dot(w1t_ref[...], normed) + b1_ref[...]
    cumulative = 0.5 + 0.5 * lax.erf(hidden * 0.7071067811865476)
    act = (hidden * cumulative).astype(BF16)
    x2 = x1 + (dot(w2t_ref[...], act) + column(vec_ref, 12))
    return hat_two, rstd_two, normed, hidden, cumulative, act, x2


def forward_kernel(ext_ref, row_ref, q_ref, top_ref, bot_ref, x0_ref, kv_ref, vec_ref, rw_ref, wprojt_ref, w1t_ref, b1_ref, w2t_ref,
                   hat_ref, terms_ref, att_ref, stat_ref, pool_ref, ka_ref, kn_ref, v_ref, ztop_ref, zbot_ref, *, offset, key_rows):
    image = pl.program_id(0)
    height = ext_ref[offset + image, 0]
    breadth = ext_ref[offset + image, 1]
    row_ok = row_ref[0] * ROWS < height
    depth = DIM + aug_rows(key_rows)
    values = key_tables(kv_ref, row_ref[0], key_rows, height, breadth, ka_ref, kn_ref)
    v_ref[...] = values.astype(BF16)
    lane = lane_ids(CANVAS_W, DIM)
    for halo_ref, dst_ref, tap_row, target in ((top_ref, ztop_ref, 0, 0), (bot_ref, zbot_ref, 2, 96)):
        halo = halo_ref[0].astype(F32)
        left = jnp.where(lane == 0, 0.0, pltpu.roll(halo, 1, 1))
        right = jnp.where(lane == CANVAS_W - 1, 0.0, pltpu.roll(halo, CANVAS_W - 1, 1))
        taps = [column(vec_ref, 15 + 3 * tap_row + k) for k in range(3)]
        spread_halo(dst_ref, taps[0] * left + taps[1] * halo + taps[2] * right, target)
    pool_ref[...] = jnp.zeros_like(pool_ref)

    def step(pair, carry):
        lanes = pair_lanes(pair)
        window = q_ref[0, :, pl.ds(pl.multiple_of(pair * PAIR, 128), PAIR + 512)].astype(F32)
        pre = []
        for tile in range(2):
            sums = []
            for side in range(2):
                shifts = col_shifts(window, 256 + 256 * tile + 128 * side)
                sums.append([sum(column(vec_ref, 15 + 3 * r + c) * shifts[c] for c in range(3)) for r in range(3)])
            halo = pl.ds(pl.multiple_of((2 * pair + tile) * 128, 128), 128)
            down = rows_down(sums[0][0], sums[1][0], ztop_ref[:, halo])
            up = rows_up(sums[0][2], sums[1][2], zbot_ref[:, halo])
            pre += [sums[side][1] + down[side] + up[side] for side in range(2)]
        hat, rstd = normalized(jnp.concatenate(pre, axis=1))
        hat_ref[0, :, lanes] = hat
        query = (hat * column(vec_ref, 3) + column(vec_ref, 4)).astype(BF16)
        terms = relative_terms(dot(rw_ref[pair], query), key_rows) * (DIM**0.5)
        high = terms.astype(BF16).astype(F32)
        extra = jnp.concatenate([high, terms - high, jnp.ones((16, PAIR), F32)], axis=0).astype(BF16)
        terms_ref[0, :, lanes] = extra
        scores = dot(kn_ref[:, :depth], jnp.concatenate([query, extra], axis=0))
        peak = jnp.max(scores, axis=0, keepdims=True)
        weights = jnp.exp2((scores - peak) * EXP2_SCALE)
        total = jnp.sum(weights, axis=0, keepdims=True)
        probs = (weights * (1.0 / total)).astype(BF16)
        stat_ref[0, 0:1, lanes] = peak
        stat_ref[0, 1:2, lanes] = 1.0 / total
        stat_ref[0, 2:3, lanes] = rstd
        attended = (dot(v_ref[...], probs) + query.astype(F32)).astype(BF16)
        att_ref[0, :, lanes] = attended
        x1 = x0_ref[0, :, lanes] + (dot(wprojt_ref[...], attended) + column(vec_ref, 9))
        x2 = mlp_forward(x1, vec_ref, w1t_ref, b1_ref, w2t_ref)[-1]
        hat_three, _ = normalized(x2)
        pool_ref[0] += fold_lanes(hat_three * pair_mask(pair, breadth, row_ok))
        return carry

    lax.fori_loop(0, pair_count(breadth), step, 0)


def specs():
    whole = lambda *shape: pl.BlockSpec(shape, lambda i, *_: (0,) * len(shape))
    per = lambda *shape: pl.BlockSpec((1,) + shape, lambda i, *_: (i,) + (0,) * len(shape))
    return whole, per


def call_forward(ext, row, q, top, bot, x0, kv, wts, offset):
    whole, per = specs()
    images, key_rows = q.shape[0], kv.shape[0]
    more = aug_rows(key_rows)
    shapes = [((DIM, TOKENS), F32), ((more, TOKENS), BF16), ((DIM, TOKENS), BF16), ((8, TOKENS), F32), ((DIM, 128), F32)]
    keys = key_rows * 32
    return pl.pallas_call(
        functools.partial(forward_kernel, offset=offset, key_rows=key_rows),
        grid_spec=pltpu.PrefetchScalarGridSpec(
            num_scalar_prefetch=2, grid=(images,),
            in_specs=[
                per(DIM, PADDED), per(DIM, CANVAS_W), per(DIM, CANVAS_W), per(DIM, TOKENS),
                pl.BlockSpec((key_rows, 1, 2 * DIM, 32), lambda i, *_: (0, i, 0, 0)),
                whole(DIM, 64), whole(PAIRS, 8 * WIN + 8 * key_rows, DIM), whole(DIM, DIM), whole(MLP, DIM), whole(MLP, 1),
                whole(DIM, MLP)],
            out_specs=[per(*s) for s, _ in shapes],
            scratch_shapes=[
                pltpu.VMEM((DIM + more, keys), BF16), pltpu.VMEM((keys, 256), BF16), pltpu.VMEM((DIM, keys), BF16),
                pltpu.VMEM((DIM, 1024), F32), pltpu.VMEM((DIM, 1024), F32)]),
        out_shape=[jax.ShapeDtypeStruct((images,) + s, t) for s, t in shapes],
        compiler_params=pltpu.CompilerParams(vmem_limit_bytes=VMEM_BYTES),
        cost_estimate=pl.CostEstimate(flops=images * 5_000_000_000, bytes_accessed=images * 4_000_000, transcendentals=0),
        name="forward",
    )(ext, row, q, top, bot, x0, kv, wts["vec"], wts["rw"], wts["wproj_t"], wts["w1_t"], wts["b1"], wts["w2_t"])


def backward_kernel(ext_ref, row_ref, hat_ref, terms_ref, att_ref, stat_ref, x0_ref, q_ref, top_ref, bot_ref, kv_ref, gvec_ref, vec_ref,
                    rwt_ref, wprojt_ref, wproj_ref, w1t_ref, w1_ref, b1_ref, w2t_ref, w2_ref,
                    dx1_ref, dq_ref, up_ref, down_ref, dkv_ref, a2_ref, a1_ref, ap_ref, av_ref, ak_ref, ar_ref,
                    ka_ref, kn_ref, vn_ref, dp_ref, qtop_ref, qbot_ref, ru_ref, rd_ref, dk_ref, dv_ref, *, offset, key_rows):
    image = pl.program_id(0)
    height = ext_ref[offset + image, 0]
    breadth = ext_ref[offset + image, 1]
    row_ok = row_ref[0] * ROWS < height
    depth = DIM + aug_rows(key_rows)
    count = pair_count(breadth)

    @pl.when(image == 0)
    def _():
        for ref in (a2_ref, a1_ref, ap_ref, av_ref, ak_ref, ar_ref, ru_ref, rd_ref):
            ref[...] = jnp.zeros_like(ref)

    values = key_tables(kv_ref, row_ref[0], key_rows, height, breadth, ka_ref, kn_ref)
    padded_values = jnp.concatenate([values, jnp.zeros((128 - DIM, values.shape[1]), F32)], axis=0)
    vn_ref[...] = jnp.transpose(padded_values).astype(BF16)
    spread_halo(qtop_ref, top_ref[0].astype(F32), 0)
    spread_halo(qbot_ref, bot_ref[0].astype(F32), 96)
    dk_ref[...] = jnp.zeros_like(dk_ref)
    dv_ref[...] = jnp.zeros_like(dv_ref)
    dp_ref[...] = jnp.zeros_like(dp_ref)

    def step(pair, carry):
        lanes = pair_lanes(pair)
        ones = jnp.ones((16, PAIR), BF16)
        attended = att_ref[0, :, lanes]
        x1 = x0_ref[0, :, lanes] + (dot(wprojt_ref[...], attended) + column(vec_ref, 9))
        hat_two, rstd_two, normed, hidden, cumulative, act, x2 = mlp_forward(x1, vec_ref, w1t_ref, b1_ref, w2t_ref)
        hat_three, rstd_three = normalized(x2)
        grad_x2 = norm_back(gvec_ref[0] * pair_mask(pair, breadth, row_ok), hat_three, rstd_three, column(vec_ref, 13))
        grad_mlp = grad_x2.astype(BF16)
        a2_ref[...] += dot_nt(grad_mlp, jnp.concatenate([act, ones], axis=0))
        slope = cumulative + hidden * (jnp.exp(hidden * hidden * -0.5) * 0.3989422804014327)
        grad_hidden = (dot(w2_ref[...], grad_mlp) * slope).astype(BF16)
        a1_ref[...] += dot_nt(jnp.concatenate([normed, ones], axis=0), grad_hidden)
        grad_normed = dot(w1_ref[...], grad_hidden)
        av_ref[0] += fold_lanes(grad_normed * hat_two)
        av_ref[1] += fold_lanes(grad_normed)
        grad_x1 = grad_x2 + norm_back(grad_normed, hat_two, rstd_two, column(vec_ref, 10))
        dx1_ref[0, :, lanes] = grad_x1
        grad_proj = grad_x1.astype(BF16)
        ap_ref[...] += dot_nt(jnp.concatenate([attended, ones], axis=0), grad_proj)
        grad_att = dot(wproj_ref[...], grad_proj)
        grad_att_low = grad_att.astype(BF16)
        hat = hat_ref[0, :, lanes]
        query = (hat * column(vec_ref, 3) + column(vec_ref, 4)).astype(BF16)
        scores = dot(kn_ref[:, :depth], jnp.concatenate([query, terms_ref[0, :, lanes]], axis=0))
        probs = jnp.exp2((scores - stat_ref[0, 0:1, lanes]) * EXP2_SCALE) * stat_ref[0, 1:2, lanes]
        dv_ref[...] += dot_nt(grad_att_low, probs.astype(BF16))
        grad_probs = dot(vn_ref[:, :DIM], grad_att_low)
        inner = jnp.sum(probs * grad_probs, axis=0, keepdims=True)
        grad_scores = (probs * (grad_probs - inner)).astype(BF16)
        dk_ref[...] += dot_nt(query, grad_scores)
        back = dot(ka_ref[: DIM + key_rows + 32, :], grad_scores)
        spread = relative_spread(back[DIM:], key_rows)
        ar_ref[pair] += dot_nt(query, spread)
        grad_query = grad_att + back[:DIM] * SCALE + dot(rwt_ref[pair], spread)
        av_ref[2] += fold_lanes(grad_query * hat)
        av_ref[3] += fold_lanes(grad_query)
        dp_ref[:, pair_lanes(pair, 256)] = norm_back(grad_query, hat, stat_ref[0, 2:3, lanes], column(vec_ref, 3))
        return carry

    lax.fori_loop(0, count, step, 0)
    for i in range(key_rows):
        slot = reverse_bits(jnp.bitwise_xor(row_ref[0], i), key_rows)
        dkv_ref[slot, 0, 0:DIM, :] = dk_ref[:, 32 * i : 32 * i + 32] * SCALE
        dkv_ref[slot, 0, DIM : 2 * DIM, :] = dv_ref[:, 32 * i : 32 * i + 32]

    def pool_step(pair, carry):
        window = dp_ref[:, pl.ds(pl.multiple_of(pair * PAIR, 128), PAIR + 512)]
        for tile in range(2):
            base = pair * PAIR + 256 * tile
            halo = pl.ds(pl.multiple_of((2 * pair + tile) * 128, 128), 128)
            query = [q_ref[0, :, pl.ds(pl.multiple_of(base + 256 + 128 * side, 128), 128)].astype(F32) for side in range(2)]
            above = rows_down(query[0], query[1], qtop_ref[:, halo])
            under = rows_up(query[0], query[1], qbot_ref[:, halo])
            sums = []
            for side in range(2):
                left, here, right = col_shifts(window, 256 + 256 * tile + 128 * side)
                shifts = (right, here, left)
                sums.append([sum(column(vec_ref, 15 + 3 * r + c) * shifts[c] for c in range(3)) for r in range(3)])
                for r, rows in enumerate((above[side], query[side], under[side])):
                    for c in range(3):
                        ak_ref[3 * r + c] += shifts[c] * rows
            zero = jnp.zeros((DIM, 128), F32)
            up = rows_up(sums[0][0], sums[1][0], zero)
            down = rows_down(sums[0][2], sums[1][2], zero)
            for side in range(2):
                dq_ref[0, :, pl.ds(pl.multiple_of(base + 128 * side, 128), 128)] = sums[side][1] + up[side] + down[side]
            ru_ref[:, halo] = up[2]
            rd_ref[:, halo] = down[2]
        return carry

    def pool_idle(pair, carry):
        for ref in (ru_ref, rd_ref):
            ref[:, pl.ds(pl.multiple_of(pair * 256, 128), 256)] = jnp.zeros((DIM, 256), F32)
        return carry

    lax.fori_loop(0, count, pool_step, 0)
    lax.fori_loop(count, PAIRS, pool_idle, 0)
    up_ref[0] = gather_halo(ru_ref, 96).astype(BF16)
    down_ref[0] = gather_halo(rd_ref, 0).astype(BF16)


def call_backward(ext, row, hat, terms, att, stat, x0, q, top, bot, kv, gvec, wts, offset):
    whole, per = specs()
    images, key_rows = q.shape[0], kv.shape[0]
    more = aug_rows(key_rows)
    keys = key_rows * 32
    window = 8 * WIN + 8 * key_rows
    heads = pl.BlockSpec((key_rows, 1, 2 * DIM, 32), lambda i, *_: (0, i, 0, 0))
    shapes = [((DIM, TOKENS), F32), ((DIM, TOKENS), F32), ((DIM, CANVAS_W), BF16), ((DIM, CANVAS_W), BF16)]
    sums = [(DIM, MLP + 16), (DIM + 16, MLP), (DIM + 16, DIM), (4, DIM, 128), (9, DIM, 128), (PAIRS, DIM, window)]
    return pl.pallas_call(
        functools.partial(backward_kernel, offset=offset, key_rows=key_rows),
        grid_spec=pltpu.PrefetchScalarGridSpec(
            num_scalar_prefetch=2, grid=(images,),
            in_specs=[
                per(DIM, TOKENS), per(more, TOKENS), per(DIM, TOKENS), per(8, TOKENS), per(DIM, TOKENS), per(DIM, PADDED),
                per(DIM, CANVAS_W), per(DIM, CANVAS_W), heads, per(DIM, 1), whole(DIM, 64), whole(PAIRS, DIM, window),
                whole(DIM, DIM), whole(DIM, DIM), whole(MLP, DIM), whole(DIM, MLP), whole(MLP, 1), whole(DIM, MLP), whole(MLP, DIM)],
            out_specs=[per(*s) for s, _ in shapes] + [heads] + [whole(*s) for s in sums],
            scratch_shapes=[
                pltpu.VMEM((DIM + more, keys), BF16), pltpu.VMEM((keys, 256), BF16), pltpu.VMEM((keys, 128), BF16),
                pltpu.VMEM((DIM, PADDED), F32)] + [pltpu.VMEM((DIM, 1024), F32)] * 4 + [pltpu.VMEM((DIM, keys), F32)] * 2),
        out_shape=[jax.ShapeDtypeStruct((images,) + s, t) for s, t in shapes]
        + [jax.ShapeDtypeStruct((key_rows, images, 2 * DIM, 32), F32)] + [jax.ShapeDtypeStruct(s, F32) for s in sums],
        compiler_params=pltpu.CompilerParams(vmem_limit_bytes=VMEM_BYTES),
        cost_estimate=pl.CostEstimate(flops=images * 12_000_000_000, bytes_accessed=images * 6_000_000, transcendentals=0),
        name="backward",
    )(ext, row, hat, terms, att, stat, x0, q, top, bot, kv, gvec, wts["vec"], wts["rw_t"], wts["wproj_t"], wts["wproj"],
      wts["w1_t"], wts["w1"], wts["b1"], wts["w2_t"], wts["w2"])


def embed_back_kernel(ext_ref, row_ref, patch_ref, dq_ref, dx1_ref, rtop_ref, rbot_ref, nsel_ref, kvt_ref, pre_ref, under_ref,
                      wp_ref, vec_ref, wqkv_ref, kexp_ref, tapt_ref,
                      aq_ref, akv_ref, apatch_ref, av_ref, ak_ref, dn_ref, rim_ref, *, offset):
    image = pl.program_id(0)
    height = ext_ref[offset + image, 0]
    breadth = ext_ref[offset + image, 1]
    row_ok = row_ref[0] * ROWS < height

    @pl.when(image == 0)
    def _():
        for ref in (aq_ref, akv_ref, apatch_ref, av_ref, ak_ref, dn_ref, rim_ref):
            ref[...] = jnp.zeros_like(ref)

    zero = jnp.zeros((2 * DIM, 32), F32)
    own = pre_ref[0]
    under = under_ref[0]
    wide = jnp.concatenate([under, under, under, zero, own, own, own, zero, own, own, own, zero], axis=1)
    taps = kvt_ref[0].astype(F32)
    ak_ref[...] += taps * wide
    grad_taps = (wide * kexp_ref[...]).astype(BF16)
    akv_ref[...] += dot_nt(jnp.concatenate([nsel_ref[0], jnp.ones((16, 384), BF16)], axis=0), grad_taps)
    grad_sel = dot(wqkv_ref[:, DIM : 3 * DIM], grad_taps)
    for k, start in enumerate((224, 0, 32)):
        part = grad_sel[:, 128 * k : 128 * k + 128]
        high = part.astype(BF16)
        low = (part - high.astype(F32)).astype(BF16)
        both = dot(jnp.concatenate([high, low], axis=0), tapt_ref[...])
        line = both[:DIM] + both[DIM:]
        for tile in range(TILES):
            dn_ref[:, 256 * tile + start : 256 * tile + start + 32] = line[:, 32 * tile : 32 * tile + 32]
    for halo_ref, start in ((rtop_ref, 0), (rbot_ref, 224)):
        line = halo_ref[0].astype(F32)
        for tile in range(TILES):
            rim_ref[:, 256 * tile + start : 256 * tile + start + 32] = line[:, 32 * tile : 32 * tile + 32]

    def step(pair, carry):
        lanes = pair_lanes(pair)
        mask = pair_mask(pair, breadth, row_ok)
        patches = patch_ref[0, :, lanes]
        x0 = (dot(wp_ref[...], patches) + column(vec_ref, 0)) * mask
        hat, rstd = normalized(x0)
        normed = (hat * column(vec_ref, 1) + column(vec_ref, 2)).astype(BF16)
        grad_q = (dq_ref[0, :, lanes] + rim_ref[:, lanes]).astype(BF16)
        aq_ref[...] += dot_nt(jnp.concatenate([normed, jnp.ones((16, PAIR), BF16)], axis=0), grad_q)
        grad_n = dot(wqkv_ref[:, 0:DIM], grad_q) + dn_ref[:, lanes]
        av_ref[1] += fold_lanes(grad_n * hat)
        av_ref[2] += fold_lanes(grad_n)
        grad_embed = (dx1_ref[0, :, lanes] + norm_back(grad_n, hat, rstd, column(vec_ref, 1))) * mask
        av_ref[0] += fold_lanes(grad_embed)
        high = grad_embed.astype(BF16)
        low = (grad_embed - high.astype(F32)).astype(BF16)
        apatch_ref[...] += dot_nt(jnp.concatenate([high, low], axis=0), patches)
        return carry

    lax.fori_loop(0, pair_count(breadth), step, 0)


def call_embed_back(ext, row, patches, dq, dx1, rtop, rbot, nsel, kvt, pre, under, consts, wts, offset):
    whole, per = specs()
    images = dq.shape[0]
    sums = [(DIM + 16, DIM), (DIM + 16, 2 * DIM), (2 * DIM, PATCH_ROWS), (3, DIM, 128), (2 * DIM, 384)]
    return pl.pallas_call(
        functools.partial(embed_back_kernel, offset=offset),
        grid_spec=pltpu.PrefetchScalarGridSpec(
            num_scalar_prefetch=2, grid=(images,),
            in_specs=[
                per(PATCH_ROWS, TOKENS), per(DIM, TOKENS), per(DIM, TOKENS), per(DIM, CANVAS_W), per(DIM, CANVAS_W),
                per(DIM, 384), per(2 * DIM, 384), per(2 * DIM, 32), per(2 * DIM, 32),
                whole(DIM, PATCH_ROWS), whole(DIM, 64), whole(DIM, 3 * DIM), whole(2 * DIM, 384), whole(128, CANVAS_W)],
            out_specs=[whole(*s) for s in sums],
            scratch_shapes=[pltpu.VMEM((DIM, TOKENS), F32), pltpu.VMEM((DIM, TOKENS), F32)]),
        out_shape=[jax.ShapeDtypeStruct(s, F32) for s in sums],
        compiler_params=pltpu.CompilerParams(vmem_limit_bytes=VMEM_BYTES),
        cost_estimate=pl.CostEstimate(flops=images * 3_000_000_000, bytes_accessed=images * 3_000_000, transcendentals=0),
        name="embed_back",
    )(ext, row, patches, dq, dx1, rtop, rbot, nsel, kvt, pre, under, wts["wp"], wts["vec"], wts["wqkv"], wts["kexp"], consts["tap_t"])


def bit_count(size):
    return size.bit_length() - 1


def swap(value, axis, bit):
    size = lax.axis_size(axis)
    return lax.ppermute(value, axis, [(i, i ^ (1 << bit)) for i in range(size)])


def shifted(value, axis, step):
    size = lax.axis_size(axis)
    pairs = [(i, i + step) for i in range(size) if 0 <= i + step < size]
    return lax.ppermute(value, axis, pairs)


def summed(value, axis):
    for bit in range(bit_count(lax.axis_size(axis))):
        value = value + swap(value, axis, bit)
    return value


def gather_slots(value, axis):
    value = value[None]
    for bit in reversed(range(bit_count(lax.axis_size(axis)))):
        value = jnp.concatenate([value, swap(value, axis, bit)], axis=0)
    return value


def scatter_slots(value, axis):
    for bit in range(bit_count(lax.axis_size(axis))):
        half = value.shape[0] // 2
        value = value[:half] + swap(value[half:], axis, bit)
    return value[0]


def gather_params(value):
    dims = []
    for axis in ("img", "row"):
        index = lax.axis_index(axis)
        for bit in reversed(range(bit_count(lax.axis_size(axis)))):
            other = swap(value, axis, bit)
            mine_second = (index >> bit) & 1 == 1
            value = jnp.stack([jnp.where(mine_second, other, value), jnp.where(mine_second, value, other)])
            dims.append((axis, bit))
    dims = dims[::-1]
    wanted = [("img", b) for b in reversed(range(bit_count(lax.axis_size("img"))))]
    wanted += [("row", b) for b in reversed(range(bit_count(lax.axis_size("row"))))]
    order = [dims.index(d) for d in wanted]
    value = jnp.transpose(value, order + [value.ndim - 2, value.ndim - 1])
    return value.reshape(-1)


def scatter_grads(flat):
    rows, imgs = lax.axis_size("row"), lax.axis_size("img")
    names = [("img", b) for b in reversed(range(bit_count(imgs)))] + [("row", b) for b in reversed(range(bit_count(rows)))]
    leaf = flat.shape[0] // (rows * imgs)
    value = flat.reshape((2,) * len(names) + (leaf // 128, 128))
    for axis, bits in (("row", range(bit_count(rows))), ("img", range(bit_count(imgs)))):
        index = lax.axis_index(axis)
        for bit in bits:
            place = names.index((axis, bit))
            names.pop(place)
            own = (index >> bit) & 1
            keep = lax.dynamic_index_in_dim(value, own, place, False)
            send = lax.dynamic_index_in_dim(value, 1 - own, place, False)
            value = keep + swap(send, axis, bit)
    return value.reshape(leaf)


def segment_list(canvas_rows, canvas_cols):
    return [
        ("w_patch", (3 * PATCH * PATCH, DIM)),
        ("w_qkv", (DIM, 3 * DIM)),
        ("w_proj", (DIM, DIM)),
        ("w_fc1", (DIM, MLP)),
        ("w_fc2", (MLP, DIM)),
        ("w_head", (DIM, CLASSES)),
        ("rel_rows", (2 * canvas_rows - 8, DIM)),
        ("rel_cols", (2 * canvas_cols - 8, DIM)),
        ("small", (49, DIM)),
        ("b_head", (CLASSES,)),
    ]


def unpack(flat_vec, segments):
    pieces = {}
    position = 0
    for seg_name, seg_shape in segments:
        entries = int(np.prod(seg_shape))
        pieces[seg_name] = flat_vec[position : position + entries].reshape(seg_shape)
        position += entries
    return pieces


def patch_rows(weight):
    taps = jnp.pad(weight.reshape(PATCH, PATCH, 3, DIM), ((0, 1), (0, 0), (0, 1), (0, 0)))
    parts = []
    for piece in (taps[:, 3:7], taps[:, 0:3]):
        phases = piece.shape[1]
        parts.append(jnp.transpose(piece.reshape(2, 4, phases, 4, DIM), (0, 2, 1, 3, 4)).reshape(32 * phases, DIM))
    return jnp.concatenate(parts, axis=0)


def patch_rows_back(grad):
    rows = grad.T
    parts = []
    for piece, phases in ((rows[128:], 3), (rows[:128], 4)):
        taps = jnp.transpose(piece.reshape(2, phases, 4, 4, DIM), (0, 2, 1, 3, 4)).reshape(8, phases, 4, DIM)
        parts.append(taps[:PATCH, :, :3])
    return jnp.concatenate(parts, axis=1).reshape(3 * PATCH * PATCH, DIM)


def relative_windows(rel_rows, rel_cols, row_index, key_rows):
    offsets = jnp.flip(rel_cols.reshape(-1, 8, DIM), 0)
    offsets = jnp.transpose(jnp.pad(offsets, ((0, 1), (0, 0), (0, 0))), (1, 0, 2))
    blocks = rel_rows.reshape(2 * key_rows - 1, 8, DIM)
    rows = jnp.transpose(jnp.flip(lax.dynamic_slice_in_dim(blocks, row_index, key_rows, 0), 0), (1, 0, 2))
    rows = rows.reshape(8 * key_rows, DIM)
    windows = []
    for pair in range(PAIRS):
        cols = offsets[:, 24 - 8 * pair : 24 - 8 * pair + WIN].reshape(8 * WIN, DIM)
        windows.append(jnp.concatenate([cols, rows], axis=0))
    return jnp.stack(windows)


def relative_windows_back(grad, row_index, key_rows):
    grad = jnp.transpose(grad, (0, 2, 1))
    cols = grad[:, : 8 * WIN].reshape(PAIRS, 8, WIN, DIM)
    total = 0.0
    for pair in range(PAIRS):
        start = 24 - 8 * pair
        total = total + jnp.pad(cols[pair], ((0, 0), (start, 64 - start - WIN), (0, 0)))
    rel_cols = jnp.flip(jnp.transpose(total[:, :63], (1, 0, 2)), 0).reshape(-1, DIM)
    rows = jnp.sum(grad[:, 8 * WIN :], axis=0).reshape(8, key_rows, DIM)
    rows = jnp.flip(jnp.transpose(rows, (1, 0, 2)), 0)
    blocks = lax.dynamic_update_slice_in_dim(jnp.zeros((2 * key_rows - 1, 8, DIM), F32), rows, row_index, 0)
    return blocks.reshape(-1, DIM), rel_cols


def prepare(weights, row_index, key_rows):
    small = weights["small"]
    vec = jnp.pad(small.astype(F32).T, ((0, 0), (0, 15)))
    kernels = small[9:27].reshape(2, 3, 3, DIM).astype(F32)
    keep = np.ones((3, 4, 32), np.float32)
    keep[:, 3] = 0.0
    keep[:, 0, 0] = 0.0
    expanded = jnp.pad(jnp.transpose(kernels, (0, 3, 1, 2)), ((0, 0), (0, 0), (0, 0), (0, 1)))
    kexp = (expanded[..., None] * keep).reshape(2 * DIM, 384)
    windows = relative_windows(weights["rel_rows"], weights["rel_cols"], row_index, key_rows)
    return {
        "vec": vec,
        "kexp": kexp,
        "wp": patch_rows(weights["w_patch"]).T,
        "wqkv": weights["w_qkv"],
        "wqkv_t": weights["w_qkv"].T,
        "b_kv": small[43:45].astype(F32).reshape(2 * DIM, 1),
        "wproj": weights["w_proj"],
        "wproj_t": weights["w_proj"].T,
        "w1": weights["w_fc1"],
        "w1_t": weights["w_fc1"].T,
        "b1": small[45:49].astype(F32).reshape(MLP, 1),
        "w2": weights["w_fc2"],
        "w2_t": weights["w_fc2"].T,
        "rw": windows,
        "rw_t": jnp.transpose(windows, (0, 2, 1)),
    }


def image_loss(pooled, head_w, head_b, teacher, labels, image_total):
    logits = jnp.dot(pooled, head_w, precision=HIGHEST_PREC) + head_b
    log_student = jax.nn.log_softmax(logits, axis=-1)
    log_teacher = jax.nn.log_softmax(teacher, axis=-1)
    onehot = (jnp.arange(CLASSES)[None, :] == labels[:, None]).astype(F32)
    per_image = jnp.sum(jnp.exp(log_teacher) * (log_teacher - log_student), axis=-1) - jnp.sum(onehot * log_student, axis=-1)
    return jnp.sum(per_image) / image_total


def body(flat_params, first_moment, second_moment, pixels, extents, labels, teacher):
    key_rows = lax.axis_size("row")
    row_index = lax.axis_index("row")
    row_lead = row_index == 0
    segments = segment_list(ROWS * key_rows, CANVAS_W)
    full_params = gather_params(flat_params.astype(BF16).reshape(-1, 128))
    weights = unpack(full_params, segments)
    wts = prepare(weights, row_index, key_rows)
    tap = tap_matrix()
    consts = {"perm": jnp.asarray(deinterleave_matrix(), BF16), "tap": jnp.asarray(tap, BF16), "tap_t": jnp.asarray(tap.T, BF16)}
    vectors = weights["small"][27:42].astype(F32)
    row = row_index.astype(jnp.int32).reshape(1)
    images = pixels.shape[0]
    parts = 2
    size = images // parts
    image_total = images * lax.axis_size("img") * 1.0
    head_w = weights["w_head"].astype(F32)
    head_b = weights["b_head"].astype(F32)

    saved = []
    for part in range(parts):
        patches, x0, q, first, last, nsel, kvt, below, own = call_embed(extents, row, pixels, consts, wts, size, part * size)
        top = shifted(last, "row", 1)
        bot = shifted(first, "row", -1)
        got = shifted(below, "row", 1)
        kv = gather_slots(call_pool_norm(own, got, wts["vec"]), "row")
        saved.append(dict(patches=patches, x0=x0, q=q, top=top, bot=bot, nsel=nsel, kvt=kvt, own=own, got=got, kv=kv))
    for part in range(parts):
        s = saved[part]
        s["fwd"] = call_forward(extents, row, s["q"], s["top"], s["bot"], s["x0"], s["kv"], wts, part * size)
    total = {}

    def add(name, value):
        total[name] = total[name] + value if name in total else value

    loss_value = 0.0
    for part in range(parts):
        s = saved[part]
        hat, terms, att, stat, pool = s["fwd"]
        local = jnp.sum(pool, axis=-1)
        everywhere = summed(local, "row")
        ext = extents[part * size : part * size + size]
        counts = (ext[:, 0] * ext[:, 1]).astype(F32)[:, None]
        pooled = (everywhere * vectors[13] + counts * vectors[14]) / counts

        def loss_of(pooled_now, w, b):
            return image_loss(pooled_now, w, b, teacher[part * size : part * size + size], labels[part * size : part * size + size], image_total)

        loss_part, loss_back = jax.vjp(loss_of, pooled, head_w, head_b)
        grad_pooled, grad_w, grad_b = loss_back(jnp.ones_like(loss_part))
        loss_value = loss_value + loss_part
        add("w_head", grad_w)
        add("b_head", grad_b)
        gvec = grad_pooled / counts
        local_count = jnp.where(row_index * ROWS < ext[:, 0], ROWS * ext[:, 1], 0).astype(F32)[:, None]
        add("g_three", jnp.sum(gvec * local, axis=0))
        add("b_three", jnp.sum(gvec * local_count, axis=0))
        s["bwd"] = call_backward(extents, row, hat, terms, att, stat, s["x0"], s["q"], s["top"], s["bot"], s["kv"], gvec[:, :, None], wts, part * size)
    for part in range(parts):
        s = saved[part]
        dx1, dq, up, down, dkv, a2, a1, ap, av, ak, ar = s["bwd"]
        for name, value in (("a2", a2), ("a1", a1), ("ap", ap), ("av", av), ("ak", ak), ("ar", ar)):
            add(name, value)
        rtop = shifted(down, "row", 1)
        rbot = shifted(up, "row", -1)
        grad_kv = scatter_slots(dkv, "row")
        pre, pool_sums = call_pool_back(s["own"], s["got"], grad_kv, wts["vec"])
        add("pool_sums", pool_sums)
        under = shifted(pre, "row", -1)
        aq, akv, apatch, av1, akt = call_embed_back(
            extents, row, s["patches"], dq, dx1, rtop, rbot, s["nsel"], s["kvt"], pre, under, consts, wts, part * size)
        for name, value in (("aq", aq), ("akv", akv), ("apatch", apatch), ("av1", av1), ("akt", akt)):
            add(name, value)

    t = total
    lead = jnp.where(row_lead, 1.0, 0.0)
    av, av1 = jnp.sum(t["av"], axis=-1), jnp.sum(t["av1"], axis=-1)
    pool_sums = jnp.sum(t["pool_sums"], axis=-1)
    rel_rows, rel_cols = relative_windows_back(t["ar"], row_index, key_rows)
    taps = jnp.sum(t["akt"].reshape(2, DIM, 3, 4, 32)[:, :, :, :3], axis=-1)
    kernels = jnp.concatenate([jnp.sum(t["ak"], axis=-1), jnp.transpose(taps, (0, 2, 3, 1)).reshape(18, DIM)], axis=0)
    grad_vectors = jnp.stack([
        av1[0], av1[1], av1[2], av[2], av[3], pool_sums[0], pool_sums[1], pool_sums[2], pool_sums[3],
        t["ap"][DIM], av[0], av[1], t["a2"][:, MLP], t["g_three"], t["b_three"]])
    pieces = [
        patch_rows_back(t["apatch"][:DIM] + t["apatch"][DIM:]),
        jnp.concatenate([t["aq"][:DIM], t["akv"][:DIM]], axis=1),
        t["ap"][:DIM],
        t["a1"][:DIM],
        t["a2"][:, :MLP].T,
        t["w_head"] * lead,
        rel_rows,
        rel_cols,
        kernels,
        grad_vectors,
        t["aq"][DIM],
        t["akv"][DIM],
        t["a1"][DIM],
        t["b_head"] * lead,
    ]
    joined = jnp.concatenate([piece.reshape(-1) for piece in pieces])
    grad_flat = jnp.pad(joined, (0, full_params.shape[0] - joined.shape[0]))
    grad_shard = scatter_grads(grad_flat)
    norm_sq = summed(jnp.sum(grad_shard * grad_shard), "row")
    both = summed(jnp.stack([norm_sq, loss_value]), "img")
    grad_norm = jnp.sqrt(both[0])
    clip_factor = jnp.minimum(1.0, CLIP_NORM / (grad_norm + 1e-06))
    clipped = grad_shard * clip_factor
    moment_one = BETA_FIRST * first_moment + (1.0 - BETA_FIRST) * clipped
    moment_two = BETA_SECOND * second_moment + (1.0 - BETA_SECOND) * clipped * clipped
    fix_one = 1.0 - BETA_FIRST**STEP
    fix_two = 1.0 - BETA_SECOND**STEP
    update = moment_one / fix_one / (jnp.sqrt(moment_two / fix_two) + ADAM_EPS) + WEIGHT_DECAY * flat_params
    new_params = flat_params - LEARN_RATE * update
    return (new_params, moment_one, moment_two, grad_norm, both[1])


def solution(mesh):
    placed = (
        P(("img", "row")),
        P(("img", "row")),
        P(("img", "row")),
        P("img", "row", None, None, None),
        P("img", None),
        P("img"),
        P("img", None),
    )
    return jax.shard_map(
        body,
        mesh=mesh,
        in_specs=placed,
        out_specs=(P(("img", "row")), P(("img", "row")), P(("img", "row")), P(), P()),
        check_vma=False,
    )
```

```python
import functools

import jax
import jax.numpy as jnp
import numpy as np
from jax import lax
from jax.experimental import pallas as pl
from jax.experimental.pallas import tpu as pltpu
from jax.sharding import PartitionSpec as P

DIM = 96
MLP = 384
CLASSES = 1000
PATCH = 7
ROWS = 8
STEP = 7
CANVAS_W = 256

HIGHEST_PREC = lax.Precision.HIGHEST
CLIP_NORM = 0.02
LEARN_RATE = 0.05
WEIGHT_DECAY = 0.05
BETA_FIRST = 0.5
BETA_SECOND = 0.5
ADAM_EPS = 1e-08
NORM_EPS = 1e-06
NEG_FILL = -1e30

F32 = jnp.float32
BF16 = jnp.bfloat16
SCALE = DIM ** (-0.5)
EXP2_SCALE = SCALE * 1.4426950408889634

TOKENS = ROWS * CANVAS_W
PAIR = 512
PAIRS = TOKENS // PAIR
TILES = CANVAS_W // 32
GROUP = 2
PADDED = TOKENS + 512
WIN = 40
PATCH_ROWS = 224
VMEM_BYTES = 56 * 1024 * 1024


def deinterleave_matrix():
    out = np.zeros((4, 128, 4, 4, 32), np.float32)
    for row in range(4):
        for phase in range(4):
            for col in range(32):
                out[row, 4 * col + phase, phase, row, col] = 1.0
    return out.reshape(512, 512)


def tap_matrix():
    out = np.zeros((CANVAS_W, 128), np.float32)
    for tap in range(3):
        for key in range(32):
            col = 8 * key + tap - 1
            if col >= 0:
                out[col, tap * 32 + key] = 1.0
    return out


def dot(a, b):
    return jnp.dot(a, b, preferred_element_type=F32)


def dot_nt(a, b):
    return lax.dot_general(a, b, (((1,), (1,)), ((), ())), preferred_element_type=F32)


def normalized(x):
    mean = jnp.sum(x, axis=0, keepdims=True) * (1.0 / DIM)
    centered = x - mean
    var = jnp.sum(centered * centered, axis=0, keepdims=True) * (1.0 / DIM)
    rstd = lax.rsqrt(var + NORM_EPS)
    return centered * rstd, rstd


def norm_back(grad, hat, rstd, gain):
    inner = grad * gain
    mean_one = jnp.sum(inner, axis=0, keepdims=True) * (1.0 / DIM)
    mean_two = jnp.sum(inner * hat, axis=0, keepdims=True) * (1.0 / DIM)
    return rstd * (inner - mean_one - hat * mean_two)


def by_lanes(fn, *arrays):
    parts = [fn(k, *(a[:, 128 * k : 128 * k + 128] for a in arrays)) for k in range(arrays[0].shape[1] // 128)]
    return tuple(jnp.concatenate(column, axis=1) for column in zip(*parts))


def by_blocks(fn, height, *arrays):
    rows = []
    for top in range(0, arrays[0].shape[0], height):
        rows.append(by_lanes(lambda k, *block: fn(slice(top, top + height), *block), *(a[top : top + height] for a in arrays)))
    return tuple(jnp.concatenate(column, axis=0) for column in zip(*rows))


def fold_lanes(x):
    total = x[:, 0:128]
    for k in range(1, x.shape[1] // 128):
        total = total + x[:, 128 * k : 128 * k + 128]
    return total


def place_of(index):
    return index + 27 if index < 15 else index - 15 if index < 42 else index


def column(vec_ref, index):
    place = place_of(index)
    return vec_ref[:, place : place + 1]


def fill_wide(wide_ref, vec_ref, indices):
    for k, index in enumerate(indices):
        wide_ref[k] = jnp.broadcast_to(column(vec_ref, index), (DIM, 128))


def wide(wide_ref, k, width=PAIR):
    return jnp.concatenate([wide_ref[k]] * (width // 128), axis=1)


def lane_ids(width, rows=1):
    return lax.broadcasted_iota(jnp.int32, (rows, width), 1)


def pair_mask(pair, breadths, row_oks):
    lane = lane_ids(PAIR)
    col = pair * 64 + (lane >> 8) * 32 + (lane & 31)
    return jnp.concatenate([jnp.where((col < w) & ok, 1.0, 0.0).astype(F32) for w, ok in zip(breadths, row_oks)], axis=1)


def pair_lanes(pair, base=0):
    return pl.ds(pl.multiple_of(pair * PAIR + base, 128), PAIR)


def load_pair(ref, pair):
    lanes = pair_lanes(pair)
    return jnp.concatenate([ref[g, :, lanes] for g in range(GROUP)], axis=1)


def store_pair(ref, pair, value, base=0):
    for g in range(GROUP):
        ref[g, :, pair_lanes(pair, base)] = value[:, PAIR * g : PAIR * g + PAIR]


def by_image(value):
    return [value[:, PAIR * g : PAIR * g + PAIR] for g in range(GROUP)]


def pair_count(breadths):
    widest = breadths[0]
    for breadth in breadths[1:]:
        widest = jnp.maximum(widest, breadth)
    return jnp.minimum((widest >> 6) + 1, PAIRS)


def group_extents(ext_ref, row_ref, offset):
    images = [pl.program_id(0) * GROUP + g for g in range(GROUP)]
    heights = [ext_ref[offset + image, 0] for image in images]
    breadths = [ext_ref[offset + image, 1] for image in images]
    return images, heights, breadths, [row_ref[0] * ROWS < height for height in heights]


def col_shifts(window, base):
    lane = lane_ids(128, window.shape[0])
    here = window[:, base : base + 128]
    before = window[:, base - 256 : base - 128]
    after = window[:, base + 256 : base + 384]
    left = jnp.where((lane & 31) == 0, pltpu.roll(before, 97, 1), pltpu.roll(here, 1, 1))
    right = jnp.where((lane & 31) == 31, pltpu.roll(after, 31, 1), pltpu.roll(here, 127, 1))
    return left, here, right


def rows_down(first, second, entering):
    lane = lane_ids(128, first.shape[0])
    a, b = pltpu.roll(first, 32, 1), pltpu.roll(second, 32, 1)
    return jnp.where(lane < 32, entering, a), jnp.where(lane < 32, a, b), b


def rows_up(first, second, entering):
    lane = lane_ids(128, first.shape[0])
    a, b = pltpu.roll(first, 96, 1), pltpu.roll(second, 96, 1)
    return jnp.where(lane >= 96, b, a), jnp.where(lane >= 96, entering, b), a


def spread_halo(dst_ref, halo, target):
    for tile in range(TILES):
        block = halo[:, 128 * (tile // 4) : 128 * (tile // 4) + 128]
        shift = (target - 32 * (tile % 4)) % 128
        dst_ref[:, 128 * tile : 128 * tile + 128] = pltpu.roll(block, shift, 1) if shift else block


def store_lanes(dst_ref, value, image):
    place = image & 3
    lane = lane_ids(128, value.shape[0])
    dst_ref[...] = jnp.where((lane >> 5) == place, pltpu.roll(value, place * 32, 1), dst_ref[...])


def take_lanes(value, image, target):
    return pltpu.roll(value, (4 + target - (image & 3)) * 32 & 127, 1)


def gather_halo(src_ref, target):
    lane = lane_ids(128, DIM)
    blocks = []
    for half in range(2):
        total = None
        for k in range(4):
            tile = 4 * half + k
            block = src_ref[:, 128 * tile : 128 * tile + 128]
            shift = (32 * k - target) % 128
            block = pltpu.roll(block, shift, 1) if shift else block
            total = block if total is None else jnp.where((lane >> 5) == k, block, total)
        blocks.append(total)
    return jnp.concatenate(blocks, axis=1)


def reverse_bits(value, count):
    result = 0
    for bit in range(count.bit_length() - 1):
        result = result * 2 + ((value >> bit) & 1)
    return result


def key_tables(kv_ref, image, key_rows, height, breadth, ka_ref, kn_ref):
    lane = lane_ids(128, 2 * DIM)
    blocks = []
    for i in range(0, key_rows, 4):
        block = take_lanes(kv_ref[i].astype(F32), image, 0)
        for k in range(1, 4):
            block = jnp.where((lane >> 5) == k, take_lanes(kv_ref[i + k].astype(F32), image, k), block)
        blocks.append(block)
    both = jnp.concatenate(blocks, axis=1)
    total = key_rows * 32
    more = aug_rows(key_rows)
    rank = lax.broadcasted_iota(jnp.int32, (more, total), 0)
    key = lax.broadcasted_iota(jnp.int32, (more, total), 1)
    key_r, key_c = key >> 5, key & 31
    half = key_rows + 32
    low = rank >= half
    rank_in = jnp.where(low, rank - half, rank)
    hit = rank_in == jnp.where(rank_in < key_rows, key_r, key_c + key_rows)
    invalid = (key_r * ROWS >= height) | (key_c * ROWS >= breadth)
    table = jnp.where(rank < 2 * half, jnp.where(hit, 1.0, 0.0), 0.0)
    table = jnp.where((rank == 2 * half) & invalid, NEG_FILL, table)
    full = jnp.concatenate([both[:DIM], table, jnp.zeros((256 - DIM - more, total), F32)], axis=0)
    ka_ref[...] = full[: DIM + more].astype(BF16)
    kn_ref[...] = jnp.transpose(full).astype(BF16)
    return both[DIM:]


def aug_rows(key_rows):
    return 2 * key_rows + 64 + 16


def embed_kernel(ext_ref, row_ref, order_ref, *refs, offset):
    pix_refs, tail_refs, refs = refs[:GROUP], refs[GROUP : 2 * GROUP], refs[2 * GROUP :]
    (perm_ref, tap_ref, wp_ref, wqkv_ref, vec_ref, bkv_ref, kexp_ref,
     patch_ref, x0_ref, q_ref, first_ref, last_ref, nsel_ref, kvt_ref, below_ref, own_ref, s_ref, n_ref, wide_ref) = refs
    images, heights, breadths, row_oks = group_extents(ext_ref, row_ref, offset)

    @pl.when(pl.program_id(0) == 0)
    def _():
        s_ref[...] = jnp.zeros_like(s_ref)
        fill_wide(wide_ref, vec_ref, [0, 1, 2, 42])

    lane = lane_ids(1024, 144)
    for g in range(GROUP):
        for r in range(ROWS):
            for a in range(4):
                s_ref[16 * r + 4 * a : 16 * r + 4 * a + 3, :] = pix_refs[g][0, r, a].astype(F32)
        for a in range(3):
            s_ref[128 + 4 * a : 128 + 4 * a + 3, :] = tail_refs[g][0, 0, a].astype(F32)
        for shifted in range(2):
            rows = s_ref[...]
            if shifted:
                rows = jnp.where(lane < 4, 0.0, pltpu.roll(rows, 4, 1))
            rows = rows.astype(BF16)
            stack = []
            for start in (0, 4, 1, 5):
                for tile in range(TILES):
                    stack.append(jnp.concatenate(
                        [rows[16 * (start + k) : 16 * (start + k) + 16, 128 * tile : 128 * tile + 128] for k in range(4)], axis=1))
            out = dot(jnp.concatenate(stack, axis=0), perm_ref[...]).astype(BF16)
            for which, start in enumerate((0, 4, 1, 5)):
                half, side = which // 2, which % 2
                for tile in range(TILES):
                    block = out[128 * which + 16 * tile : 128 * which + 16 * tile + 16]
                    for phase in range(shifted, 4):
                        top = 64 * half + 16 * phase if not shifted else 128 + 48 * half + 16 * (phase - 1)
                        patch_ref[g, top : top + 16, 256 * tile + 128 * side : 256 * tile + 128 * side + 128] = block[
                            :, 128 * phase : 128 * phase + 128]

    count = pair_count(breadths)

    def active(pair, carry):
        def first_norm(k, embed, mask):
            x0 = (embed + wide_ref[0]) * mask
            hat, _ = normalized(x0)
            return x0, (hat * wide_ref[1] + wide_ref[2]).astype(BF16)

        x0, normed = by_lanes(first_norm, dot(wp_ref[...], load_pair(patch_ref, pair)), pair_mask(pair, breadths, row_oks))
        store_pair(x0_ref, pair, x0)
        store_pair(n_ref, pair, normed.astype(F32))
        (query,) = by_lanes(lambda k, out: ((out + wide_ref[3]).astype(BF16),), dot(wqkv_ref[0:DIM, :], normed))
        store_pair(q_ref, pair, query, 256)
        return carry

    def idle(pair, carry):
        for g in range(GROUP):
            n_ref[g, :, pair_lanes(pair)] = jnp.zeros((DIM, PAIR), F32)
            q_ref[g, :, pair_lanes(pair, 256)] = jnp.zeros((DIM, PAIR), BF16)
        return carry

    lax.fori_loop(0, count, active, 0)
    lax.fori_loop(count, PAIRS, idle, 0)
    for g in range(GROUP):
        q_ref[g, :, 0:256] = jnp.zeros((DIM, 256), BF16)
        q_ref[g, :, 256 + TOKENS : 512 + TOKENS] = jnp.zeros((DIM, 256), BF16)
    rows = []
    for start in (224, 0, 32):
        rows.append(jnp.concatenate(
            [n_ref[g, :, 256 * t + start : 256 * t + start + 32] for g in range(GROUP) for t in range(TILES)], axis=1).astype(BF16))
    edge = dot(wqkv_ref[0:DIM, :], jnp.concatenate(rows[:2], axis=1))
    (edge,) = by_lanes(lambda k, out: ((out + wide_ref[3]).astype(BF16),), edge)
    nsel = dot(jnp.concatenate([row[:, CANVAS_W * g : CANVAS_W * g + CANVAS_W] for g in range(GROUP) for row in rows], axis=0), tap_ref[...])
    nsel = jnp.concatenate([nsel[DIM * k : DIM * k + DIM] for k in range(3 * GROUP)], axis=1).astype(BF16)
    taps = (dot(wqkv_ref[DIM : 3 * DIM, :], nsel) + bkv_ref[...]).astype(BF16)
    for g in range(GROUP):
        last_ref[g] = edge[:, CANVAS_W * g : CANVAS_W * g + CANVAS_W]
        first_ref[g] = edge[:, CANVAS_W * (GROUP + g) : CANVAS_W * (GROUP + g) + CANVAS_W]
        nsel_ref[g] = nsel[:, 384 * g : 384 * g + 384]
        kvt_ref[g] = taps[:, 384 * g : 384 * g + 384]
        product = taps[:, 384 * g : 384 * g + 384].astype(F32) * kexp_ref[...]
        sums = []
        for k in range(3):
            part = product[:, 128 * k : 128 * k + 128]
            sums.append(part + pltpu.roll(part, 96, 1) + pltpu.roll(part, 64, 1))
        store_lanes(below_ref, sums[0], images[g])
        store_lanes(own_ref, sums[1] + sums[2], images[g])


def key_lanes(*lead):
    return pl.BlockSpec(lead + (128,), lambda i, *_: (0,) * len(lead) + (i * GROUP >> 2,))


def specs():
    whole = lambda *shape: pl.BlockSpec(shape, lambda i, *_: (0,) * len(shape))
    per = lambda *shape: pl.BlockSpec((GROUP,) + shape, lambda i, *_: (i,) + (0,) * len(shape))
    return whole, per


def call_embed(ext, row, order, pixels, consts, wts, images, offset):
    whole, per = specs()
    shapes = [
        ((PATCH_ROWS, TOKENS), BF16), ((DIM, TOKENS), F32), ((DIM, PADDED), BF16), ((DIM, CANVAS_W), BF16),
        ((DIM, CANVAS_W), BF16), ((DIM, 384), BF16), ((2 * DIM, 384), BF16)]
    pix = [pl.BlockSpec((1, ROWS, 4, 3, 1024), lambda i, ext, row, order, g=g: (order[offset + i * GROUP + g], 0, 0, 0, 0)) for g in range(GROUP)]
    tail = [pl.BlockSpec((1, 1, 4, 3, 1024), lambda i, ext, row, order, g=g: (order[offset + i * GROUP + g], ROWS - 1, 1, 0, 0)) for g in range(GROUP)]
    return pl.pallas_call(
        functools.partial(embed_kernel, offset=offset),
        grid_spec=pltpu.PrefetchScalarGridSpec(
            num_scalar_prefetch=3, grid=(images // GROUP,),
            in_specs=pix + tail + [
                whole(512, 512), whole(CANVAS_W, 128), whole(DIM, PATCH_ROWS), whole(3 * DIM, DIM), whole(DIM, 64),
                whole(2 * DIM, 1), whole(2 * DIM, 384)],
            out_specs=[per(*s) for s, _ in shapes] + [key_lanes(2 * DIM)] * 2,
            scratch_shapes=[pltpu.VMEM((144, 1024), F32), pltpu.VMEM((GROUP, DIM, TOKENS), F32), pltpu.VMEM((4, DIM, 128), F32)]),
        out_shape=[jax.ShapeDtypeStruct((images,) + s, t) for s, t in shapes]
        + [jax.ShapeDtypeStruct((2 * DIM, 32 * images), F32)] * 2,
        compiler_params=pltpu.CompilerParams(vmem_limit_bytes=VMEM_BYTES),
        cost_estimate=pl.CostEstimate(flops=images * 2_000_000_000, bytes_accessed=images * 4_000_000, transcendentals=0),
        name="embed",
    )(ext, row, order, *[pixels] * (2 * GROUP), consts["perm"], consts["tap"], wts["wp"], wts["wqkv_t"], wts["vec"], wts["b_kv"], wts["kexp"])


def pool_norm_kernel(own_ref, got_ref, vec_ref, kv_ref):
    for member in range(2):
        part = slice(member * DIM, member * DIM + DIM)
        hat, _ = normalized(own_ref[part] + got_ref[part])
        kv_ref[part] = (hat * column(vec_ref, 5 + 2 * member) + column(vec_ref, 6 + 2 * member)).astype(BF16)


def call_pool_norm(own, got, vec):
    return pl.pallas_call(
        pool_norm_kernel, out_shape=jax.ShapeDtypeStruct(own.shape, BF16), name="pool_norm",
        cost_estimate=pl.CostEstimate(flops=own.size * 10, bytes_accessed=own.size * 10, transcendentals=0))(own, got, vec)


def pool_back_kernel(own_ref, got_ref, grad_ref, vec_ref, pre_ref, sums_ref):
    for member in range(2):
        part = slice(member * DIM, member * DIM + DIM)
        hat, rstd = normalized(own_ref[part] + got_ref[part])
        grad = grad_ref[part].astype(F32)
        pre_ref[part] = norm_back(grad, hat, rstd, column(vec_ref, 5 + 2 * member))
        sums_ref[2 * member] = fold_lanes(grad * hat)
        sums_ref[2 * member + 1] = fold_lanes(grad)


def call_pool_back(own, got, grad, vec):
    return pl.pallas_call(
        pool_back_kernel,
        out_shape=[jax.ShapeDtypeStruct(own.shape, F32), jax.ShapeDtypeStruct((4, DIM, 128), F32)], name="pool_back",
        cost_estimate=pl.CostEstimate(flops=own.size * 20, bytes_accessed=own.size * 16, transcendentals=0))(own, got, grad, vec)


def lane_bit(lane, bit):
    return (lane & bit) != 0


def relative_terms(block, products, key_rows):
    lane = lane_ids(128, WIN)
    parts = [products[WIN * s : WIN * s + WIN] for s in range(8)]
    for bit in (1, 2, 4):
        chosen = lane_bit(lane, bit)
        parts = [jnp.where(chosen, parts[2 * k + 1], parts[2 * k]) for k in range(len(parts) // 2)]
    by_col = parts[0]
    for bit, step in ((8, 1), (16, 2)):
        by_col = jnp.where(lane_bit(lane, bit), by_col, pltpu.roll(by_col, WIN - step, 0))
    by_col = by_col[0:32] if block & 2 else by_col[4:36]
    lane = lane_ids(128, key_rows)
    rows = products[8 * WIN :]
    parts = [rows[key_rows * r : key_rows * r + key_rows] for r in range(4 * (block & 1), 4 * (block & 1) + 4)]
    for bit in (32, 64):
        chosen = lane_bit(lane, bit)
        parts = [jnp.where(chosen, parts[2 * k + 1], parts[2 * k]) for k in range(len(parts) // 2)]
    return jnp.concatenate([parts[0], by_col], axis=0)


def relative_spread(block, grad_terms, key_rows):
    lane = lane_ids(128, WIN)
    by_row = grad_terms[:key_rows]
    if block & 2:
        pieces = [grad_terms[key_rows:], jnp.zeros((WIN - 32, 128), F32)]
    else:
        pieces = [jnp.zeros((4, 128), F32), grad_terms[key_rows:], jnp.zeros((WIN - 36, 128), F32)]
    by_col = jnp.concatenate(pieces, axis=0)
    for bit, step in ((8, 1), (16, 2)):
        by_col = jnp.where(lane_bit(lane, bit), by_col, pltpu.roll(by_col, step, 0))
    parts = [jnp.where((lane & 7) == s, by_col, 0.0) for s in range(8)]
    lane = lane_ids(128, key_rows)
    for r in range(8):
        hit = (lane >> 5) == r - 4 * (block & 1)
        parts.append(jnp.where(hit, by_row, 0.0) if r // 4 == block & 1 else jnp.zeros((key_rows, 128), F32))
    return jnp.concatenate(parts, axis=0).astype(BF16)


def gelu_parts(hidden, slope=False):
    cumulative = 0.5 + 0.5 * lax.erf(hidden * 0.7071067811865476)
    act = (hidden * cumulative).astype(BF16)
    if not slope:
        return (act,)
    return act, cumulative + hidden * (jnp.exp(hidden * hidden * -0.5) * 0.3989422804014327)


def forward_kernel(ext_ref, row_ref, q_ref, top_ref, bot_ref, x0_ref, kv_ref, vec_ref, rw_ref, wprojt_ref, w1t_ref, b1_ref, w2t_ref,
                   hat_ref, terms_ref, att_ref, stat_ref, pool_ref, ka_ref, kn_ref, v_ref, ztop_ref, zbot_ref, pre_ref, wide_ref, wb1_ref,
                   *, offset, key_rows):
    images, heights, breadths, row_oks = group_extents(ext_ref, row_ref, offset)
    depth = DIM + aug_rows(key_rows)

    @pl.when(pl.program_id(0) == 0)
    def _():
        fill_wide(wide_ref, vec_ref, list(range(15, 24)) + [3, 4, 9, 10, 11, 12])
        wb1_ref[...] = jnp.broadcast_to(b1_ref[...], (MLP, 128))

    lane = lane_ids(CANVAS_W, DIM)
    for g in range(GROUP):
        v_ref[g] = key_tables(kv_ref, images[g], key_rows, heights[g], breadths[g], ka_ref, kn_ref.at[g]).astype(BF16)
        for halo_ref, dst_ref, tap_row, target in ((top_ref, ztop_ref, 0, 0), (bot_ref, zbot_ref, 2, 96)):
            halo = halo_ref[g].astype(F32)
            left = jnp.where(lane == 0, 0.0, pltpu.roll(halo, 1, 1))
            right = jnp.where(lane == CANVAS_W - 1, 0.0, pltpu.roll(halo, CANVAS_W - 1, 1))
            taps = [wide(wide_ref, 3 * tap_row + k, CANVAS_W) for k in range(3)]
            spread_halo(dst_ref.at[g], taps[0] * left + taps[1] * halo + taps[2] * right, target)
    pool_ref[...] = jnp.zeros_like(pool_ref)

    def step(pair, carry):
        for group in range(0, DIM, 16):
            part = slice(group, group + 16)
            taps = [wide_ref[k, part] for k in range(9)]
            for g in range(GROUP):
                window = q_ref[g, part, pl.ds(pl.multiple_of(pair * PAIR, 128), PAIR + 512)].astype(F32)
                for tile in range(2):
                    sums = []
                    for side in range(2):
                        shifts = col_shifts(window, 256 + 256 * tile + 128 * side)
                        sums.append([sum(taps[3 * r + c] * shifts[c] for c in range(3)) for r in range(3)])
                    halo = pl.ds(pl.multiple_of((2 * pair + tile) * 128, 128), 128)
                    down = rows_down(sums[0][0], sums[1][0], ztop_ref[g, part, halo])
                    up = rows_up(sums[0][2], sums[1][2], zbot_ref[g, part, halo])
                    for side in range(2):
                        base = PAIR * g + 256 * tile + 128 * side
                        pre_ref[part, base : base + 128] = sums[side][1] + down[side] + up[side]

        def query_of(k, pre):
            hat, rstd = normalized(pre)
            return hat, (hat * wide_ref[9] + wide_ref[10]).astype(BF16), rstd

        hat, query, rstd = by_lanes(query_of, pre_ref[...])
        store_pair(hat_ref, pair, hat)

        def extra_of(k, products):
            terms = relative_terms(k, products, key_rows) * (DIM**0.5)
            high = terms.astype(BF16).astype(F32)
            return (jnp.concatenate([high, terms - high, jnp.ones((16, 128), F32)], axis=0).astype(BF16),)

        (extra,) = by_lanes(extra_of, dot(rw_ref[pair], query))
        store_pair(terms_ref, pair, extra)

        def softmax(k, scores):
            peak = jnp.max(scores, axis=0, keepdims=True)
            weights = jnp.exp2((scores - peak) * EXP2_SCALE)
            inverse = 1.0 / jnp.sum(weights, axis=0, keepdims=True)
            return (weights * inverse).astype(BF16), peak, inverse

        long_query = by_image(jnp.concatenate([query, extra], axis=0))
        scores = jnp.concatenate([dot(kn_ref[g, :, :depth], long_query[g]) for g in range(GROUP)], axis=1)
        probs, peak, inverse = by_lanes(softmax, scores)
        store_pair(stat_ref, pair, jnp.concatenate([peak, inverse, rstd, jnp.zeros((5, GROUP * PAIR), F32)], axis=0))
        mixed = by_image(probs)
        mixed = jnp.concatenate([dot(v_ref[g], mixed[g]) for g in range(GROUP)], axis=1)
        attended = (mixed + query.astype(F32)).astype(BF16)
        store_pair(att_ref, pair, attended)

        def second_norm(k, x0, out):
            x1 = x0 + (out + wide_ref[11])
            hat_two, _ = normalized(x1)
            return x1, (hat_two * wide_ref[12] + wide_ref[13]).astype(BF16)

        x1, normed = by_lanes(second_norm, load_pair(x0_ref, pair), dot(wprojt_ref[...], attended))
        (act,) = by_blocks(lambda part, hidden: gelu_parts(hidden + wb1_ref[part]), 64, dot(w1t_ref[...], normed))

        def third_norm(k, x1, out, mask):
            hat_three, _ = normalized(x1 + (out + wide_ref[14]))
            return (hat_three * mask,)

        (kept,) = by_lanes(third_norm, x1, dot(w2t_ref[...], act), pair_mask(pair, breadths, row_oks))
        for g, part in enumerate(by_image(kept)):
            pool_ref[g] += fold_lanes(part)
        return carry

    lax.fori_loop(0, pair_count(breadths), step, 0)


def call_forward(ext, row, q, top, bot, x0, kv, wts, offset):
    whole, per = specs()
    images, key_rows = q.shape[0], kv.shape[0]
    more = aug_rows(key_rows)
    shapes = [((DIM, TOKENS), F32), ((more, TOKENS), BF16), ((DIM, TOKENS), BF16), ((8, TOKENS), F32), ((DIM, 128), F32)]
    keys = key_rows * 32
    return pl.pallas_call(
        functools.partial(forward_kernel, offset=offset, key_rows=key_rows),
        grid_spec=pltpu.PrefetchScalarGridSpec(
            num_scalar_prefetch=2, grid=(images // GROUP,),
            in_specs=[
                per(DIM, PADDED), per(DIM, CANVAS_W), per(DIM, CANVAS_W), per(DIM, TOKENS),
                key_lanes(key_rows, 2 * DIM),
                whole(DIM, 64), whole(PAIRS, 8 * WIN + 8 * key_rows, DIM), whole(DIM, DIM), whole(MLP, DIM), whole(MLP, 1),
                whole(DIM, MLP)],
            out_specs=[per(*s) for s, _ in shapes],
            scratch_shapes=[
                pltpu.VMEM((DIM + more, keys), BF16), pltpu.VMEM((GROUP, keys, 256), BF16), pltpu.VMEM((GROUP, DIM, keys), BF16),
                pltpu.VMEM((GROUP, DIM, 1024), F32), pltpu.VMEM((GROUP, DIM, 1024), F32), pltpu.VMEM((DIM, GROUP * PAIR), F32),
                pltpu.VMEM((15, DIM, 128), F32), pltpu.VMEM((MLP, 128), F32)]),
        out_shape=[jax.ShapeDtypeStruct((images,) + s, t) for s, t in shapes],
        compiler_params=pltpu.CompilerParams(vmem_limit_bytes=VMEM_BYTES),
        cost_estimate=pl.CostEstimate(flops=images * 5_000_000_000, bytes_accessed=images * 4_000_000, transcendentals=0),
        name="forward",
    )(ext, row, q, top, bot, x0, kv, wts["vec"], wts["rw"], wts["wproj_t"], wts["w1_t"], wts["b1"], wts["w2_t"])


def backward_kernel(ext_ref, row_ref, hat_ref, terms_ref, att_ref, stat_ref, x0_ref, q_ref, top_ref, bot_ref, kv_ref, gvec_ref, vec_ref,
                    rwt_ref, wprojt_ref, wproj_ref, w1t_ref, w1_ref, b1_ref, w2t_ref, w2_ref,
                    dx1_ref, dq_ref, up_ref, down_ref, dkv_ref, a2_ref, a1_ref, ap_ref, av_ref, ak_ref, ar_ref,
                    ka_ref, kn_ref, vn_ref, dp_ref, qtop_ref, qbot_ref, ru_ref, rd_ref, dk_ref, dv_ref, wide_ref, wb1_ref,
                    *, offset, key_rows, slots):
    images, heights, breadths, row_oks = group_extents(ext_ref, row_ref, offset)
    depth = DIM + aug_rows(key_rows)
    count = pair_count(breadths)

    @pl.when(pl.program_id(0) == 0)
    def _():
        for ref in (a2_ref, a1_ref, ap_ref, av_ref, ak_ref, ar_ref, ru_ref, rd_ref):
            ref[...] = jnp.zeros_like(ref)
        fill_wide(wide_ref, vec_ref, list(range(15, 24)) + [3, 4, 9, 10, 11, 12, 13])
        wb1_ref[...] = jnp.broadcast_to(b1_ref[...], (MLP, 128))

    for g in range(GROUP):
        values = key_tables(kv_ref, images[g], key_rows, heights[g], breadths[g], ka_ref.at[g], kn_ref.at[g])
        padded_values = jnp.concatenate([values, jnp.zeros((128 - DIM, values.shape[1]), F32)], axis=0)
        vn_ref[g] = jnp.transpose(padded_values).astype(BF16)
        spread_halo(qtop_ref.at[g], top_ref[g].astype(F32), 0)
        spread_halo(qbot_ref.at[g], bot_ref[g].astype(F32), 96)
    for ref in (dk_ref, dv_ref, dp_ref):
        ref[...] = jnp.zeros_like(ref)

    def step(pair, carry):
        ones = jnp.ones((16, GROUP * PAIR), BF16)
        attended = load_pair(att_ref, pair)

        def second_norm(k, x0, out):
            x1 = x0 + (out + wide_ref[11])
            hat, rstd = normalized(x1)
            return x1, hat, rstd, (hat * wide_ref[12] + wide_ref[13]).astype(BF16)

        x1, hat_two, rstd_two, normed = by_lanes(second_norm, load_pair(x0_ref, pair), dot(wprojt_ref[...], attended))
        act, slope = by_blocks(lambda part, hidden: gelu_parts(hidden + wb1_ref[part], True), 64, dot(w1t_ref[...], normed))

        def third_norm(k, x1, out, mask):
            hat, rstd = normalized(x1 + (out + wide_ref[14]))
            grad = norm_back(gvec_ref[k * 128 // PAIR] * mask, hat, rstd, wide_ref[15])
            return grad, grad.astype(BF16)

        grad_x2, grad_mlp = by_lanes(third_norm, x1, dot(w2t_ref[...], act), pair_mask(pair, breadths, row_oks))
        a2_ref[...] += dot_nt(grad_mlp, jnp.concatenate([act, ones], axis=0))
        (grad_hidden,) = by_blocks(lambda part, grad, slope: ((grad * slope).astype(BF16),), 64, dot(w2_ref[...], grad_mlp), slope)
        a1_ref[...] += dot_nt(jnp.concatenate([normed, ones], axis=0), grad_hidden)

        def second_back(k, grad, hat, rstd, grad_x2):
            total = grad_x2 + norm_back(grad, hat, rstd, wide_ref[12])
            return total, total.astype(BF16), grad * hat

        grad_normed = dot(w1_ref[...], grad_hidden)
        grad_x1, grad_proj, scaled = by_lanes(second_back, grad_normed, hat_two, rstd_two, grad_x2)
        av_ref[0] += fold_lanes(scaled)
        av_ref[1] += fold_lanes(grad_normed)
        store_pair(dx1_ref, pair, grad_x1)
        ap_ref[...] += dot_nt(jnp.concatenate([attended, ones], axis=0), grad_proj)
        grad_att = dot(wproj_ref[...], grad_proj)
        grad_att_low = grad_att.astype(BF16)
        hat = load_pair(hat_ref, pair)
        (query,) = by_lanes(lambda k, hat: ((hat * wide_ref[9] + wide_ref[10]).astype(BF16),), hat)
        long_query = by_image(jnp.concatenate([query, load_pair(terms_ref, pair)], axis=0))
        scores = jnp.concatenate([dot(kn_ref[g, :, :depth], long_query[g]) for g in range(GROUP)], axis=1)
        low = by_image(grad_att_low)
        grad_probs = jnp.concatenate([dot(vn_ref[g, :, :DIM], low[g]) for g in range(GROUP)], axis=1)
        stat = load_pair(stat_ref, pair)

        def softmax_back(k, scores, grad_probs, stat):
            probs = jnp.exp2((scores - stat[0:1]) * EXP2_SCALE) * stat[1:2]
            inner = jnp.sum(probs * grad_probs, axis=0, keepdims=True)
            return probs.astype(BF16), (probs * (grad_probs - inner)).astype(BF16)

        probs, grad_scores = by_lanes(softmax_back, scores, grad_probs, stat)
        probs, grad_scores, queries = by_image(probs), by_image(grad_scores), by_image(query)
        back = []
        for g in range(GROUP):
            back.append(dot(ka_ref[g, : DIM + key_rows + 32, :], grad_scores[g]))
            dv_ref[g] += dot_nt(low[g], probs[g])
            dk_ref[g] += dot_nt(queries[g], grad_scores[g])
        back = jnp.concatenate(back, axis=1)
        (spread,) = by_lanes(lambda k, terms: (relative_spread(k, terms, key_rows),), back[DIM:])
        ar_ref[pair] += dot_nt(query, spread)

        def query_back(k, grad_att, back, far, hat, stat):
            grad = grad_att + back * SCALE + far
            return norm_back(grad, hat, stat[2:3], wide_ref[9]), grad * hat, grad

        grad_pre, scaled, grad = by_lanes(query_back, grad_att, back[:DIM], dot(rwt_ref[pair], spread), hat, stat)
        av_ref[2] += fold_lanes(scaled)
        av_ref[3] += fold_lanes(grad)
        store_pair(dp_ref, pair, grad_pre, 256)
        return carry

    lax.fori_loop(0, count, step, 0)
    lane = lane_ids(128, 2 * DIM)
    for g in range(GROUP):
        for i in range(key_rows):
            block = slice(128 * (i // 4), 128 * (i // 4) + 128)
            value = jnp.concatenate([dk_ref[g, :, block] * SCALE, dv_ref[g, :, block]], axis=0)
            value = pltpu.roll(value, (4 + (images[g] & 3) - i % 4) * 32 & 127, 1)
            slot = reverse_bits(jnp.bitwise_xor(row_ref[0], i), key_rows) if slots else i
            dkv_ref[slot] = jnp.where((lane >> 5) == (images[g] & 3), value, dkv_ref[slot])

    def pool_step(pair, carry):
        for group in range(0, DIM, 16):
            part = slice(group, group + 16)
            taps = [wide_ref[k, part] for k in range(9)]
            grads = [None] * 9
            for g in range(GROUP):
                window = dp_ref[g, part, pl.ds(pl.multiple_of(pair * PAIR, 128), PAIR + 512)]
                for tile in range(2):
                    base = pair * PAIR + 256 * tile
                    halo = pl.ds(pl.multiple_of((2 * pair + tile) * 128, 128), 128)
                    query = [q_ref[g, part, pl.ds(pl.multiple_of(base + 256 + 128 * side, 128), 128)].astype(F32) for side in range(2)]
                    above = rows_down(query[0], query[1], qtop_ref[g, part, halo])
                    under = rows_up(query[0], query[1], qbot_ref[g, part, halo])
                    sums = []
                    for side in range(2):
                        left, here, right = col_shifts(window, 256 + 256 * tile + 128 * side)
                        shifts = (right, here, left)
                        sums.append([sum(taps[3 * r + c] * shifts[c] for c in range(3)) for r in range(3)])
                        for r, rows in enumerate((above[side], query[side], under[side])):
                            for c in range(3):
                                term = shifts[c] * rows
                                grads[3 * r + c] = term if grads[3 * r + c] is None else grads[3 * r + c] + term
                    zero = jnp.zeros((16, 128), F32)
                    up = rows_up(sums[0][0], sums[1][0], zero)
                    down = rows_down(sums[0][2], sums[1][2], zero)
                    for side in range(2):
                        lanes = pl.ds(pl.multiple_of(base + 128 * side, 128), 128)
                        dq_ref[g, part, lanes] = sums[side][1] + up[side] + down[side]
                    ru_ref[g, part, halo] = up[2]
                    rd_ref[g, part, halo] = down[2]
            for k in range(9):
                ak_ref[k, part] += grads[k]
        return carry

    def pool_idle(pair, carry):
        for ref in (ru_ref, rd_ref):
            for g in range(GROUP):
                ref[g, :, pl.ds(pl.multiple_of(pair * 256, 128), 256)] = jnp.zeros((DIM, 256), F32)
        return carry

    lax.fori_loop(0, count, pool_step, 0)
    lax.fori_loop(count, PAIRS, pool_idle, 0)
    for g in range(GROUP):
        up_ref[g] = gather_halo(ru_ref.at[g], 96).astype(BF16)
        down_ref[g] = gather_halo(rd_ref.at[g], 0).astype(BF16)


def call_backward(ext, row, hat, terms, att, stat, x0, q, top, bot, kv, gvec, wts, offset, slots=False):
    whole, per = specs()
    images, key_rows = q.shape[0], kv.shape[0]
    more = aug_rows(key_rows)
    keys = key_rows * 32
    window = 8 * WIN + 8 * key_rows
    heads = key_lanes(key_rows, 2 * DIM)
    shapes = [((DIM, TOKENS), F32), ((DIM, TOKENS), F32), ((DIM, CANVAS_W), BF16), ((DIM, CANVAS_W), BF16)]
    sums = [(DIM, MLP + 16), (DIM + 16, MLP), (DIM + 16, DIM), (4, DIM, 128), (9, DIM, 128), (PAIRS, DIM, window)]
    return pl.pallas_call(
        functools.partial(backward_kernel, offset=offset, key_rows=key_rows, slots=slots),
        grid_spec=pltpu.PrefetchScalarGridSpec(
            num_scalar_prefetch=2, grid=(images // GROUP,),
            in_specs=[
                per(DIM, TOKENS), per(more, TOKENS), per(DIM, TOKENS), per(8, TOKENS), per(DIM, TOKENS), per(DIM, PADDED),
                per(DIM, CANVAS_W), per(DIM, CANVAS_W), heads, per(DIM, 1), whole(DIM, 64), whole(PAIRS, DIM, window),
                whole(DIM, DIM), whole(DIM, DIM), whole(MLP, DIM), whole(DIM, MLP), whole(MLP, 1), whole(DIM, MLP), whole(MLP, DIM)],
            out_specs=[per(*s) for s, _ in shapes] + [heads] + [whole(*s) for s in sums],
            scratch_shapes=[
                pltpu.VMEM((GROUP, DIM + more, keys), BF16), pltpu.VMEM((GROUP, keys, 256), BF16), pltpu.VMEM((GROUP, keys, 128), BF16),
                pltpu.VMEM((GROUP, DIM, PADDED), F32)] + [pltpu.VMEM((GROUP, DIM, 1024), F32)] * 4
            + [pltpu.VMEM((GROUP, DIM, keys), F32)] * 2 + [pltpu.VMEM((16, DIM, 128), F32), pltpu.VMEM((MLP, 128), F32)]),
        out_shape=[jax.ShapeDtypeStruct((images,) + s, t) for s, t in shapes]
        + [jax.ShapeDtypeStruct((key_rows, 2 * DIM, 32 * images), F32)] + [jax.ShapeDtypeStruct(s, F32) for s in sums],
        compiler_params=pltpu.CompilerParams(vmem_limit_bytes=VMEM_BYTES),
        cost_estimate=pl.CostEstimate(flops=images * 12_000_000_000, bytes_accessed=images * 6_000_000, transcendentals=0),
        name="backward",
    )(ext, row, hat, terms, att, stat, x0, q, top, bot, kv, gvec, wts["vec"], wts["rw_t"], wts["wproj_t"], wts["wproj"],
      wts["w1_t"], wts["w1"], wts["b1"], wts["w2_t"], wts["w2"])


def embed_back_kernel(ext_ref, row_ref, patch_ref, dq_ref, dx1_ref, rtop_ref, rbot_ref, nsel_ref, kvt_ref, pre_ref, under_ref,
                      wp_ref, vec_ref, wqkv_ref, kexp_ref, tapt_ref,
                      aq_ref, akv_ref, apatch_ref, av_ref, ak_ref, dn_ref, rim_ref, wide_ref, *, offset):
    images, heights, breadths, row_oks = group_extents(ext_ref, row_ref, offset)

    @pl.when(pl.program_id(0) == 0)
    def _():
        for ref in (aq_ref, akv_ref, apatch_ref, av_ref, ak_ref, dn_ref, rim_ref):
            ref[...] = jnp.zeros_like(ref)
        fill_wide(wide_ref, vec_ref, [0, 1, 2])

    lane = lane_ids(128, 2 * DIM)

    def thrice(value, image):
        block = jnp.where((lane >> 5) == 1, take_lanes(value, image, 1), take_lanes(value, image, 0))
        block = jnp.where((lane >> 5) == 2, take_lanes(value, image, 2), block)
        return jnp.where((lane >> 5) == 3, 0.0, block)

    grad_taps = []
    for g in range(GROUP):
        own = thrice(pre_ref[...], images[g])
        spread = jnp.concatenate([thrice(under_ref[...], images[g]), own, own], axis=1)
        ak_ref[...] += kvt_ref[g].astype(F32) * spread
        grad_taps.append((spread * kexp_ref[...]).astype(BF16))
    grad_taps = jnp.concatenate(grad_taps, axis=1)
    nsel = jnp.concatenate([nsel_ref[g] for g in range(GROUP)], axis=1)
    akv_ref[...] += dot_nt(jnp.concatenate([nsel, jnp.ones((16, 384 * GROUP), BF16)], axis=0), grad_taps)
    grad_sel = dot(wqkv_ref[:, DIM : 3 * DIM], grad_taps)
    high = grad_sel.astype(BF16)
    low = (grad_sel - high.astype(F32)).astype(BF16)
    parts = [piece[:, 128 * k : 128 * k + 128] for k in range(3 * GROUP) for piece in (high, low)]
    lines = dot(jnp.concatenate(parts, axis=0), tapt_ref[...])
    for g in range(GROUP):
        for k, start in enumerate((224, 0, 32)):
            first = 2 * DIM * (3 * g + k)
            line = lines[first : first + DIM] + lines[first + DIM : first + 2 * DIM]
            for tile in range(TILES):
                dn_ref[g, :, 256 * tile + start : 256 * tile + start + 32] = line[:, 32 * tile : 32 * tile + 32]
        for halo_ref, start in ((rtop_ref, 0), (rbot_ref, 224)):
            line = halo_ref[g].astype(F32)
            for tile in range(TILES):
                rim_ref[g, :, 256 * tile + start : 256 * tile + start + 32] = line[:, 32 * tile : 32 * tile + 32]

    def step(pair, carry):
        mask = pair_mask(pair, breadths, row_oks)
        patches = load_pair(patch_ref, pair)

        def first_norm(k, embed, mask, grad, rim):
            hat, rstd = normalized((embed + wide_ref[0]) * mask)
            return hat, rstd, (hat * wide_ref[1] + wide_ref[2]).astype(BF16), (grad + rim).astype(BF16)

        hat, rstd, normed, grad_q = by_lanes(first_norm, dot(wp_ref[...], patches), mask, load_pair(dq_ref, pair), load_pair(rim_ref, pair))
        aq_ref[...] += dot_nt(jnp.concatenate([normed, jnp.ones((16, GROUP * PAIR), BF16)], axis=0), grad_q)

        def first_back(k, out, extra, hat, rstd, mask, dx1):
            grad = out + extra
            total = (dx1 + norm_back(grad, hat, rstd, wide_ref[1])) * mask
            high = total.astype(BF16)
            return jnp.concatenate([high, (total - high.astype(F32)).astype(BF16)], axis=0), total, grad * hat, grad

        both, total, scaled, grad = by_lanes(
            first_back, dot(wqkv_ref[:, 0:DIM], grad_q), load_pair(dn_ref, pair), hat, rstd, mask, load_pair(dx1_ref, pair))
        av_ref[0] += fold_lanes(total)
        av_ref[1] += fold_lanes(scaled)
        av_ref[2] += fold_lanes(grad)
        apatch_ref[...] += dot_nt(both, patches)
        return carry

    lax.fori_loop(0, pair_count(breadths), step, 0)


def call_embed_back(ext, row, patches, dq, dx1, rtop, rbot, nsel, kvt, pre, under, consts, wts, offset):
    whole, per = specs()
    images = dq.shape[0]
    sums = [(DIM + 16, DIM), (DIM + 16, 2 * DIM), (2 * DIM, PATCH_ROWS), (3, DIM, 128), (2 * DIM, 384)]
    return pl.pallas_call(
        functools.partial(embed_back_kernel, offset=offset),
        grid_spec=pltpu.PrefetchScalarGridSpec(
            num_scalar_prefetch=2, grid=(images // GROUP,),
            in_specs=[
                per(PATCH_ROWS, TOKENS), per(DIM, TOKENS), per(DIM, TOKENS), per(DIM, CANVAS_W), per(DIM, CANVAS_W),
                per(DIM, 384), per(2 * DIM, 384), key_lanes(2 * DIM), key_lanes(2 * DIM),
                whole(DIM, PATCH_ROWS), whole(DIM, 64), whole(DIM, 3 * DIM), whole(2 * DIM, 384), whole(128, CANVAS_W)],
            out_specs=[whole(*s) for s in sums],
            scratch_shapes=[pltpu.VMEM((GROUP, DIM, TOKENS), F32)] * 2 + [pltpu.VMEM((3, DIM, 128), F32)]),
        out_shape=[jax.ShapeDtypeStruct(s, F32) for s in sums],
        compiler_params=pltpu.CompilerParams(vmem_limit_bytes=VMEM_BYTES),
        cost_estimate=pl.CostEstimate(flops=images * 3_000_000_000, bytes_accessed=images * 3_000_000, transcendentals=0),
        name="embed_back",
    )(ext, row, patches, dq, dx1, rtop, rbot, nsel, kvt, pre, under, wts["wp"], wts["vec"], wts["wqkv"], wts["kexp"], consts["tap_t"])


def bit_count(size):
    return size.bit_length() - 1


def swap(value, axis, bit):
    size = lax.axis_size(axis)
    return lax.ppermute(value, axis, [(i, i ^ (1 << bit)) for i in range(size)])


def shifted(value, axis, step):
    size = lax.axis_size(axis)
    pairs = [(i, i + step) for i in range(size) if 0 <= i + step < size]
    return lax.ppermute(value, axis, pairs)


def summed(value, axis):
    for bit in range(bit_count(lax.axis_size(axis))):
        value = value + swap(value, axis, bit)
    return value


def scatter_slots(value, axis):
    for bit in range(bit_count(lax.axis_size(axis))):
        half = value.shape[0] // 2
        value = value[:half] + swap(value[half:], axis, bit)
    return value[0]


def gather_params(value):
    dims = []
    for axis in ("img", "row"):
        index = lax.axis_index(axis)
        for bit in reversed(range(bit_count(lax.axis_size(axis)))):
            other = swap(value, axis, bit)
            mine_second = (index >> bit) & 1 == 1
            value = jnp.stack([jnp.where(mine_second, other, value), jnp.where(mine_second, value, other)])
            dims.append((axis, bit))
    dims = dims[::-1]
    wanted = [("img", b) for b in reversed(range(bit_count(lax.axis_size("img"))))]
    wanted += [("row", b) for b in reversed(range(bit_count(lax.axis_size("row"))))]
    order = [dims.index(d) for d in wanted]
    value = jnp.transpose(value, order + [value.ndim - 2, value.ndim - 1])
    return value.reshape(-1)


def scatter_grads(flat):
    rows, imgs = lax.axis_size("row"), lax.axis_size("img")
    names = [("img", b) for b in reversed(range(bit_count(imgs)))] + [("row", b) for b in reversed(range(bit_count(rows)))]
    leaf = flat.shape[0] // (rows * imgs)
    value = flat.reshape((2,) * len(names) + (leaf // 128, 128))
    for axis, bits in (("row", range(bit_count(rows))), ("img", range(bit_count(imgs)))):
        index = lax.axis_index(axis)
        for bit in bits:
            place = names.index((axis, bit))
            names.pop(place)
            own = (index >> bit) & 1
            keep = lax.dynamic_index_in_dim(value, own, place, False)
            send = lax.dynamic_index_in_dim(value, 1 - own, place, False)
            value = keep + swap(send, axis, bit)
    return value.reshape(leaf)


def segment_list(canvas_rows, canvas_cols):
    return [
        ("w_patch", (3 * PATCH * PATCH, DIM)),
        ("w_qkv", (DIM, 3 * DIM)),
        ("w_proj", (DIM, DIM)),
        ("w_fc1", (DIM, MLP)),
        ("w_fc2", (MLP, DIM)),
        ("w_head", (DIM, CLASSES)),
        ("rel_rows", (2 * canvas_rows - 8, DIM)),
        ("rel_cols", (2 * canvas_cols - 8, DIM)),
        ("small", (49, DIM)),
        ("b_head", (CLASSES,)),
    ]


def unpack(flat_vec, segments):
    pieces = {}
    position = 0
    for seg_name, seg_shape in segments:
        entries = int(np.prod(seg_shape))
        pieces[seg_name] = flat_vec[position : position + entries].reshape(seg_shape)
        position += entries
    return pieces


def patch_rows(weight):
    taps = jnp.pad(weight.reshape(PATCH, PATCH, 3, DIM), ((0, 1), (0, 0), (0, 1), (0, 0)))
    parts = []
    for piece in (taps[:, 3:7], taps[:, 0:3]):
        phases = piece.shape[1]
        parts.append(jnp.transpose(piece.reshape(2, 4, phases, 4, DIM), (0, 2, 1, 3, 4)).reshape(32 * phases, DIM))
    return jnp.concatenate(parts, axis=0)


def patch_rows_back(grad):
    rows = grad.T
    parts = []
    for piece, phases in ((rows[128:], 3), (rows[:128], 4)):
        taps = jnp.transpose(piece.reshape(2, phases, 4, 4, DIM), (0, 2, 1, 3, 4)).reshape(8, phases, 4, DIM)
        parts.append(taps[:PATCH, :, :3])
    return jnp.concatenate(parts, axis=1).reshape(3 * PATCH * PATCH, DIM)


def relative_windows(rel_rows, rel_cols, row_index, key_rows):
    offsets = jnp.flip(rel_cols.reshape(-1, 8, DIM), 0)
    offsets = jnp.transpose(jnp.pad(offsets, ((0, 1), (0, 0), (0, 0))), (1, 0, 2))
    blocks = rel_rows.reshape(2 * key_rows - 1, 8, DIM)
    rows = jnp.transpose(jnp.flip(lax.dynamic_slice_in_dim(blocks, row_index, key_rows, 0), 0), (1, 0, 2))
    rows = rows.reshape(8 * key_rows, DIM)
    windows = []
    for pair in range(PAIRS):
        cols = offsets[:, 24 - 8 * pair : 24 - 8 * pair + WIN].reshape(8 * WIN, DIM)
        windows.append(jnp.concatenate([cols, rows], axis=0))
    return jnp.stack(windows)


def relative_windows_back(grad, row_index, key_rows):
    grad = jnp.transpose(grad, (0, 2, 1))
    cols = grad[:, : 8 * WIN].reshape(PAIRS, 8, WIN, DIM)
    total = 0.0
    for pair in range(PAIRS):
        start = 24 - 8 * pair
        total = total + jnp.pad(cols[pair], ((0, 0), (start, 64 - start - WIN), (0, 0)))
    rel_cols = jnp.flip(jnp.transpose(total[:, :63], (1, 0, 2)), 0).reshape(-1, DIM)
    rows = jnp.sum(grad[:, 8 * WIN :], axis=0).reshape(8, key_rows, DIM)
    rows = jnp.flip(jnp.transpose(rows, (1, 0, 2)), 0)
    blocks = lax.dynamic_update_slice_in_dim(jnp.zeros((2 * key_rows - 1, 8, DIM), F32), rows, row_index, 0)
    return blocks.reshape(-1, DIM), rel_cols


def tap_keep():
    keep = np.ones((3, 4, 32), np.float32)
    keep[:, 3] = 0.0
    keep[:, 0, 0] = 0.0
    return keep


def prepare(weights, row_index, key_rows):
    small = weights["small"]
    vec = jnp.pad(small.astype(F32).T, ((0, 0), (0, 15)))
    kernels = small[9:27].reshape(2, 3, 3, DIM).astype(F32)
    expanded = jnp.pad(jnp.transpose(kernels, (0, 3, 1, 2)), ((0, 0), (0, 0), (0, 0), (0, 1)))
    kexp = (expanded[..., None] * tap_keep()).reshape(2 * DIM, 384)
    windows = relative_windows(weights["rel_rows"], weights["rel_cols"], row_index, key_rows)
    return {
        "vec": vec,
        "kexp": kexp,
        "wp": patch_rows(weights["w_patch"]).T,
        "wqkv": weights["w_qkv"],
        "wqkv_t": weights["w_qkv"].T,
        "b_kv": small[43:45].astype(F32).reshape(2 * DIM, 1),
        "wproj": weights["w_proj"],
        "wproj_t": weights["w_proj"].T,
        "w1": weights["w_fc1"],
        "w1_t": weights["w_fc1"].T,
        "b1": small[45:49].astype(F32).reshape(MLP, 1),
        "w2": weights["w_fc2"],
        "w2_t": weights["w_fc2"].T,
        "rw": windows,
        "rw_t": jnp.transpose(windows, (0, 2, 1)),
    }


def image_loss(pooled, head_w, head_b, teacher, labels, image_total):
    logits = jnp.dot(pooled, head_w, precision=HIGHEST_PREC) + head_b
    log_student = jax.nn.log_softmax(logits, axis=-1)
    log_teacher = jax.nn.log_softmax(teacher, axis=-1)
    onehot = (jnp.arange(CLASSES)[None, :] == labels[:, None]).astype(F32)
    per_image = jnp.sum(jnp.exp(log_teacher) * (log_teacher - log_student), axis=-1) - jnp.sum(onehot * log_student, axis=-1)
    return jnp.sum(per_image) / image_total


def body(flat_params, first_moment, second_moment, pixels, extents, labels, teacher):
    key_rows = lax.axis_size("row")
    row_index = lax.axis_index("row")
    row_lead = row_index == 0
    segments = segment_list(ROWS * key_rows, CANVAS_W)
    full_params = gather_params(flat_params.astype(BF16).reshape(-1, 128))
    weights = unpack(full_params, segments)
    wts = prepare(weights, row_index, key_rows)
    tap = tap_matrix()
    consts = {"perm": jnp.asarray(deinterleave_matrix(), BF16), "tap": jnp.asarray(tap, BF16), "tap_t": jnp.asarray(tap.T, BF16)}
    vectors = weights["small"][27:42].astype(F32)
    row = row_index.astype(jnp.int32).reshape(1)
    images = pixels.shape[0]
    parts = 1
    size = images // parts
    image_total = images * lax.axis_size("img") * 1.0
    head_w = weights["w_head"].astype(F32)
    head_b = weights["b_head"].astype(F32)

    ids = jnp.arange(images)
    widths = extents[:, 1]
    ahead = (widths[None, :] > widths[:, None]) | ((widths[None, :] == widths[:, None]) & (ids[None, :] < ids[:, None]))
    places = jnp.sum(ahead.astype(jnp.int32), axis=1)
    chosen = places[None, :] == ids[:, None]
    order = jnp.sum(jnp.where(chosen, ids[None, :], 0), axis=1)
    ext = jnp.sum(jnp.where(chosen[:, :, None], extents[None], 0), axis=1)

    saved = []
    for part in range(parts):
        patches, x0, q, first, last, nsel, kvt, below, own = call_embed(ext, row, order, pixels, consts, wts, size, part * size)
        top = shifted(last, "row", 1)
        bot = shifted(first, "row", -1)
        got = shifted(below, "row", 1)
        kv = lax.all_gather(call_pool_norm(own, got, wts["vec"]), "row", axis=0)
        saved.append(dict(patches=patches, x0=x0, q=q, top=top, bot=bot, nsel=nsel, kvt=kvt, own=own, got=got, kv=kv))
    for part in range(parts):
        s = saved[part]
        s["fwd"] = call_forward(ext, row, s["q"], s["top"], s["bot"], s["x0"], s["kv"], wts, part * size)
    total = {}

    def add(name, value):
        total[name] = total[name] + value if name in total else value

    sorted_local = jnp.sum(jnp.concatenate([s["fwd"][-1] for s in saved], axis=0), axis=-1)
    local = jnp.sum(jnp.where(chosen[:, :, None], sorted_local[:, None, :], 0.0), axis=0)
    everywhere = summed(local, "row")
    counts = (extents[:, 0] * extents[:, 1]).astype(F32)[:, None]
    pooled = (everywhere * vectors[13] + counts * vectors[14]) / counts

    def loss_of(pooled_now, w, b):
        return image_loss(pooled_now, w, b, teacher, labels, image_total)

    loss_value, loss_back = jax.vjp(loss_of, pooled, head_w, head_b)
    grad_pooled, total["w_head"], total["b_head"] = loss_back(jnp.ones_like(loss_value))
    gvec = grad_pooled / counts
    local_count = jnp.where(row_index * ROWS < extents[:, 0], ROWS * extents[:, 1], 0).astype(F32)[:, None]
    total["g_three"] = jnp.sum(gvec * local, axis=0)
    total["b_three"] = jnp.sum(gvec * local_count, axis=0)
    gvec = jnp.sum(jnp.where(chosen[:, :, None], gvec[None], 0.0), axis=1)[:, :, None]
    for part in range(parts):
        s = saved[part]
        s["bwd"] = call_backward(ext, row, *s["fwd"][:4], s["x0"], s["q"], s["top"], s["bot"], s["kv"], gvec[part * size : part * size + size], wts, part * size, part == parts - 1)
    for part in range(parts):
        s = saved[part]
        dx1, dq, up, down, dkv, a2, a1, ap, av, ak, ar = s["bwd"]
        for name, value in (("a2", a2), ("a1", a1), ("ap", ap), ("av", av), ("ak", ak), ("ar", ar)):
            add(name, value)
        rtop = shifted(down, "row", 1)
        rbot = shifted(up, "row", -1)
        grad_kv = scatter_slots(dkv, "row") if part == parts - 1 else lax.psum_scatter(dkv, "row", scatter_dimension=0)
        pre, pool_sums = call_pool_back(s["own"], s["got"], grad_kv, wts["vec"])
        add("pool_sums", pool_sums)
        under = shifted(pre, "row", -1)
        aq, akv, apatch, av1, akt = call_embed_back(
            ext, row, s["patches"], dq, dx1, rtop, rbot, s["nsel"], s["kvt"], pre, under, consts, wts, part * size)
        for name, value in (("aq", aq), ("akv", akv), ("apatch", apatch), ("av1", av1), ("akt", akt)):
            add(name, value)

    t = total
    lead = jnp.where(row_lead, 1.0, 0.0)
    av, av1 = jnp.sum(t["av"], axis=-1), jnp.sum(t["av1"], axis=-1)
    pool_sums = jnp.sum(t["pool_sums"], axis=-1)
    rel_rows, rel_cols = relative_windows_back(t["ar"], row_index, key_rows)
    taps = jnp.sum((t["akt"].reshape(2, DIM, 3, 4, 32) * tap_keep())[:, :, :, :3], axis=-1)
    kernels = jnp.concatenate([jnp.sum(t["ak"], axis=-1), jnp.transpose(taps, (0, 2, 3, 1)).reshape(18, DIM)], axis=0)
    grad_vectors = jnp.stack([
        av1[0], av1[1], av1[2], av[2], av[3], pool_sums[0], pool_sums[1], pool_sums[2], pool_sums[3],
        t["ap"][DIM], av[0], av[1], t["a2"][:, MLP], t["g_three"], t["b_three"]])
    pieces = [
        patch_rows_back(t["apatch"][:DIM] + t["apatch"][DIM:]),
        jnp.concatenate([t["aq"][:DIM], t["akv"][:DIM]], axis=1),
        t["ap"][:DIM],
        t["a1"][:DIM],
        t["a2"][:, :MLP].T,
        t["w_head"] * lead,
        rel_rows,
        rel_cols,
        kernels,
        grad_vectors,
        t["aq"][DIM],
        t["akv"][DIM],
        t["a1"][DIM],
        t["b_head"] * lead,
    ]
    joined = jnp.concatenate([piece.reshape(-1) for piece in pieces])
    grad_flat = jnp.pad(joined, (0, full_params.shape[0] - joined.shape[0]))
    grad_shard = scatter_grads(grad_flat)
    norm_sq = summed(jnp.sum(grad_shard * grad_shard), "row")
    both = summed(jnp.stack([norm_sq, loss_value]), "img")
    grad_norm = jnp.sqrt(both[0])
    clip_factor = jnp.minimum(1.0, CLIP_NORM / (grad_norm + 1e-06))
    clipped = grad_shard * clip_factor
    moment_one = BETA_FIRST * first_moment + (1.0 - BETA_FIRST) * clipped
    moment_two = BETA_SECOND * second_moment + (1.0 - BETA_SECOND) * clipped * clipped
    fix_one = 1.0 - BETA_FIRST**STEP
    fix_two = 1.0 - BETA_SECOND**STEP
    update = moment_one / fix_one / (jnp.sqrt(moment_two / fix_two) + ADAM_EPS) + WEIGHT_DECAY * flat_params
    new_params = flat_params - LEARN_RATE * update
    return (new_params, moment_one, moment_two, grad_norm, both[1])


def solution(mesh):
    placed = (
        P(("img", "row")),
        P(("img", "row")),
        P(("img", "row")),
        P("img", "row", None, None, None),
        P("img", None),
        P("img"),
        P("img", None),
    )
    return jax.shard_map(
        body,
        mesh=mesh,
        in_specs=placed,
        out_specs=(P(("img", "row")), P(("img", "row")), P(("img", "row")), P(), P()),
        check_vma=False,
    )
```

```python
import functools

import jax
import jax.numpy as jnp
import numpy as np
from jax import lax
from jax.experimental import pallas as pl
from jax.experimental.pallas import tpu as pltpu
from jax.sharding import PartitionSpec as P

DIM = 96
MLP = 384
CLASSES = 1000
PATCH = 7
ROWS = 8
STEP = 7
CANVAS_W = 256

HIGHEST_PREC = lax.Precision.HIGHEST
CLIP_NORM = 0.02
LEARN_RATE = 0.05
WEIGHT_DECAY = 0.05
BETA_FIRST = 0.5
BETA_SECOND = 0.5
ADAM_EPS = 1e-08
NORM_EPS = 1e-06
NEG_FILL = -1e30

F32 = jnp.float32
BF16 = jnp.bfloat16
SCALE = DIM ** (-0.5)
EXP2_SCALE = SCALE * 1.4426950408889634

TOKENS = ROWS * CANVAS_W
PAIR = 512
PAIRS = TOKENS // PAIR
TILES = CANVAS_W // 32
GROUP = 2
PADDED = TOKENS + 512
WIN = 40
PATCH_ROWS = 224
VMEM_BYTES = 56 * 1024 * 1024


def deinterleave_matrix():
    out = np.zeros((4, 128, 4, 4, 32), np.float32)
    for row in range(4):
        for phase in range(4):
            for col in range(32):
                out[row, 4 * col + phase, phase, row, col] = 1.0
    return out.reshape(512, 512)


def tap_matrix():
    out = np.zeros((CANVAS_W, 128), np.float32)
    for tap in range(3):
        for key in range(32):
            col = 8 * key + tap - 1
            if col >= 0:
                out[col, tap * 32 + key] = 1.0
    return out


def dot(a, b):
    return jnp.dot(a, b, preferred_element_type=F32)


def dot_nt(a, b):
    return lax.dot_general(a, b, (((1,), (1,)), ((), ())), preferred_element_type=F32)


def normalized(x):
    mean = jnp.sum(x, axis=0, keepdims=True) * (1.0 / DIM)
    centered = x - mean
    var = jnp.sum(centered * centered, axis=0, keepdims=True) * (1.0 / DIM)
    rstd = lax.rsqrt(var + NORM_EPS)
    return centered * rstd, rstd


def norm_back(grad, hat, rstd, gain):
    inner = grad * gain
    mean_one = jnp.sum(inner, axis=0, keepdims=True) * (1.0 / DIM)
    mean_two = jnp.sum(inner * hat, axis=0, keepdims=True) * (1.0 / DIM)
    return rstd * (inner - mean_one - hat * mean_two)


def by_lanes(fn, *arrays):
    parts = [fn(k, *(a[:, 128 * k : 128 * k + 128] for a in arrays)) for k in range(arrays[0].shape[1] // 128)]
    return tuple(jnp.concatenate(column, axis=1) for column in zip(*parts))


def by_blocks(fn, height, *arrays):
    rows = []
    for top in range(0, arrays[0].shape[0], height):
        rows.append(by_lanes(lambda k, *block: fn(slice(top, top + height), *block), *(a[top : top + height] for a in arrays)))
    return tuple(jnp.concatenate(column, axis=0) for column in zip(*rows))


def fold_lanes(x):
    total = x[:, 0:128]
    for k in range(1, x.shape[1] // 128):
        total = total + x[:, 128 * k : 128 * k + 128]
    return total


def place_of(index):
    return index + 27 if index < 15 else index - 15 if index < 42 else index


def column(vec_ref, index):
    place = place_of(index)
    return vec_ref[:, place : place + 1]


def fill_wide(wide_ref, vec_ref, indices):
    for k, index in enumerate(indices):
        wide_ref[k] = jnp.broadcast_to(column(vec_ref, index), (DIM, 128))


def wide(wide_ref, k, width=PAIR):
    return jnp.concatenate([wide_ref[k]] * (width // 128), axis=1)


def lane_ids(width, rows=1):
    return lax.broadcasted_iota(jnp.int32, (rows, width), 1)


def pair_mask(pair, breadths, row_oks):
    lane = lane_ids(PAIR)
    col = pair * 64 + (lane >> 8) * 32 + (lane & 31)
    return jnp.concatenate([jnp.where((col < w) & ok, 1.0, 0.0).astype(F32) for w, ok in zip(breadths, row_oks)], axis=1)


def pair_lanes(pair, base=0):
    return pl.ds(pl.multiple_of(pair * PAIR + base, 128), PAIR)


def load_pair(ref, pair):
    lanes = pair_lanes(pair)
    return jnp.concatenate([ref[g, :, lanes] for g in range(GROUP)], axis=1)


def store_pair(ref, pair, value, base=0):
    for g in range(GROUP):
        ref[g, :, pair_lanes(pair, base)] = value[:, PAIR * g : PAIR * g + PAIR]


def by_image(value):
    return [value[:, PAIR * g : PAIR * g + PAIR] for g in range(GROUP)]


def pair_count(breadths):
    widest = breadths[0]
    for breadth in breadths[1:]:
        widest = jnp.maximum(widest, breadth)
    return jnp.minimum((widest >> 6) + 1, PAIRS)


def group_extents(ext_ref, row_ref, offset, group=None):
    group = pl.program_id(0) if group is None else group
    images = [group * GROUP + g for g in range(GROUP)]
    heights = [ext_ref[offset + image, 0] for image in images]
    breadths = [ext_ref[offset + image, 1] for image in images]
    return images, heights, breadths, [row_ref[0] * ROWS < height for height in heights]


def col_shifts(window, base):
    lane = lane_ids(128, window.shape[0])
    here = window[:, base : base + 128]
    before = window[:, base - 256 : base - 128]
    after = window[:, base + 256 : base + 384]
    left = jnp.where((lane & 31) == 0, pltpu.roll(before, 97, 1), pltpu.roll(here, 1, 1))
    right = jnp.where((lane & 31) == 31, pltpu.roll(after, 31, 1), pltpu.roll(here, 127, 1))
    return left.astype(F32), here.astype(F32), right.astype(F32)


def rows_down(first, second, entering):
    lane = lane_ids(128, first.shape[0])
    a, b = pltpu.roll(first, 32, 1), pltpu.roll(second, 32, 1)
    return jnp.where(lane < 32, entering, a), jnp.where(lane < 32, a, b), b


def rows_up(first, second, entering):
    lane = lane_ids(128, first.shape[0])
    a, b = pltpu.roll(first, 96, 1), pltpu.roll(second, 96, 1)
    return jnp.where(lane >= 96, b, a), jnp.where(lane >= 96, entering, b), a


def spread_halo(dst_ref, halo, target):
    for tile in range(TILES):
        block = halo[:, 128 * (tile // 4) : 128 * (tile // 4) + 128]
        shift = (target - 32 * (tile % 4)) % 128
        dst_ref[:, 128 * tile : 128 * tile + 128] = pltpu.roll(block, shift, 1) if shift else block


def store_lanes(dst_ref, value, image):
    place = image & 3
    lane = lane_ids(128, value.shape[0])
    dst_ref[...] = jnp.where((lane >> 5) == place, pltpu.roll(value, place * 32, 1), dst_ref[...])


def take_lanes(value, image, target):
    return pltpu.roll(value, (4 + target - (image & 3)) * 32 & 127, 1)


def gather_halo(src_ref, target):
    lane = lane_ids(128, DIM)
    blocks = []
    for half in range(2):
        total = None
        for k in range(4):
            tile = 4 * half + k
            block = src_ref[:, 128 * tile : 128 * tile + 128]
            shift = (32 * k - target) % 128
            block = pltpu.roll(block, shift, 1) if shift else block
            total = block if total is None else jnp.where((lane >> 5) == k, block, total)
        blocks.append(total)
    return jnp.concatenate(blocks, axis=1)


def reverse_bits(value, count):
    result = 0
    for bit in range(count.bit_length() - 1):
        result = result * 2 + ((value >> bit) & 1)
    return result


def key_tables(kv_ref, image, key_rows, height, breadth, ka_ref, kn_ref):
    lane = lane_ids(128, 2 * DIM)
    blocks = []
    for i in range(0, key_rows, 4):
        block = take_lanes(kv_ref[i].astype(F32), image, 0)
        for k in range(1, 4):
            block = jnp.where((lane >> 5) == k, take_lanes(kv_ref[i + k].astype(F32), image, k), block)
        blocks.append(block)
    both = jnp.concatenate(blocks, axis=1)
    total = key_rows * 32
    more = aug_rows(key_rows)
    rank = lax.broadcasted_iota(jnp.int32, (more, total), 0)
    key = lax.broadcasted_iota(jnp.int32, (more, total), 1)
    key_r, key_c = key >> 5, key & 31
    half = key_rows + 32
    low = rank >= half
    rank_in = jnp.where(low, rank - half, rank)
    hit = rank_in == jnp.where(rank_in < key_rows, key_r, key_c + key_rows)
    invalid = (key_r * ROWS >= height) | (key_c * ROWS >= breadth)
    table = jnp.where(rank < 2 * half, jnp.where(hit, 1.0, 0.0), 0.0)
    table = jnp.where((rank == 2 * half) & invalid, NEG_FILL, table)
    full = jnp.concatenate([both[:DIM], table, jnp.zeros((256 - DIM - more, total), F32)], axis=0)
    ka_ref[...] = full[: DIM + more].astype(BF16)
    kn_ref[...] = jnp.transpose(full).astype(BF16)
    return both[DIM:]


def aug_rows(key_rows):
    return 2 * key_rows + 64 + 16


def embed_kernel(ext_ref, row_ref, order_ref, *refs, offset):
    pix_refs, tail_refs, refs = refs[:GROUP], refs[GROUP : 2 * GROUP], refs[2 * GROUP :]
    (perm_ref, tap_ref, wp_ref, wqkv_ref, vec_ref, bkv_ref, kexp_ref,
     patch_ref, x0_ref, q_ref, first_ref, last_ref, nsel_ref, kvt_ref, below_ref, own_ref, s_ref, n_ref, wide_ref) = refs
    images, heights, breadths, row_oks = group_extents(ext_ref, row_ref, offset)

    @pl.when(pl.program_id(0) == 0)
    def _():
        s_ref[...] = jnp.zeros_like(s_ref)
        fill_wide(wide_ref, vec_ref, [0, 1, 2, 42])

    lane = lane_ids(1024, 144)
    for g in range(GROUP):
        for r in range(ROWS):
            for a in range(4):
                s_ref[16 * r + 4 * a : 16 * r + 4 * a + 3, :] = pix_refs[g][0, r, a].astype(F32)
        for a in range(3):
            s_ref[128 + 4 * a : 128 + 4 * a + 3, :] = tail_refs[g][0, 0, a].astype(F32)
        for shifted in range(2):
            rows = s_ref[...]
            if shifted:
                rows = jnp.where(lane < 4, 0.0, pltpu.roll(rows, 4, 1))
            rows = rows.astype(BF16)
            stack = []
            for start in (0, 4, 1, 5):
                for tile in range(TILES):
                    stack.append(jnp.concatenate(
                        [rows[16 * (start + k) : 16 * (start + k) + 16, 128 * tile : 128 * tile + 128] for k in range(4)], axis=1))
            out = dot(jnp.concatenate(stack, axis=0), perm_ref[...]).astype(BF16)
            for which, start in enumerate((0, 4, 1, 5)):
                half, side = which // 2, which % 2
                for tile in range(TILES):
                    block = out[128 * which + 16 * tile : 128 * which + 16 * tile + 16]
                    for phase in range(shifted, 4):
                        top = 64 * half + 16 * phase if not shifted else 128 + 48 * half + 16 * (phase - 1)
                        patch_ref[g, top : top + 16, 256 * tile + 128 * side : 256 * tile + 128 * side + 128] = block[
                            :, 128 * phase : 128 * phase + 128]

    count = pair_count(breadths)

    def active(pair, carry):
        def first_norm(k, embed, mask):
            x0 = (embed + wide_ref[0]) * mask
            hat, _ = normalized(x0)
            return x0, (hat * wide_ref[1] + wide_ref[2]).astype(BF16)

        x0, normed = by_lanes(first_norm, dot(wp_ref[...], load_pair(patch_ref, pair)), pair_mask(pair, breadths, row_oks))
        store_pair(x0_ref, pair, x0)
        store_pair(n_ref, pair, normed.astype(F32))
        (query,) = by_lanes(lambda k, out: ((out + wide_ref[3]).astype(BF16),), dot(wqkv_ref[0:DIM, :], normed))
        store_pair(q_ref, pair, query, 256)
        return carry

    def idle(pair, carry):
        for g in range(GROUP):
            n_ref[g, :, pair_lanes(pair)] = jnp.zeros((DIM, PAIR), F32)
            q_ref[g, :, pair_lanes(pair, 256)] = jnp.zeros((DIM, PAIR), BF16)
        return carry

    lax.fori_loop(0, count, active, 0)
    lax.fori_loop(count, PAIRS, idle, 0)
    for g in range(GROUP):
        q_ref[g, :, 0:256] = jnp.zeros((DIM, 256), BF16)
        q_ref[g, :, 256 + TOKENS : 512 + TOKENS] = jnp.zeros((DIM, 256), BF16)
    rows = []
    for start in (224, 0, 32):
        rows.append(jnp.concatenate(
            [n_ref[g, :, 256 * t + start : 256 * t + start + 32] for g in range(GROUP) for t in range(TILES)], axis=1).astype(BF16))
    edge = dot(wqkv_ref[0:DIM, :], jnp.concatenate(rows[:2], axis=1))
    (edge,) = by_lanes(lambda k, out: ((out + wide_ref[3]).astype(BF16),), edge)
    nsel = dot(jnp.concatenate([row[:, CANVAS_W * g : CANVAS_W * g + CANVAS_W] for g in range(GROUP) for row in rows], axis=0), tap_ref[...])
    nsel = jnp.concatenate([nsel[DIM * k : DIM * k + DIM] for k in range(3 * GROUP)], axis=1).astype(BF16)
    taps = (dot(wqkv_ref[DIM : 3 * DIM, :], nsel) + bkv_ref[...]).astype(BF16)
    for g in range(GROUP):
        last_ref[g] = edge[:, CANVAS_W * g : CANVAS_W * g + CANVAS_W]
        first_ref[g] = edge[:, CANVAS_W * (GROUP + g) : CANVAS_W * (GROUP + g) + CANVAS_W]
        nsel_ref[g] = nsel[:, 384 * g : 384 * g + 384]
        kvt_ref[g] = taps[:, 384 * g : 384 * g + 384]
        product = taps[:, 384 * g : 384 * g + 384].astype(F32) * kexp_ref[...]
        sums = []
        for k in range(3):
            part = product[:, 128 * k : 128 * k + 128]
            sums.append(part + pltpu.roll(part, 96, 1) + pltpu.roll(part, 64, 1))
        store_lanes(below_ref, sums[0], images[g])
        store_lanes(own_ref, sums[1] + sums[2], images[g])


def key_lanes(*lead):
    return pl.BlockSpec(lead + (128,), lambda i, *_: (0,) * len(lead) + (i * GROUP >> 2,))


def specs():
    whole = lambda *shape: pl.BlockSpec(shape, lambda i, *_: (0,) * len(shape))
    per = lambda *shape: pl.BlockSpec((GROUP,) + shape, lambda i, *_: (i,) + (0,) * len(shape))
    return whole, per


def call_embed(ext, row, order, pixels, consts, wts, images, offset):
    whole, per = specs()
    shapes = [
        ((PATCH_ROWS, TOKENS), BF16), ((DIM, TOKENS), F32), ((DIM, PADDED), BF16), ((DIM, CANVAS_W), BF16),
        ((DIM, CANVAS_W), BF16), ((DIM, 384), BF16), ((2 * DIM, 384), BF16)]
    pix = [pl.BlockSpec((1, ROWS, 4, 3, 1024), lambda i, ext, row, order, g=g: (order[offset + i * GROUP + g], 0, 0, 0, 0)) for g in range(GROUP)]
    tail = [pl.BlockSpec((1, 1, 4, 3, 1024), lambda i, ext, row, order, g=g: (order[offset + i * GROUP + g], ROWS - 1, 1, 0, 0)) for g in range(GROUP)]
    return pl.pallas_call(
        functools.partial(embed_kernel, offset=offset),
        grid_spec=pltpu.PrefetchScalarGridSpec(
            num_scalar_prefetch=3, grid=(images // GROUP,),
            in_specs=pix + tail + [
                whole(512, 512), whole(CANVAS_W, 128), whole(DIM, PATCH_ROWS), whole(3 * DIM, DIM), whole(DIM, 64),
                whole(2 * DIM, 1), whole(2 * DIM, 384)],
            out_specs=[per(*s) for s, _ in shapes] + [key_lanes(2 * DIM)] * 2,
            scratch_shapes=[pltpu.VMEM((144, 1024), F32), pltpu.VMEM((GROUP, DIM, TOKENS), F32), pltpu.VMEM((4, DIM, 128), F32)]),
        out_shape=[jax.ShapeDtypeStruct((images,) + s, t) for s, t in shapes]
        + [jax.ShapeDtypeStruct((2 * DIM, 32 * images), F32)] * 2,
        compiler_params=pltpu.CompilerParams(vmem_limit_bytes=VMEM_BYTES),
        cost_estimate=pl.CostEstimate(flops=images * 2_000_000_000, bytes_accessed=images * 4_000_000, transcendentals=0),
        name="embed",
    )(ext, row, order, *[pixels] * (2 * GROUP), consts["perm"], consts["tap"], wts["wp"], wts["wqkv_t"], wts["vec"], wts["b_kv"], wts["kexp"])


def pool_norm_kernel(own_ref, got_ref, vec_ref, kv_ref):
    for member in range(2):
        part = slice(member * DIM, member * DIM + DIM)
        hat, _ = normalized(own_ref[part] + got_ref[part])
        kv_ref[part] = (hat * column(vec_ref, 5 + 2 * member) + column(vec_ref, 6 + 2 * member)).astype(BF16)


def call_pool_norm(own, got, vec):
    return pl.pallas_call(
        pool_norm_kernel, out_shape=jax.ShapeDtypeStruct(own.shape, BF16), name="pool_norm",
        cost_estimate=pl.CostEstimate(flops=own.size * 10, bytes_accessed=own.size * 10, transcendentals=0))(own, got, vec)


def pool_back_kernel(own_ref, got_ref, grad_ref, vec_ref, pre_ref, sums_ref):
    for member in range(2):
        part = slice(member * DIM, member * DIM + DIM)
        hat, rstd = normalized(own_ref[part] + got_ref[part])
        grad = grad_ref[part].astype(F32)
        pre_ref[part] = norm_back(grad, hat, rstd, column(vec_ref, 5 + 2 * member))
        sums_ref[2 * member] = fold_lanes(grad * hat)
        sums_ref[2 * member + 1] = fold_lanes(grad)


def call_pool_back(own, got, grad, vec):
    return pl.pallas_call(
        pool_back_kernel,
        out_shape=[jax.ShapeDtypeStruct(own.shape, F32), jax.ShapeDtypeStruct((4, DIM, 128), F32)], name="pool_back",
        cost_estimate=pl.CostEstimate(flops=own.size * 20, bytes_accessed=own.size * 16, transcendentals=0))(own, got, grad, vec)


def lane_bit(lane, bit):
    return (lane & bit) != 0


def relative_terms(block, products, key_rows):
    lane = lane_ids(128, WIN)
    parts = [products[WIN * s : WIN * s + WIN] for s in range(8)]
    for bit in (1, 2, 4):
        chosen = lane_bit(lane, bit)
        parts = [jnp.where(chosen, parts[2 * k + 1], parts[2 * k]) for k in range(len(parts) // 2)]
    by_col = parts[0]
    for bit, step in ((8, 1), (16, 2)):
        by_col = jnp.where(lane_bit(lane, bit), by_col, pltpu.roll(by_col, WIN - step, 0))
    by_col = by_col[0:32] if block & 2 else by_col[4:36]
    lane = lane_ids(128, key_rows)
    rows = products[8 * WIN :]
    parts = [rows[key_rows * r : key_rows * r + key_rows] for r in range(4 * (block & 1), 4 * (block & 1) + 4)]
    for bit in (32, 64):
        chosen = lane_bit(lane, bit)
        parts = [jnp.where(chosen, parts[2 * k + 1], parts[2 * k]) for k in range(len(parts) // 2)]
    return jnp.concatenate([parts[0], by_col], axis=0)


def relative_spread(block, grad_terms, key_rows):
    lane = lane_ids(128, WIN)
    by_row = grad_terms[:key_rows]
    if block & 2:
        pieces = [grad_terms[key_rows:], jnp.zeros((WIN - 32, 128), F32)]
    else:
        pieces = [jnp.zeros((4, 128), F32), grad_terms[key_rows:], jnp.zeros((WIN - 36, 128), F32)]
    by_col = jnp.concatenate(pieces, axis=0)
    for bit, step in ((8, 1), (16, 2)):
        by_col = jnp.where(lane_bit(lane, bit), by_col, pltpu.roll(by_col, step, 0))
    parts = [jnp.where((lane & 7) == s, by_col, 0.0) for s in range(8)]
    lane = lane_ids(128, key_rows)
    for r in range(8):
        hit = (lane >> 5) == r - 4 * (block & 1)
        parts.append(jnp.where(hit, by_row, 0.0) if r // 4 == block & 1 else jnp.zeros((key_rows, 128), F32))
    return jnp.concatenate(parts, axis=0).astype(BF16)


def gelu_parts(hidden):
    cumulative = 0.5 + 0.5 * lax.erf(hidden * 0.7071067811865476)
    slope = cumulative + hidden * (jnp.exp(hidden * hidden * -0.5) * 0.3989422804014327)
    return (hidden * cumulative).astype(BF16), slope.astype(BF16)


def forward_kernel(ext_ref, row_ref, q_ref, top_ref, bot_ref, x0_ref, kv_ref, vec_ref, rw_ref, wprojt_ref, w1t_ref, b1_ref, w2t_ref,
                   hat_ref, query_ref, terms_ref, att_ref, act_ref, slope_ref, hat2_ref, hat3_ref, stat_ref, pool_ref, ka_ref, kn_ref, v_ref, ztop_ref, zbot_ref, pre_ref, wide_ref, wb1_ref,
                   *, offset, key_rows):
    images, heights, breadths, row_oks = group_extents(ext_ref, row_ref, offset)
    depth = DIM + aug_rows(key_rows)

    @pl.when(pl.program_id(0) == 0)
    def _():
        fill_wide(wide_ref, vec_ref, list(range(15, 24)) + [3, 4, 9, 10, 11, 12])
        wb1_ref[...] = jnp.broadcast_to(b1_ref[...], (MLP, 128))

    lane = lane_ids(CANVAS_W, DIM)
    for g in range(GROUP):
        v_ref[g] = key_tables(kv_ref, images[g], key_rows, heights[g], breadths[g], ka_ref, kn_ref.at[g]).astype(BF16)
        for halo_ref, dst_ref, tap_row, target in ((top_ref, ztop_ref, 0, 0), (bot_ref, zbot_ref, 2, 96)):
            halo = halo_ref[g].astype(F32)
            left = jnp.where(lane == 0, 0.0, pltpu.roll(halo, 1, 1))
            right = jnp.where(lane == CANVAS_W - 1, 0.0, pltpu.roll(halo, CANVAS_W - 1, 1))
            taps = [wide(wide_ref, 3 * tap_row + k, CANVAS_W) for k in range(3)]
            spread_halo(dst_ref.at[g], taps[0] * left + taps[1] * halo + taps[2] * right, target)
    pool_ref[...] = jnp.zeros_like(pool_ref)

    def step(pair, carry):
        for group in range(0, DIM, 16):
            part = slice(group, group + 16)
            taps = [wide_ref[k, part] for k in range(9)]
            for g in range(GROUP):
                window = q_ref[g, part, pl.ds(pl.multiple_of(pair * PAIR, 128), PAIR + 512)]
                for tile in range(2):
                    sums = []
                    for side in range(2):
                        shifts = col_shifts(window, 256 + 256 * tile + 128 * side)
                        sums.append([sum(taps[3 * r + c] * shifts[c] for c in range(3)) for r in range(3)])
                    halo = pl.ds(pl.multiple_of((2 * pair + tile) * 128, 128), 128)
                    down = rows_down(sums[0][0], sums[1][0], ztop_ref[g, part, halo])
                    up = rows_up(sums[0][2], sums[1][2], zbot_ref[g, part, halo])
                    for side in range(2):
                        base = PAIR * g + 256 * tile + 128 * side
                        pre_ref[part, base : base + 128] = sums[side][1] + down[side] + up[side]

        def query_of(k, pre):
            hat, rstd = normalized(pre)
            return hat.astype(BF16), (hat * wide_ref[9] + wide_ref[10]).astype(BF16), rstd

        hat, query, rstd = by_lanes(query_of, pre_ref[...])
        store_pair(hat_ref, pair, hat)
        store_pair(query_ref, pair, query)

        def extra_of(k, products):
            terms = relative_terms(k, products, key_rows) * (DIM**0.5)
            high = terms.astype(BF16).astype(F32)
            return (jnp.concatenate([high, terms - high, jnp.ones((16, 128), F32)], axis=0).astype(BF16),)

        (extra,) = by_lanes(extra_of, dot(rw_ref[pair], query))
        store_pair(terms_ref, pair, extra)

        def softmax(k, scores):
            peak = jnp.max(scores, axis=0, keepdims=True)
            weights = jnp.exp2((scores - peak) * EXP2_SCALE)
            inverse = 1.0 / jnp.sum(weights, axis=0, keepdims=True)
            return (weights * inverse).astype(BF16), peak, inverse

        long_query = by_image(jnp.concatenate([query, extra], axis=0))
        scores = jnp.concatenate([dot(kn_ref[g, :, :depth], long_query[g]) for g in range(GROUP)], axis=1)
        probs, peak, inverse = by_lanes(softmax, scores)
        mixed = by_image(probs)
        mixed = jnp.concatenate([dot(v_ref[g], mixed[g]) for g in range(GROUP)], axis=1)
        attended = (mixed + query.astype(F32)).astype(BF16)
        store_pair(att_ref, pair, attended)

        def second_norm(k, x0, out):
            x1 = x0 + (out + wide_ref[11])
            hat, rstd = normalized(x1)
            return x1, (hat * wide_ref[12] + wide_ref[13]).astype(BF16), hat.astype(BF16), rstd

        x1, normed, hat_two, rstd_two = by_lanes(second_norm, load_pair(x0_ref, pair), dot(wprojt_ref[...], attended))
        store_pair(hat2_ref, pair, hat_two)
        act, slope = by_blocks(lambda part, hidden: gelu_parts(hidden + wb1_ref[part]), 64, dot(w1t_ref[...], normed))
        store_pair(act_ref, pair, act)
        store_pair(slope_ref, pair, slope)

        def third_norm(k, x1, out, mask):
            hat, rstd = normalized(x1 + (out + wide_ref[14]))
            return hat * mask, hat.astype(BF16), rstd

        kept, hat_three, rstd_three = by_lanes(third_norm, x1, dot(w2t_ref[...], act), pair_mask(pair, breadths, row_oks))
        store_pair(hat3_ref, pair, hat_three)
        stats = [peak, inverse, rstd, rstd_two, rstd_three, jnp.zeros((3, GROUP * PAIR), F32)]
        store_pair(stat_ref, pair, jnp.concatenate(stats, axis=0))
        for g, part in enumerate(by_image(kept)):
            pool_ref[g] += fold_lanes(part)
        return carry

    lax.fori_loop(0, pair_count(breadths), step, 0)


def call_forward(ext, row, q, top, bot, x0, kv, wts, offset):
    whole, per = specs()
    images, key_rows = q.shape[0], kv.shape[0]
    more = aug_rows(key_rows)
    shapes = [(rows, BF16) for rows in (DIM, DIM, more, DIM, MLP, MLP, DIM, DIM)]
    shapes = [((rows, TOKENS), kind) for rows, kind in shapes] + [((8, TOKENS), F32), ((DIM, 128), F32)]
    keys = key_rows * 32
    return pl.pallas_call(
        functools.partial(forward_kernel, offset=offset, key_rows=key_rows),
        grid_spec=pltpu.PrefetchScalarGridSpec(
            num_scalar_prefetch=2, grid=(images // GROUP,),
            in_specs=[
                per(DIM, PADDED), per(DIM, CANVAS_W), per(DIM, CANVAS_W), per(DIM, TOKENS),
                key_lanes(key_rows, 2 * DIM),
                whole(DIM, 64), whole(PAIRS, 8 * WIN + 8 * key_rows, DIM), whole(DIM, DIM), whole(MLP, DIM), whole(MLP, 1),
                whole(DIM, MLP)],
            out_specs=[per(*s) for s, _ in shapes],
            scratch_shapes=[
                pltpu.VMEM((DIM + more, keys), BF16), pltpu.VMEM((GROUP, keys, 256), BF16), pltpu.VMEM((GROUP, DIM, keys), BF16),
                pltpu.VMEM((GROUP, DIM, 1024), F32), pltpu.VMEM((GROUP, DIM, 1024), F32), pltpu.VMEM((DIM, GROUP * PAIR), F32),
                pltpu.VMEM((15, DIM, 128), F32), pltpu.VMEM((MLP, 128), F32)]),
        out_shape=[jax.ShapeDtypeStruct((images,) + s, t) for s, t in shapes],
        compiler_params=pltpu.CompilerParams(vmem_limit_bytes=VMEM_BYTES),
        cost_estimate=pl.CostEstimate(flops=images * 5_000_000_000, bytes_accessed=images * 4_000_000, transcendentals=0),
        name="forward",
    )(ext, row, q, top, bot, x0, kv, wts["vec"], wts["rw"], wts["wproj_t"], wts["w1_t"], wts["b1"], wts["w2_t"])


def backward_kernel(ext_ref, row_ref, hat_ref, query_ref, terms_ref, att_ref, act_ref, slope_ref, hat2_ref, hat3_ref, stat_ref, q_ref, top_ref, bot_ref, kv_ref,
                    gvec_ref, vec_ref, rwt_ref, wproj_ref, w1_ref, w2_ref,
                    dx1_ref, dq_ref, up_ref, down_ref, dkv_ref, a2_ref, a1_ref, ap_ref, av_ref, ak_ref, ar_ref,
                    ka_ref, kn_ref, vn_ref, dp_ref, qtop_ref, qbot_ref, ru_ref, rd_ref, dk_ref, dv_ref, wide_ref, *, offset, key_rows):
    now = pl.program_id(0)
    steps = pl.num_programs(0) - 1
    images, heights, breadths, row_oks = group_extents(ext_ref, row_ref, offset, jnp.minimum(now, steps - 1))
    _, _, former, _ = group_extents(ext_ref, row_ref, offset, jnp.maximum(now - 1, 0))
    depth = DIM + aug_rows(key_rows)
    count = jnp.where(now < steps, pair_count(breadths), 0)
    former_count = pair_count(former)
    dp_now, dp_former = now & 1, (now & 1) ^ 1

    @pl.when(pl.program_id(0) == 0)
    def _():
        for ref in (a2_ref, a1_ref, ap_ref, av_ref, ak_ref, ar_ref, ru_ref, rd_ref):
            ref[...] = jnp.zeros_like(ref)
        fill_wide(wide_ref, vec_ref, list(range(15, 24)) + [3, 10, 11, 13])
        dp_ref[...] = jnp.zeros_like(dp_ref)

    for g in range(GROUP):
        values = key_tables(kv_ref, images[g], key_rows, heights[g], breadths[g], ka_ref.at[g], kn_ref.at[g])
        padded_values = jnp.concatenate([values, jnp.zeros((128 - DIM, values.shape[1]), F32)], axis=0)
        vn_ref[g] = jnp.transpose(padded_values).astype(BF16)
        spread_halo(qtop_ref.at[g], top_ref[g], 0)
        spread_halo(qbot_ref.at[g], bot_ref[g], 96)
    for ref in (dk_ref, dv_ref, dp_ref.at[dp_now]):
        ref[...] = jnp.zeros_like(ref)

    def step(pair, carry):
        ones = jnp.ones((16, GROUP * PAIR), BF16)
        stat = load_pair(stat_ref, pair)

        def third_back(k, hat, stat, mask):
            grad = norm_back(gvec_ref[k * 128 // PAIR] * mask, hat.astype(F32), stat[4:5], wide_ref[12])
            return grad, grad.astype(BF16)

        grad_x2, grad_mlp = by_lanes(third_back, load_pair(hat3_ref, pair), stat, pair_mask(pair, breadths, row_oks))
        act = load_pair(act_ref, pair)
        a2_ref[...] += dot_nt(grad_mlp, jnp.concatenate([act, ones], axis=0))
        (grad_hidden,) = by_blocks(
            lambda part, grad, slope: ((grad * slope.astype(F32)).astype(BF16),), 64, dot(w2_ref[...], grad_mlp), load_pair(slope_ref, pair))
        hat_two = load_pair(hat2_ref, pair)
        (normed,) = by_lanes(lambda k, hat: ((hat.astype(F32) * wide_ref[10] + wide_ref[11]).astype(BF16),), hat_two)
        a1_ref[...] += dot_nt(jnp.concatenate([normed, ones], axis=0), grad_hidden)

        def second_back(k, grad, hat, stat, grad_x2):
            hat = hat.astype(F32)
            total = grad_x2 + norm_back(grad, hat, stat[3:4], wide_ref[10])
            return total.astype(BF16), grad * hat

        grad_normed = dot(w1_ref[...], grad_hidden)
        grad_proj, scaled = by_lanes(second_back, grad_normed, hat_two, stat, grad_x2)
        av_ref[0] += fold_lanes(scaled)
        av_ref[1] += fold_lanes(grad_normed)
        store_pair(dx1_ref, pair, grad_proj)
        attended = load_pair(att_ref, pair)
        ap_ref[...] += dot_nt(jnp.concatenate([attended, ones], axis=0), grad_proj)
        grad_att = dot(wproj_ref[...], grad_proj)
        grad_att_low = grad_att.astype(BF16)
        hat = load_pair(hat_ref, pair)
        query = load_pair(query_ref, pair)
        long_query = by_image(jnp.concatenate([query, load_pair(terms_ref, pair)], axis=0))
        scores = jnp.concatenate([dot(kn_ref[g, :, :depth], long_query[g]) for g in range(GROUP)], axis=1)
        low = by_image(grad_att_low)
        grad_probs = jnp.concatenate([dot(vn_ref[g, :, :DIM], low[g]) for g in range(GROUP)], axis=1)

        def softmax_back(k, scores, grad_probs, stat):
            probs = jnp.exp2((scores - stat[0:1]) * EXP2_SCALE) * stat[1:2]
            inner = jnp.sum(probs * grad_probs, axis=0, keepdims=True)
            return probs.astype(BF16), (probs * (grad_probs - inner)).astype(BF16)

        probs, grad_scores = by_lanes(softmax_back, scores, grad_probs, stat)
        probs, grad_scores, queries = by_image(probs), by_image(grad_scores), by_image(query)
        back = []
        for g in range(GROUP):
            back.append(dot(ka_ref[g, : DIM + key_rows + 32, :], grad_scores[g]))
            dv_ref[g] += dot_nt(low[g], probs[g])
            dk_ref[g] += dot_nt(queries[g], grad_scores[g])
        back = jnp.concatenate(back, axis=1)
        (spread,) = by_lanes(lambda k, terms: (relative_spread(k, terms, key_rows),), back[DIM:])
        ar_ref[pair] += dot_nt(query, spread)

        def query_back(k, grad_att, back, far, hat, stat):
            grad = grad_att + back * SCALE + far
            hat = hat.astype(F32)
            return norm_back(grad, hat, stat[2:3], wide_ref[9]), grad * hat, grad

        grad_pre, scaled, grad = by_lanes(query_back, grad_att, back[:DIM], dot(rwt_ref[pair], spread), hat, stat)
        av_ref[2] += fold_lanes(scaled)
        av_ref[3] += fold_lanes(grad)
        store_pair(dp_ref.at[dp_now], pair, grad_pre.astype(BF16), 256)
        return carry

    def pool_step(pair, carry):
        for group in range(0, DIM, 16):
            part = slice(group, group + 16)
            taps = [wide_ref[k, part] for k in range(9)]
            grads = [None] * 9
            for g in range(GROUP):
                window = dp_ref[dp_former, g, part, pl.ds(pl.multiple_of(pair * PAIR, 128), PAIR + 512)]
                for tile in range(2):
                    base = pair * PAIR + 256 * tile
                    halo = pl.ds(pl.multiple_of((2 * pair + tile) * 128, 128), 128)
                    query = [q_ref[g, part, pl.ds(pl.multiple_of(base + 256 + 128 * side, 128), 128)] for side in range(2)]
                    above = rows_down(query[0], query[1], qtop_ref[g, part, halo])
                    under = rows_up(query[0], query[1], qbot_ref[g, part, halo])
                    sums = []
                    for side in range(2):
                        left, here, right = col_shifts(window, 256 + 256 * tile + 128 * side)
                        shifts = (right, here, left)
                        sums.append([sum(taps[3 * r + c] * shifts[c] for c in range(3)) for r in range(3)])
                        for r, rows in enumerate((above[side], query[side], under[side])):
                            rows = rows.astype(F32)
                            for c in range(3):
                                term = shifts[c] * rows
                                grads[3 * r + c] = term if grads[3 * r + c] is None else grads[3 * r + c] + term
                    zero = jnp.zeros((16, 128), F32)
                    up = rows_up(sums[0][0], sums[1][0], zero)
                    down = rows_down(sums[0][2], sums[1][2], zero)
                    for side in range(2):
                        lanes = pl.ds(pl.multiple_of(base + 128 * side, 128), 128)
                        dq_ref[g, part, lanes] = (sums[side][1] + up[side] + down[side]).astype(BF16)
                    ru_ref[g, part, halo] = up[2]
                    rd_ref[g, part, halo] = down[2]
            for k in range(9):
                ak_ref[k, part] += grads[k]
        return carry

    def pool_idle(pair, carry):
        for ref in (ru_ref, rd_ref):
            for g in range(GROUP):
                ref[g, :, pl.ds(pl.multiple_of(pair * 256, 128), 256)] = jnp.zeros((DIM, 256), F32)
        return carry

    lax.fori_loop(0, count, lambda pair, carry: step(pair, pool_step(pair, carry)), 0)
    lax.fori_loop(count, former_count, pool_step, 0)
    lax.fori_loop(former_count, PAIRS, pool_idle, 0)

    @pl.when(now < steps)
    def _():
        lane = lane_ids(128, 2 * DIM)
        for g in range(GROUP):
            for i in range(key_rows):
                block = slice(128 * (i // 4), 128 * (i // 4) + 128)
                value = jnp.concatenate([dk_ref[g, :, block] * SCALE, dv_ref[g, :, block]], axis=0)
                value = pltpu.roll(value, (4 + (images[g] & 3) - i % 4) * 32 & 127, 1)
                slot = reverse_bits(jnp.bitwise_xor(row_ref[0], i), key_rows)
                dkv_ref[slot] = jnp.where((lane >> 5) == (images[g] & 3), value, dkv_ref[slot])

    for g in range(GROUP):
        up_ref[g] = gather_halo(ru_ref.at[g], 96).astype(BF16)
        down_ref[g] = gather_halo(rd_ref.at[g], 0).astype(BF16)


def call_backward(ext, row, saved, q, top, bot, kv, gvec, wts, offset):
    whole, _ = specs()
    images, key_rows = q.shape[0], kv.shape[0]
    more = aug_rows(key_rows)
    keys = key_rows * 32
    window = 8 * WIN + 8 * key_rows
    steps = images // GROUP
    now = lambda *shape: pl.BlockSpec((GROUP,) + shape, lambda i, *_: (jnp.minimum(i, steps - 1),) + (0,) * len(shape))
    former = lambda *shape: pl.BlockSpec((GROUP,) + shape, lambda i, *_: (jnp.maximum(i - 1, 0),) + (0,) * len(shape))
    heads = pl.BlockSpec((key_rows, 2 * DIM, 128), lambda i, *_: (0, 0, jnp.minimum(i, steps - 1) * GROUP >> 2))
    shapes = [(DIM, TOKENS), (DIM, TOKENS), (DIM, CANVAS_W), (DIM, CANVAS_W)]
    sums = [(DIM, MLP + 16), (DIM + 16, MLP), (DIM + 16, DIM), (4, DIM, 128), (9, DIM, 128), (PAIRS, DIM, window)]
    return pl.pallas_call(
        functools.partial(backward_kernel, offset=offset, key_rows=key_rows),
        grid_spec=pltpu.PrefetchScalarGridSpec(
            num_scalar_prefetch=2, grid=(steps + 1,),
            in_specs=[now(rows, TOKENS) for rows in (DIM, DIM, more, DIM, MLP, MLP, DIM, DIM, 8)] + [
                former(DIM, PADDED), former(DIM, CANVAS_W), former(DIM, CANVAS_W), heads, now(DIM, 1), whole(DIM, 64), whole(PAIRS, DIM, window),
                whole(DIM, DIM), whole(DIM, MLP), whole(MLP, DIM)],
            out_specs=[now(*shapes[0])] + [former(*s) for s in shapes[1:]] + [heads] + [whole(*s) for s in sums],
            scratch_shapes=[
                pltpu.VMEM((GROUP, DIM + more, keys), BF16), pltpu.VMEM((GROUP, keys, 256), BF16), pltpu.VMEM((GROUP, keys, 128), BF16),
                pltpu.VMEM((2, GROUP, DIM, PADDED), BF16)] + [pltpu.VMEM((GROUP, DIM, 1024), BF16)] * 2
            + [pltpu.VMEM((GROUP, DIM, 1024), F32)] * 2 + [pltpu.VMEM((GROUP, DIM, keys), F32)] * 2 + [pltpu.VMEM((13, DIM, 128), F32)]),
        out_shape=[jax.ShapeDtypeStruct((images,) + s, BF16) for s in shapes]
        + [jax.ShapeDtypeStruct((key_rows, 2 * DIM, 32 * images), F32)] + [jax.ShapeDtypeStruct(s, F32) for s in sums],
        compiler_params=pltpu.CompilerParams(vmem_limit_bytes=VMEM_BYTES),
        cost_estimate=pl.CostEstimate(flops=images * 12_000_000_000, bytes_accessed=images * 6_000_000, transcendentals=0),
        name="backward",
    )(ext, row, *saved, q, top, bot, kv, gvec, wts["vec"], wts["rw_t"], wts["wproj"], wts["w1"], wts["w2"])


def embed_back_kernel(ext_ref, row_ref, patch_ref, dq_ref, dx1_ref, rtop_ref, rbot_ref, nsel_ref, kvt_ref, pre_ref, under_ref,
                      wp_ref, vec_ref, wqkv_ref, kexp_ref, tapt_ref,
                      aq_ref, akv_ref, apatch_ref, av_ref, ak_ref, dn_ref, rim_ref, wide_ref, *, offset):
    images, heights, breadths, row_oks = group_extents(ext_ref, row_ref, offset)

    @pl.when(pl.program_id(0) == 0)
    def _():
        for ref in (aq_ref, akv_ref, apatch_ref, av_ref, ak_ref, dn_ref, rim_ref):
            ref[...] = jnp.zeros_like(ref)
        fill_wide(wide_ref, vec_ref, [0, 1, 2])

    lane = lane_ids(128, 2 * DIM)

    def thrice(value, image):
        block = jnp.where((lane >> 5) == 1, take_lanes(value, image, 1), take_lanes(value, image, 0))
        block = jnp.where((lane >> 5) == 2, take_lanes(value, image, 2), block)
        return jnp.where((lane >> 5) == 3, 0.0, block)

    grad_taps = []
    for g in range(GROUP):
        own = thrice(pre_ref[...], images[g])
        spread = jnp.concatenate([thrice(under_ref[...], images[g]), own, own], axis=1)
        ak_ref[...] += kvt_ref[g].astype(F32) * spread
        grad_taps.append((spread * kexp_ref[...]).astype(BF16))
    grad_taps = jnp.concatenate(grad_taps, axis=1)
    nsel = jnp.concatenate([nsel_ref[g] for g in range(GROUP)], axis=1)
    akv_ref[...] += dot_nt(jnp.concatenate([nsel, jnp.ones((16, 384 * GROUP), BF16)], axis=0), grad_taps)
    grad_sel = dot(wqkv_ref[:, DIM : 3 * DIM], grad_taps)
    parts = [grad_sel.astype(BF16)[:, 128 * k : 128 * k + 128] for k in range(3 * GROUP)]
    lines = dot(jnp.concatenate(parts, axis=0), tapt_ref[...])
    for g in range(GROUP):
        for k, start in enumerate((224, 0, 32)):
            first = DIM * (3 * g + k)
            line = lines[first : first + DIM]
            for tile in range(TILES):
                dn_ref[g, :, 256 * tile + start : 256 * tile + start + 32] = line[:, 32 * tile : 32 * tile + 32]
        for halo_ref, start in ((rtop_ref, 0), (rbot_ref, 224)):
            line = halo_ref[g].astype(F32)
            for tile in range(TILES):
                rim_ref[g, :, 256 * tile + start : 256 * tile + start + 32] = line[:, 32 * tile : 32 * tile + 32]

    def step(pair, carry):
        mask = pair_mask(pair, breadths, row_oks)
        patches = load_pair(patch_ref, pair)

        def first_norm(k, embed, mask, grad, rim):
            hat, rstd = normalized((embed + wide_ref[0]) * mask)
            return hat, rstd, (hat * wide_ref[1] + wide_ref[2]).astype(BF16), (grad.astype(F32) + rim).astype(BF16)

        hat, rstd, normed, grad_q = by_lanes(first_norm, dot(wp_ref[...], patches), mask, load_pair(dq_ref, pair), load_pair(rim_ref, pair))
        aq_ref[...] += dot_nt(jnp.concatenate([normed, jnp.ones((16, GROUP * PAIR), BF16)], axis=0), grad_q)

        def first_back(k, out, extra, hat, rstd, mask, dx1):
            grad = out + extra
            total = (dx1.astype(F32) + norm_back(grad, hat, rstd, wide_ref[1])) * mask
            return total.astype(BF16), total, grad * hat, grad

        low, total, scaled, grad = by_lanes(
            first_back, dot(wqkv_ref[:, 0:DIM], grad_q), load_pair(dn_ref, pair), hat, rstd, mask, load_pair(dx1_ref, pair))
        av_ref[0] += fold_lanes(total)
        av_ref[1] += fold_lanes(scaled)
        av_ref[2] += fold_lanes(grad)
        apatch_ref[...] += dot_nt(low, patches)
        return carry

    lax.fori_loop(0, pair_count(breadths), step, 0)


def call_embed_back(ext, row, patches, dq, dx1, rtop, rbot, nsel, kvt, pre, under, consts, wts, offset):
    whole, per = specs()
    images = dq.shape[0]
    sums = [(DIM + 16, DIM), (DIM + 16, 2 * DIM), (DIM, PATCH_ROWS), (3, DIM, 128), (2 * DIM, 384)]
    return pl.pallas_call(
        functools.partial(embed_back_kernel, offset=offset),
        grid_spec=pltpu.PrefetchScalarGridSpec(
            num_scalar_prefetch=2, grid=(images // GROUP,),
            in_specs=[
                per(PATCH_ROWS, TOKENS), per(DIM, TOKENS), per(DIM, TOKENS), per(DIM, CANVAS_W), per(DIM, CANVAS_W),
                per(DIM, 384), per(2 * DIM, 384), key_lanes(2 * DIM), key_lanes(2 * DIM),
                whole(DIM, PATCH_ROWS), whole(DIM, 64), whole(DIM, 3 * DIM), whole(2 * DIM, 384), whole(128, CANVAS_W)],
            out_specs=[whole(*s) for s in sums],
            scratch_shapes=[pltpu.VMEM((GROUP, DIM, TOKENS), F32)] * 2 + [pltpu.VMEM((3, DIM, 128), F32)]),
        out_shape=[jax.ShapeDtypeStruct(s, F32) for s in sums],
        compiler_params=pltpu.CompilerParams(vmem_limit_bytes=VMEM_BYTES),
        cost_estimate=pl.CostEstimate(flops=images * 3_000_000_000, bytes_accessed=images * 3_000_000, transcendentals=0),
        name="embed_back",
    )(ext, row, patches, dq, dx1, rtop, rbot, nsel, kvt, pre, under, wts["wp"], wts["vec"], wts["wqkv"], wts["kexp"], consts["tap_t"])


def bit_count(size):
    return size.bit_length() - 1


def swap(value, axis, bit):
    size = lax.axis_size(axis)
    return lax.ppermute(value, axis, [(i, i ^ (1 << bit)) for i in range(size)])


def shifted(value, axis, step):
    size = lax.axis_size(axis)
    pairs = [(i, i + step) for i in range(size) if 0 <= i + step < size]
    return lax.ppermute(value, axis, pairs)


def summed(value, axis):
    for bit in range(bit_count(lax.axis_size(axis))):
        value = value + swap(value, axis, bit)
    return value


def scatter_slots(value, axis):
    for bit in range(bit_count(lax.axis_size(axis))):
        half = value.shape[0] // 2
        value = value[:half] + swap(value[half:].astype(BF16), axis, bit).astype(F32)
    return value[0]


def gather_params(value):
    dims = []
    for axis in ("img", "row"):
        index = lax.axis_index(axis)
        for bit in reversed(range(bit_count(lax.axis_size(axis)))):
            other = swap(value, axis, bit)
            mine_second = (index >> bit) & 1 == 1
            value = jnp.stack([jnp.where(mine_second, other, value), jnp.where(mine_second, value, other)])
            dims.append((axis, bit))
    dims = dims[::-1]
    wanted = [("img", b) for b in reversed(range(bit_count(lax.axis_size("img"))))]
    wanted += [("row", b) for b in reversed(range(bit_count(lax.axis_size("row"))))]
    order = [dims.index(d) for d in wanted]
    value = jnp.transpose(value, order + [value.ndim - 2, value.ndim - 1])
    return value.reshape(-1)


def scatter_grads(flat):
    rows, imgs = lax.axis_size("row"), lax.axis_size("img")
    names = [("img", b) for b in reversed(range(bit_count(imgs)))] + [("row", b) for b in reversed(range(bit_count(rows)))]
    leaf = flat.shape[0] // (rows * imgs)
    value = flat.reshape((2,) * len(names) + (leaf // 128, 128))
    for axis, bits in (("row", range(bit_count(rows))), ("img", range(bit_count(imgs)))):
        index = lax.axis_index(axis)
        for bit in bits:
            place = names.index((axis, bit))
            names.pop(place)
            own = (index >> bit) & 1
            keep = lax.dynamic_index_in_dim(value, own, place, False)
            send = lax.dynamic_index_in_dim(value, 1 - own, place, False)
            value = keep + swap(send, axis, bit)
    return value.reshape(leaf)


def segment_list(canvas_rows, canvas_cols):
    return [
        ("w_patch", (3 * PATCH * PATCH, DIM)),
        ("w_qkv", (DIM, 3 * DIM)),
        ("w_proj", (DIM, DIM)),
        ("w_fc1", (DIM, MLP)),
        ("w_fc2", (MLP, DIM)),
        ("w_head", (DIM, CLASSES)),
        ("rel_rows", (2 * canvas_rows - 8, DIM)),
        ("rel_cols", (2 * canvas_cols - 8, DIM)),
        ("small", (49, DIM)),
        ("b_head", (CLASSES,)),
    ]


def unpack(flat_vec, segments):
    pieces = {}
    position = 0
    for seg_name, seg_shape in segments:
        entries = int(np.prod(seg_shape))
        pieces[seg_name] = flat_vec[position : position + entries].reshape(seg_shape)
        position += entries
    return pieces


def patch_rows(weight):
    taps = jnp.pad(weight.reshape(PATCH, PATCH, 3, DIM), ((0, 1), (0, 0), (0, 1), (0, 0)))
    parts = []
    for piece in (taps[:, 3:7], taps[:, 0:3]):
        phases = piece.shape[1]
        parts.append(jnp.transpose(piece.reshape(2, 4, phases, 4, DIM), (0, 2, 1, 3, 4)).reshape(32 * phases, DIM))
    return jnp.concatenate(parts, axis=0)


def patch_rows_back(grad):
    rows = grad.T
    parts = []
    for piece, phases in ((rows[128:], 3), (rows[:128], 4)):
        taps = jnp.transpose(piece.reshape(2, phases, 4, 4, DIM), (0, 2, 1, 3, 4)).reshape(8, phases, 4, DIM)
        parts.append(taps[:PATCH, :, :3])
    return jnp.concatenate(parts, axis=1).reshape(3 * PATCH * PATCH, DIM)


def relative_windows(rel_rows, rel_cols, row_index, key_rows):
    offsets = jnp.flip(rel_cols.reshape(-1, 8, DIM), 0)
    offsets = jnp.transpose(jnp.pad(offsets, ((0, 1), (0, 0), (0, 0))), (1, 0, 2))
    blocks = rel_rows.reshape(2 * key_rows - 1, 8, DIM)
    rows = jnp.transpose(jnp.flip(lax.dynamic_slice_in_dim(blocks, row_index, key_rows, 0), 0), (1, 0, 2))
    rows = rows.reshape(8 * key_rows, DIM)
    windows = []
    for pair in range(PAIRS):
        cols = offsets[:, 24 - 8 * pair : 24 - 8 * pair + WIN].reshape(8 * WIN, DIM)
        windows.append(jnp.concatenate([cols, rows], axis=0))
    return jnp.stack(windows)


def relative_windows_back(grad, row_index, key_rows):
    grad = jnp.transpose(grad, (0, 2, 1))
    cols = grad[:, : 8 * WIN].reshape(PAIRS, 8, WIN, DIM)
    total = 0.0
    for pair in range(PAIRS):
        start = 24 - 8 * pair
        total = total + jnp.pad(cols[pair], ((0, 0), (start, 64 - start - WIN), (0, 0)))
    rel_cols = jnp.flip(jnp.transpose(total[:, :63], (1, 0, 2)), 0).reshape(-1, DIM)
    rows = jnp.sum(grad[:, 8 * WIN :], axis=0).reshape(8, key_rows, DIM)
    rows = jnp.flip(jnp.transpose(rows, (1, 0, 2)), 0)
    blocks = lax.dynamic_update_slice_in_dim(jnp.zeros((2 * key_rows - 1, 8, DIM), F32), rows, row_index, 0)
    return blocks.reshape(-1, DIM), rel_cols


def tap_keep():
    keep = np.ones((3, 4, 32), np.float32)
    keep[:, 3] = 0.0
    keep[:, 0, 0] = 0.0
    return keep


def prepare(weights, row_index, key_rows):
    small = weights["small"]
    vec = jnp.pad(small.astype(F32).T, ((0, 0), (0, 15)))
    kernels = small[9:27].reshape(2, 3, 3, DIM).astype(F32)
    expanded = jnp.pad(jnp.transpose(kernels, (0, 3, 1, 2)), ((0, 0), (0, 0), (0, 0), (0, 1)))
    kexp = (expanded[..., None] * tap_keep()).reshape(2 * DIM, 384)
    windows = relative_windows(weights["rel_rows"], weights["rel_cols"], row_index, key_rows)
    return {
        "vec": vec,
        "kexp": kexp,
        "wp": patch_rows(weights["w_patch"]).T,
        "wqkv": weights["w_qkv"],
        "wqkv_t": weights["w_qkv"].T,
        "b_kv": small[43:45].astype(F32).reshape(2 * DIM, 1),
        "wproj": weights["w_proj"],
        "wproj_t": weights["w_proj"].T,
        "w1": weights["w_fc1"],
        "w1_t": weights["w_fc1"].T,
        "b1": small[45:49].astype(F32).reshape(MLP, 1),
        "w2": weights["w_fc2"],
        "w2_t": weights["w_fc2"].T,
        "rw": windows,
        "rw_t": jnp.transpose(windows, (0, 2, 1)),
    }


def image_loss(pooled, head_w, head_b, teacher, labels, image_total):
    logits = jnp.dot(pooled, head_w, precision=HIGHEST_PREC) + head_b
    log_student = jax.nn.log_softmax(logits, axis=-1)
    log_teacher = jax.nn.log_softmax(teacher, axis=-1)
    onehot = (jnp.arange(CLASSES)[None, :] == labels[:, None]).astype(F32)
    per_image = jnp.sum(jnp.exp(log_teacher) * (log_teacher - log_student), axis=-1) - jnp.sum(onehot * log_student, axis=-1)
    return jnp.sum(per_image) / image_total


def body(flat_params, first_moment, second_moment, pixels, extents, labels, teacher):
    key_rows = lax.axis_size("row")
    row_index = lax.axis_index("row")
    row_lead = row_index == 0
    segments = segment_list(ROWS * key_rows, CANVAS_W)
    full_params = gather_params(flat_params.astype(BF16).reshape(-1, 128))
    weights = unpack(full_params, segments)
    wts = prepare(weights, row_index, key_rows)
    tap = tap_matrix()
    consts = {"perm": jnp.asarray(deinterleave_matrix(), BF16), "tap": jnp.asarray(tap, BF16), "tap_t": jnp.asarray(tap.T, BF16)}
    vectors = weights["small"][27:42].astype(F32)
    row = row_index.astype(jnp.int32).reshape(1)
    images = pixels.shape[0]
    parts = 1
    size = images // parts
    image_total = images * lax.axis_size("img") * 1.0
    head_w = weights["w_head"].astype(F32)
    head_b = weights["b_head"].astype(F32)

    ids = jnp.arange(images)
    widths = extents[:, 1]
    ahead = (widths[None, :] > widths[:, None]) | ((widths[None, :] == widths[:, None]) & (ids[None, :] < ids[:, None]))
    places = jnp.sum(ahead.astype(jnp.int32), axis=1)
    chosen = places[None, :] == ids[:, None]
    order = jnp.sum(jnp.where(chosen, ids[None, :], 0), axis=1)
    ext = jnp.sum(jnp.where(chosen[:, :, None], extents[None], 0), axis=1)

    saved = []
    for part in range(parts):
        patches, x0, q, first, last, nsel, kvt, below, own = call_embed(ext, row, order, pixels, consts, wts, size, part * size)
        top = shifted(last, "row", 1)
        bot = shifted(first, "row", -1)
        got = shifted(below, "row", 1)
        kv = lax.all_gather(call_pool_norm(own, got, wts["vec"]), "row", axis=0)
        saved.append(dict(patches=patches, x0=x0, q=q, top=top, bot=bot, nsel=nsel, kvt=kvt, own=own, got=got, kv=kv))
    for part in range(parts):
        s = saved[part]
        s["fwd"] = call_forward(ext, row, s["q"], s["top"], s["bot"], s["x0"], s["kv"], wts, part * size)
    total = {}

    def add(name, value):
        total[name] = total[name] + value if name in total else value

    sorted_local = jnp.sum(jnp.concatenate([s["fwd"][-1] for s in saved], axis=0), axis=-1)
    local = jnp.sum(jnp.where(chosen[:, :, None], sorted_local[:, None, :], 0.0), axis=0)
    everywhere = summed(local, "row")
    counts = (extents[:, 0] * extents[:, 1]).astype(F32)[:, None]
    pooled = (everywhere * vectors[13] + counts * vectors[14]) / counts

    def loss_of(pooled_now, w, b):
        return image_loss(pooled_now, w, b, teacher, labels, image_total)

    loss_value, loss_back = jax.vjp(loss_of, pooled, head_w, head_b)
    grad_pooled, total["w_head"], total["b_head"] = loss_back(jnp.ones_like(loss_value))
    gvec = grad_pooled / counts
    local_count = jnp.where(row_index * ROWS < extents[:, 0], ROWS * extents[:, 1], 0).astype(F32)[:, None]
    total["g_three"] = jnp.sum(gvec * local, axis=0)
    total["b_three"] = jnp.sum(gvec * local_count, axis=0)
    gvec = jnp.sum(jnp.where(chosen[:, :, None], gvec[None], 0.0), axis=1)[:, :, None]
    for part in range(parts):
        s = saved[part]
        s["bwd"] = call_backward(ext, row, s["fwd"][:-1], s["q"], s["top"], s["bot"], s["kv"], gvec[part * size : part * size + size], wts, part * size)
    for part in range(parts):
        s = saved[part]
        dx1, dq, up, down, dkv, a2, a1, ap, av, ak, ar = s["bwd"]
        for name, value in (("a2", a2), ("a1", a1), ("ap", ap), ("av", av), ("ak", ak), ("ar", ar)):
            add(name, value)
        rtop = shifted(down, "row", 1)
        rbot = shifted(up, "row", -1)
        grad_kv = scatter_slots(dkv, "row")
        pre, pool_sums = call_pool_back(s["own"], s["got"], grad_kv, wts["vec"])
        add("pool_sums", pool_sums)
        under = shifted(pre, "row", -1)
        aq, akv, apatch, av1, akt = call_embed_back(
            ext, row, s["patches"], dq, dx1, rtop, rbot, s["nsel"], s["kvt"], pre, under, consts, wts, part * size)
        for name, value in (("aq", aq), ("akv", akv), ("apatch", apatch), ("av1", av1), ("akt", akt)):
            add(name, value)

    t = total
    lead = jnp.where(row_lead, 1.0, 0.0)
    av, av1 = jnp.sum(t["av"], axis=-1), jnp.sum(t["av1"], axis=-1)
    pool_sums = jnp.sum(t["pool_sums"], axis=-1)
    rel_rows, rel_cols = relative_windows_back(t["ar"], row_index, key_rows)
    taps = jnp.sum((t["akt"].reshape(2, DIM, 3, 4, 32) * tap_keep())[:, :, :, :3], axis=-1)
    kernels = jnp.concatenate([jnp.sum(t["ak"], axis=-1), jnp.transpose(taps, (0, 2, 3, 1)).reshape(18, DIM)], axis=0)
    grad_vectors = jnp.stack([
        av1[0], av1[1], av1[2], av[2], av[3], pool_sums[0], pool_sums[1], pool_sums[2], pool_sums[3],
        t["ap"][DIM], av[0], av[1], t["a2"][:, MLP], t["g_three"], t["b_three"]])
    pieces = [
        patch_rows_back(t["apatch"]),
        jnp.concatenate([t["aq"][:DIM], t["akv"][:DIM]], axis=1),
        t["ap"][:DIM],
        t["a1"][:DIM],
        t["a2"][:, :MLP].T,
        t["w_head"] * lead,
        rel_rows,
        rel_cols,
        kernels,
        grad_vectors,
        t["aq"][DIM],
        t["akv"][DIM],
        t["a1"][DIM],
        t["b_head"] * lead,
    ]
    joined = jnp.concatenate([piece.reshape(-1) for piece in pieces])
    grad_flat = jnp.pad(joined, (0, full_params.shape[0] - joined.shape[0]))
    grad_shard = scatter_grads(grad_flat)
    norm_sq = summed(jnp.sum(grad_shard * grad_shard), "row")
    both = summed(jnp.stack([norm_sq, loss_value]), "img")
    grad_norm = jnp.sqrt(both[0])
    clip_factor = jnp.minimum(1.0, CLIP_NORM / (grad_norm + 1e-06))
    clipped = grad_shard * clip_factor
    moment_one = BETA_FIRST * first_moment + (1.0 - BETA_FIRST) * clipped
    moment_two = BETA_SECOND * second_moment + (1.0 - BETA_SECOND) * clipped * clipped
    fix_one = 1.0 - BETA_FIRST**STEP
    fix_two = 1.0 - BETA_SECOND**STEP
    update = moment_one / fix_one / (jnp.sqrt(moment_two / fix_two) + ADAM_EPS) + WEIGHT_DECAY * flat_params
    new_params = flat_params - LEARN_RATE * update
    return (new_params, moment_one, moment_two, grad_norm, both[1])


def solution(mesh):
    placed = (
        P(("img", "row")),
        P(("img", "row")),
        P(("img", "row")),
        P("img", "row", None, None, None),
        P("img", None),
        P("img"),
        P("img", None),
    )
    return jax.shard_map(
        body,
        mesh=mesh,
        in_specs=placed,
        out_specs=(P(("img", "row")), P(("img", "row")), P(("img", "row")), P(), P()),
        check_vma=False,
    )
```

```python
import functools

import jax
import jax.numpy as jnp
import numpy as np
from jax import lax
from jax.experimental import pallas as pl
from jax.experimental.pallas import tpu as pltpu
from jax.sharding import PartitionSpec as P

DIM = 96
MLP = 384
CLASSES = 1000
PATCH = 7
ROWS = 8
STEP = 7
CANVAS_W = 256

HIGHEST_PREC = lax.Precision.HIGHEST
CLIP_NORM = 0.02
LEARN_RATE = 0.05
WEIGHT_DECAY = 0.05
BETA_FIRST = 0.5
BETA_SECOND = 0.5
ADAM_EPS = 1e-08
NORM_EPS = 1e-06
NEG_FILL = -1e30

F32 = jnp.float32
BF16 = jnp.bfloat16
SCALE = DIM ** (-0.5)
EXP2_SCALE = SCALE * 1.4426950408889634

TOKENS = ROWS * CANVAS_W
PAIR = 512
PAIRS = TOKENS // PAIR
TILES = CANVAS_W // 32
GROUP = 2
PADDED = TOKENS + 512
WIN = 40
PATCH_ROWS = 256
VMEM_BYTES = 56 * 1024 * 1024


def deinterleave_matrix():
    out = np.zeros((4, 128, 4, 4, 32), np.float32)
    for row in range(4):
        for phase in range(4):
            for col in range(32):
                out[row, 4 * col + phase, phase, row, col] = 1.0
    return out.reshape(512, 512)


def tap_matrix():
    out = np.zeros((CANVAS_W, 128), np.float32)
    for tap in range(3):
        for key in range(32):
            col = 8 * key + tap - 1
            if col >= 0:
                out[col, tap * 32 + key] = 1.0
    return out


def dot(a, b):
    return jnp.dot(a, b, preferred_element_type=F32)


def dot_nt(a, b):
    return lax.dot_general(a, b, (((1,), (1,)), ((), ())), preferred_element_type=F32)


def normalized(x):
    mean = jnp.sum(x, axis=0, keepdims=True) * (1.0 / DIM)
    centered = x - mean
    var = jnp.sum(centered * centered, axis=0, keepdims=True) * (1.0 / DIM)
    rstd = lax.rsqrt(var + NORM_EPS)
    return centered * rstd, rstd


def norm_back(grad, hat, rstd, gain):
    inner = grad * gain
    mean_one = jnp.sum(inner, axis=0, keepdims=True) * (1.0 / DIM)
    mean_two = jnp.sum(inner * hat, axis=0, keepdims=True) * (1.0 / DIM)
    return rstd * (inner - mean_one - hat * mean_two)


def by_lanes(fn, *arrays):
    parts = [fn(k, *(a[:, 128 * k : 128 * k + 128] for a in arrays)) for k in range(arrays[0].shape[1] // 128)]
    return tuple(jnp.concatenate(column, axis=1) for column in zip(*parts))


def by_blocks(fn, height, *arrays):
    rows = []
    for top in range(0, arrays[0].shape[0], height):
        rows.append(by_lanes(lambda k, *block: fn(slice(top, top + height), *block), *(a[top : top + height] for a in arrays)))
    return tuple(jnp.concatenate(column, axis=0) for column in zip(*rows))


def fold_lanes(x):
    total = x[:, 0:128]
    for k in range(1, x.shape[1] // 128):
        total = total + x[:, 128 * k : 128 * k + 128]
    return total


def place_of(index):
    return index + 27 if index < 15 else index - 15 if index < 42 else index


def column(vec_ref, index):
    place = place_of(index)
    return vec_ref[:, place : place + 1]


def fill_wide(wide_ref, vec_ref, indices):
    for k, index in enumerate(indices):
        wide_ref[k] = jnp.broadcast_to(column(vec_ref, index), (DIM, 128))


def fill_taps(taps_ref, vec_ref):
    lane = lane_ids(128, DIM)
    for member in range(2):
        for r in range(3):
            block = jnp.zeros((DIM, 128), F32)
            for c in range(3):
                block = jnp.where((lane >> 5) == c, column(vec_ref, 24 + 9 * member + 3 * r + c), block)
            taps_ref[DIM * member : DIM * member + DIM, 128 * r : 128 * r + 128] = jnp.where(lane == 0, 0.0, block)


def fill_bias(bias_ref, vec_ref):
    for k in range(MLP // DIM):
        bias_ref[DIM * k : DIM * k + DIM] = jnp.broadcast_to(vec_ref[:, 45 + k : 46 + k], (DIM, 128))


def fill_transpose(dst_ref, src_ref):
    rows, cols = src_ref.shape
    value = src_ref[...].astype(F32)
    value = jnp.pad(value, ((0, -rows % 128), (0, -cols % 128)))
    dst_ref[...] = jnp.transpose(value)[:cols, :rows].astype(BF16)


def wide(wide_ref, k, width=PAIR):
    return jnp.concatenate([wide_ref[k]] * (width // 128), axis=1)


def lane_ids(width, rows=1):
    return lax.broadcasted_iota(jnp.int32, (rows, width), 1)


def pair_mask(pair, breadths, row_oks):
    lane = lane_ids(PAIR)
    col = pair * 64 + (lane >> 8) * 32 + (lane & 31)
    return jnp.concatenate([jnp.where((col < w) & ok, 1.0, 0.0).astype(F32) for w, ok in zip(breadths, row_oks)], axis=1)


def pair_lanes(pair, base=0):
    return pl.ds(pl.multiple_of(pair * PAIR + base, 128), PAIR)


def load_pair(ref, pair):
    lanes = pair_lanes(pair)
    return jnp.concatenate([ref[g, :, lanes] for g in range(GROUP)], axis=1)


def store_pair(ref, pair, value, base=0):
    for g in range(GROUP):
        ref[g, :, pair_lanes(pair, base)] = value[:, PAIR * g : PAIR * g + PAIR]


def by_image(value):
    return [value[:, PAIR * g : PAIR * g + PAIR] for g in range(GROUP)]


def pair_count(breadths):
    widest = breadths[0]
    for breadth in breadths[1:]:
        widest = jnp.maximum(widest, breadth)
    return jnp.minimum((widest >> 6) + 1, PAIRS)


def group_extents(ext_ref, row_ref, offset, group=None):
    group = pl.program_id(0) if group is None else group
    images = [group * GROUP + g for g in range(GROUP)]
    heights = [ext_ref[offset + image, 0] for image in images]
    breadths = [ext_ref[offset + image, 1] for image in images]
    return images, heights, breadths, [row_ref[0] * ROWS < height for height in heights]


def col_shifts(window, base):
    lane = lane_ids(128, window.shape[0])
    here = window[:, base : base + 128]
    before = window[:, base - 256 : base - 128]
    after = window[:, base + 256 : base + 384]
    left = jnp.where((lane & 31) == 0, pltpu.roll(before, 97, 1), pltpu.roll(here, 1, 1))
    right = jnp.where((lane & 31) == 31, pltpu.roll(after, 31, 1), pltpu.roll(here, 127, 1))
    return left.astype(F32), here.astype(F32), right.astype(F32)


def rows_down(first, second, entering):
    lane = lane_ids(128, first.shape[0])
    a, b = pltpu.roll(first, 32, 1), pltpu.roll(second, 32, 1)
    return jnp.where(lane < 32, entering, a), jnp.where(lane < 32, a, b), b


def rows_up(first, second, entering):
    lane = lane_ids(128, first.shape[0])
    a, b = pltpu.roll(first, 96, 1), pltpu.roll(second, 96, 1)
    return jnp.where(lane >= 96, b, a), jnp.where(lane >= 96, entering, b), a


def spread_halo(dst_ref, halo, target):
    for tile in range(TILES):
        block = halo[:, 128 * (tile // 4) : 128 * (tile // 4) + 128]
        shift = (target - 32 * (tile % 4)) % 128
        dst_ref[:, 128 * tile : 128 * tile + 128] = pltpu.roll(block, shift, 1) if shift else block


def store_lanes(dst_ref, value, image):
    place = image & 3
    lane = lane_ids(128, value.shape[0])
    dst_ref[...] = jnp.where((lane >> 5) == place, pltpu.roll(value, place * 32, 1), dst_ref[...])


def take_lanes(value, image, target):
    return pltpu.roll(value, (4 + target - (image & 3)) * 32 & 127, 1)


def gather_halo(src_ref, target):
    lane = lane_ids(128, DIM)
    blocks = []
    for half in range(2):
        total = None
        for k in range(4):
            tile = 4 * half + k
            block = src_ref[:, 128 * tile : 128 * tile + 128]
            shift = (32 * k - target) % 128
            block = pltpu.roll(block, shift, 1) if shift else block
            total = block if total is None else jnp.where((lane >> 5) == k, block, total)
        blocks.append(total)
    return jnp.concatenate(blocks, axis=1)


def reverse_bits(value, count):
    result = 0
    for bit in range(count.bit_length() - 1):
        result = result * 2 + ((value >> bit) & 1)
    return result


def key_tables(kv_ref, image, key_rows, height, breadth, ka_ref, kn_ref):
    lane = lane_ids(128, 2 * DIM)
    blocks = []
    for i in range(0, key_rows, 4):
        block = take_lanes(kv_ref[i].astype(F32), image, 0)
        for k in range(1, 4):
            block = jnp.where((lane >> 5) == k, take_lanes(kv_ref[i + k].astype(F32), image, k), block)
        blocks.append(block)
    both = jnp.concatenate(blocks, axis=1)
    total = key_rows * 32
    more = aug_rows(key_rows)
    rank = lax.broadcasted_iota(jnp.int32, (more, total), 0)
    key = lax.broadcasted_iota(jnp.int32, (more, total), 1)
    key_r, key_c = key >> 5, key & 31
    half = key_rows + 32
    low = rank >= half
    rank_in = jnp.where(low, rank - half, rank)
    hit = rank_in == jnp.where(rank_in < key_rows, key_r, key_c + key_rows)
    invalid = (key_r * ROWS >= height) | (key_c * ROWS >= breadth)
    table = jnp.where(rank < 2 * half, jnp.where(hit, 1.0, 0.0), 0.0)
    table = jnp.where((rank == 2 * half) & invalid, NEG_FILL, table)
    full = jnp.concatenate([both[:DIM], table, jnp.zeros((256 - DIM - more, total), F32)], axis=0)
    ka_ref[...] = full[: DIM + more].astype(BF16)
    kn_ref[...] = jnp.transpose(full).astype(BF16)
    return both[DIM:]


def aug_rows(key_rows):
    return 2 * key_rows + 64 + 16


def pixel_rows(pix_ref, s_ref):
    for a in range(4):
        for ch in range(3):
            block = pix_ref[0, a, ch].astype(F32)
            for tile in range(TILES):
                s_ref[tile, pl.ds(4 * a + ch, ROWS, stride=16), :] = block[:, 128 * tile : 128 * tile + 128]
    for a in range(3):
        for ch in range(3):
            block = pix_ref[0, 4 + a, ch].astype(F32)
            for tile in range(TILES):
                s_ref[tile, 128 + 4 * a + ch : 129 + 4 * a + ch, :] = block[ROWS - 1 : ROWS, 128 * tile : 128 * tile + 128]


def patch_blocks(s_ref, perm, shifted, sets):
    rows = [s_ref[tile] for tile in range(TILES)]
    if shifted:
        first = lane_ids(128, 144) < 4
        rolled = [pltpu.roll(block, 4, 1) for block in rows]
        rows = [jnp.where(first, rolled[tile - 1] if tile else 0.0, rolled[tile]) for tile in range(TILES)]
    rows = [block.astype(BF16) for block in rows]
    stack = []
    for chosen in sets:
        for tile in range(TILES):
            stack.append(jnp.concatenate([rows[tile][16 * r : 16 * r + 16] for r in chosen], axis=1))
    return dot(jnp.concatenate(stack, axis=0), perm).astype(BF16)


def edge_kernel(ext_ref, row_ref, order_ref, *refs, offset):
    pix_refs, refs = refs[:GROUP], refs[GROUP:]
    (perm_ref, tap_ref, wp_ref, wqkv_ref, vec_ref,
     first_ref, last_ref, nsel_ref, kvt_ref, below_ref, own_ref, s_ref, p_ref, wide_ref, kexp_ref) = refs
    images, heights, breadths, row_oks = group_extents(ext_ref, row_ref, offset)

    @pl.when(pl.program_id(0) == 0)
    def _():
        s_ref[...] = jnp.zeros_like(s_ref)
        fill_wide(wide_ref, vec_ref, [0, 1, 2, 42, 43, 44])
        fill_taps(kexp_ref, vec_ref)

    lane = lane_ids(1024)
    masks = []
    for g in range(GROUP):
        pixel_rows(pix_refs[g], s_ref)
        for shifted in range(2):
            out = patch_blocks(s_ref, perm_ref[...], shifted, ((7, 0, 1, 1), (8, 1, 2, 2)))
            for half in range(2):
                for tile in range(TILES):
                    block = out[128 * half + 16 * tile : 128 * half + 16 * tile + 16]
                    for phase in range(4):
                        top = 128 * shifted + 64 * half + 16 * phase
                        p_ref[top : top + 16, 1024 * g + 128 * tile : 1024 * g + 128 * tile + 128] = block[:, 128 * phase : 128 * phase + 128]
        col = (lane >> 7) * 32 + (lane & 31)
        masks.append(jnp.where((col < breadths[g]) & row_oks[g], 1.0, 0.0).astype(F32))

    def first_norm(k, embed, mask):
        hat, _ = normalized((embed + wide_ref[0]) * mask)
        return ((hat * wide_ref[1] + wide_ref[2]).astype(BF16).astype(F32),)

    (normed,) = by_lanes(first_norm, dot(wp_ref[...], p_ref[...]), jnp.concatenate(masks, axis=1))
    rows = []
    for slot in range(3):
        rows.append(jnp.concatenate([gather_halo(normed[:, 1024 * g : 1024 * g + 1024], 32 * slot) for g in range(GROUP)], axis=1).astype(BF16))
    edge = dot(wqkv_ref[0:DIM, :], jnp.concatenate(rows[:2], axis=1))
    (edge,) = by_lanes(lambda k, out: ((out + wide_ref[3]).astype(BF16),), edge)
    nsel = dot(jnp.concatenate([row[:, CANVAS_W * g : CANVAS_W * g + CANVAS_W] for g in range(GROUP) for row in rows], axis=0), tap_ref[...])
    nsel = jnp.concatenate([nsel[DIM * k : DIM * k + DIM] for k in range(3 * GROUP)], axis=1).astype(BF16)
    bias = jnp.concatenate([wide_ref[4], wide_ref[5]], axis=0)
    (taps,) = by_lanes(lambda k, out: ((out + bias).astype(BF16),), dot(wqkv_ref[DIM : 3 * DIM, :], nsel))
    for g in range(GROUP):
        last_ref[g] = edge[:, CANVAS_W * g : CANVAS_W * g + CANVAS_W]
        first_ref[g] = edge[:, CANVAS_W * (GROUP + g) : CANVAS_W * (GROUP + g) + CANVAS_W]
        nsel_ref[g] = nsel[:, 384 * g : 384 * g + 384]
        kvt_ref[g] = taps[:, 384 * g : 384 * g + 384]
        product = taps[:, 384 * g : 384 * g + 384].astype(F32) * kexp_ref[...]
        sums = []
        for k in range(3):
            part = product[:, 128 * k : 128 * k + 128]
            sums.append(part + pltpu.roll(part, 96, 1) + pltpu.roll(part, 64, 1))
        store_lanes(below_ref, sums[0], images[g])
        store_lanes(own_ref, sums[1] + sums[2], images[g])


def embed_kernel(ext_ref, row_ref, order_ref, *refs, offset):
    pix_refs, refs = refs[:GROUP], refs[GROUP:]
    perm_ref, wp_ref, wqkv_ref, vec_ref, patch_ref, x0_ref, q_ref, s_ref, wide_ref = refs
    images, heights, breadths, row_oks = group_extents(ext_ref, row_ref, offset)

    @pl.when(pl.program_id(0) == 0)
    def _():
        s_ref[...] = jnp.zeros_like(s_ref)
        fill_wide(wide_ref, vec_ref, [0, 1, 2, 42])

    for g in range(GROUP):
        pixel_rows(pix_refs[g], s_ref)
        for shifted in range(2):
            out = patch_blocks(s_ref, perm_ref[...], shifted, ((0, 1, 2, 3), (4, 5, 6, 7), (1, 2, 3, 4), (5, 6, 7, 8)))
            for which in range(4):
                half, side = which // 2, which % 2
                for tile in range(TILES):
                    block = out[128 * which + 16 * tile : 128 * which + 16 * tile + 16]
                    for phase in range(4):
                        top = 128 * shifted + 64 * half + 16 * phase
                        patch_ref[g, top : top + 16, 256 * tile + 128 * side : 256 * tile + 128 * side + 128] = block[
                            :, 128 * phase : 128 * phase + 128]

    count = pair_count(breadths)

    def active(pair, carry):
        def first_norm(k, embed, mask):
            x0 = (embed + wide_ref[0]) * mask
            hat, _ = normalized(x0)
            return x0, (hat * wide_ref[1] + wide_ref[2]).astype(BF16)

        x0, normed = by_lanes(first_norm, dot(wp_ref[...], load_pair(patch_ref, pair)), pair_mask(pair, breadths, row_oks))
        store_pair(x0_ref, pair, x0)
        (query,) = by_lanes(lambda k, out: ((out + wide_ref[3]).astype(BF16),), dot(wqkv_ref[0:DIM, :], normed))
        store_pair(q_ref, pair, query, 256)
        return carry

    def idle(pair, carry):
        for g in range(GROUP):
            q_ref[g, :, pair_lanes(pair, 256)] = jnp.zeros((DIM, PAIR), BF16)
        return carry

    lax.fori_loop(0, count, active, 0)
    lax.fori_loop(count, PAIRS, idle, 0)
    for g in range(GROUP):
        q_ref[g, :, 0:256] = jnp.zeros((DIM, 256), BF16)
        q_ref[g, :, 256 + TOKENS : 512 + TOKENS] = jnp.zeros((DIM, 256), BF16)


def key_lanes(*lead):
    return pl.BlockSpec(lead + (128,), lambda i, *_: (0,) * len(lead) + (i * GROUP >> 2,))


def specs():
    whole = lambda *shape: pl.BlockSpec(shape, lambda i, *_: (0,) * len(shape))
    per = lambda *shape: pl.BlockSpec((GROUP,) + shape, lambda i, *_: (i,) + (0,) * len(shape))
    return whole, per


def pixel_specs(offset):
    return [pl.BlockSpec((1, PATCH, 3, ROWS, 1024), lambda i, ext, row, order, g=g: (order[offset + i * GROUP + g], 0, 0, 0, 0)) for g in range(GROUP)]


def call_edge(ext, row, order, pixels, consts, wts, images, offset):
    whole, per = specs()
    shapes = [(DIM, CANVAS_W), (DIM, CANVAS_W), (DIM, 384), (2 * DIM, 384)]
    return pl.pallas_call(
        functools.partial(edge_kernel, offset=offset),
        grid_spec=pltpu.PrefetchScalarGridSpec(
            num_scalar_prefetch=3, grid=(images // GROUP,),
            in_specs=pixel_specs(offset) + [
                whole(512, 512), whole(CANVAS_W, 128), whole(DIM, PATCH_ROWS), whole(3 * DIM, DIM), whole(DIM, 64)],
            out_specs=[per(*s) for s in shapes] + [key_lanes(2 * DIM)] * 2,
            scratch_shapes=[pltpu.VMEM((TILES, 144, 128), F32), pltpu.VMEM((PATCH_ROWS, 1024 * GROUP), BF16), pltpu.VMEM((6, DIM, 128), F32),
                            pltpu.VMEM((2 * DIM, 384), F32)]),
        out_shape=[jax.ShapeDtypeStruct((images,) + s, BF16) for s in shapes]
        + [jax.ShapeDtypeStruct((2 * DIM, 32 * images), F32)] * 2,
        compiler_params=pltpu.CompilerParams(vmem_limit_bytes=VMEM_BYTES),
        cost_estimate=pl.CostEstimate(flops=images * 1_000_000_000, bytes_accessed=images * 1_000_000, transcendentals=0),
        name="edge",
    )(ext, row, order, *[pixels] * GROUP, consts["perm"], consts["tap"], wts["wp"], wts["wqkv_t"], wts["vec"])


def call_embed(ext, row, order, pixels, consts, wts, images, offset):
    whole, per = specs()
    shapes = [((PATCH_ROWS, TOKENS), BF16), ((DIM, TOKENS), F32), ((DIM, PADDED), BF16)]
    return pl.pallas_call(
        functools.partial(embed_kernel, offset=offset),
        grid_spec=pltpu.PrefetchScalarGridSpec(
            num_scalar_prefetch=3, grid=(images // GROUP,),
            in_specs=pixel_specs(offset) + [whole(512, 512), whole(DIM, PATCH_ROWS), whole(3 * DIM, DIM), whole(DIM, 64)],
            out_specs=[per(*s) for s, _ in shapes],
            scratch_shapes=[pltpu.VMEM((TILES, 144, 128), F32), pltpu.VMEM((4, DIM, 128), F32)]),
        out_shape=[jax.ShapeDtypeStruct((images,) + s, t) for s, t in shapes],
        compiler_params=pltpu.CompilerParams(vmem_limit_bytes=VMEM_BYTES),
        cost_estimate=pl.CostEstimate(flops=images * 2_000_000_000, bytes_accessed=images * 4_000_000, transcendentals=0),
        name="embed",
    )(ext, row, order, *[pixels] * GROUP, consts["perm"], wts["wp"], wts["wqkv_t"], wts["vec"])


def pool_norm_kernel(own_ref, got_ref, vec_ref, kv_ref):
    for member in range(2):
        part = slice(member * DIM, member * DIM + DIM)
        hat, _ = normalized(own_ref[part] + got_ref[part])
        kv_ref[part] = (hat * column(vec_ref, 5 + 2 * member) + column(vec_ref, 6 + 2 * member)).astype(BF16)


def call_pool_norm(own, got, vec):
    return pl.pallas_call(
        pool_norm_kernel, out_shape=jax.ShapeDtypeStruct(own.shape, BF16), name="pool_norm",
        cost_estimate=pl.CostEstimate(flops=own.size * 10, bytes_accessed=own.size * 10, transcendentals=0))(own, got, vec)


def pool_back_kernel(own_ref, got_ref, grad_ref, vec_ref, pre_ref, sums_ref):
    for member in range(2):
        part = slice(member * DIM, member * DIM + DIM)
        hat, rstd = normalized(own_ref[part] + got_ref[part])
        grad = grad_ref[part].astype(F32)
        pre_ref[part] = norm_back(grad, hat, rstd, column(vec_ref, 5 + 2 * member))
        sums_ref[2 * member] = fold_lanes(grad * hat)
        sums_ref[2 * member + 1] = fold_lanes(grad)


def call_pool_back(own, got, grad, vec):
    return pl.pallas_call(
        pool_back_kernel,
        out_shape=[jax.ShapeDtypeStruct(own.shape, F32), jax.ShapeDtypeStruct((4, DIM, 128), F32)], name="pool_back",
        cost_estimate=pl.CostEstimate(flops=own.size * 20, bytes_accessed=own.size * 16, transcendentals=0))(own, got, grad, vec)


def lane_bit(lane, bit):
    return (lane & bit) != 0


def relative_terms(block, products, key_rows):
    lane = lane_ids(128, WIN)
    parts = [products[WIN * s : WIN * s + WIN] for s in range(8)]
    for bit in (1, 2, 4):
        chosen = lane_bit(lane, bit)
        parts = [jnp.where(chosen, parts[2 * k + 1], parts[2 * k]) for k in range(len(parts) // 2)]
    by_col = parts[0]
    for bit, step in ((8, 1), (16, 2)):
        by_col = jnp.where(lane_bit(lane, bit), by_col, pltpu.roll(by_col, WIN - step, 0))
    by_col = by_col[0:32] if block & 2 else by_col[4:36]
    lane = lane_ids(128, key_rows)
    rows = products[8 * WIN :]
    parts = [rows[key_rows * r : key_rows * r + key_rows] for r in range(4 * (block & 1), 4 * (block & 1) + 4)]
    for bit in (32, 64):
        chosen = lane_bit(lane, bit)
        parts = [jnp.where(chosen, parts[2 * k + 1], parts[2 * k]) for k in range(len(parts) // 2)]
    return jnp.concatenate([parts[0], by_col], axis=0)


def relative_spread(block, grad_terms, key_rows):
    lane = lane_ids(128, WIN)
    by_row = grad_terms[:key_rows]
    if block & 2:
        pieces = [grad_terms[key_rows:], jnp.zeros((WIN - 32, 128), F32)]
    else:
        pieces = [jnp.zeros((4, 128), F32), grad_terms[key_rows:], jnp.zeros((WIN - 36, 128), F32)]
    by_col = jnp.concatenate(pieces, axis=0)
    for bit, step in ((8, 1), (16, 2)):
        by_col = jnp.where(lane_bit(lane, bit), by_col, pltpu.roll(by_col, step, 0))
    parts = [jnp.where((lane & 7) == s, by_col, 0.0) for s in range(8)]
    lane = lane_ids(128, key_rows)
    for r in range(8):
        hit = (lane >> 5) == r - 4 * (block & 1)
        parts.append(jnp.where(hit, by_row, 0.0) if r // 4 == block & 1 else jnp.zeros((key_rows, 128), F32))
    return jnp.concatenate(parts, axis=0).astype(BF16)


def gelu_parts(hidden):
    cumulative = 0.5 + 0.5 * lax.erf(hidden * 0.7071067811865476)
    slope = cumulative + hidden * (jnp.exp(hidden * hidden * -0.5) * 0.3989422804014327)
    return (hidden * cumulative).astype(BF16), slope.astype(BF16)


def forward_kernel(ext_ref, row_ref, q_ref, top_ref, bot_ref, x0_ref, kv_ref, vec_ref, rw_ref, wproj_ref, w1_ref, w2_ref,
                   hat_ref, query_ref, terms_ref, att_ref, act_ref, slope_ref, hat2_ref, hat3_ref, stat_ref, pool_ref, ka_ref, kn_ref, v_ref, ztop_ref, zbot_ref, pre_ref, wide_ref, wb1_ref, wprojt_ref, w1t_ref, w2t_ref,
                   *, offset, key_rows):
    images, heights, breadths, row_oks = group_extents(ext_ref, row_ref, offset)
    depth = DIM + aug_rows(key_rows)

    @pl.when(pl.program_id(0) == 0)
    def _():
        fill_wide(wide_ref, vec_ref, list(range(15, 24)) + [3, 4, 9, 10, 11, 12])
        fill_bias(wb1_ref, vec_ref)
        fill_transpose(wprojt_ref, wproj_ref)
        fill_transpose(w1t_ref, w1_ref)
        fill_transpose(w2t_ref, w2_ref)

    lane = lane_ids(CANVAS_W, DIM)
    for g in range(GROUP):
        v_ref[g] = key_tables(kv_ref, images[g], key_rows, heights[g], breadths[g], ka_ref, kn_ref.at[g]).astype(BF16)
        for halo_ref, dst_ref, tap_row, target in ((top_ref, ztop_ref, 0, 0), (bot_ref, zbot_ref, 2, 96)):
            halo = halo_ref[g].astype(F32)
            left = jnp.where(lane == 0, 0.0, pltpu.roll(halo, 1, 1))
            right = jnp.where(lane == CANVAS_W - 1, 0.0, pltpu.roll(halo, CANVAS_W - 1, 1))
            taps = [wide(wide_ref, 3 * tap_row + k, CANVAS_W) for k in range(3)]
            spread_halo(dst_ref.at[g], taps[0] * left + taps[1] * halo + taps[2] * right, target)
    pool_ref[...] = jnp.zeros_like(pool_ref)

    def step(pair, carry):
        for group in range(0, DIM, 16):
            part = slice(group, group + 16)
            taps = [wide_ref[k, part] for k in range(9)]
            for g in range(GROUP):
                window = q_ref[g, part, pl.ds(pl.multiple_of(pair * PAIR, 128), PAIR + 512)]
                for tile in range(2):
                    sums = []
                    for side in range(2):
                        shifts = col_shifts(window, 256 + 256 * tile + 128 * side)
                        sums.append([sum(taps[3 * r + c] * shifts[c] for c in range(3)) for r in range(3)])
                    halo = pl.ds(pl.multiple_of((2 * pair + tile) * 128, 128), 128)
                    down = rows_down(sums[0][0], sums[1][0], ztop_ref[g, part, halo])
                    up = rows_up(sums[0][2], sums[1][2], zbot_ref[g, part, halo])
                    for side in range(2):
                        base = PAIR * g + 256 * tile + 128 * side
                        pre_ref[part, base : base + 128] = sums[side][1] + down[side] + up[side]

        def query_of(k, pre):
            hat, rstd = normalized(pre)
            return hat.astype(BF16), (hat * wide_ref[9] + wide_ref[10]).astype(BF16), rstd

        hat, query, rstd = by_lanes(query_of, pre_ref[...])
        store_pair(hat_ref, pair, hat)
        store_pair(query_ref, pair, query)

        def extra_of(k, products):
            terms = relative_terms(k, products, key_rows) * (DIM**0.5)
            high = terms.astype(BF16).astype(F32)
            return (jnp.concatenate([high, terms - high, jnp.ones((16, 128), F32)], axis=0).astype(BF16),)

        (extra,) = by_lanes(extra_of, dot(rw_ref[pair], query))
        store_pair(terms_ref, pair, extra)

        def softmax(k, scores):
            peak = jnp.max(scores, axis=0, keepdims=True)
            weights = jnp.exp2((scores - peak) * EXP2_SCALE)
            inverse = 1.0 / jnp.sum(weights, axis=0, keepdims=True)
            return (weights * inverse).astype(BF16), peak, inverse

        long_query = by_image(jnp.concatenate([query, extra], axis=0))
        scores = jnp.concatenate([dot(kn_ref[g, :, :depth], long_query[g]) for g in range(GROUP)], axis=1)
        probs, peak, inverse = by_lanes(softmax, scores)
        mixed = by_image(probs)
        mixed = jnp.concatenate([dot(v_ref[g], mixed[g]) for g in range(GROUP)], axis=1)
        attended = (mixed + query.astype(F32)).astype(BF16)
        store_pair(att_ref, pair, attended)

        def second_norm(k, x0, out):
            x1 = x0 + (out + wide_ref[11])
            hat, rstd = normalized(x1)
            return x1, (hat * wide_ref[12] + wide_ref[13]).astype(BF16), hat.astype(BF16), rstd

        x1, normed, hat_two, rstd_two = by_lanes(second_norm, load_pair(x0_ref, pair), dot(wprojt_ref[...], attended))
        store_pair(hat2_ref, pair, hat_two)
        act, slope = by_blocks(lambda part, hidden: gelu_parts(hidden + wb1_ref[part]), 64, dot(w1t_ref[...], normed))
        store_pair(act_ref, pair, act)
        store_pair(slope_ref, pair, slope)

        def third_norm(k, x1, out, mask):
            hat, rstd = normalized(x1 + (out + wide_ref[14]))
            return hat * mask, hat.astype(BF16), rstd

        kept, hat_three, rstd_three = by_lanes(third_norm, x1, dot(w2t_ref[...], act), pair_mask(pair, breadths, row_oks))
        store_pair(hat3_ref, pair, hat_three)
        stats = [peak, inverse, rstd, rstd_two, rstd_three, jnp.zeros((3, GROUP * PAIR), F32)]
        store_pair(stat_ref, pair, jnp.concatenate(stats, axis=0))
        for g, part in enumerate(by_image(kept)):
            pool_ref[g] += fold_lanes(part)
        return carry

    lax.fori_loop(0, pair_count(breadths), step, 0)


def call_forward(ext, row, q, top, bot, x0, kv, wts, offset):
    whole, per = specs()
    images, key_rows = q.shape[0], kv.shape[0]
    more = aug_rows(key_rows)
    shapes = [(rows, BF16) for rows in (DIM, DIM, more, DIM, MLP, MLP, DIM, DIM)]
    shapes = [((rows, TOKENS), kind) for rows, kind in shapes] + [((8, TOKENS), F32), ((DIM, 128), F32)]
    keys = key_rows * 32
    return pl.pallas_call(
        functools.partial(forward_kernel, offset=offset, key_rows=key_rows),
        grid_spec=pltpu.PrefetchScalarGridSpec(
            num_scalar_prefetch=2, grid=(images // GROUP,),
            in_specs=[
                per(DIM, PADDED), per(DIM, CANVAS_W), per(DIM, CANVAS_W), per(DIM, TOKENS),
                key_lanes(key_rows, 2 * DIM),
                whole(DIM, 64), whole(PAIRS, 8 * WIN + 8 * key_rows, DIM), whole(DIM, DIM), whole(DIM, MLP), whole(MLP, DIM)],
            out_specs=[per(*s) for s, _ in shapes],
            scratch_shapes=[
                pltpu.VMEM((DIM + more, keys), BF16), pltpu.VMEM((GROUP, keys, 256), BF16), pltpu.VMEM((GROUP, DIM, keys), BF16),
                pltpu.VMEM((GROUP, DIM, 1024), F32), pltpu.VMEM((GROUP, DIM, 1024), F32), pltpu.VMEM((DIM, GROUP * PAIR), F32),
                pltpu.VMEM((15, DIM, 128), F32), pltpu.VMEM((MLP, 128), F32),
                pltpu.VMEM((DIM, DIM), BF16), pltpu.VMEM((MLP, DIM), BF16), pltpu.VMEM((DIM, MLP), BF16)]),
        out_shape=[jax.ShapeDtypeStruct((images,) + s, t) for s, t in shapes],
        compiler_params=pltpu.CompilerParams(vmem_limit_bytes=VMEM_BYTES),
        cost_estimate=pl.CostEstimate(flops=images * 5_000_000_000, bytes_accessed=images * 4_000_000, transcendentals=0),
        name="forward",
    )(ext, row, q, top, bot, x0, kv, wts["vec"], wts["rw"], wts["wproj"], wts["w1"], wts["w2"])


def backward_kernel(ext_ref, row_ref, hat_ref, query_ref, terms_ref, att_ref, act_ref, slope_ref, hat2_ref, hat3_ref, stat_ref, q_ref, top_ref, bot_ref, kv_ref,
                    gvec_ref, vec_ref, rwt_ref, wproj_ref, w1_ref, w2_ref,
                    dx1_ref, dq_ref, up_ref, down_ref, dkv_ref, a2_ref, a1_ref, ap_ref, av_ref, ak_ref, ar_ref,
                    ka_ref, kn_ref, vn_ref, dp_ref, qtop_ref, qbot_ref, ru_ref, rd_ref, dk_ref, dv_ref, wide_ref, *, offset, key_rows):
    now = pl.program_id(0)
    steps = pl.num_programs(0) - 1
    images, heights, breadths, row_oks = group_extents(ext_ref, row_ref, offset, jnp.minimum(now, steps - 1))
    _, _, former, _ = group_extents(ext_ref, row_ref, offset, jnp.maximum(now - 1, 0))
    depth = DIM + aug_rows(key_rows)
    count = jnp.where(now < steps, pair_count(breadths), 0)
    former_count = pair_count(former)
    dp_now, dp_former = now & 1, (now & 1) ^ 1

    @pl.when(pl.program_id(0) == 0)
    def _():
        for ref in (a2_ref, a1_ref, ap_ref, av_ref, ak_ref, ar_ref, ru_ref, rd_ref):
            ref[...] = jnp.zeros_like(ref)
        fill_wide(wide_ref, vec_ref, list(range(15, 24)) + [3, 10, 11, 13])
        dp_ref[...] = jnp.zeros_like(dp_ref)

    for g in range(GROUP):
        values = key_tables(kv_ref, images[g], key_rows, heights[g], breadths[g], ka_ref.at[g], kn_ref.at[g])
        padded_values = jnp.concatenate([values, jnp.zeros((128 - DIM, values.shape[1]), F32)], axis=0)
        vn_ref[g] = jnp.transpose(padded_values).astype(BF16)
        spread_halo(qtop_ref.at[g], top_ref[g], 0)
        spread_halo(qbot_ref.at[g], bot_ref[g], 96)
    for ref in (dk_ref, dv_ref, dp_ref.at[dp_now]):
        ref[...] = jnp.zeros_like(ref)

    def step(pair, carry):
        ones = jnp.ones((16, GROUP * PAIR), BF16)
        stat = load_pair(stat_ref, pair)

        def third_back(k, hat, stat, mask):
            grad = norm_back(gvec_ref[k * 128 // PAIR] * mask, hat.astype(F32), stat[4:5], wide_ref[12])
            return grad, grad.astype(BF16)

        grad_x2, grad_mlp = by_lanes(third_back, load_pair(hat3_ref, pair), stat, pair_mask(pair, breadths, row_oks))
        act = load_pair(act_ref, pair)
        a2_ref[...] += dot_nt(jnp.concatenate([act, ones], axis=0), grad_mlp)
        (grad_hidden,) = by_blocks(
            lambda part, grad, slope: ((grad * slope.astype(F32)).astype(BF16),), 64, dot(w2_ref[...], grad_mlp), load_pair(slope_ref, pair))
        hat_two = load_pair(hat2_ref, pair)
        (normed,) = by_lanes(lambda k, hat: ((hat.astype(F32) * wide_ref[10] + wide_ref[11]).astype(BF16),), hat_two)
        a1_ref[...] += dot_nt(jnp.concatenate([normed, ones], axis=0), grad_hidden)

        def second_back(k, grad, hat, stat, grad_x2):
            hat = hat.astype(F32)
            total = grad_x2 + norm_back(grad, hat, stat[3:4], wide_ref[10])
            return total.astype(BF16), grad * hat

        grad_normed = dot(w1_ref[...], grad_hidden)
        grad_proj, scaled = by_lanes(second_back, grad_normed, hat_two, stat, grad_x2)
        av_ref[0] += fold_lanes(scaled)
        av_ref[1] += fold_lanes(grad_normed)
        store_pair(dx1_ref, pair, grad_proj)
        attended = load_pair(att_ref, pair)
        ap_ref[...] += dot_nt(jnp.concatenate([attended, ones], axis=0), grad_proj)
        grad_att = dot(wproj_ref[...], grad_proj)
        grad_att_low = grad_att.astype(BF16)
        hat = load_pair(hat_ref, pair)
        query = load_pair(query_ref, pair)
        long_query = by_image(jnp.concatenate([query, load_pair(terms_ref, pair)], axis=0))
        scores = jnp.concatenate([dot(kn_ref[g, :, :depth], long_query[g]) for g in range(GROUP)], axis=1)
        low = by_image(grad_att_low)
        grad_probs = jnp.concatenate([dot(vn_ref[g, :, :DIM], low[g]) for g in range(GROUP)], axis=1)

        def softmax_back(k, scores, grad_probs, stat):
            probs = jnp.exp2((scores - stat[0:1]) * EXP2_SCALE) * stat[1:2]
            inner = jnp.sum(probs * grad_probs, axis=0, keepdims=True)
            return probs.astype(BF16), (probs * (grad_probs - inner)).astype(BF16)

        probs, grad_scores = by_lanes(softmax_back, scores, grad_probs, stat)
        probs, grad_scores, queries = by_image(probs), by_image(grad_scores), by_image(query)
        back = []
        for g in range(GROUP):
            back.append(dot(ka_ref[g, : DIM + key_rows + 32, :], grad_scores[g]))
            dv_ref[g] += dot_nt(low[g], probs[g])
            dk_ref[g] += dot_nt(queries[g], grad_scores[g])
        back = jnp.concatenate(back, axis=1)
        (spread,) = by_lanes(lambda k, terms: (relative_spread(k, terms, key_rows),), back[DIM:])
        ar_ref[pair] += dot_nt(spread, query)

        def query_back(k, grad_att, back, far, hat, stat):
            grad = grad_att + back * SCALE + far
            hat = hat.astype(F32)
            return norm_back(grad, hat, stat[2:3], wide_ref[9]), grad * hat, grad

        grad_pre, scaled, grad = by_lanes(query_back, grad_att, back[:DIM], dot(rwt_ref[pair], spread), hat, stat)
        av_ref[2] += fold_lanes(scaled)
        av_ref[3] += fold_lanes(grad)
        store_pair(dp_ref.at[dp_now], pair, grad_pre.astype(BF16), 256)
        return carry

    def pool_step(pair, carry):
        for group in range(0, DIM, 16):
            part = slice(group, group + 16)
            taps = [wide_ref[k, part] for k in range(9)]
            grads = [None] * 9
            for g in range(GROUP):
                window = dp_ref[dp_former, g, part, pl.ds(pl.multiple_of(pair * PAIR, 128), PAIR + 512)]
                for tile in range(2):
                    base = pair * PAIR + 256 * tile
                    halo = pl.ds(pl.multiple_of((2 * pair + tile) * 128, 128), 128)
                    query = [q_ref[g, part, pl.ds(pl.multiple_of(base + 256 + 128 * side, 128), 128)] for side in range(2)]
                    above = rows_down(query[0], query[1], qtop_ref[g, part, halo])
                    under = rows_up(query[0], query[1], qbot_ref[g, part, halo])
                    sums = []
                    for side in range(2):
                        left, here, right = col_shifts(window, 256 + 256 * tile + 128 * side)
                        shifts = (right, here, left)
                        sums.append([sum(taps[3 * r + c] * shifts[c] for c in range(3)) for r in range(3)])
                        for r, rows in enumerate((above[side], query[side], under[side])):
                            rows = rows.astype(F32)
                            for c in range(3):
                                term = shifts[c] * rows
                                grads[3 * r + c] = term if grads[3 * r + c] is None else grads[3 * r + c] + term
                    zero = jnp.zeros((16, 128), F32)
                    up = rows_up(sums[0][0], sums[1][0], zero)
                    down = rows_down(sums[0][2], sums[1][2], zero)
                    for side in range(2):
                        lanes = pl.ds(pl.multiple_of(base + 128 * side, 128), 128)
                        dq_ref[g, part, lanes] = (sums[side][1] + up[side] + down[side]).astype(BF16)
                    ru_ref[g, part, halo] = up[2]
                    rd_ref[g, part, halo] = down[2]
            for k in range(9):
                ak_ref[k, part] += grads[k]
        return carry

    def pool_idle(pair, carry):
        for ref in (ru_ref, rd_ref):
            for g in range(GROUP):
                ref[g, :, pl.ds(pl.multiple_of(pair * 256, 128), 256)] = jnp.zeros((DIM, 256), F32)
        return carry

    lax.fori_loop(0, count, lambda pair, carry: step(pair, pool_step(pair, carry)), 0)
    lax.fori_loop(count, former_count, pool_step, 0)
    lax.fori_loop(former_count, PAIRS, pool_idle, 0)

    @pl.when(now < steps)
    def _():
        lane = lane_ids(128, 2 * DIM)
        for g in range(GROUP):
            for i in range(key_rows):
                block = slice(128 * (i // 4), 128 * (i // 4) + 128)
                value = jnp.concatenate([dk_ref[g, :, block] * SCALE, dv_ref[g, :, block]], axis=0)
                value = pltpu.roll(value, (4 + (images[g] & 3) - i % 4) * 32 & 127, 1)
                slot = reverse_bits(jnp.bitwise_xor(row_ref[0], i), key_rows)
                dkv_ref[slot] = jnp.where((lane >> 5) == (images[g] & 3), value, dkv_ref[slot])

    for g in range(GROUP):
        up_ref[g] = gather_halo(ru_ref.at[g], 96).astype(BF16)
        down_ref[g] = gather_halo(rd_ref.at[g], 0).astype(BF16)


def call_backward(ext, row, saved, q, top, bot, kv, gvec, wts, offset):
    whole, _ = specs()
    images, key_rows = q.shape[0], kv.shape[0]
    more = aug_rows(key_rows)
    keys = key_rows * 32
    window = 8 * WIN + 8 * key_rows
    steps = images // GROUP
    now = lambda *shape: pl.BlockSpec((GROUP,) + shape, lambda i, *_: (jnp.minimum(i, steps - 1),) + (0,) * len(shape))
    former = lambda *shape: pl.BlockSpec((GROUP,) + shape, lambda i, *_: (jnp.maximum(i - 1, 0),) + (0,) * len(shape))
    heads = pl.BlockSpec((key_rows, 2 * DIM, 128), lambda i, *_: (0, 0, jnp.minimum(i, steps - 1) * GROUP >> 2))
    shapes = [(DIM, TOKENS), (DIM, TOKENS), (DIM, CANVAS_W), (DIM, CANVAS_W)]
    sums = [(MLP + 16, DIM), (DIM + 16, MLP), (DIM + 16, DIM), (4, DIM, 128), (9, DIM, 128), (PAIRS, window, DIM)]
    return pl.pallas_call(
        functools.partial(backward_kernel, offset=offset, key_rows=key_rows),
        grid_spec=pltpu.PrefetchScalarGridSpec(
            num_scalar_prefetch=2, grid=(steps + 1,),
            in_specs=[now(rows, TOKENS) for rows in (DIM, DIM, more, DIM, MLP, MLP, DIM, DIM, 8)] + [
                former(DIM, PADDED), former(DIM, CANVAS_W), former(DIM, CANVAS_W), heads, now(DIM, 1), whole(DIM, 64), whole(PAIRS, DIM, window),
                whole(DIM, DIM), whole(DIM, MLP), whole(MLP, DIM)],
            out_specs=[now(*shapes[0])] + [former(*s) for s in shapes[1:]] + [heads] + [whole(*s) for s in sums],
            scratch_shapes=[
                pltpu.VMEM((GROUP, DIM + more, keys), BF16), pltpu.VMEM((GROUP, keys, 256), BF16), pltpu.VMEM((GROUP, keys, 128), BF16),
                pltpu.VMEM((2, GROUP, DIM, PADDED), BF16)] + [pltpu.VMEM((GROUP, DIM, 1024), BF16)] * 2
            + [pltpu.VMEM((GROUP, DIM, 1024), F32)] * 2 + [pltpu.VMEM((GROUP, DIM, keys), F32)] * 2 + [pltpu.VMEM((13, DIM, 128), F32)]),
        out_shape=[jax.ShapeDtypeStruct((images,) + s, BF16) for s in shapes]
        + [jax.ShapeDtypeStruct((key_rows, 2 * DIM, 32 * images), F32)] + [jax.ShapeDtypeStruct(s, F32) for s in sums],
        compiler_params=pltpu.CompilerParams(vmem_limit_bytes=VMEM_BYTES),
        cost_estimate=pl.CostEstimate(flops=images * 12_000_000_000, bytes_accessed=images * 6_000_000, transcendentals=0),
        name="backward",
    )(ext, row, *saved, q, top, bot, kv, gvec, wts["vec"], wts["rw_t"], wts["wproj"], wts["w1"], wts["w2"])


def embed_back_kernel(ext_ref, row_ref, patch_ref, dq_ref, dx1_ref, rtop_ref, rbot_ref, nsel_ref, kvt_ref, pre_ref, under_ref,
                      wp_ref, vec_ref, wqkv_ref, tapt_ref,
                      aq_ref, akv_ref, apatch_ref, av_ref, ak_ref, dn_ref, rim_ref, wide_ref, kexp_ref, *, offset):
    images, heights, breadths, row_oks = group_extents(ext_ref, row_ref, offset)

    @pl.when(pl.program_id(0) == 0)
    def _():
        for ref in (aq_ref, akv_ref, apatch_ref, av_ref, ak_ref, dn_ref, rim_ref):
            ref[...] = jnp.zeros_like(ref)
        fill_wide(wide_ref, vec_ref, [0, 1, 2])
        fill_taps(kexp_ref, vec_ref)

    lane = lane_ids(128, 2 * DIM)

    def thrice(value, image):
        block = jnp.where((lane >> 5) == 1, take_lanes(value, image, 1), take_lanes(value, image, 0))
        block = jnp.where((lane >> 5) == 2, take_lanes(value, image, 2), block)
        return jnp.where((lane >> 5) == 3, 0.0, block)

    grad_taps = []
    for g in range(GROUP):
        own = thrice(pre_ref[...], images[g])
        spread = jnp.concatenate([thrice(under_ref[...], images[g]), own, own], axis=1)
        ak_ref[...] += kvt_ref[g].astype(F32) * spread
        grad_taps.append((spread * kexp_ref[...]).astype(BF16))
    grad_taps = jnp.concatenate(grad_taps, axis=1)
    nsel = jnp.concatenate([nsel_ref[g] for g in range(GROUP)], axis=1)
    akv_ref[...] += dot_nt(jnp.concatenate([nsel, jnp.ones((16, 384 * GROUP), BF16)], axis=0), grad_taps)
    grad_sel = dot(wqkv_ref[:, DIM : 3 * DIM], grad_taps)
    parts = [grad_sel.astype(BF16)[:, 128 * k : 128 * k + 128] for k in range(3 * GROUP)]
    lines = dot(jnp.concatenate(parts, axis=0), tapt_ref[...])
    for g in range(GROUP):
        for k, start in enumerate((224, 0, 32)):
            first = DIM * (3 * g + k)
            line = lines[first : first + DIM]
            for tile in range(TILES):
                dn_ref[g, :, 256 * tile + start : 256 * tile + start + 32] = line[:, 32 * tile : 32 * tile + 32]
        for halo_ref, start in ((rtop_ref, 0), (rbot_ref, 224)):
            line = halo_ref[g].astype(F32)
            for tile in range(TILES):
                rim_ref[g, :, 256 * tile + start : 256 * tile + start + 32] = line[:, 32 * tile : 32 * tile + 32]

    def step(pair, carry):
        mask = pair_mask(pair, breadths, row_oks)
        patches = load_pair(patch_ref, pair)

        def first_norm(k, embed, mask, grad, rim):
            hat, rstd = normalized((embed + wide_ref[0]) * mask)
            return hat, rstd, (hat * wide_ref[1] + wide_ref[2]).astype(BF16), (grad.astype(F32) + rim).astype(BF16)

        hat, rstd, normed, grad_q = by_lanes(first_norm, dot(wp_ref[...], patches), mask, load_pair(dq_ref, pair), load_pair(rim_ref, pair))
        aq_ref[...] += dot_nt(jnp.concatenate([normed, jnp.ones((16, GROUP * PAIR), BF16)], axis=0), grad_q)

        def first_back(k, out, extra, hat, rstd, mask, dx1):
            grad = out + extra
            total = (dx1.astype(F32) + norm_back(grad, hat, rstd, wide_ref[1])) * mask
            return total.astype(BF16), total, grad * hat, grad

        low, total, scaled, grad = by_lanes(
            first_back, dot(wqkv_ref[:, 0:DIM], grad_q), load_pair(dn_ref, pair), hat, rstd, mask, load_pair(dx1_ref, pair))
        av_ref[0] += fold_lanes(total)
        av_ref[1] += fold_lanes(scaled)
        av_ref[2] += fold_lanes(grad)
        apatch_ref[...] += dot_nt(low, patches)
        return carry

    lax.fori_loop(0, pair_count(breadths), step, 0)


def call_embed_back(ext, row, patches, dq, dx1, rtop, rbot, nsel, kvt, pre, under, consts, wts, offset):
    whole, per = specs()
    images = dq.shape[0]
    sums = [(DIM + 16, DIM), (DIM + 16, 2 * DIM), (DIM, PATCH_ROWS), (3, DIM, 128), (2 * DIM, 384)]
    return pl.pallas_call(
        functools.partial(embed_back_kernel, offset=offset),
        grid_spec=pltpu.PrefetchScalarGridSpec(
            num_scalar_prefetch=2, grid=(images // GROUP,),
            in_specs=[
                per(PATCH_ROWS, TOKENS), per(DIM, TOKENS), per(DIM, TOKENS), per(DIM, CANVAS_W), per(DIM, CANVAS_W),
                per(DIM, 384), per(2 * DIM, 384), key_lanes(2 * DIM), key_lanes(2 * DIM),
                whole(DIM, PATCH_ROWS), whole(DIM, 64), whole(DIM, 3 * DIM), whole(128, CANVAS_W)],
            out_specs=[whole(*s) for s in sums],
            scratch_shapes=[pltpu.VMEM((GROUP, DIM, TOKENS), F32)] * 2 + [pltpu.VMEM((3, DIM, 128), F32), pltpu.VMEM((2 * DIM, 384), F32)]),
        out_shape=[jax.ShapeDtypeStruct(s, F32) for s in sums],
        compiler_params=pltpu.CompilerParams(vmem_limit_bytes=VMEM_BYTES),
        cost_estimate=pl.CostEstimate(flops=images * 3_000_000_000, bytes_accessed=images * 3_000_000, transcendentals=0),
        name="embed_back",
    )(ext, row, patches, dq, dx1, rtop, rbot, nsel, kvt, pre, under, wts["wp"], wts["vec"], wts["wqkv"], consts["tap_t"])


def bit_count(size):
    return size.bit_length() - 1


def swap(value, axis, bit):
    size = lax.axis_size(axis)
    return lax.ppermute(value, axis, [(i, i ^ (1 << bit)) for i in range(size)])


def shifted(value, axis, step):
    size = lax.axis_size(axis)
    pairs = [(i, i + step) for i in range(size) if 0 <= i + step < size]
    return lax.ppermute(value, axis, pairs)


def summed(value, axis):
    for bit in range(bit_count(lax.axis_size(axis))):
        value = value + swap(value, axis, bit)
    return value


def scatter_step(value, axis, bit):
    half = value.shape[0] // 2
    return value[:half] + swap(value[half:].astype(BF16), axis, bit).astype(F32)


def together(*values):
    return lax.optimization_barrier(values)


def gather_params(value):
    dims = []
    for axis in ("img", "row"):
        index = lax.axis_index(axis)
        for bit in reversed(range(bit_count(lax.axis_size(axis)))):
            other = swap(value, axis, bit)
            mine_second = (index >> bit) & 1 == 1
            value = jnp.stack([jnp.where(mine_second, other, value), jnp.where(mine_second, value, other)])
            dims.append((axis, bit))
    dims = dims[::-1]
    wanted = [("img", b) for b in reversed(range(bit_count(lax.axis_size("img"))))]
    wanted += [("row", b) for b in reversed(range(bit_count(lax.axis_size("row"))))]
    order = [dims.index(d) for d in wanted]
    value = jnp.transpose(value, order + [value.ndim - 2, value.ndim - 1])
    return value.reshape(-1)


def scatter_grads(flat):
    rows, imgs = lax.axis_size("row"), lax.axis_size("img")
    names = [("img", b) for b in reversed(range(bit_count(imgs)))] + [("row", b) for b in reversed(range(bit_count(rows)))]
    leaf = flat.shape[0] // (rows * imgs)
    value = flat.reshape((2,) * len(names) + (leaf // 128, 128))
    for axis, bits in (("row", range(bit_count(rows))), ("img", range(bit_count(imgs)))):
        index = lax.axis_index(axis)
        for bit in bits:
            place = names.index((axis, bit))
            names.pop(place)
            own = (index >> bit) & 1
            keep = lax.dynamic_index_in_dim(value, own, place, False)
            send = lax.dynamic_index_in_dim(value, 1 - own, place, False)
            value = keep + swap(send, axis, bit)
    return value.reshape(leaf)


def segment_list(canvas_rows, canvas_cols):
    return [
        ("w_patch", (3 * PATCH * PATCH, DIM)),
        ("w_qkv", (DIM, 3 * DIM)),
        ("w_proj", (DIM, DIM)),
        ("w_fc1", (DIM, MLP)),
        ("w_fc2", (MLP, DIM)),
        ("w_head", (DIM, CLASSES)),
        ("rel_rows", (2 * canvas_rows - 8, DIM)),
        ("rel_cols", (2 * canvas_cols - 8, DIM)),
        ("small", (49, DIM)),
        ("b_head", (CLASSES,)),
    ]


def unpack(flat_vec, segments):
    pieces = {}
    position = 0
    for seg_name, seg_shape in segments:
        entries = int(np.prod(seg_shape))
        pieces[seg_name] = flat_vec[position : position + entries].reshape(seg_shape)
        position += entries
    return pieces


def patch_rows(weight):
    taps = jnp.pad(weight.reshape(PATCH, PATCH, 3, DIM), ((0, 1), (0, 0), (0, 1), (0, 0)))
    parts = []
    for piece in (taps[:, 3:7], jnp.pad(taps[:, 0:3], ((0, 0), (1, 0), (0, 0), (0, 0)))):
        parts.append(jnp.transpose(piece.reshape(2, 4, 4, 4, DIM), (0, 2, 1, 3, 4)).reshape(128, DIM))
    return jnp.concatenate(parts, axis=0)


def patch_rows_back(grad):
    taps = jnp.transpose(grad.T.reshape(2, 2, 4, 4, 4, DIM), (0, 1, 3, 2, 4, 5)).reshape(2, 8, 4, 4, DIM)
    return jnp.concatenate([taps[1, :PATCH, 1:, :3], taps[0, :PATCH, :, :3]], axis=1).reshape(3 * PATCH * PATCH, DIM)


def relative_windows(rel_rows, rel_cols, row_index, key_rows):
    offsets = jnp.flip(rel_cols.reshape(-1, 8, DIM), 0)
    offsets = jnp.transpose(jnp.pad(offsets, ((0, 1), (0, 0), (0, 0))), (1, 0, 2))
    blocks = rel_rows.reshape(2 * key_rows - 1, 8, DIM)
    rows = jnp.transpose(jnp.flip(lax.dynamic_slice_in_dim(blocks, row_index, key_rows, 0), 0), (1, 0, 2))
    rows = rows.reshape(8 * key_rows, DIM)
    windows = []
    for pair in range(PAIRS):
        cols = offsets[:, 24 - 8 * pair : 24 - 8 * pair + WIN].reshape(8 * WIN, DIM)
        windows.append(jnp.concatenate([cols, rows], axis=0))
    return jnp.stack(windows)


def relative_windows_back(grad, row_index, key_rows):
    cols = grad[:, : 8 * WIN].reshape(PAIRS, 8, WIN, DIM)
    total = 0.0
    for pair in range(PAIRS):
        start = 24 - 8 * pair
        total = total + jnp.pad(cols[pair], ((0, 0), (start, 64 - start - WIN), (0, 0)))
    rel_cols = jnp.flip(jnp.transpose(total[:, :63], (1, 0, 2)), 0).reshape(-1, DIM)
    rows = jnp.sum(grad[:, 8 * WIN :], axis=0).reshape(8, key_rows, DIM)
    rows = jnp.flip(jnp.transpose(rows, (1, 0, 2)), 0)
    blocks = lax.dynamic_update_slice_in_dim(jnp.zeros((2 * key_rows - 1, 8, DIM), F32), rows, row_index, 0)
    return blocks.reshape(-1, DIM), rel_cols


def tap_keep():
    keep = np.ones((3, 4, 32), np.float32)
    keep[:, 3] = 0.0
    keep[:, 0, 0] = 0.0
    return keep


def prepare(weights, row_index, key_rows):
    small = weights["small"]
    vec = jnp.pad(small.astype(F32).T, ((0, 0), (0, 15)))
    windows = relative_windows(weights["rel_rows"], weights["rel_cols"], row_index, key_rows)
    return {
        "vec": vec,
        "wp": patch_rows(weights["w_patch"]).T,
        "wqkv": weights["w_qkv"],
        "wqkv_t": weights["w_qkv"].T,
        "wproj": weights["w_proj"],
        "w1": weights["w_fc1"],
        "w2": weights["w_fc2"],
        "rw": windows,
        "rw_t": jnp.transpose(windows, (0, 2, 1)),
    }


def image_loss(pooled, head_w, head_b, log_teacher, labels, image_total):
    logits = jnp.dot(pooled, head_w, precision=HIGHEST_PREC) + head_b
    log_student = jax.nn.log_softmax(logits, axis=-1)
    onehot = (jnp.arange(CLASSES)[None, :] == labels[:, None]).astype(F32)
    per_image = jnp.sum(jnp.exp(log_teacher) * (log_teacher - log_student), axis=-1) - jnp.sum(onehot * log_student, axis=-1)
    return jnp.sum(per_image) / image_total


def body(flat_params, first_moment, second_moment, pixels, extents, labels, teacher):
    key_rows = lax.axis_size("row")
    row_index = lax.axis_index("row")
    row_lead = row_index == 0
    segments = segment_list(ROWS * key_rows, CANVAS_W)
    full_params = gather_params(flat_params.astype(BF16).reshape(-1, 128))
    weights = unpack(full_params, segments)
    wts = prepare(weights, row_index, key_rows)
    tap = tap_matrix()
    consts = {"perm": jnp.asarray(deinterleave_matrix(), BF16), "tap": jnp.asarray(tap, BF16), "tap_t": jnp.asarray(tap.T, BF16)}
    vectors = weights["small"][27:42].astype(F32)
    row = row_index.astype(jnp.int32).reshape(1)
    images = pixels.shape[0]
    parts = 1
    size = images // parts
    image_total = images * lax.axis_size("img") * 1.0
    head_w = weights["w_head"].astype(F32)
    head_b = weights["b_head"].astype(F32)

    ids = jnp.arange(images)
    widths = extents[:, 1]
    ahead = (widths[None, :] > widths[:, None]) | ((widths[None, :] == widths[:, None]) & (ids[None, :] < ids[:, None]))
    places = jnp.sum(ahead.astype(jnp.int32), axis=1)
    chosen = places[None, :] == ids[:, None]
    order = jnp.sum(jnp.where(chosen, ids[None, :], 0), axis=1)
    ext = jnp.sum(jnp.where(chosen[:, :, None], extents[None], 0), axis=1)

    log_teacher = jax.nn.log_softmax(teacher, axis=-1)
    pixel_view = jnp.transpose(pixels, (0, 2, 3, 1, 4))
    saved = []
    for part in range(parts):
        first, last, nsel, kvt, below, own = call_edge(ext, row, order, pixel_view, consts, wts, size, part * size)
        got = shifted(below, "row", 1)
        kv = lax.all_gather(call_pool_norm(own, got, wts["vec"]), "row", axis=0)
        top = shifted(last, "row", 1)
        bot = shifted(first, "row", -1)
        names = sorted(wts)
        after, log_teacher, *values = together(ext, log_teacher, *[wts[name] for name in names])
        wts = dict(zip(names, values))
        patches, x0, q = call_embed(after, row, order, pixel_view, consts, wts, size, part * size)
        saved.append(dict(patches=patches, x0=x0, q=q, top=top, bot=bot, nsel=nsel, kvt=kvt, own=own, got=got, kv=kv))
    for part in range(parts):
        s = saved[part]
        s["fwd"] = call_forward(ext, row, s["q"], s["top"], s["bot"], s["x0"], s["kv"], wts, part * size)
    total = {}

    def add(name, value):
        total[name] = total[name] + value if name in total else value

    sorted_local = jnp.sum(jnp.concatenate([s["fwd"][-1] for s in saved], axis=0), axis=-1)
    local = jnp.sum(jnp.where(chosen[:, :, None], sorted_local[:, None, :], 0.0), axis=0)
    everywhere = summed(local, "row")
    counts = (extents[:, 0] * extents[:, 1]).astype(F32)[:, None]
    pooled = (everywhere * vectors[13] + counts * vectors[14]) / counts

    def loss_of(pooled_now, w, b):
        return image_loss(pooled_now, w, b, log_teacher, labels, image_total)

    loss_value, loss_back = jax.vjp(loss_of, pooled, head_w, head_b)
    grad_pooled, total["w_head"], total["b_head"] = loss_back(jnp.ones_like(loss_value))
    gvec = grad_pooled / counts
    local_count = jnp.where(row_index * ROWS < extents[:, 0], ROWS * extents[:, 1], 0).astype(F32)[:, None]
    total["g_three"] = jnp.sum(gvec * local, axis=0)
    total["b_three"] = jnp.sum(gvec * local_count, axis=0)
    gvec = jnp.sum(jnp.where(chosen[:, :, None], gvec[None], 0.0), axis=1)[:, :, None]
    for part in range(parts):
        s = saved[part]
        s["bwd"] = call_backward(ext, row, s["fwd"][:-1], s["q"], s["top"], s["bot"], s["kv"], gvec[part * size : part * size + size], wts, part * size)
    for part in range(parts):
        s = saved[part]
        dx1, dq, up, down, dkv, a2, a1, ap, av, ak, ar = s["bwd"]
        for name, value in (("a2", a2), ("a1", a1), ("ap", ap), ("av", av), ("ak", ak), ("ar", ar)):
            add(name, value)
        bits = bit_count(key_rows)
        for bit in range(bits):
            if bit == bits - 1:
                dkv, up, down = together(dkv, up, down)
                rtop = shifted(down, "row", 1)
                rbot = shifted(up, "row", -1)
            dkv = scatter_step(dkv, "row", bit)
        grad_kv = dkv[0]
        pre, pool_sums = call_pool_back(s["own"], s["got"], grad_kv, wts["vec"])
        add("pool_sums", pool_sums)
        under = shifted(pre, "row", -1)
        aq, akv, apatch, av1, akt = call_embed_back(
            ext, row, s["patches"], dq, dx1, rtop, rbot, s["nsel"], s["kvt"], pre, under, consts, wts, part * size)
        for name, value in (("aq", aq), ("akv", akv), ("apatch", apatch), ("av1", av1), ("akt", akt)):
            add(name, value)

    t = total
    lead = jnp.where(row_lead, 1.0, 0.0)
    av, av1 = jnp.sum(t["av"], axis=-1), jnp.sum(t["av1"], axis=-1)
    pool_sums = jnp.sum(t["pool_sums"], axis=-1)
    rel_rows, rel_cols = relative_windows_back(t["ar"], row_index, key_rows)
    taps = jnp.sum((t["akt"].reshape(2, DIM, 3, 4, 32) * tap_keep())[:, :, :, :3], axis=-1)
    kernels = jnp.concatenate([jnp.sum(t["ak"], axis=-1), jnp.transpose(taps, (0, 2, 3, 1)).reshape(18, DIM)], axis=0)
    grad_vectors = jnp.stack([
        av1[0], av1[1], av1[2], av[2], av[3], pool_sums[0], pool_sums[1], pool_sums[2], pool_sums[3],
        t["ap"][DIM], av[0], av[1], t["a2"][MLP], t["g_three"], t["b_three"]])
    pieces = [
        patch_rows_back(t["apatch"]),
        jnp.concatenate([t["aq"][:DIM], t["akv"][:DIM]], axis=1),
        t["ap"][:DIM],
        t["a1"][:DIM],
        t["a2"][:MLP],
        t["w_head"] * lead,
        rel_rows,
        rel_cols,
        kernels,
        grad_vectors,
        t["aq"][DIM],
        t["akv"][DIM],
        t["a1"][DIM],
        t["b_head"] * lead,
    ]
    joined = jnp.concatenate([piece.reshape(-1) for piece in pieces])
    grad_flat = jnp.pad(joined, (0, full_params.shape[0] - joined.shape[0]))
    grad_shard = scatter_grads(grad_flat)
    norm_sq = summed(jnp.sum(grad_shard * grad_shard), "row")
    both = summed(jnp.stack([norm_sq, loss_value]), "img")
    grad_norm = jnp.sqrt(both[0])
    clip_factor = jnp.minimum(1.0, CLIP_NORM / (grad_norm + 1e-06))
    clipped = grad_shard * clip_factor
    moment_one = BETA_FIRST * first_moment + (1.0 - BETA_FIRST) * clipped
    moment_two = BETA_SECOND * second_moment + (1.0 - BETA_SECOND) * clipped * clipped
    fix_one = 1.0 - BETA_FIRST**STEP
    fix_two = 1.0 - BETA_SECOND**STEP
    update = moment_one / fix_one / (jnp.sqrt(moment_two / fix_two) + ADAM_EPS) + WEIGHT_DECAY * flat_params
    new_params = flat_params - LEARN_RATE * update
    return (new_params, moment_one, moment_two, grad_norm, both[1])


def solution(mesh):
    placed = (
        P(("img", "row")),
        P(("img", "row")),
        P(("img", "row")),
        P("img", "row", None, None, None),
        P("img", None),
        P("img"),
        P("img", None),
    )
    return jax.shard_map(
        body,
        mesh=mesh,
        in_specs=placed,
        out_specs=(P(("img", "row")), P(("img", "row")), P(("img", "row")), P(), P()),
        check_vma=False,
    )
```

```python
import functools

import jax
import jax.numpy as jnp
import numpy as np
from jax import lax
from jax.experimental import pallas as pl
from jax.experimental.pallas import tpu as pltpu
from jax.sharding import PartitionSpec as P

DIM = 96
MLP = 384
CLASSES = 1000
PATCH = 7
ROWS = 8
STEP = 7
CANVAS_W = 256

HIGHEST_PREC = lax.Precision.HIGHEST
CLIP_NORM = 0.02
LEARN_RATE = 0.05
WEIGHT_DECAY = 0.05
BETA_FIRST = 0.5
BETA_SECOND = 0.5
ADAM_EPS = 1e-08
NORM_EPS = 1e-06
NEG_FILL = -1e30

F32 = jnp.float32
BF16 = jnp.bfloat16
SCALE = DIM ** (-0.5)
EXP2_SCALE = SCALE * 1.4426950408889634

TOKENS = ROWS * CANVAS_W
PAIR = 512
PAIRS = TOKENS // PAIR
TILES = CANVAS_W // 32
GROUP = 2
PADDED = TOKENS + 512
WIN = 40
PATCH_ROWS = 256
VMEM_BYTES = 56 * 1024 * 1024


def deinterleave_matrix():
    out = np.zeros((4, 128, 4, 4, 32), np.float32)
    for row in range(4):
        for phase in range(4):
            for col in range(32):
                out[row, 4 * col + phase, phase, row, col] = 1.0
    return out.reshape(512, 512)


def tap_matrix():
    out = np.zeros((CANVAS_W, 128), np.float32)
    for tap in range(3):
        for key in range(32):
            col = 8 * key + tap - 1
            if col >= 0:
                out[col, tap * 32 + key] = 1.0
    return out


def dot(a, b):
    return jnp.dot(a, b, preferred_element_type=F32)


def dot_nt(a, b):
    return lax.dot_general(a, b, (((1,), (1,)), ((), ())), preferred_element_type=F32)


def normalized(x):
    mean = jnp.sum(x, axis=0, keepdims=True) * (1.0 / DIM)
    centered = x - mean
    var = jnp.sum(centered * centered, axis=0, keepdims=True) * (1.0 / DIM)
    rstd = lax.rsqrt(var + NORM_EPS)
    return centered * rstd, rstd


def norm_back(grad, hat, rstd, gain):
    inner = grad * gain
    mean_one = jnp.sum(inner, axis=0, keepdims=True) * (1.0 / DIM)
    mean_two = jnp.sum(inner * hat, axis=0, keepdims=True) * (1.0 / DIM)
    return rstd * (inner - mean_one - hat * mean_two)


def by_lanes(fn, *arrays):
    parts = [fn(k, *(a[:, 128 * k : 128 * k + 128] for a in arrays)) for k in range(arrays[0].shape[1] // 128)]
    return tuple(jnp.concatenate(column, axis=1) for column in zip(*parts))


def by_blocks(fn, height, *arrays):
    rows = []
    for top in range(0, arrays[0].shape[0], height):
        rows.append(by_lanes(lambda k, *block: fn(slice(top, top + height), *block), *(a[top : top + height] for a in arrays)))
    return tuple(jnp.concatenate(column, axis=0) for column in zip(*rows))


def fold_lanes(x):
    total = x[:, 0:128]
    for k in range(1, x.shape[1] // 128):
        total = total + x[:, 128 * k : 128 * k + 128]
    return total


def place_of(index):
    return index + 27 if index < 15 else index - 15 if index < 42 else index


def column(vec_ref, index):
    place = place_of(index)
    return vec_ref[:, place : place + 1]


def fill_wide(wide_ref, vec_ref, indices):
    for k, index in enumerate(indices):
        wide_ref[k] = jnp.broadcast_to(column(vec_ref, index), (DIM, 128))


def fill_taps(taps_ref, vec_ref):
    lane = lane_ids(128, DIM)
    for member in range(2):
        for r in range(3):
            block = jnp.zeros((DIM, 128), F32)
            for c in range(3):
                block = jnp.where((lane >> 5) == c, column(vec_ref, 24 + 9 * member + 3 * r + c), block)
            taps_ref[DIM * member : DIM * member + DIM, 128 * r : 128 * r + 128] = jnp.where(lane == 0, 0.0, block)


def fill_bias(bias_ref, vec_ref):
    for k in range(MLP // DIM):
        bias_ref[DIM * k : DIM * k + DIM] = jnp.broadcast_to(vec_ref[:, 45 + k : 46 + k], (DIM, 128))


def fill_transpose(dst_ref, src_ref):
    rows, cols = src_ref.shape
    value = src_ref[...].astype(F32)
    value = jnp.pad(value, ((0, -rows % 128), (0, -cols % 128)))
    dst_ref[...] = jnp.transpose(value)[:cols, :rows].astype(BF16)


def wide(wide_ref, k, width=PAIR):
    return jnp.concatenate([wide_ref[k]] * (width // 128), axis=1)


def lane_ids(width, rows=1):
    return lax.broadcasted_iota(jnp.int32, (rows, width), 1)


def pair_mask(pair, breadths, row_oks):
    lane = lane_ids(PAIR)
    col = pair * 64 + (lane >> 8) * 32 + (lane & 31)
    return jnp.concatenate([jnp.where((col < w) & ok, 1.0, 0.0).astype(F32) for w, ok in zip(breadths, row_oks)], axis=1)


def pair_lanes(pair, base=0):
    return pl.ds(pl.multiple_of(pair * PAIR + base, 128), PAIR)


def load_pair(ref, pair):
    lanes = pair_lanes(pair)
    return jnp.concatenate([ref[g, :, lanes] for g in range(GROUP)], axis=1)


def store_pair(ref, pair, value, base=0):
    for g in range(GROUP):
        ref[g, :, pair_lanes(pair, base)] = value[:, PAIR * g : PAIR * g + PAIR]


def by_image(value):
    return [value[:, PAIR * g : PAIR * g + PAIR] for g in range(GROUP)]


def pair_count(breadths):
    widest = breadths[0]
    for breadth in breadths[1:]:
        widest = jnp.maximum(widest, breadth)
    return jnp.minimum((widest >> 6) + 1, PAIRS)


def group_extents(ext_ref, row_ref, offset, group=None):
    group = pl.program_id(0) if group is None else group
    images = [group * GROUP + g for g in range(GROUP)]
    heights = [ext_ref[offset + image, 0] for image in images]
    breadths = [ext_ref[offset + image, 1] for image in images]
    return images, heights, breadths, [row_ref[0] * ROWS < height for height in heights]


def col_shifts(window, base):
    lane = lane_ids(128, window.shape[0])
    here = window[:, base : base + 128]
    before = window[:, base - 256 : base - 128]
    after = window[:, base + 256 : base + 384]
    left = jnp.where((lane & 31) == 0, pltpu.roll(before, 97, 1), pltpu.roll(here, 1, 1))
    right = jnp.where((lane & 31) == 31, pltpu.roll(after, 31, 1), pltpu.roll(here, 127, 1))
    return left.astype(F32), here.astype(F32), right.astype(F32)


def rows_down(first, second, entering):
    lane = lane_ids(128, first.shape[0])
    a, b = pltpu.roll(first, 32, 1), pltpu.roll(second, 32, 1)
    return jnp.where(lane < 32, entering, a), jnp.where(lane < 32, a, b), b


def rows_up(first, second, entering):
    lane = lane_ids(128, first.shape[0])
    a, b = pltpu.roll(first, 96, 1), pltpu.roll(second, 96, 1)
    return jnp.where(lane >= 96, b, a), jnp.where(lane >= 96, entering, b), a


def spread_halo(dst_ref, halo, target):
    for tile in range(TILES):
        block = halo[:, 128 * (tile // 4) : 128 * (tile // 4) + 128]
        shift = (target - 32 * (tile % 4)) % 128
        dst_ref[:, 128 * tile : 128 * tile + 128] = pltpu.roll(block, shift, 1) if shift else block


def store_lanes(dst_ref, value, image):
    place = image & 3
    lane = lane_ids(128, value.shape[0])
    dst_ref[...] = jnp.where((lane >> 5) == place, pltpu.roll(value, place * 32, 1), dst_ref[...])


def take_lanes(value, image, target):
    return pltpu.roll(value, (4 + target - (image & 3)) * 32 & 127, 1)


def gather_halo(src_ref, target):
    lane = lane_ids(128, DIM)
    blocks = []
    for half in range(2):
        total = None
        for k in range(4):
            tile = 4 * half + k
            block = src_ref[:, 128 * tile : 128 * tile + 128]
            shift = (32 * k - target) % 128
            block = pltpu.roll(block, shift, 1) if shift else block
            total = block if total is None else jnp.where((lane >> 5) == k, block, total)
        blocks.append(total)
    return jnp.concatenate(blocks, axis=1)


def reverse_bits(value, count):
    result = 0
    for bit in range(count.bit_length() - 1):
        result = result * 2 + ((value >> bit) & 1)
    return result


def key_tables(kv_ref, image, key_rows, height, breadth, ka_ref, kn_ref):
    lane = lane_ids(128, 2 * DIM)
    blocks = []
    for i in range(0, key_rows, 4):
        block = take_lanes(kv_ref[i].astype(F32), image, 0)
        for k in range(1, 4):
            block = jnp.where((lane >> 5) == k, take_lanes(kv_ref[i + k].astype(F32), image, k), block)
        blocks.append(block)
    both = jnp.concatenate(blocks, axis=1)
    total = key_rows * 32
    more = aug_rows(key_rows)
    rank = lax.broadcasted_iota(jnp.int32, (more, total), 0)
    key = lax.broadcasted_iota(jnp.int32, (more, total), 1)
    key_r, key_c = key >> 5, key & 31
    half = key_rows + 32
    low = rank >= half
    rank_in = jnp.where(low, rank - half, rank)
    hit = rank_in == jnp.where(rank_in < key_rows, key_r, key_c + key_rows)
    invalid = (key_r * ROWS >= height) | (key_c * ROWS >= breadth)
    table = jnp.where(rank < 2 * half, jnp.where(hit, 1.0, 0.0), 0.0)
    table = jnp.where((rank == 2 * half) & invalid, NEG_FILL, table)
    full = jnp.concatenate([both[:DIM], table, jnp.zeros((256 - DIM - more, total), F32)], axis=0)
    ka_ref[...] = full[: DIM + more].astype(BF16)
    kn_ref[...] = jnp.transpose(full).astype(BF16)
    return both[DIM:]


def aug_rows(key_rows):
    return 2 * key_rows + 64 + 16


def pixel_rows(pix_ref, s_ref):
    for a in range(4):
        for ch in range(3):
            block = pix_ref[0, a, ch].astype(F32)
            for tile in range(TILES):
                s_ref[tile, pl.ds(4 * a + ch, ROWS, stride=16), :] = block[:, 128 * tile : 128 * tile + 128]
    for a in range(3):
        for ch in range(3):
            block = pix_ref[0, 4 + a, ch].astype(F32)
            for tile in range(TILES):
                s_ref[tile, 128 + 4 * a + ch : 129 + 4 * a + ch, :] = block[ROWS - 1 : ROWS, 128 * tile : 128 * tile + 128]


def patch_blocks(s_ref, perm, shifted, sets):
    rows = [s_ref[tile] for tile in range(TILES)]
    if shifted:
        first = lane_ids(128, 144) < 4
        rolled = [pltpu.roll(block, 4, 1) for block in rows]
        rows = [jnp.where(first, rolled[tile - 1] if tile else 0.0, rolled[tile]) for tile in range(TILES)]
    rows = [block.astype(BF16) for block in rows]
    stack = []
    for chosen in sets:
        for tile in range(TILES):
            stack.append(jnp.concatenate([rows[tile][16 * r : 16 * r + 16] for r in chosen], axis=1))
    return dot(jnp.concatenate(stack, axis=0), perm).astype(BF16)


def edge_kernel(ext_ref, row_ref, order_ref, *refs, offset):
    pix_refs, refs = refs[:GROUP], refs[GROUP:]
    (perm_ref, tap_ref, wp_ref, wqkv_ref, vec_ref,
     first_ref, last_ref, nsel_ref, kvt_ref, below_ref, own_ref, s_ref, p_ref, wide_ref, kexp_ref) = refs
    images, heights, breadths, row_oks = group_extents(ext_ref, row_ref, offset)

    @pl.when(pl.program_id(0) == 0)
    def _():
        s_ref[...] = jnp.zeros_like(s_ref)
        fill_wide(wide_ref, vec_ref, [0, 1, 2, 42, 43, 44])
        fill_taps(kexp_ref, vec_ref)

    lane = lane_ids(1024)
    masks = []
    for g in range(GROUP):
        pixel_rows(pix_refs[g], s_ref)
        for shifted in range(2):
            out = patch_blocks(s_ref, perm_ref[...], shifted, ((7, 0, 1, 1), (8, 1, 2, 2)))
            for half in range(2):
                for tile in range(TILES):
                    block = out[128 * half + 16 * tile : 128 * half + 16 * tile + 16]
                    for phase in range(4):
                        top = 128 * shifted + 64 * half + 16 * phase
                        p_ref[top : top + 16, 1024 * g + 128 * tile : 1024 * g + 128 * tile + 128] = block[:, 128 * phase : 128 * phase + 128]
        col = (lane >> 7) * 32 + (lane & 31)
        masks.append(jnp.where((col < breadths[g]) & row_oks[g], 1.0, 0.0).astype(F32))

    def first_norm(k, embed, mask):
        hat, _ = normalized((embed + wide_ref[0]) * mask)
        return ((hat * wide_ref[1] + wide_ref[2]).astype(BF16),)

    (normed,) = by_lanes(first_norm, dot(wp_ref[...], p_ref[...]), jnp.concatenate(masks, axis=1))
    rows = []
    for slot in range(3):
        rows.append(jnp.concatenate([gather_halo(normed[:, 1024 * g : 1024 * g + 1024], 32 * slot) for g in range(GROUP)], axis=1))
    edge = dot(wqkv_ref[0:DIM, :], jnp.concatenate(rows[:2], axis=1))
    (edge,) = by_lanes(lambda k, out: ((out + wide_ref[3]).astype(BF16),), edge)
    nsel = dot(jnp.concatenate([row[:, CANVAS_W * g : CANVAS_W * g + CANVAS_W] for g in range(GROUP) for row in rows], axis=0), tap_ref[...])
    nsel = jnp.concatenate([nsel[DIM * k : DIM * k + DIM] for k in range(3 * GROUP)], axis=1).astype(BF16)
    bias = jnp.concatenate([wide_ref[4], wide_ref[5]], axis=0)
    (taps,) = by_lanes(lambda k, out: ((out + bias).astype(BF16),), dot(wqkv_ref[DIM : 3 * DIM, :], nsel))
    for g in range(GROUP):
        last_ref[g] = edge[:, CANVAS_W * g : CANVAS_W * g + CANVAS_W]
        first_ref[g] = edge[:, CANVAS_W * (GROUP + g) : CANVAS_W * (GROUP + g) + CANVAS_W]
        nsel_ref[g] = nsel[:, 384 * g : 384 * g + 384]
        kvt_ref[g] = taps[:, 384 * g : 384 * g + 384]
        product = taps[:, 384 * g : 384 * g + 384].astype(F32) * kexp_ref[...]
        sums = []
        for k in range(3):
            part = product[:, 128 * k : 128 * k + 128]
            sums.append(part + pltpu.roll(part, 96, 1) + pltpu.roll(part, 64, 1))
        store_lanes(below_ref, sums[0], images[g])
        store_lanes(own_ref, sums[1] + sums[2], images[g])


def embed_kernel(ext_ref, row_ref, order_ref, *refs, offset):
    pix_refs, refs = refs[:GROUP], refs[GROUP:]
    perm_ref, wp_ref, wqkv_ref, vec_ref, patch_ref, x0_ref, q_ref, s_ref, wide_ref = refs
    images, heights, breadths, row_oks = group_extents(ext_ref, row_ref, offset)

    @pl.when(pl.program_id(0) == 0)
    def _():
        s_ref[...] = jnp.zeros_like(s_ref)
        fill_wide(wide_ref, vec_ref, [0, 1, 2, 42])

    for g in range(GROUP):
        pixel_rows(pix_refs[g], s_ref)
        for shifted in range(2):
            out = patch_blocks(s_ref, perm_ref[...], shifted, ((0, 1, 2, 3), (4, 5, 6, 7), (1, 2, 3, 4), (5, 6, 7, 8)))
            for which in range(4):
                half, side = which // 2, which % 2
                for tile in range(TILES):
                    block = out[128 * which + 16 * tile : 128 * which + 16 * tile + 16]
                    for phase in range(4):
                        top = 128 * shifted + 64 * half + 16 * phase
                        patch_ref[g, top : top + 16, 256 * tile + 128 * side : 256 * tile + 128 * side + 128] = block[
                            :, 128 * phase : 128 * phase + 128]

    count = pair_count(breadths)

    def active(pair, carry):
        def first_norm(k, embed, mask):
            x0 = (embed + wide_ref[0]) * mask
            hat, _ = normalized(x0)
            return x0, (hat * wide_ref[1] + wide_ref[2]).astype(BF16)

        x0, normed = by_lanes(first_norm, dot(wp_ref[...], load_pair(patch_ref, pair)), pair_mask(pair, breadths, row_oks))
        store_pair(x0_ref, pair, x0)
        (query,) = by_lanes(lambda k, out: ((out + wide_ref[3]).astype(BF16),), dot(wqkv_ref[0:DIM, :], normed))
        store_pair(q_ref, pair, query, 256)
        return carry

    def idle(pair, carry):
        for g in range(GROUP):
            q_ref[g, :, pair_lanes(pair, 256)] = jnp.zeros((DIM, PAIR), BF16)
        return carry

    lax.fori_loop(0, count, active, 0)
    lax.fori_loop(count, PAIRS, idle, 0)
    for g in range(GROUP):
        q_ref[g, :, 0:256] = jnp.zeros((DIM, 256), BF16)
        q_ref[g, :, 256 + TOKENS : 512 + TOKENS] = jnp.zeros((DIM, 256), BF16)


def key_lanes(*lead):
    return pl.BlockSpec(lead + (128,), lambda i, *_: (0,) * len(lead) + (i * GROUP >> 2,))


def specs():
    whole = lambda *shape: pl.BlockSpec(shape, lambda i, *_: (0,) * len(shape))
    per = lambda *shape: pl.BlockSpec((GROUP,) + shape, lambda i, *_: (i,) + (0,) * len(shape))
    return whole, per


def pixel_specs(offset):
    return [pl.BlockSpec((1, PATCH, 3, ROWS, 1024), lambda i, ext, row, order, g=g: (order[offset + i * GROUP + g], 0, 0, 0, 0)) for g in range(GROUP)]


def call_edge(ext, row, order, pixels, consts, wts, images, offset):
    whole, per = specs()
    shapes = [(DIM, CANVAS_W), (DIM, CANVAS_W), (DIM, 384), (2 * DIM, 384)]
    return pl.pallas_call(
        functools.partial(edge_kernel, offset=offset),
        grid_spec=pltpu.PrefetchScalarGridSpec(
            num_scalar_prefetch=3, grid=(images // GROUP,),
            in_specs=pixel_specs(offset) + [
                whole(512, 512), whole(CANVAS_W, 128), whole(DIM, PATCH_ROWS), whole(3 * DIM, DIM), whole(DIM, 64)],
            out_specs=[per(*s) for s in shapes] + [key_lanes(2 * DIM)] * 2,
            scratch_shapes=[pltpu.VMEM((TILES, 144, 128), F32), pltpu.VMEM((PATCH_ROWS, 1024 * GROUP), BF16), pltpu.VMEM((6, DIM, 128), F32),
                            pltpu.VMEM((2 * DIM, 384), F32)]),
        out_shape=[jax.ShapeDtypeStruct((images,) + s, BF16) for s in shapes]
        + [jax.ShapeDtypeStruct((2 * DIM, 32 * images), F32)] * 2,
        compiler_params=pltpu.CompilerParams(vmem_limit_bytes=VMEM_BYTES),
        cost_estimate=pl.CostEstimate(flops=images * 1_000_000_000, bytes_accessed=images * 1_000_000, transcendentals=0),
        name="edge",
    )(ext, row, order, *[pixels] * GROUP, consts["perm"], consts["tap"], wts["wp"], wts["wqkv_t"], wts["vec"])


def call_embed(ext, row, order, pixels, consts, wts, images, offset):
    whole, per = specs()
    shapes = [((PATCH_ROWS, TOKENS), BF16), ((DIM, TOKENS), F32), ((DIM, PADDED), BF16)]
    return pl.pallas_call(
        functools.partial(embed_kernel, offset=offset),
        grid_spec=pltpu.PrefetchScalarGridSpec(
            num_scalar_prefetch=3, grid=(images // GROUP,),
            in_specs=pixel_specs(offset) + [whole(512, 512), whole(DIM, PATCH_ROWS), whole(3 * DIM, DIM), whole(DIM, 64)],
            out_specs=[per(*s) for s, _ in shapes],
            scratch_shapes=[pltpu.VMEM((TILES, 144, 128), F32), pltpu.VMEM((4, DIM, 128), F32)]),
        out_shape=[jax.ShapeDtypeStruct((images,) + s, t) for s, t in shapes],
        compiler_params=pltpu.CompilerParams(vmem_limit_bytes=VMEM_BYTES),
        cost_estimate=pl.CostEstimate(flops=images * 2_000_000_000, bytes_accessed=images * 4_000_000, transcendentals=0),
        name="embed",
    )(ext, row, order, *[pixels] * GROUP, consts["perm"], wts["wp"], wts["wqkv_t"], wts["vec"])


def pool_norm_kernel(own_ref, got_ref, vec_ref, kv_ref):
    for member in range(2):
        part = slice(member * DIM, member * DIM + DIM)
        hat, _ = normalized(own_ref[part] + got_ref[part])
        kv_ref[part] = (hat * column(vec_ref, 5 + 2 * member) + column(vec_ref, 6 + 2 * member)).astype(BF16)


def call_pool_norm(own, got, vec):
    return pl.pallas_call(
        pool_norm_kernel, out_shape=jax.ShapeDtypeStruct(own.shape, BF16), name="pool_norm",
        cost_estimate=pl.CostEstimate(flops=own.size * 10, bytes_accessed=own.size * 10, transcendentals=0))(own, got, vec)


def pool_back_kernel(own_ref, got_ref, grad_ref, vec_ref, pre_ref, sums_ref):
    for member in range(2):
        part = slice(member * DIM, member * DIM + DIM)
        hat, rstd = normalized(own_ref[part] + got_ref[part])
        grad = grad_ref[part].astype(F32)
        pre_ref[part] = norm_back(grad, hat, rstd, column(vec_ref, 5 + 2 * member))
        sums_ref[2 * member] = fold_lanes(grad * hat)
        sums_ref[2 * member + 1] = fold_lanes(grad)


def call_pool_back(own, got, grad, vec):
    return pl.pallas_call(
        pool_back_kernel,
        out_shape=[jax.ShapeDtypeStruct(own.shape, F32), jax.ShapeDtypeStruct((4, DIM, 128), F32)], name="pool_back",
        cost_estimate=pl.CostEstimate(flops=own.size * 20, bytes_accessed=own.size * 16, transcendentals=0))(own, got, grad, vec)


def lane_bit(lane, bit):
    return (lane & bit) != 0


def relative_terms(block, products, key_rows):
    lane = lane_ids(128, WIN)
    parts = [products[WIN * s : WIN * s + WIN] for s in range(8)]
    for bit in (1, 2, 4):
        chosen = lane_bit(lane, bit)
        parts = [jnp.where(chosen, parts[2 * k + 1], parts[2 * k]) for k in range(len(parts) // 2)]
    by_col = parts[0]
    for bit, step in ((8, 1), (16, 2)):
        by_col = jnp.where(lane_bit(lane, bit), by_col, pltpu.roll(by_col, WIN - step, 0))
    by_col = by_col[0:32] if block & 2 else by_col[4:36]
    lane = lane_ids(128, key_rows)
    rows = products[8 * WIN :]
    parts = [rows[key_rows * r : key_rows * r + key_rows] for r in range(4 * (block & 1), 4 * (block & 1) + 4)]
    for bit in (32, 64):
        chosen = lane_bit(lane, bit)
        parts = [jnp.where(chosen, parts[2 * k + 1], parts[2 * k]) for k in range(len(parts) // 2)]
    return jnp.concatenate([parts[0], by_col], axis=0)


def relative_spread(block, grad_terms, key_rows):
    lane = lane_ids(128, WIN)
    by_row = grad_terms[:key_rows]
    if block & 2:
        pieces = [grad_terms[key_rows:], jnp.zeros((WIN - 32, 128), F32)]
    else:
        pieces = [jnp.zeros((4, 128), F32), grad_terms[key_rows:], jnp.zeros((WIN - 36, 128), F32)]
    by_col = jnp.concatenate(pieces, axis=0)
    for bit, step in ((8, 1), (16, 2)):
        by_col = jnp.where(lane_bit(lane, bit), by_col, pltpu.roll(by_col, step, 0))
    parts = [jnp.where((lane & 7) == s, by_col, 0.0) for s in range(8)]
    lane = lane_ids(128, key_rows)
    for r in range(8):
        hit = (lane >> 5) == r - 4 * (block & 1)
        parts.append(jnp.where(hit, by_row, 0.0) if r // 4 == block & 1 else jnp.zeros((key_rows, 128), F32))
    return jnp.concatenate(parts, axis=0).astype(BF16)


def gelu_parts(hidden):
    cumulative = 0.5 + 0.5 * lax.erf(hidden * 0.7071067811865476)
    slope = cumulative + hidden * (jnp.exp(hidden * hidden * -0.5) * 0.3989422804014327)
    return (hidden * cumulative).astype(BF16), slope.astype(BF16)


def forward_kernel(ext_ref, row_ref, q_ref, top_ref, bot_ref, x0_ref, kv_ref, vec_ref, rw_ref, wproj_ref, w1_ref, w2_ref,
                   hat_ref, query_ref, terms_ref, att_ref, act_ref, slope_ref, hat2_ref, hat3_ref, stat_ref, pool_ref, ka_ref, kn_ref, v_ref, ztop_ref, zbot_ref, pre_ref, wide_ref, wb1_ref, wprojt_ref, w1t_ref, w2t_ref,
                   *, offset, key_rows):
    images, heights, breadths, row_oks = group_extents(ext_ref, row_ref, offset)
    depth = DIM + aug_rows(key_rows)

    @pl.when(pl.program_id(0) == 0)
    def _():
        fill_wide(wide_ref, vec_ref, list(range(15, 24)) + [3, 4, 9, 10, 11, 12])
        fill_bias(wb1_ref, vec_ref)
        fill_transpose(wprojt_ref, wproj_ref)
        fill_transpose(w1t_ref, w1_ref)
        fill_transpose(w2t_ref, w2_ref)

    lane = lane_ids(CANVAS_W, DIM)
    for g in range(GROUP):
        v_ref[g] = key_tables(kv_ref, images[g], key_rows, heights[g], breadths[g], ka_ref, kn_ref.at[g]).astype(BF16)
        for halo_ref, dst_ref, tap_row, target in ((top_ref, ztop_ref, 0, 0), (bot_ref, zbot_ref, 2, 96)):
            halo = halo_ref[g].astype(F32)
            left = jnp.where(lane == 0, 0.0, pltpu.roll(halo, 1, 1))
            right = jnp.where(lane == CANVAS_W - 1, 0.0, pltpu.roll(halo, CANVAS_W - 1, 1))
            taps = [wide(wide_ref, 3 * tap_row + k, CANVAS_W) for k in range(3)]
            spread_halo(dst_ref.at[g], taps[0] * left + taps[1] * halo + taps[2] * right, target)
    pool_ref[...] = jnp.zeros_like(pool_ref)

    def step(pair, carry):
        for group in range(0, DIM, 16):
            part = slice(group, group + 16)
            taps = [wide_ref[k, part] for k in range(9)]
            for g in range(GROUP):
                window = q_ref[g, part, pl.ds(pl.multiple_of(pair * PAIR, 128), PAIR + 512)]
                for tile in range(2):
                    sums = []
                    for side in range(2):
                        shifts = col_shifts(window, 256 + 256 * tile + 128 * side)
                        sums.append([sum(taps[3 * r + c] * shifts[c] for c in range(3)) for r in range(3)])
                    halo = pl.ds(pl.multiple_of((2 * pair + tile) * 128, 128), 128)
                    down = rows_down(sums[0][0], sums[1][0], ztop_ref[g, part, halo])
                    up = rows_up(sums[0][2], sums[1][2], zbot_ref[g, part, halo])
                    for side in range(2):
                        base = PAIR * g + 256 * tile + 128 * side
                        pre_ref[part, base : base + 128] = sums[side][1] + down[side] + up[side]

        def query_of(k, pre):
            hat, rstd = normalized(pre)
            return hat.astype(BF16), (hat * wide_ref[9] + wide_ref[10]).astype(BF16), rstd

        hat, query, rstd = by_lanes(query_of, pre_ref[...])
        store_pair(hat_ref, pair, hat)
        store_pair(query_ref, pair, query)

        def extra_of(k, products):
            terms = relative_terms(k, products, key_rows) * (DIM**0.5)
            high = terms.astype(BF16).astype(F32)
            return (jnp.concatenate([high, terms - high, jnp.ones((16, 128), F32)], axis=0).astype(BF16),)

        (extra,) = by_lanes(extra_of, dot(rw_ref[pair], query))
        store_pair(terms_ref, pair, extra)

        def softmax(k, scores):
            peak = jnp.max(scores, axis=0, keepdims=True)
            weights = jnp.exp2((scores - peak) * EXP2_SCALE)
            inverse = 1.0 / jnp.sum(weights, axis=0, keepdims=True)
            return (weights * inverse).astype(BF16), peak, inverse

        long_query = by_image(jnp.concatenate([query, extra], axis=0))
        scores = jnp.concatenate([dot(kn_ref[g, :, :depth], long_query[g]) for g in range(GROUP)], axis=1)
        probs, peak, inverse = by_lanes(softmax, scores)
        mixed = by_image(probs)
        mixed = jnp.concatenate([dot(v_ref[g], mixed[g]) for g in range(GROUP)], axis=1)
        attended = (mixed + query.astype(F32)).astype(BF16)
        store_pair(att_ref, pair, attended)

        def second_norm(k, x0, out):
            x1 = x0 + (out + wide_ref[11])
            hat, rstd = normalized(x1)
            return x1, (hat * wide_ref[12] + wide_ref[13]).astype(BF16), hat.astype(BF16), rstd

        x1, normed, hat_two, rstd_two = by_lanes(second_norm, load_pair(x0_ref, pair), dot(wprojt_ref[...], attended))
        store_pair(hat2_ref, pair, hat_two)
        act, slope = by_blocks(lambda part, hidden: gelu_parts(hidden + wb1_ref[part]), 64, dot(w1t_ref[...], normed))
        store_pair(act_ref, pair, act)
        store_pair(slope_ref, pair, slope)

        def third_norm(k, x1, out, mask):
            hat, rstd = normalized(x1 + (out + wide_ref[14]))
            return hat * mask, hat.astype(BF16), rstd

        kept, hat_three, rstd_three = by_lanes(third_norm, x1, dot(w2t_ref[...], act), pair_mask(pair, breadths, row_oks))
        store_pair(hat3_ref, pair, hat_three)
        stats = [peak, inverse, rstd, rstd_two, rstd_three, jnp.zeros((3, GROUP * PAIR), F32)]
        store_pair(stat_ref, pair, jnp.concatenate(stats, axis=0))
        for g, part in enumerate(by_image(kept)):
            pool_ref[g] += fold_lanes(part)
        return carry

    lax.fori_loop(0, pair_count(breadths), step, 0)


def call_forward(ext, row, q, top, bot, x0, kv, wts, offset):
    whole, per = specs()
    images, key_rows = q.shape[0], kv.shape[0]
    more = aug_rows(key_rows)
    shapes = [(rows, BF16) for rows in (DIM, DIM, more, DIM, MLP, MLP, DIM, DIM)]
    shapes = [((rows, TOKENS), kind) for rows, kind in shapes] + [((8, TOKENS), F32), ((DIM, 128), F32)]
    keys = key_rows * 32
    return pl.pallas_call(
        functools.partial(forward_kernel, offset=offset, key_rows=key_rows),
        grid_spec=pltpu.PrefetchScalarGridSpec(
            num_scalar_prefetch=2, grid=(images // GROUP,),
            in_specs=[
                per(DIM, PADDED), per(DIM, CANVAS_W), per(DIM, CANVAS_W), per(DIM, TOKENS),
                key_lanes(key_rows, 2 * DIM),
                whole(DIM, 64), whole(PAIRS, 8 * WIN + 8 * key_rows, DIM), whole(DIM, DIM), whole(DIM, MLP), whole(MLP, DIM)],
            out_specs=[per(*s) for s, _ in shapes],
            scratch_shapes=[
                pltpu.VMEM((DIM + more, keys), BF16), pltpu.VMEM((GROUP, keys, 256), BF16), pltpu.VMEM((GROUP, DIM, keys), BF16),
                pltpu.VMEM((GROUP, DIM, 1024), F32), pltpu.VMEM((GROUP, DIM, 1024), F32), pltpu.VMEM((DIM, GROUP * PAIR), F32),
                pltpu.VMEM((15, DIM, 128), F32), pltpu.VMEM((MLP, 128), F32),
                pltpu.VMEM((DIM, DIM), BF16), pltpu.VMEM((MLP, DIM), BF16), pltpu.VMEM((DIM, MLP), BF16)]),
        out_shape=[jax.ShapeDtypeStruct((images,) + s, t) for s, t in shapes],
        compiler_params=pltpu.CompilerParams(vmem_limit_bytes=VMEM_BYTES),
        cost_estimate=pl.CostEstimate(flops=images * 5_000_000_000, bytes_accessed=images * 4_000_000, transcendentals=0),
        name="forward",
    )(ext, row, q, top, bot, x0, kv, wts["vec"], wts["rw"], wts["wproj"], wts["w1"], wts["w2"])


def backward_kernel(ext_ref, row_ref, hat_ref, query_ref, terms_ref, att_ref, act_ref, slope_ref, hat2_ref, hat3_ref, stat_ref, q_ref, top_ref, bot_ref, kv_ref,
                    gvec_ref, vec_ref, rwt_ref, wproj_ref, w1_ref, w2_ref,
                    dx1_ref, dq_ref, up_ref, down_ref, dkv_ref, a2_ref, a1_ref, ap_ref, av_ref, ak_ref, ar_ref,
                    ka_ref, kn_ref, vn_ref, dp_ref, qtop_ref, qbot_ref, ru_ref, rd_ref, dk_ref, dv_ref, wide_ref, *, offset, key_rows):
    now = pl.program_id(0)
    steps = pl.num_programs(0) - 1
    images, heights, breadths, row_oks = group_extents(ext_ref, row_ref, offset, jnp.minimum(now, steps - 1))
    _, _, former, _ = group_extents(ext_ref, row_ref, offset, jnp.maximum(now - 1, 0))
    depth = DIM + aug_rows(key_rows)
    count = jnp.where(now < steps, pair_count(breadths), 0)
    former_count = pair_count(former)
    dp_now, dp_former = now & 1, (now & 1) ^ 1

    @pl.when(pl.program_id(0) == 0)
    def _():
        for ref in (a2_ref, a1_ref, ap_ref, av_ref, ak_ref, ar_ref, ru_ref, rd_ref):
            ref[...] = jnp.zeros_like(ref)
        fill_wide(wide_ref, vec_ref, list(range(15, 24)) + [3, 10, 11, 13])
        dp_ref[...] = jnp.zeros_like(dp_ref)

    for g in range(GROUP):
        values = key_tables(kv_ref, images[g], key_rows, heights[g], breadths[g], ka_ref.at[g], kn_ref.at[g])
        padded_values = jnp.concatenate([values, jnp.zeros((128 - DIM, values.shape[1]), F32)], axis=0)
        vn_ref[g] = jnp.transpose(padded_values).astype(BF16)
        spread_halo(qtop_ref.at[g], top_ref[g], 0)
        spread_halo(qbot_ref.at[g], bot_ref[g], 96)
    for ref in (dk_ref, dv_ref, dp_ref.at[dp_now]):
        ref[...] = jnp.zeros_like(ref)

    def step(pair, carry):
        ones = jnp.ones((16, GROUP * PAIR), BF16)
        stat = load_pair(stat_ref, pair)

        def third_back(k, hat, stat, mask):
            grad = norm_back(gvec_ref[k * 128 // PAIR] * mask, hat.astype(F32), stat[4:5], wide_ref[12])
            return grad, grad.astype(BF16)

        grad_x2, grad_mlp = by_lanes(third_back, load_pair(hat3_ref, pair), stat, pair_mask(pair, breadths, row_oks))
        act = load_pair(act_ref, pair)
        a2_ref[...] += dot_nt(jnp.concatenate([act, ones], axis=0), grad_mlp)
        (grad_hidden,) = by_blocks(
            lambda part, grad, slope: ((grad * slope.astype(F32)).astype(BF16),), 64, dot(w2_ref[...], grad_mlp), load_pair(slope_ref, pair))
        hat_two = load_pair(hat2_ref, pair)
        (normed,) = by_lanes(lambda k, hat: ((hat.astype(F32) * wide_ref[10] + wide_ref[11]).astype(BF16),), hat_two)
        a1_ref[...] += dot_nt(jnp.concatenate([normed, ones], axis=0), grad_hidden)

        def second_back(k, grad, hat, stat, grad_x2):
            hat = hat.astype(F32)
            total = grad_x2 + norm_back(grad, hat, stat[3:4], wide_ref[10])
            return total.astype(BF16), grad * hat

        grad_normed = dot(w1_ref[...], grad_hidden)
        grad_proj, scaled = by_lanes(second_back, grad_normed, hat_two, stat, grad_x2)
        av_ref[0] += fold_lanes(scaled)
        av_ref[1] += fold_lanes(grad_normed)
        store_pair(dx1_ref, pair, grad_proj)
        attended = load_pair(att_ref, pair)
        ap_ref[...] += dot_nt(jnp.concatenate([attended, ones], axis=0), grad_proj)
        grad_att = dot(wproj_ref[...], grad_proj)
        grad_att_low = grad_att.astype(BF16)
        hat = load_pair(hat_ref, pair)
        query = load_pair(query_ref, pair)
        long_query = by_image(jnp.concatenate([query, load_pair(terms_ref, pair)], axis=0))
        scores = jnp.concatenate([dot(kn_ref[g, :, :depth], long_query[g]) for g in range(GROUP)], axis=1)
        low = by_image(grad_att_low)
        grad_probs = jnp.concatenate([dot(vn_ref[g, :, :DIM], low[g]) for g in range(GROUP)], axis=1)

        def softmax_back(k, scores, grad_probs, stat):
            probs = jnp.exp2((scores - stat[0:1]) * EXP2_SCALE) * stat[1:2]
            inner = jnp.sum(probs * grad_probs, axis=0, keepdims=True)
            return probs.astype(BF16), (probs * (grad_probs - inner)).astype(BF16)

        probs, grad_scores = by_lanes(softmax_back, scores, grad_probs, stat)
        probs, grad_scores, queries = by_image(probs), by_image(grad_scores), by_image(query)
        back = []
        for g in range(GROUP):
            back.append(dot(ka_ref[g, : DIM + key_rows + 32, :], grad_scores[g]))
            dv_ref[g] += dot_nt(low[g], probs[g])
            dk_ref[g] += dot_nt(queries[g], grad_scores[g])
        back = jnp.concatenate(back, axis=1)
        (spread,) = by_lanes(lambda k, terms: (relative_spread(k, terms, key_rows),), back[DIM:])
        ar_ref[pair] += dot_nt(spread, query)

        def query_back(k, grad_att, back, far, hat, stat):
            grad = grad_att + back * SCALE + far
            hat = hat.astype(F32)
            return norm_back(grad, hat, stat[2:3], wide_ref[9]), grad * hat, grad

        grad_pre, scaled, grad = by_lanes(query_back, grad_att, back[:DIM], dot(rwt_ref[pair], spread), hat, stat)
        av_ref[2] += fold_lanes(scaled)
        av_ref[3] += fold_lanes(grad)
        store_pair(dp_ref.at[dp_now], pair, grad_pre.astype(BF16), 256)
        return carry

    def pool_step(pair, carry):
        for group in range(0, DIM, 16):
            part = slice(group, group + 16)
            taps = [wide_ref[k, part] for k in range(9)]
            grads = [None] * 9
            for g in range(GROUP):
                window = dp_ref[dp_former, g, part, pl.ds(pl.multiple_of(pair * PAIR, 128), PAIR + 512)]
                for tile in range(2):
                    base = pair * PAIR + 256 * tile
                    halo = pl.ds(pl.multiple_of((2 * pair + tile) * 128, 128), 128)
                    query = [q_ref[g, part, pl.ds(pl.multiple_of(base + 256 + 128 * side, 128), 128)] for side in range(2)]
                    above = rows_down(query[0], query[1], qtop_ref[g, part, halo])
                    under = rows_up(query[0], query[1], qbot_ref[g, part, halo])
                    sums = []
                    for side in range(2):
                        left, here, right = col_shifts(window, 256 + 256 * tile + 128 * side)
                        shifts = (right, here, left)
                        sums.append([sum(taps[3 * r + c] * shifts[c] for c in range(3)) for r in range(3)])
                        for r, rows in enumerate((above[side], query[side], under[side])):
                            rows = rows.astype(F32)
                            for c in range(3):
                                term = shifts[c] * rows
                                grads[3 * r + c] = term if grads[3 * r + c] is None else grads[3 * r + c] + term
                    zero = jnp.zeros((16, 128), F32)
                    up = rows_up(sums[0][0], sums[1][0], zero)
                    down = rows_down(sums[0][2], sums[1][2], zero)
                    for side in range(2):
                        lanes = pl.ds(pl.multiple_of(base + 128 * side, 128), 128)
                        dq_ref[g, part, lanes] = (sums[side][1] + up[side] + down[side]).astype(BF16)
                    ru_ref[g, part, halo] = up[2]
                    rd_ref[g, part, halo] = down[2]
            for k in range(9):
                ak_ref[k, part] += grads[k]
        return carry

    def pool_idle(pair, carry):
        for ref in (ru_ref, rd_ref):
            for g in range(GROUP):
                ref[g, :, pl.ds(pl.multiple_of(pair * 256, 128), 256)] = jnp.zeros((DIM, 256), F32)
        return carry

    lax.fori_loop(0, count, lambda pair, carry: step(pair, pool_step(pair, carry)), 0)
    lax.fori_loop(count, former_count, pool_step, 0)
    lax.fori_loop(former_count, PAIRS, pool_idle, 0)

    @pl.when(now < steps)
    def _():
        lane = lane_ids(128, 2 * DIM)
        for g in range(GROUP):
            for i in range(key_rows):
                block = slice(128 * (i // 4), 128 * (i // 4) + 128)
                value = jnp.concatenate([dk_ref[g, :, block] * SCALE, dv_ref[g, :, block]], axis=0)
                value = pltpu.roll(value, (4 + (images[g] & 3) - i % 4) * 32 & 127, 1)
                slot = reverse_bits(jnp.bitwise_xor(row_ref[0], i), key_rows)
                dkv_ref[slot] = jnp.where((lane >> 5) == (images[g] & 3), value, dkv_ref[slot])

    for g in range(GROUP):
        up_ref[g] = gather_halo(ru_ref.at[g], 96).astype(BF16)
        down_ref[g] = gather_halo(rd_ref.at[g], 0).astype(BF16)


def call_backward(ext, row, saved, q, top, bot, kv, gvec, wts, offset):
    whole, _ = specs()
    images, key_rows = q.shape[0], kv.shape[0]
    more = aug_rows(key_rows)
    keys = key_rows * 32
    window = 8 * WIN + 8 * key_rows
    steps = images // GROUP
    now = lambda *shape: pl.BlockSpec((GROUP,) + shape, lambda i, *_: (jnp.minimum(i, steps - 1),) + (0,) * len(shape))
    former = lambda *shape: pl.BlockSpec((GROUP,) + shape, lambda i, *_: (jnp.maximum(i - 1, 0),) + (0,) * len(shape))
    heads = pl.BlockSpec((key_rows, 2 * DIM, 128), lambda i, *_: (0, 0, jnp.minimum(i, steps - 1) * GROUP >> 2))
    shapes = [(DIM, TOKENS), (DIM, TOKENS), (DIM, CANVAS_W), (DIM, CANVAS_W)]
    sums = [(MLP + 16, DIM), (DIM + 16, MLP), (DIM + 16, DIM), (4, DIM, 128), (9, DIM, 128), (PAIRS, window, DIM)]
    return pl.pallas_call(
        functools.partial(backward_kernel, offset=offset, key_rows=key_rows),
        grid_spec=pltpu.PrefetchScalarGridSpec(
            num_scalar_prefetch=2, grid=(steps + 1,),
            in_specs=[now(rows, TOKENS) for rows in (DIM, DIM, more, DIM, MLP, MLP, DIM, DIM, 8)] + [
                former(DIM, PADDED), former(DIM, CANVAS_W), former(DIM, CANVAS_W), heads, now(DIM, 1), whole(DIM, 64), whole(PAIRS, DIM, window),
                whole(DIM, DIM), whole(DIM, MLP), whole(MLP, DIM)],
            out_specs=[now(*shapes[0])] + [former(*s) for s in shapes[1:]] + [heads] + [whole(*s) for s in sums],
            scratch_shapes=[
                pltpu.VMEM((GROUP, DIM + more, keys), BF16), pltpu.VMEM((GROUP, keys, 256), BF16), pltpu.VMEM((GROUP, keys, 128), BF16),
                pltpu.VMEM((2, GROUP, DIM, PADDED), BF16)] + [pltpu.VMEM((GROUP, DIM, 1024), BF16)] * 2
            + [pltpu.VMEM((GROUP, DIM, 1024), F32)] * 2 + [pltpu.VMEM((GROUP, DIM, keys), F32)] * 2 + [pltpu.VMEM((13, DIM, 128), F32)]),
        out_shape=[jax.ShapeDtypeStruct((images,) + s, BF16) for s in shapes]
        + [jax.ShapeDtypeStruct((key_rows, 2 * DIM, 32 * images), F32)] + [jax.ShapeDtypeStruct(s, F32) for s in sums],
        compiler_params=pltpu.CompilerParams(vmem_limit_bytes=VMEM_BYTES),
        cost_estimate=pl.CostEstimate(flops=images * 12_000_000_000, bytes_accessed=images * 6_000_000, transcendentals=0),
        name="backward",
    )(ext, row, *saved, q, top, bot, kv, gvec, wts["vec"], wts["rw_t"], wts["wproj"], wts["w1"], wts["w2"])


def embed_back_kernel(ext_ref, row_ref, patch_ref, dq_ref, dx1_ref, rtop_ref, rbot_ref, nsel_ref, kvt_ref, pre_ref, under_ref,
                      wp_ref, vec_ref, wqkv_ref, tapt_ref,
                      aq_ref, akv_ref, apatch_ref, av_ref, ak_ref, dn_ref, rim_ref, wide_ref, kexp_ref, *, offset):
    images, heights, breadths, row_oks = group_extents(ext_ref, row_ref, offset)

    @pl.when(pl.program_id(0) == 0)
    def _():
        for ref in (aq_ref, akv_ref, apatch_ref, av_ref, ak_ref, dn_ref, rim_ref):
            ref[...] = jnp.zeros_like(ref)
        fill_wide(wide_ref, vec_ref, [0, 1, 2])
        fill_taps(kexp_ref, vec_ref)

    lane = lane_ids(128, 2 * DIM)

    def thrice(value, image):
        block = jnp.where((lane >> 5) == 1, take_lanes(value, image, 1), take_lanes(value, image, 0))
        block = jnp.where((lane >> 5) == 2, take_lanes(value, image, 2), block)
        return jnp.where((lane >> 5) == 3, 0.0, block)

    grad_taps = []
    for g in range(GROUP):
        own = thrice(pre_ref[...], images[g])
        spread = jnp.concatenate([thrice(under_ref[...].astype(F32), images[g]), own, own], axis=1)
        ak_ref[...] += kvt_ref[g].astype(F32) * spread
        grad_taps.append((spread * kexp_ref[...]).astype(BF16))
    grad_taps = jnp.concatenate(grad_taps, axis=1)
    nsel = jnp.concatenate([nsel_ref[g] for g in range(GROUP)], axis=1)
    akv_ref[...] += dot_nt(jnp.concatenate([nsel, jnp.ones((16, 384 * GROUP), BF16)], axis=0), grad_taps)
    grad_sel = dot(wqkv_ref[:, DIM : 3 * DIM], grad_taps)
    parts = [grad_sel.astype(BF16)[:, 128 * k : 128 * k + 128] for k in range(3 * GROUP)]
    lines = dot(jnp.concatenate(parts, axis=0), tapt_ref[...])
    for g in range(GROUP):
        for k, start in enumerate((224, 0, 32)):
            first = DIM * (3 * g + k)
            line = lines[first : first + DIM]
            for tile in range(TILES):
                dn_ref[g, :, 256 * tile + start : 256 * tile + start + 32] = line[:, 32 * tile : 32 * tile + 32]
        for halo_ref, start in ((rtop_ref, 0), (rbot_ref, 224)):
            line = halo_ref[g].astype(F32)
            for tile in range(TILES):
                rim_ref[g, :, 256 * tile + start : 256 * tile + start + 32] = line[:, 32 * tile : 32 * tile + 32]

    def step(pair, carry):
        mask = pair_mask(pair, breadths, row_oks)
        patches = load_pair(patch_ref, pair)

        def first_norm(k, embed, mask, grad, rim):
            hat, rstd = normalized((embed + wide_ref[0]) * mask)
            return hat, rstd, (hat * wide_ref[1] + wide_ref[2]).astype(BF16), (grad.astype(F32) + rim).astype(BF16)

        hat, rstd, normed, grad_q = by_lanes(first_norm, dot(wp_ref[...], patches), mask, load_pair(dq_ref, pair), load_pair(rim_ref, pair))
        aq_ref[...] += dot_nt(jnp.concatenate([normed, jnp.ones((16, GROUP * PAIR), BF16)], axis=0), grad_q)

        def first_back(k, out, extra, hat, rstd, mask, dx1):
            grad = out + extra
            total = (dx1.astype(F32) + norm_back(grad, hat, rstd, wide_ref[1])) * mask
            return total.astype(BF16), total, grad * hat, grad

        low, total, scaled, grad = by_lanes(
            first_back, dot(wqkv_ref[:, 0:DIM], grad_q), load_pair(dn_ref, pair), hat, rstd, mask, load_pair(dx1_ref, pair))
        av_ref[0] += fold_lanes(total)
        av_ref[1] += fold_lanes(scaled)
        av_ref[2] += fold_lanes(grad)
        apatch_ref[...] += dot_nt(low, patches)
        return carry

    lax.fori_loop(0, pair_count(breadths), step, 0)


def call_embed_back(ext, row, patches, dq, dx1, rtop, rbot, nsel, kvt, pre, under, consts, wts, offset):
    whole, per = specs()
    images = dq.shape[0]
    sums = [(DIM + 16, DIM), (DIM + 16, 2 * DIM), (DIM, PATCH_ROWS), (3, DIM, 128), (2 * DIM, 384)]
    return pl.pallas_call(
        functools.partial(embed_back_kernel, offset=offset),
        grid_spec=pltpu.PrefetchScalarGridSpec(
            num_scalar_prefetch=2, grid=(images // GROUP,),
            in_specs=[
                per(PATCH_ROWS, TOKENS), per(DIM, TOKENS), per(DIM, TOKENS), per(DIM, CANVAS_W), per(DIM, CANVAS_W),
                per(DIM, 384), per(2 * DIM, 384), key_lanes(2 * DIM), key_lanes(2 * DIM),
                whole(DIM, PATCH_ROWS), whole(DIM, 64), whole(DIM, 3 * DIM), whole(128, CANVAS_W)],
            out_specs=[whole(*s) for s in sums],
            scratch_shapes=[pltpu.VMEM((GROUP, DIM, TOKENS), F32)] * 2 + [pltpu.VMEM((3, DIM, 128), F32), pltpu.VMEM((2 * DIM, 384), F32)]),
        out_shape=[jax.ShapeDtypeStruct(s, F32) for s in sums],
        compiler_params=pltpu.CompilerParams(vmem_limit_bytes=VMEM_BYTES),
        cost_estimate=pl.CostEstimate(flops=images * 3_000_000_000, bytes_accessed=images * 3_000_000, transcendentals=0),
        name="embed_back",
    )(ext, row, patches, dq, dx1, rtop, rbot, nsel, kvt, pre, under, wts["wp"], wts["vec"], wts["wqkv"], consts["tap_t"])


def bit_count(size):
    return size.bit_length() - 1


def swap(value, axis, bit):
    size = lax.axis_size(axis)
    return lax.ppermute(value, axis, [(i, i ^ (1 << bit)) for i in range(size)])


def shifted(value, axis, step):
    size = lax.axis_size(axis)
    pairs = [(i, i + step) for i in range(size) if 0 <= i + step < size]
    return lax.ppermute(value, axis, pairs)


def summed(value, axis):
    for bit in range(bit_count(lax.axis_size(axis))):
        value = value + swap(value, axis, bit)
    return value


def scatter_step(value, axis, bit):
    half = value.shape[0] // 2
    return value[:half] + swap(value[half:].astype(BF16), axis, bit).astype(F32)


def together(*values):
    return lax.optimization_barrier(values)


def gather_params(value):
    dims = []
    for axis in ("img", "row"):
        index = lax.axis_index(axis)
        for bit in reversed(range(bit_count(lax.axis_size(axis)))):
            other = swap(value, axis, bit)
            mine_second = (index >> bit) & 1 == 1
            value = jnp.stack([jnp.where(mine_second, other, value), jnp.where(mine_second, value, other)])
            dims.append((axis, bit))
    dims = dims[::-1]
    wanted = [("img", b) for b in reversed(range(bit_count(lax.axis_size("img"))))]
    wanted += [("row", b) for b in reversed(range(bit_count(lax.axis_size("row"))))]
    order = [dims.index(d) for d in wanted]
    value = jnp.transpose(value, order + [value.ndim - 2, value.ndim - 1])
    return value.reshape(-1)


def sum_grads(flat, extra):
    rows, imgs = lax.axis_size("row"), lax.axis_size("img")
    bits = bit_count(rows)
    leaf = flat.shape[0] // (rows * imgs)
    value = flat.reshape((imgs,) + (2,) * bits + (leaf // 128, 128))
    index = lax.axis_index("row")
    for bit in range(bits):
        place = value.ndim - 3
        own = (index >> bit) & 1
        keep = lax.dynamic_index_in_dim(value, own, place, False)
        send = lax.dynamic_index_in_dim(value, 1 - own, place, False)
        value = keep + swap(send, "row", bit)
    value = jnp.concatenate([value.reshape(imgs * leaf // 128, 128), jnp.full((8, 128), extra)], axis=0)
    value = summed(value, "img")
    return value[:-8], value[-1, 0]


def segment_list(canvas_rows, canvas_cols):
    return [
        ("w_patch", (3 * PATCH * PATCH, DIM)),
        ("w_qkv", (DIM, 3 * DIM)),
        ("w_proj", (DIM, DIM)),
        ("w_fc1", (DIM, MLP)),
        ("w_fc2", (MLP, DIM)),
        ("w_head", (DIM, CLASSES)),
        ("rel_rows", (2 * canvas_rows - 8, DIM)),
        ("rel_cols", (2 * canvas_cols - 8, DIM)),
        ("small", (49, DIM)),
        ("b_head", (CLASSES,)),
    ]


def unpack(flat_vec, segments):
    pieces = {}
    position = 0
    for seg_name, seg_shape in segments:
        entries = int(np.prod(seg_shape))
        pieces[seg_name] = flat_vec[position : position + entries].reshape(seg_shape)
        position += entries
    return pieces


def patch_rows(weight):
    taps = jnp.pad(weight.reshape(PATCH, PATCH, 3, DIM), ((0, 1), (0, 0), (0, 1), (0, 0)))
    parts = []
    for piece in (taps[:, 3:7], jnp.pad(taps[:, 0:3], ((0, 0), (1, 0), (0, 0), (0, 0)))):
        parts.append(jnp.transpose(piece.reshape(2, 4, 4, 4, DIM), (0, 2, 1, 3, 4)).reshape(128, DIM))
    return jnp.concatenate(parts, axis=0)


def patch_rows_back(grad):
    taps = jnp.transpose(grad.T.reshape(2, 2, 4, 4, 4, DIM), (0, 1, 3, 2, 4, 5)).reshape(2, 8, 4, 4, DIM)
    return jnp.concatenate([taps[1, :PATCH, 1:, :3], taps[0, :PATCH, :, :3]], axis=1).reshape(3 * PATCH * PATCH, DIM)


def relative_windows(rel_rows, rel_cols, row_index, key_rows):
    offsets = jnp.flip(rel_cols.reshape(-1, 8, DIM), 0)
    offsets = jnp.transpose(jnp.pad(offsets, ((0, 1), (0, 0), (0, 0))), (1, 0, 2))
    blocks = rel_rows.reshape(2 * key_rows - 1, 8, DIM)
    rows = jnp.transpose(jnp.flip(lax.dynamic_slice_in_dim(blocks, row_index, key_rows, 0), 0), (1, 0, 2))
    rows = rows.reshape(8 * key_rows, DIM)
    windows = []
    for pair in range(PAIRS):
        cols = offsets[:, 24 - 8 * pair : 24 - 8 * pair + WIN].reshape(8 * WIN, DIM)
        windows.append(jnp.concatenate([cols, rows], axis=0))
    return jnp.stack(windows)


def relative_windows_back(grad, row_index, key_rows):
    cols = grad[:, : 8 * WIN].reshape(PAIRS, 8, WIN, DIM)
    total = 0.0
    for pair in range(PAIRS):
        start = 24 - 8 * pair
        total = total + jnp.pad(cols[pair], ((0, 0), (start, 64 - start - WIN), (0, 0)))
    rel_cols = jnp.flip(jnp.transpose(total[:, :63], (1, 0, 2)), 0).reshape(-1, DIM)
    rows = jnp.sum(grad[:, 8 * WIN :], axis=0).reshape(8, key_rows, DIM)
    rows = jnp.flip(jnp.transpose(rows, (1, 0, 2)), 0)
    blocks = lax.dynamic_update_slice_in_dim(jnp.zeros((2 * key_rows - 1, 8, DIM), F32), rows, row_index, 0)
    return blocks.reshape(-1, DIM), rel_cols


def tap_keep():
    keep = np.ones((3, 4, 32), np.float32)
    keep[:, 3] = 0.0
    keep[:, 0, 0] = 0.0
    return keep


def prepare(weights, row_index, key_rows):
    small = weights["small"]
    vec = jnp.pad(small.astype(F32).T, ((0, 0), (0, 15)))
    windows = relative_windows(weights["rel_rows"], weights["rel_cols"], row_index, key_rows)
    return {
        "vec": vec,
        "wp": patch_rows(weights["w_patch"]).T,
        "wqkv": weights["w_qkv"],
        "wqkv_t": weights["w_qkv"].T,
        "wproj": weights["w_proj"],
        "w1": weights["w_fc1"],
        "w2": weights["w_fc2"],
        "rw": windows,
        "rw_t": jnp.transpose(windows, (0, 2, 1)),
    }


def image_loss(pooled, head_w, head_b, log_teacher, labels, image_total):
    logits = jnp.dot(pooled, head_w, precision=HIGHEST_PREC) + head_b
    log_student = jax.nn.log_softmax(logits, axis=-1)
    onehot = (jnp.arange(CLASSES)[None, :] == labels[:, None]).astype(F32)
    per_image = jnp.sum(jnp.exp(log_teacher) * (log_teacher - log_student), axis=-1) - jnp.sum(onehot * log_student, axis=-1)
    return jnp.sum(per_image) / image_total


def body(flat_params, first_moment, second_moment, pixels, extents, labels, teacher):
    key_rows = lax.axis_size("row")
    row_index = lax.axis_index("row")
    row_lead = row_index == 0
    segments = segment_list(ROWS * key_rows, CANVAS_W)
    full_params = gather_params(flat_params.astype(BF16).reshape(-1, 128))
    weights = unpack(full_params, segments)
    wts = prepare(weights, row_index, key_rows)
    tap = tap_matrix()
    consts = {"perm": jnp.asarray(deinterleave_matrix(), BF16), "tap": jnp.asarray(tap, BF16), "tap_t": jnp.asarray(tap.T, BF16)}
    vectors = weights["small"][27:42].astype(F32)
    row = row_index.astype(jnp.int32).reshape(1)
    images = pixels.shape[0]
    parts = 1
    size = images // parts
    image_total = images * lax.axis_size("img") * 1.0
    head_w = weights["w_head"].astype(F32)
    head_b = weights["b_head"].astype(F32)

    ids = jnp.arange(images)
    widths = extents[:, 1]
    ahead = (widths[None, :] > widths[:, None]) | ((widths[None, :] == widths[:, None]) & (ids[None, :] < ids[:, None]))
    places = jnp.sum(ahead.astype(jnp.int32), axis=1)
    chosen = places[None, :] == ids[:, None]
    order = jnp.sum(jnp.where(chosen, ids[None, :], 0), axis=1)
    ext = jnp.sum(jnp.where(chosen[:, :, None], extents[None], 0), axis=1)

    log_teacher = jax.nn.log_softmax(teacher, axis=-1)
    pixel_view = jnp.transpose(pixels, (0, 2, 3, 1, 4))
    saved = []
    for part in range(parts):
        first, last, nsel, kvt, below, own = call_edge(ext, row, order, pixel_view, consts, wts, size, part * size)
        got = shifted(below, "row", 1)
        kv = lax.all_gather(call_pool_norm(own, got, wts["vec"]), "row", axis=0)
        top = shifted(last, "row", 1)
        bot = shifted(first, "row", -1)
        names = sorted(wts)
        after, log_teacher, *values = together(ext, log_teacher, *[wts[name] for name in names])
        wts = dict(zip(names, values))
        patches, x0, q = call_embed(after, row, order, pixel_view, consts, wts, size, part * size)
        saved.append(dict(patches=patches, x0=x0, q=q, top=top, bot=bot, nsel=nsel, kvt=kvt, own=own, got=got, kv=kv))
    for part in range(parts):
        s = saved[part]
        s["fwd"] = call_forward(ext, row, s["q"], s["top"], s["bot"], s["x0"], s["kv"], wts, part * size)
    total = {}

    def add(name, value):
        total[name] = total[name] + value if name in total else value

    sorted_local = jnp.sum(jnp.concatenate([s["fwd"][-1] for s in saved], axis=0), axis=-1)
    local = jnp.sum(jnp.where(chosen[:, :, None], sorted_local[:, None, :], 0.0), axis=0)
    everywhere = summed(local, "row")
    counts = (extents[:, 0] * extents[:, 1]).astype(F32)[:, None]
    pooled = (everywhere * vectors[13] + counts * vectors[14]) / counts

    def loss_of(pooled_now, w, b):
        return image_loss(pooled_now, w, b, log_teacher, labels, image_total)

    loss_value, loss_back = jax.vjp(loss_of, pooled, head_w, head_b)
    grad_pooled, total["w_head"], total["b_head"] = loss_back(jnp.ones_like(loss_value))
    gvec = grad_pooled / counts
    local_count = jnp.where(row_index * ROWS < extents[:, 0], ROWS * extents[:, 1], 0).astype(F32)[:, None]
    total["g_three"] = jnp.sum(gvec * local, axis=0)
    total["b_three"] = jnp.sum(gvec * local_count, axis=0)
    gvec = jnp.sum(jnp.where(chosen[:, :, None], gvec[None], 0.0), axis=1)[:, :, None]
    for part in range(parts):
        s = saved[part]
        s["bwd"] = call_backward(ext, row, s["fwd"][:-1], s["q"], s["top"], s["bot"], s["kv"], gvec[part * size : part * size + size], wts, part * size)
    for part in range(parts):
        s = saved[part]
        dx1, dq, up, down, dkv, *sums = s["bwd"]
        for bit in range(bit_count(key_rows)):
            if bit == 1:
                dkv, up, down = together(dkv, up, down)
                rtop = shifted(down, "row", 1)
                rbot = shifted(up, "row", -1)
            dkv = scatter_step(dkv, "row", bit)
            if bit == 1:
                dkv, *sums = together(dkv, *sums)
        for name, value in zip(("a2", "a1", "ap", "av", "ak", "ar"), sums):
            add(name, value)
        grad_kv = dkv[0]
        pre, pool_sums = call_pool_back(s["own"], s["got"], grad_kv, wts["vec"])
        add("pool_sums", pool_sums)
        under = shifted(pre.astype(BF16), "row", -1)
        aq, akv, apatch, av1, akt = call_embed_back(
            ext, row, s["patches"], dq, dx1, rtop, rbot, s["nsel"], s["kvt"], pre, under, consts, wts, part * size)
        for name, value in (("aq", aq), ("akv", akv), ("apatch", apatch), ("av1", av1), ("akt", akt)):
            add(name, value)

    t = total
    lead = jnp.where(row_lead, 1.0, 0.0)
    av, av1 = jnp.sum(t["av"], axis=-1), jnp.sum(t["av1"], axis=-1)
    pool_sums = jnp.sum(t["pool_sums"], axis=-1)
    rel_rows, rel_cols = relative_windows_back(t["ar"], row_index, key_rows)
    taps = jnp.sum((t["akt"].reshape(2, DIM, 3, 4, 32) * tap_keep())[:, :, :, :3], axis=-1)
    kernels = jnp.concatenate([jnp.sum(t["ak"], axis=-1), jnp.transpose(taps, (0, 2, 3, 1)).reshape(18, DIM)], axis=0)
    grad_vectors = jnp.stack([
        av1[0], av1[1], av1[2], av[2], av[3], pool_sums[0], pool_sums[1], pool_sums[2], pool_sums[3],
        t["ap"][DIM], av[0], av[1], t["a2"][MLP], t["g_three"], t["b_three"]])
    pieces = [
        patch_rows_back(t["apatch"]),
        jnp.concatenate([t["aq"][:DIM], t["akv"][:DIM]], axis=1),
        t["ap"][:DIM],
        t["a1"][:DIM],
        t["a2"][:MLP],
        t["w_head"] * lead,
        rel_rows,
        rel_cols,
        kernels,
        grad_vectors,
        t["aq"][DIM],
        t["akv"][DIM],
        t["a1"][DIM],
        t["b_head"] * lead,
    ]
    joined = jnp.concatenate([piece.reshape(-1) for piece in pieces])
    grad_flat = jnp.pad(joined, (0, full_params.shape[0] - joined.shape[0]))
    shares, loss_sum = sum_grads(grad_flat, loss_value)
    norm_sq = summed(jnp.sum(shares * shares), "row")
    lines = flat_params.shape[0] // 128
    grad_shard = lax.dynamic_slice_in_dim(shares, lax.axis_index("img") * lines, lines, 0).reshape(-1)
    grad_norm = jnp.sqrt(norm_sq)
    clip_factor = jnp.minimum(1.0, CLIP_NORM / (grad_norm + 1e-06))
    clipped = grad_shard * clip_factor
    moment_one = BETA_FIRST * first_moment + (1.0 - BETA_FIRST) * clipped
    moment_two = BETA_SECOND * second_moment + (1.0 - BETA_SECOND) * clipped * clipped
    fix_one = 1.0 - BETA_FIRST**STEP
    fix_two = 1.0 - BETA_SECOND**STEP
    update = moment_one / fix_one / (jnp.sqrt(moment_two / fix_two) + ADAM_EPS) + WEIGHT_DECAY * flat_params
    new_params = flat_params - LEARN_RATE * update
    return (new_params, moment_one, moment_two, grad_norm, loss_sum)


def solution(mesh):
    placed = (
        P(("img", "row")),
        P(("img", "row")),
        P(("img", "row")),
        P("img", "row", None, None, None),
        P("img", None),
        P("img"),
        P("img", None),
    )
    return jax.shard_map(
        body,
        mesh=mesh,
        in_specs=placed,
        out_specs=(P(("img", "row")), P(("img", "row")), P(("img", "row")), P(), P()),
        check_vma=False,
    )
```

```python
import functools

import jax
import jax.numpy as jnp
import numpy as np
from jax import lax
from jax.experimental import pallas as pl
from jax.experimental.pallas import tpu as pltpu
from jax.sharding import PartitionSpec as P

DIM = 96
MLP = 384
CLASSES = 1000
PATCH = 7
ROWS = 8
STEP = 7
CANVAS_W = 256

HIGHEST_PREC = lax.Precision.HIGHEST
CLIP_NORM = 0.02
LEARN_RATE = 0.05
WEIGHT_DECAY = 0.05
BETA_FIRST = 0.5
BETA_SECOND = 0.5
ADAM_EPS = 1e-08
NORM_EPS = 1e-06
NEG_FILL = -1e30

F32 = jnp.float32
BF16 = jnp.bfloat16
SCALE = DIM ** (-0.5)
EXP2_SCALE = SCALE * 1.4426950408889634

TOKENS = ROWS * CANVAS_W
PAIR = 512
PAIRS = TOKENS // PAIR
TILES = CANVAS_W // 32
GROUP = 2
WIDE = 4
PADDED = TOKENS + 512
WIN = 40
PATCH_ROWS = 256
VMEM_BYTES = 56 * 1024 * 1024


def deinterleave_matrix():
    out = np.zeros((4, 128, 4, 4, 32), np.float32)
    for row in range(4):
        for phase in range(4):
            for col in range(32):
                out[row, 4 * col + phase, phase, row, col] = 1.0
    return out.reshape(512, 512)


def tap_matrix():
    out = np.zeros((CANVAS_W, 128), np.float32)
    for tap in range(3):
        for key in range(32):
            col = 8 * key + tap - 1
            if col >= 0:
                out[col, tap * 32 + key] = 1.0
    return out


def dot(a, b):
    return jnp.dot(a, b, preferred_element_type=F32)


def dot_nt(a, b):
    return lax.dot_general(a, b, (((1,), (1,)), ((), ())), preferred_element_type=F32)


def normalized(x):
    mean = jnp.sum(x, axis=0, keepdims=True) * (1.0 / DIM)
    centered = x - mean
    var = jnp.sum(centered * centered, axis=0, keepdims=True) * (1.0 / DIM)
    rstd = lax.rsqrt(var + NORM_EPS)
    return centered * rstd, rstd


def norm_back(grad, hat, rstd, gain):
    inner = grad * gain
    mean_one = jnp.sum(inner, axis=0, keepdims=True) * (1.0 / DIM)
    mean_two = jnp.sum(inner * hat, axis=0, keepdims=True) * (1.0 / DIM)
    return rstd * (inner - mean_one - hat * mean_two)


def by_lanes(fn, *arrays):
    parts = [fn(k, *(a[:, 128 * k : 128 * k + 128] for a in arrays)) for k in range(arrays[0].shape[1] // 128)]
    return tuple(jnp.concatenate(column, axis=1) for column in zip(*parts))


def by_blocks(fn, height, *arrays):
    rows = []
    for top in range(0, arrays[0].shape[0], height):
        rows.append(by_lanes(lambda k, *block: fn(slice(top, top + height), *block), *(a[top : top + height] for a in arrays)))
    return tuple(jnp.concatenate(column, axis=0) for column in zip(*rows))


def fold_lanes(x):
    total = x[:, 0:128]
    for k in range(1, x.shape[1] // 128):
        total = total + x[:, 128 * k : 128 * k + 128]
    return total


def place_of(index):
    return index + 27 if index < 15 else index - 15 if index < 42 else index


def column(vec_ref, index):
    place = place_of(index)
    return vec_ref[:, place : place + 1]


def fill_wide(wide_ref, vec_ref, indices):
    for k, index in enumerate(indices):
        wide_ref[k] = jnp.broadcast_to(column(vec_ref, index), (DIM, 128))


def fill_taps(taps_ref, vec_ref):
    lane = lane_ids(128, DIM)
    for member in range(2):
        for r in range(3):
            block = jnp.zeros((DIM, 128), F32)
            for c in range(3):
                block = jnp.where((lane >> 5) == c, column(vec_ref, 24 + 9 * member + 3 * r + c), block)
            taps_ref[DIM * member : DIM * member + DIM, 128 * r : 128 * r + 128] = jnp.where(lane == 0, 0.0, block)


def fill_bias(bias_ref, vec_ref):
    for k in range(MLP // DIM):
        bias_ref[DIM * k : DIM * k + DIM] = jnp.broadcast_to(vec_ref[:, 45 + k : 46 + k], (DIM, 128))


def fill_transpose(dst_ref, src_ref):
    rows, cols = src_ref.shape
    value = src_ref[...].astype(F32)
    value = jnp.pad(value, ((0, -rows % 128), (0, -cols % 128)))
    dst_ref[...] = jnp.transpose(value)[:cols, :rows].astype(BF16)


def wide(wide_ref, k, width=PAIR):
    return jnp.concatenate([wide_ref[k]] * (width // 128), axis=1)


def lane_ids(width, rows=1):
    return lax.broadcasted_iota(jnp.int32, (rows, width), 1)


def pair_mask(pair, breadths, row_oks):
    lane = lane_ids(PAIR)
    col = pair * 64 + (lane >> 8) * 32 + (lane & 31)
    return jnp.concatenate([jnp.where((col < w) & ok, 1.0, 0.0).astype(F32) for w, ok in zip(breadths, row_oks)], axis=1)


def pair_lanes(pair, base=0):
    return pl.ds(pl.multiple_of(pair * PAIR + base, 128), PAIR)


def load_pair(ref, pair):
    lanes = pair_lanes(pair)
    return jnp.concatenate([ref[g, :, lanes] for g in range(ref.shape[0])], axis=1)


def store_pair(ref, pair, value, base=0):
    for g in range(value.shape[1] // PAIR):
        ref[g, :, pair_lanes(pair, base)] = value[:, PAIR * g : PAIR * g + PAIR]


def by_image(value):
    return [value[:, PAIR * g : PAIR * g + PAIR] for g in range(GROUP)]


def pair_count(breadths):
    widest = breadths[0]
    for breadth in breadths[1:]:
        widest = jnp.maximum(widest, breadth)
    return jnp.minimum((widest >> 6) + 1, PAIRS)


def group_extents(ext_ref, row_ref, offset, group=None, size=GROUP):
    group = pl.program_id(0) if group is None else group
    images = [group * size + g for g in range(size)]
    heights = [ext_ref[offset + image, 0] for image in images]
    breadths = [ext_ref[offset + image, 1] for image in images]
    return images, heights, breadths, [row_ref[0] * ROWS < height for height in heights]


def col_shifts(window, base):
    lane = lane_ids(128, window.shape[0])
    here = window[:, base : base + 128]
    before = window[:, base - 256 : base - 128]
    after = window[:, base + 256 : base + 384]
    left = jnp.where((lane & 31) == 0, pltpu.roll(before, 97, 1), pltpu.roll(here, 1, 1))
    right = jnp.where((lane & 31) == 31, pltpu.roll(after, 31, 1), pltpu.roll(here, 127, 1))
    return left.astype(F32), here.astype(F32), right.astype(F32)


def rows_down(first, second, entering):
    lane = lane_ids(128, first.shape[0])
    a, b = pltpu.roll(first, 32, 1), pltpu.roll(second, 32, 1)
    return jnp.where(lane < 32, entering, a), jnp.where(lane < 32, a, b), b


def rows_up(first, second, entering):
    lane = lane_ids(128, first.shape[0])
    a, b = pltpu.roll(first, 96, 1), pltpu.roll(second, 96, 1)
    return jnp.where(lane >= 96, b, a), jnp.where(lane >= 96, entering, b), a


def spread_halo(dst_ref, halo, target):
    for tile in range(TILES):
        block = halo[:, 128 * (tile // 4) : 128 * (tile // 4) + 128]
        shift = (target - 32 * (tile % 4)) % 128
        dst_ref[:, 128 * tile : 128 * tile + 128] = pltpu.roll(block, shift, 1) if shift else block


def store_lanes(dst_ref, value, image):
    place = image & 3
    lane = lane_ids(128, value.shape[0])
    dst_ref[...] = jnp.where((lane >> 5) == place, pltpu.roll(value, place * 32, 1), dst_ref[...])


def take_lanes(value, image, target):
    return pltpu.roll(value, (4 + target - (image & 3)) * 32 & 127, 1)


def gather_halo(src_ref, target):
    lane = lane_ids(128, DIM)
    blocks = []
    for half in range(2):
        total = None
        for k in range(4):
            tile = 4 * half + k
            block = src_ref[:, 128 * tile : 128 * tile + 128]
            shift = (32 * k - target) % 128
            block = pltpu.roll(block, shift, 1) if shift else block
            total = block if total is None else jnp.where((lane >> 5) == k, block, total)
        blocks.append(total)
    return jnp.concatenate(blocks, axis=1)


def reverse_bits(value, count):
    result = 0
    for bit in range(count.bit_length() - 1):
        result = result * 2 + ((value >> bit) & 1)
    return result


def key_tables(kv_ref, image, key_rows, height, breadth, ka_ref, kn_ref):
    lane = lane_ids(128, 2 * DIM)
    blocks = []
    for i in range(0, key_rows, 4):
        block = take_lanes(kv_ref[i].astype(F32), image, 0)
        for k in range(1, 4):
            block = jnp.where((lane >> 5) == k, take_lanes(kv_ref[i + k].astype(F32), image, k), block)
        blocks.append(block)
    both = jnp.concatenate(blocks, axis=1)
    total = key_rows * 32
    more = aug_rows(key_rows)
    rank = lax.broadcasted_iota(jnp.int32, (more, total), 0)
    key = lax.broadcasted_iota(jnp.int32, (more, total), 1)
    key_r, key_c = key >> 5, key & 31
    half = key_rows + 32
    low = rank >= half
    rank_in = jnp.where(low, rank - half, rank)
    hit = rank_in == jnp.where(rank_in < key_rows, key_r, key_c + key_rows)
    invalid = (key_r * ROWS >= height) | (key_c * ROWS >= breadth)
    table = jnp.where(rank < 2 * half, jnp.where(hit, 1.0, 0.0), 0.0)
    table = jnp.where((rank == 2 * half) & invalid, NEG_FILL, table)
    full = jnp.concatenate([both[:DIM], table, jnp.zeros((256 - DIM - more, total), F32)], axis=0)
    ka_ref[...] = full[: DIM + more].astype(BF16)
    kn_ref[...] = jnp.transpose(full).astype(BF16)
    return both[DIM:]


def aug_rows(key_rows):
    return 2 * key_rows + 64 + 16


def pixel_rows(pix_ref, s_ref):
    for a in range(4):
        for ch in range(3):
            block = pix_ref[0, a, ch].astype(F32)
            for tile in range(TILES):
                s_ref[tile, pl.ds(4 * a + ch, ROWS, stride=16), :] = block[:, 128 * tile : 128 * tile + 128]
    for a in range(3):
        for ch in range(3):
            block = pix_ref[0, 4 + a, ch].astype(F32)
            for tile in range(TILES):
                s_ref[tile, 128 + 4 * a + ch : 129 + 4 * a + ch, :] = block[ROWS - 1 : ROWS, 128 * tile : 128 * tile + 128]


def patch_blocks(s_ref, perm, shifted, sets):
    rows = [s_ref[tile] for tile in range(TILES)]
    if shifted:
        first = lane_ids(128, 144) < 4
        rolled = [pltpu.roll(block, 4, 1) for block in rows]
        rows = [jnp.where(first, rolled[tile - 1] if tile else 0.0, rolled[tile]) for tile in range(TILES)]
    rows = [block.astype(BF16) for block in rows]
    stack = []
    for chosen in sets:
        for tile in range(TILES):
            stack.append(jnp.concatenate([rows[tile][16 * r : 16 * r + 16] for r in chosen], axis=1))
    return dot(jnp.concatenate(stack, axis=0), perm).astype(BF16)


def edge_kernel(ext_ref, row_ref, order_ref, *refs, offset):
    pix_refs, refs = refs[:WIDE], refs[WIDE:]
    (perm_ref, tap_ref, wp_ref, wqkv_ref, vec_ref,
     first_ref, last_ref, nsel_ref, kvt_ref, below_ref, own_ref, s_ref, p_ref, wide_ref, kexp_ref) = refs
    images, heights, breadths, row_oks = group_extents(ext_ref, row_ref, offset, size=WIDE)

    @pl.when(pl.program_id(0) == 0)
    def _():
        s_ref[...] = jnp.zeros_like(s_ref)
        fill_wide(wide_ref, vec_ref, [0, 1, 2, 42, 43, 44])
        fill_taps(kexp_ref, vec_ref)

    lane = lane_ids(1024)
    masks = []
    for g in range(WIDE):
        pixel_rows(pix_refs[g], s_ref)
        for shifted in range(2):
            out = patch_blocks(s_ref, perm_ref[...], shifted, ((7, 0, 1, 1), (8, 1, 2, 2)))
            for half in range(2):
                for tile in range(TILES):
                    block = out[128 * half + 16 * tile : 128 * half + 16 * tile + 16]
                    for phase in range(4):
                        top = 128 * shifted + 64 * half + 16 * phase
                        p_ref[top : top + 16, 1024 * g + 128 * tile : 1024 * g + 128 * tile + 128] = block[:, 128 * phase : 128 * phase + 128]
        col = (lane >> 7) * 32 + (lane & 31)
        masks.append(jnp.where((col < breadths[g]) & row_oks[g], 1.0, 0.0).astype(F32))

    def first_norm(k, embed, mask):
        hat, _ = normalized((embed + wide_ref[0]) * mask)
        return ((hat * wide_ref[1] + wide_ref[2]).astype(BF16),)

    (normed,) = by_lanes(first_norm, dot(wp_ref[...], p_ref[...]), jnp.concatenate(masks, axis=1))
    rows = []
    for slot in range(3):
        rows.append(jnp.concatenate([gather_halo(normed[:, 1024 * g : 1024 * g + 1024], 32 * slot) for g in range(WIDE)], axis=1))
    edge = dot(wqkv_ref[0:DIM, :], jnp.concatenate(rows[:2], axis=1))
    (edge,) = by_lanes(lambda k, out: ((out + wide_ref[3]).astype(BF16),), edge)
    nsel = dot(jnp.concatenate([row[:, CANVAS_W * g : CANVAS_W * g + CANVAS_W] for g in range(WIDE) for row in rows], axis=0), tap_ref[...])
    nsel = jnp.concatenate([nsel[DIM * k : DIM * k + DIM] for k in range(3 * WIDE)], axis=1).astype(BF16)
    bias = jnp.concatenate([wide_ref[4], wide_ref[5]], axis=0)
    (taps,) = by_lanes(lambda k, out: ((out + bias).astype(BF16),), dot(wqkv_ref[DIM : 3 * DIM, :], nsel))
    for g in range(WIDE):
        last_ref[g] = edge[:, CANVAS_W * g : CANVAS_W * g + CANVAS_W]
        first_ref[g] = edge[:, CANVAS_W * (WIDE + g) : CANVAS_W * (WIDE + g) + CANVAS_W]
        nsel_ref[g] = nsel[:, 384 * g : 384 * g + 384]
        kvt_ref[g] = taps[:, 384 * g : 384 * g + 384]
        product = taps[:, 384 * g : 384 * g + 384].astype(F32) * kexp_ref[...]
        sums = []
        for k in range(3):
            part = product[:, 128 * k : 128 * k + 128]
            sums.append(part + pltpu.roll(part, 96, 1) + pltpu.roll(part, 64, 1))
        store_lanes(below_ref, sums[0], images[g])
        store_lanes(own_ref, sums[1] + sums[2], images[g])


def embed_kernel(ext_ref, row_ref, order_ref, *refs, offset):
    pix_refs, refs = refs[:WIDE], refs[WIDE:]
    perm_ref, wp_ref, wqkv_ref, vec_ref, patch_ref, x0_ref, q_ref, s_ref, wide_ref = refs
    images, heights, breadths, row_oks = group_extents(ext_ref, row_ref, offset, size=WIDE)

    @pl.when(pl.program_id(0) == 0)
    def _():
        s_ref[...] = jnp.zeros_like(s_ref)
        fill_wide(wide_ref, vec_ref, [0, 1, 2, 42])

    for g in range(WIDE):
        pixel_rows(pix_refs[g], s_ref)
        for shifted in range(2):
            out = patch_blocks(s_ref, perm_ref[...], shifted, ((0, 1, 2, 3), (4, 5, 6, 7), (1, 2, 3, 4), (5, 6, 7, 8)))
            for which in range(4):
                half, side = which // 2, which % 2
                for tile in range(TILES):
                    block = out[128 * which + 16 * tile : 128 * which + 16 * tile + 16]
                    for phase in range(4):
                        top = 128 * shifted + 64 * half + 16 * phase
                        patch_ref[g, top : top + 16, 256 * tile + 128 * side : 256 * tile + 128 * side + 128] = block[
                            :, 128 * phase : 128 * phase + 128]

    count = pair_count(breadths)

    def active(pair, carry):
        def first_norm(k, embed, mask):
            x0 = (embed + wide_ref[0]) * mask
            hat, _ = normalized(x0)
            return x0, (hat * wide_ref[1] + wide_ref[2]).astype(BF16)

        x0, normed = by_lanes(first_norm, dot(wp_ref[...], load_pair(patch_ref, pair)), pair_mask(pair, breadths, row_oks))
        store_pair(x0_ref, pair, x0)
        (query,) = by_lanes(lambda k, out: ((out + wide_ref[3]).astype(BF16),), dot(wqkv_ref[0:DIM, :], normed))
        store_pair(q_ref, pair, query, 256)
        return carry

    def idle(pair, carry):
        for g in range(WIDE):
            q_ref[g, :, pair_lanes(pair, 256)] = jnp.zeros((DIM, PAIR), BF16)
        return carry

    lax.fori_loop(0, count, active, 0)
    lax.fori_loop(count, PAIRS, idle, 0)
    for g in range(WIDE):
        q_ref[g, :, 0:256] = jnp.zeros((DIM, 256), BF16)
        q_ref[g, :, 256 + TOKENS : 512 + TOKENS] = jnp.zeros((DIM, 256), BF16)


def key_lanes(*lead, size=GROUP):
    return pl.BlockSpec(lead + (128,), lambda i, *_: (0,) * len(lead) + (i * size >> 2,))


def specs(size=GROUP):
    whole = lambda *shape: pl.BlockSpec(shape, lambda i, *_: (0,) * len(shape))
    per = lambda *shape: pl.BlockSpec((size,) + shape, lambda i, *_: (i,) + (0,) * len(shape))
    return whole, per


def pixel_specs(offset):
    return [pl.BlockSpec((1, PATCH, 3, ROWS, 1024), lambda i, ext, row, order, g=g: (order[offset + i * WIDE + g], 0, 0, 0, 0)) for g in range(WIDE)]


def call_edge(ext, row, order, pixels, consts, wts, images, offset):
    whole, per = specs(WIDE)
    shapes = [(DIM, CANVAS_W), (DIM, CANVAS_W), (DIM, 384), (2 * DIM, 384)]
    return pl.pallas_call(
        functools.partial(edge_kernel, offset=offset),
        grid_spec=pltpu.PrefetchScalarGridSpec(
            num_scalar_prefetch=3, grid=(images // WIDE,),
            in_specs=pixel_specs(offset) + [
                whole(512, 512), whole(CANVAS_W, 128), whole(DIM, PATCH_ROWS), whole(3 * DIM, DIM), whole(DIM, 64)],
            out_specs=[per(*s) for s in shapes] + [key_lanes(2 * DIM, size=WIDE)] * 2,
            scratch_shapes=[pltpu.VMEM((TILES, 144, 128), F32), pltpu.VMEM((PATCH_ROWS, 1024 * WIDE), BF16), pltpu.VMEM((6, DIM, 128), F32),
                            pltpu.VMEM((2 * DIM, 384), F32)]),
        out_shape=[jax.ShapeDtypeStruct((images,) + s, BF16) for s in shapes]
        + [jax.ShapeDtypeStruct((2 * DIM, 32 * images), F32)] * 2,
        compiler_params=pltpu.CompilerParams(vmem_limit_bytes=VMEM_BYTES),
        cost_estimate=pl.CostEstimate(flops=images * 1_000_000_000, bytes_accessed=images * 1_000_000, transcendentals=0),
        name="edge",
    )(ext, row, order, *[pixels] * WIDE, consts["perm"], consts["tap"], wts["wp"], wts["wqkv_t"], wts["vec"])


def call_embed(ext, row, order, pixels, consts, wts, images, offset):
    whole, per = specs(WIDE)
    shapes = [((PATCH_ROWS, TOKENS), BF16), ((DIM, TOKENS), F32), ((DIM, PADDED), BF16)]
    return pl.pallas_call(
        functools.partial(embed_kernel, offset=offset),
        grid_spec=pltpu.PrefetchScalarGridSpec(
            num_scalar_prefetch=3, grid=(images // WIDE,),
            in_specs=pixel_specs(offset) + [whole(512, 512), whole(DIM, PATCH_ROWS), whole(3 * DIM, DIM), whole(DIM, 64)],
            out_specs=[per(*s) for s, _ in shapes],
            scratch_shapes=[pltpu.VMEM((TILES, 144, 128), F32), pltpu.VMEM((4, DIM, 128), F32)]),
        out_shape=[jax.ShapeDtypeStruct((images,) + s, t) for s, t in shapes],
        compiler_params=pltpu.CompilerParams(vmem_limit_bytes=VMEM_BYTES),
        cost_estimate=pl.CostEstimate(flops=images * 2_000_000_000, bytes_accessed=images * 4_000_000, transcendentals=0),
        name="embed",
    )(ext, row, order, *[pixels] * WIDE, consts["perm"], wts["wp"], wts["wqkv_t"], wts["vec"])


def pool_norm_kernel(own_ref, got_ref, vec_ref, kv_ref):
    for member in range(2):
        part = slice(member * DIM, member * DIM + DIM)
        hat, _ = normalized(own_ref[part] + got_ref[part])
        kv_ref[part] = (hat * column(vec_ref, 5 + 2 * member) + column(vec_ref, 6 + 2 * member)).astype(BF16)


def call_pool_norm(own, got, vec):
    return pl.pallas_call(
        pool_norm_kernel, out_shape=jax.ShapeDtypeStruct(own.shape, BF16), name="pool_norm",
        cost_estimate=pl.CostEstimate(flops=own.size * 10, bytes_accessed=own.size * 10, transcendentals=0))(own, got, vec)


def pool_back_kernel(own_ref, got_ref, grad_ref, vec_ref, pre_ref, sums_ref):
    for member in range(2):
        part = slice(member * DIM, member * DIM + DIM)
        hat, rstd = normalized(own_ref[part] + got_ref[part])
        grad = grad_ref[part].astype(F32)
        pre_ref[part] = norm_back(grad, hat, rstd, column(vec_ref, 5 + 2 * member))
        sums_ref[2 * member] = fold_lanes(grad * hat)
        sums_ref[2 * member + 1] = fold_lanes(grad)


def call_pool_back(own, got, grad, vec):
    return pl.pallas_call(
        pool_back_kernel,
        out_shape=[jax.ShapeDtypeStruct(own.shape, F32), jax.ShapeDtypeStruct((4, DIM, 128), F32)], name="pool_back",
        cost_estimate=pl.CostEstimate(flops=own.size * 20, bytes_accessed=own.size * 16, transcendentals=0))(own, got, grad, vec)


def lane_bit(lane, bit):
    return (lane & bit) != 0


def relative_terms(block, products, key_rows):
    lane = lane_ids(128, WIN)
    parts = [products[WIN * s : WIN * s + WIN] for s in range(8)]
    for bit in (1, 2, 4):
        chosen = lane_bit(lane, bit)
        parts = [jnp.where(chosen, parts[2 * k + 1], parts[2 * k]) for k in range(len(parts) // 2)]
    by_col = parts[0]
    for bit, step in ((8, 1), (16, 2)):
        by_col = jnp.where(lane_bit(lane, bit), by_col, pltpu.roll(by_col, WIN - step, 0))
    by_col = by_col[0:32] if block & 2 else by_col[4:36]
    lane = lane_ids(128, key_rows)
    rows = products[8 * WIN :]
    parts = [rows[key_rows * r : key_rows * r + key_rows] for r in range(4 * (block & 1), 4 * (block & 1) + 4)]
    for bit in (32, 64):
        chosen = lane_bit(lane, bit)
        parts = [jnp.where(chosen, parts[2 * k + 1], parts[2 * k]) for k in range(len(parts) // 2)]
    return jnp.concatenate([parts[0], by_col], axis=0)


def relative_spread(block, grad_terms, key_rows):
    lane = lane_ids(128, WIN)
    by_row = grad_terms[:key_rows]
    if block & 2:
        pieces = [grad_terms[key_rows:], jnp.zeros((WIN - 32, 128), F32)]
    else:
        pieces = [jnp.zeros((4, 128), F32), grad_terms[key_rows:], jnp.zeros((WIN - 36, 128), F32)]
    by_col = jnp.concatenate(pieces, axis=0)
    for bit, step in ((8, 1), (16, 2)):
        by_col = jnp.where(lane_bit(lane, bit), by_col, pltpu.roll(by_col, step, 0))
    parts = [jnp.where((lane & 7) == s, by_col, 0.0) for s in range(8)]
    lane = lane_ids(128, key_rows)
    for r in range(8):
        hit = (lane >> 5) == r - 4 * (block & 1)
        parts.append(jnp.where(hit, by_row, 0.0) if r // 4 == block & 1 else jnp.zeros((key_rows, 128), F32))
    return jnp.concatenate(parts, axis=0).astype(BF16)


def gelu_parts(hidden):
    cumulative = 0.5 + 0.5 * lax.erf(hidden * 0.7071067811865476)
    slope = cumulative + hidden * (jnp.exp2(hidden * hidden * (-0.5 * 1.4426950408889634)) * 0.3989422804014327)
    return (hidden * cumulative).astype(BF16), slope.astype(BF16)


def forward_kernel(ext_ref, row_ref, q_ref, top_ref, bot_ref, x0_ref, kv_ref, vec_ref, rw_ref, wproj_ref, w1_ref, w2_ref,
                   hat_ref, query_ref, terms_ref, att_ref, act_ref, slope_ref, hat2_ref, hat3_ref, stat_ref, pool_ref, ka_ref, kn_ref, v_ref, ztop_ref, zbot_ref, pre_ref, wide_ref, wb1_ref, wprojt_ref, w1t_ref, w2t_ref,
                   *, offset, key_rows):
    images, heights, breadths, row_oks = group_extents(ext_ref, row_ref, offset)
    depth = DIM + aug_rows(key_rows)

    @pl.when(pl.program_id(0) == 0)
    def _():
        fill_wide(wide_ref, vec_ref, list(range(15, 24)) + [3, 4, 9, 10, 11, 12])
        fill_bias(wb1_ref, vec_ref)
        fill_transpose(wprojt_ref, wproj_ref)
        fill_transpose(w1t_ref, w1_ref)
        fill_transpose(w2t_ref, w2_ref)

    lane = lane_ids(CANVAS_W, DIM)
    for g in range(GROUP):
        v_ref[g] = key_tables(kv_ref, images[g], key_rows, heights[g], breadths[g], ka_ref, kn_ref.at[g]).astype(BF16)
        for halo_ref, dst_ref, tap_row, target in ((top_ref, ztop_ref, 0, 0), (bot_ref, zbot_ref, 2, 96)):
            halo = halo_ref[g].astype(F32)
            left = jnp.where(lane == 0, 0.0, pltpu.roll(halo, 1, 1))
            right = jnp.where(lane == CANVAS_W - 1, 0.0, pltpu.roll(halo, CANVAS_W - 1, 1))
            taps = [wide(wide_ref, 3 * tap_row + k, CANVAS_W) for k in range(3)]
            spread_halo(dst_ref.at[g], taps[0] * left + taps[1] * halo + taps[2] * right, target)
    pool_ref[...] = jnp.zeros_like(pool_ref)

    def step(pair, carry):
        for group in range(0, DIM, 16):
            part = slice(group, group + 16)
            taps = [wide_ref[k, part] for k in range(9)]
            for g in range(GROUP):
                window = q_ref[g, part, pl.ds(pl.multiple_of(pair * PAIR, 128), PAIR + 512)]
                for tile in range(2):
                    sums = []
                    for side in range(2):
                        shifts = col_shifts(window, 256 + 256 * tile + 128 * side)
                        sums.append([sum(taps[3 * r + c] * shifts[c] for c in range(3)) for r in range(3)])
                    halo = pl.ds(pl.multiple_of((2 * pair + tile) * 128, 128), 128)
                    down = rows_down(sums[0][0], sums[1][0], ztop_ref[g, part, halo])
                    up = rows_up(sums[0][2], sums[1][2], zbot_ref[g, part, halo])
                    for side in range(2):
                        base = PAIR * g + 256 * tile + 128 * side
                        pre_ref[part, base : base + 128] = sums[side][1] + down[side] + up[side]

        def query_of(k, pre):
            hat, rstd = normalized(pre)
            return hat.astype(BF16), (hat * wide_ref[9] + wide_ref[10]).astype(BF16), rstd

        hat, query, rstd = by_lanes(query_of, pre_ref[...])
        store_pair(hat_ref, pair, hat)
        store_pair(query_ref, pair, query)

        def extra_of(k, products):
            terms = relative_terms(k, products, key_rows) * (DIM**0.5)
            high = terms.astype(BF16).astype(F32)
            return (jnp.concatenate([high, terms - high, jnp.ones((16, 128), F32)], axis=0).astype(BF16),)

        (extra,) = by_lanes(extra_of, dot(rw_ref[pair], query))
        store_pair(terms_ref, pair, extra)

        def softmax(k, scores):
            peak = jnp.max(scores, axis=0, keepdims=True)
            weights = jnp.exp2((scores - peak) * EXP2_SCALE)
            inverse = 1.0 / jnp.sum(weights, axis=0, keepdims=True)
            return (weights * inverse).astype(BF16), peak, inverse

        long_query = by_image(jnp.concatenate([query, extra], axis=0))
        scores = jnp.concatenate([dot(kn_ref[g, :, :depth], long_query[g]) for g in range(GROUP)], axis=1)
        probs, peak, inverse = by_lanes(softmax, scores)
        mixed = by_image(probs)
        mixed = jnp.concatenate([dot(v_ref[g], mixed[g]) for g in range(GROUP)], axis=1)
        attended = (mixed + query.astype(F32)).astype(BF16)
        store_pair(att_ref, pair, attended)

        def second_norm(k, x0, out):
            x1 = x0 + (out + wide_ref[11])
            hat, rstd = normalized(x1)
            return x1, (hat * wide_ref[12] + wide_ref[13]).astype(BF16), hat.astype(BF16), rstd

        x1, normed, hat_two, rstd_two = by_lanes(second_norm, load_pair(x0_ref, pair), dot(wprojt_ref[...], attended))
        store_pair(hat2_ref, pair, hat_two)
        act, slope = by_blocks(lambda part, hidden: gelu_parts(hidden + wb1_ref[part]), 64, dot(w1t_ref[...], normed))
        store_pair(act_ref, pair, act)
        store_pair(slope_ref, pair, slope)

        def third_norm(k, x1, out, mask):
            hat, rstd = normalized(x1 + (out + wide_ref[14]))
            return hat * mask, hat.astype(BF16), rstd

        kept, hat_three, rstd_three = by_lanes(third_norm, x1, dot(w2t_ref[...], act), pair_mask(pair, breadths, row_oks))
        store_pair(hat3_ref, pair, hat_three)
        stats = [peak, inverse, rstd, rstd_two, rstd_three, jnp.zeros((3, GROUP * PAIR), F32)]
        store_pair(stat_ref, pair, jnp.concatenate(stats, axis=0))
        for g, part in enumerate(by_image(kept)):
            pool_ref[g] += fold_lanes(part)
        return carry

    lax.fori_loop(0, pair_count(breadths), step, 0)


def call_forward(ext, row, q, top, bot, x0, kv, wts, offset):
    whole, per = specs()
    images, key_rows = q.shape[0], kv.shape[0]
    more = aug_rows(key_rows)
    shapes = [(rows, BF16) for rows in (DIM, DIM, more, DIM, MLP, MLP, DIM, DIM)]
    shapes = [((rows, TOKENS), kind) for rows, kind in shapes] + [((8, TOKENS), F32), ((DIM, 128), F32)]
    keys = key_rows * 32
    return pl.pallas_call(
        functools.partial(forward_kernel, offset=offset, key_rows=key_rows),
        grid_spec=pltpu.PrefetchScalarGridSpec(
            num_scalar_prefetch=2, grid=(images // GROUP,),
            in_specs=[
                per(DIM, PADDED), per(DIM, CANVAS_W), per(DIM, CANVAS_W), per(DIM, TOKENS),
                key_lanes(key_rows, 2 * DIM),
                whole(DIM, 64), whole(PAIRS, 8 * WIN + 8 * key_rows, DIM), whole(DIM, DIM), whole(DIM, MLP), whole(MLP, DIM)],
            out_specs=[per(*s) for s, _ in shapes],
            scratch_shapes=[
                pltpu.VMEM((DIM + more, keys), BF16), pltpu.VMEM((GROUP, keys, 256), BF16), pltpu.VMEM((GROUP, DIM, keys), BF16),
                pltpu.VMEM((GROUP, DIM, 1024), F32), pltpu.VMEM((GROUP, DIM, 1024), F32), pltpu.VMEM((DIM, GROUP * PAIR), F32),
                pltpu.VMEM((15, DIM, 128), F32), pltpu.VMEM((MLP, 128), F32),
                pltpu.VMEM((DIM, DIM), BF16), pltpu.VMEM((MLP, DIM), BF16), pltpu.VMEM((DIM, MLP), BF16)]),
        out_shape=[jax.ShapeDtypeStruct((images,) + s, t) for s, t in shapes],
        compiler_params=pltpu.CompilerParams(vmem_limit_bytes=VMEM_BYTES),
        cost_estimate=pl.CostEstimate(flops=images * 5_000_000_000, bytes_accessed=images * 4_000_000, transcendentals=0),
        name="forward",
    )(ext, row, q, top, bot, x0, kv, wts["vec"], wts["rw"], wts["wproj"], wts["w1"], wts["w2"])


def backward_kernel(ext_ref, row_ref, hat_ref, query_ref, terms_ref, att_ref, act_ref, slope_ref, hat2_ref, hat3_ref, stat_ref, q_ref, top_ref, bot_ref, kv_ref,
                    gvec_ref, vec_ref, rwt_ref, wproj_ref, w1_ref, w2_ref,
                    dx1_ref, dq_ref, up_ref, down_ref, dkv_ref, a2_ref, a1_ref, ap_ref, av_ref, ak_ref, ar_ref,
                    ka_ref, kn_ref, vn_ref, dp_ref, qtop_ref, qbot_ref, ru_ref, rd_ref, dk_ref, dv_ref, wide_ref, *, offset, key_rows):
    now = pl.program_id(0)
    steps = pl.num_programs(0) - 1
    images, heights, breadths, row_oks = group_extents(ext_ref, row_ref, offset, jnp.minimum(now, steps - 1))
    _, _, former, _ = group_extents(ext_ref, row_ref, offset, jnp.maximum(now - 1, 0))
    depth = DIM + aug_rows(key_rows)
    count = jnp.where(now < steps, pair_count(breadths), 0)
    former_count = pair_count(former)
    dp_now, dp_former = now & 1, (now & 1) ^ 1

    @pl.when(pl.program_id(0) == 0)
    def _():
        for ref in (a2_ref, a1_ref, ap_ref, av_ref, ak_ref, ar_ref, ru_ref, rd_ref):
            ref[...] = jnp.zeros_like(ref)
        fill_wide(wide_ref, vec_ref, list(range(15, 24)) + [3, 10, 11, 13])
        dp_ref[...] = jnp.zeros_like(dp_ref)

    for g in range(GROUP):
        values = key_tables(kv_ref, images[g], key_rows, heights[g], breadths[g], ka_ref.at[g], kn_ref.at[g])
        padded_values = jnp.concatenate([values, jnp.zeros((128 - DIM, values.shape[1]), F32)], axis=0)
        vn_ref[g] = jnp.transpose(padded_values).astype(BF16)
        spread_halo(qtop_ref.at[g], top_ref[g], 0)
        spread_halo(qbot_ref.at[g], bot_ref[g], 96)
    for ref in (dk_ref, dv_ref, dp_ref.at[dp_now]):
        ref[...] = jnp.zeros_like(ref)

    def step(pair, carry):
        ones = jnp.ones((16, GROUP * PAIR), BF16)
        stat = load_pair(stat_ref, pair)

        def third_back(k, hat, stat, mask):
            grad = norm_back(gvec_ref[k * 128 // PAIR] * mask, hat.astype(F32), stat[4:5], wide_ref[12])
            return grad, grad.astype(BF16)

        grad_x2, grad_mlp = by_lanes(third_back, load_pair(hat3_ref, pair), stat, pair_mask(pair, breadths, row_oks))
        act = load_pair(act_ref, pair)
        a2_ref[...] += dot_nt(jnp.concatenate([act, ones], axis=0), grad_mlp)
        (grad_hidden,) = by_blocks(
            lambda part, grad, slope: ((grad * slope.astype(F32)).astype(BF16),), 64, dot(w2_ref[...], grad_mlp), load_pair(slope_ref, pair))
        hat_two = load_pair(hat2_ref, pair)
        (normed,) = by_lanes(lambda k, hat: ((hat.astype(F32) * wide_ref[10] + wide_ref[11]).astype(BF16),), hat_two)
        a1_ref[...] += dot_nt(jnp.concatenate([normed, ones], axis=0), grad_hidden)

        def second_back(k, grad, hat, stat, grad_x2):
            hat = hat.astype(F32)
            total = grad_x2 + norm_back(grad, hat, stat[3:4], wide_ref[10])
            return total.astype(BF16), grad * hat

        grad_normed = dot(w1_ref[...], grad_hidden)
        grad_proj, scaled = by_lanes(second_back, grad_normed, hat_two, stat, grad_x2)
        av_ref[0] += fold_lanes(scaled)
        av_ref[1] += fold_lanes(grad_normed)
        store_pair(dx1_ref, pair, grad_proj)
        attended = load_pair(att_ref, pair)
        ap_ref[...] += dot_nt(jnp.concatenate([attended, ones], axis=0), grad_proj)
        grad_att = dot(wproj_ref[...], grad_proj)
        grad_att_low = grad_att.astype(BF16)
        hat = load_pair(hat_ref, pair)
        query = load_pair(query_ref, pair)
        long_query = by_image(jnp.concatenate([query, load_pair(terms_ref, pair)], axis=0))
        scores = jnp.concatenate([dot(kn_ref[g, :, :depth], long_query[g]) for g in range(GROUP)], axis=1)
        low = by_image(grad_att_low)
        grad_probs = jnp.concatenate([dot(vn_ref[g, :, :DIM], low[g]) for g in range(GROUP)], axis=1)

        def softmax_back(k, scores, grad_probs, stat):
            probs = jnp.exp2((scores - stat[0:1]) * EXP2_SCALE) * stat[1:2]
            inner = jnp.sum(probs * grad_probs, axis=0, keepdims=True)
            return probs.astype(BF16), (probs * (grad_probs - inner)).astype(BF16)

        probs, grad_scores = by_lanes(softmax_back, scores, grad_probs, stat)
        probs, grad_scores, queries = by_image(probs), by_image(grad_scores), by_image(query)
        back = []
        for g in range(GROUP):
            back.append(dot(ka_ref[g, : DIM + key_rows + 32, :], grad_scores[g]))
            dv_ref[g] += dot_nt(low[g], probs[g])
            dk_ref[g] += dot_nt(queries[g], grad_scores[g])
        back = jnp.concatenate(back, axis=1)
        (spread,) = by_lanes(lambda k, terms: (relative_spread(k, terms, key_rows),), back[DIM:])
        ar_ref[pair] += dot_nt(spread, query)

        def query_back(k, grad_att, back, far, hat, stat):
            grad = grad_att + back * SCALE + far
            hat = hat.astype(F32)
            return norm_back(grad, hat, stat[2:3], wide_ref[9]), grad * hat, grad

        grad_pre, scaled, grad = by_lanes(query_back, grad_att, back[:DIM], dot(rwt_ref[pair], spread), hat, stat)
        av_ref[2] += fold_lanes(scaled)
        av_ref[3] += fold_lanes(grad)
        store_pair(dp_ref.at[dp_now], pair, grad_pre.astype(BF16), 256)
        return carry

    def pool_step(pair, carry):
        for group in range(0, DIM, 16):
            part = slice(group, group + 16)
            taps = [wide_ref[k, part] for k in range(9)]
            grads = [None] * 9
            for g in range(GROUP):
                window = dp_ref[dp_former, g, part, pl.ds(pl.multiple_of(pair * PAIR, 128), PAIR + 512)]
                for tile in range(2):
                    base = pair * PAIR + 256 * tile
                    halo = pl.ds(pl.multiple_of((2 * pair + tile) * 128, 128), 128)
                    query = [q_ref[g, part, pl.ds(pl.multiple_of(base + 256 + 128 * side, 128), 128)] for side in range(2)]
                    above = rows_down(query[0], query[1], qtop_ref[g, part, halo])
                    under = rows_up(query[0], query[1], qbot_ref[g, part, halo])
                    sums = []
                    for side in range(2):
                        left, here, right = col_shifts(window, 256 + 256 * tile + 128 * side)
                        shifts = (right, here, left)
                        sums.append([sum(taps[3 * r + c] * shifts[c] for c in range(3)) for r in range(3)])
                        for r, rows in enumerate((above[side], query[side], under[side])):
                            rows = rows.astype(F32)
                            for c in range(3):
                                term = shifts[c] * rows
                                grads[3 * r + c] = term if grads[3 * r + c] is None else grads[3 * r + c] + term
                    zero = jnp.zeros((16, 128), F32)
                    up = rows_up(sums[0][0], sums[1][0], zero)
                    down = rows_down(sums[0][2], sums[1][2], zero)
                    for side in range(2):
                        lanes = pl.ds(pl.multiple_of(base + 128 * side, 128), 128)
                        dq_ref[g, part, lanes] = (sums[side][1] + up[side] + down[side]).astype(BF16)
                    ru_ref[g, part, halo] = up[2].astype(BF16)
                    rd_ref[g, part, halo] = down[2].astype(BF16)
            for k in range(9):
                ak_ref[k, part] += grads[k]
        return carry

    def pool_idle(pair, carry):
        for ref in (ru_ref, rd_ref):
            for g in range(GROUP):
                ref[g, :, pl.ds(pl.multiple_of(pair * 256, 128), 256)] = jnp.zeros((DIM, 256), BF16)
        store_pair(dq_ref, pair, jnp.zeros((DIM, GROUP * PAIR), BF16))
        return carry

    def idle(pair, carry):
        store_pair(dx1_ref, pair, jnp.zeros((DIM, GROUP * PAIR), BF16))
        return carry

    lax.fori_loop(0, count, lambda pair, carry: step(pair, pool_step(pair, carry)), 0)
    lax.fori_loop(count, former_count, pool_step, 0)
    lax.fori_loop(former_count, PAIRS, pool_idle, 0)
    lax.fori_loop(jnp.where(now < steps, count, PAIRS), PAIRS, idle, 0)

    @pl.when(now < steps)
    def _():
        lane = lane_ids(128, 2 * DIM)
        for g in range(GROUP):
            for i in range(key_rows):
                block = slice(128 * (i // 4), 128 * (i // 4) + 128)
                value = jnp.concatenate([dk_ref[g, :, block] * SCALE, dv_ref[g, :, block]], axis=0)
                value = pltpu.roll(value, (4 + (images[g] & 3) - i % 4) * 32 & 127, 1)
                slot = reverse_bits(jnp.bitwise_xor(row_ref[0], i), key_rows)
                dkv_ref[slot] = jnp.where((lane >> 5) == (images[g] & 3), value, dkv_ref[slot])

    for g in range(GROUP):
        up_ref[g] = gather_halo(ru_ref.at[g], 96)
        down_ref[g] = gather_halo(rd_ref.at[g], 0)


def call_backward(ext, row, saved, q, top, bot, kv, gvec, wts, offset):
    whole, _ = specs()
    images, key_rows = q.shape[0], kv.shape[0]
    more = aug_rows(key_rows)
    keys = key_rows * 32
    window = 8 * WIN + 8 * key_rows
    steps = images // GROUP
    now = lambda *shape: pl.BlockSpec((GROUP,) + shape, lambda i, *_: (jnp.minimum(i, steps - 1),) + (0,) * len(shape))
    former = lambda *shape: pl.BlockSpec((GROUP,) + shape, lambda i, *_: (jnp.maximum(i - 1, 0),) + (0,) * len(shape))
    heads = pl.BlockSpec((key_rows, 2 * DIM, 128), lambda i, *_: (0, 0, jnp.minimum(i, steps - 1) * GROUP >> 2))
    shapes = [(DIM, TOKENS), (DIM, TOKENS), (DIM, CANVAS_W), (DIM, CANVAS_W)]
    sums = [(MLP + 16, DIM), (DIM + 16, MLP), (DIM + 16, DIM), (4, DIM, 128), (9, DIM, 128), (PAIRS, window, DIM)]
    return pl.pallas_call(
        functools.partial(backward_kernel, offset=offset, key_rows=key_rows),
        grid_spec=pltpu.PrefetchScalarGridSpec(
            num_scalar_prefetch=2, grid=(steps + 1,),
            in_specs=[now(rows, TOKENS) for rows in (DIM, DIM, more, DIM, MLP, MLP, DIM, DIM, 8)] + [
                former(DIM, PADDED), former(DIM, CANVAS_W), former(DIM, CANVAS_W), heads, now(DIM, 1), whole(DIM, 64), whole(PAIRS, DIM, window),
                whole(DIM, DIM), whole(DIM, MLP), whole(MLP, DIM)],
            out_specs=[now(*shapes[0])] + [former(*s) for s in shapes[1:]] + [heads] + [whole(*s) for s in sums],
            scratch_shapes=[
                pltpu.VMEM((GROUP, DIM + more, keys), BF16), pltpu.VMEM((GROUP, keys, 256), BF16), pltpu.VMEM((GROUP, keys, 128), BF16),
                pltpu.VMEM((2, GROUP, DIM, PADDED), BF16)] + [pltpu.VMEM((GROUP, DIM, 1024), BF16)] * 4
            + [pltpu.VMEM((GROUP, DIM, keys), F32)] * 2 + [pltpu.VMEM((13, DIM, 128), F32)]),
        out_shape=[jax.ShapeDtypeStruct((images,) + s, BF16) for s in shapes]
        + [jax.ShapeDtypeStruct((key_rows, 2 * DIM, 32 * images), F32)] + [jax.ShapeDtypeStruct(s, F32) for s in sums],
        compiler_params=pltpu.CompilerParams(vmem_limit_bytes=VMEM_BYTES),
        cost_estimate=pl.CostEstimate(flops=images * 12_000_000_000, bytes_accessed=images * 6_000_000, transcendentals=0),
        name="backward",
    )(ext, row, *saved, q, top, bot, kv, gvec, wts["vec"], wts["rw_t"], wts["wproj"], wts["w1"], wts["w2"])


def embed_back_kernel(ext_ref, row_ref, patch_ref, dq_ref, dx1_ref, rtop_ref, rbot_ref, nsel_ref, kvt_ref, pre_ref, under_ref,
                      wp_ref, vec_ref, wqkv_ref, tapt_ref,
                      aq_ref, akv_ref, apatch_ref, av_ref, ak_ref, dn_ref, rim_ref, wide_ref, kexp_ref, *, offset):
    images, heights, breadths, row_oks = group_extents(ext_ref, row_ref, offset, size=WIDE)

    @pl.when(pl.program_id(0) == 0)
    def _():
        for ref in (aq_ref, akv_ref, apatch_ref, av_ref, ak_ref, dn_ref, rim_ref):
            ref[...] = jnp.zeros_like(ref)
        fill_wide(wide_ref, vec_ref, [0, 1, 2])
        fill_taps(kexp_ref, vec_ref)

    lane = lane_ids(128, 2 * DIM)

    def thrice(value, image):
        block = jnp.where((lane >> 5) == 1, take_lanes(value, image, 1), take_lanes(value, image, 0))
        block = jnp.where((lane >> 5) == 2, take_lanes(value, image, 2), block)
        return jnp.where((lane >> 5) == 3, 0.0, block)

    grad_taps = []
    for g in range(WIDE):
        own = thrice(pre_ref[...], images[g])
        spread = jnp.concatenate([thrice(under_ref[...].astype(F32), images[g]), own, own], axis=1)
        ak_ref[...] += kvt_ref[g].astype(F32) * spread
        grad_taps.append((spread * kexp_ref[...]).astype(BF16))
    grad_taps = jnp.concatenate(grad_taps, axis=1)
    nsel = jnp.concatenate([nsel_ref[g] for g in range(WIDE)], axis=1)
    akv_ref[...] += dot_nt(jnp.concatenate([nsel, jnp.ones((16, 384 * WIDE), BF16)], axis=0), grad_taps)
    grad_sel = dot(wqkv_ref[:, DIM : 3 * DIM], grad_taps)
    parts = [grad_sel.astype(BF16)[:, 128 * k : 128 * k + 128] for k in range(3 * WIDE)]
    lines = dot(jnp.concatenate(parts, axis=0), tapt_ref[...])
    for g in range(WIDE):
        for k, start in enumerate((224, 0, 32)):
            first = DIM * (3 * g + k)
            line = lines[first : first + DIM]
            for tile in range(TILES):
                dn_ref[g, :, 256 * tile + start : 256 * tile + start + 32] = line[:, 32 * tile : 32 * tile + 32]
        for halo_ref, start in ((rtop_ref, 0), (rbot_ref, 224)):
            line = halo_ref[g].astype(F32)
            for tile in range(TILES):
                rim_ref[g, :, 256 * tile + start : 256 * tile + start + 32] = line[:, 32 * tile : 32 * tile + 32]

    def step(pair, carry):
        mask = pair_mask(pair, breadths, row_oks)
        patches = load_pair(patch_ref, pair)

        def first_norm(k, embed, mask, grad, rim):
            hat, rstd = normalized((embed + wide_ref[0]) * mask)
            return hat, rstd, (hat * wide_ref[1] + wide_ref[2]).astype(BF16), (grad.astype(F32) + rim).astype(BF16)

        hat, rstd, normed, grad_q = by_lanes(first_norm, dot(wp_ref[...], patches), mask, load_pair(dq_ref, pair), load_pair(rim_ref, pair))
        aq_ref[...] += dot_nt(jnp.concatenate([normed, jnp.ones((16, WIDE * PAIR), BF16)], axis=0), grad_q)

        def first_back(k, out, extra, hat, rstd, mask, dx1):
            grad = out + extra
            total = (dx1.astype(F32) + norm_back(grad, hat, rstd, wide_ref[1])) * mask
            return total.astype(BF16), total, grad * hat, grad

        low, total, scaled, grad = by_lanes(
            first_back, dot(wqkv_ref[:, 0:DIM], grad_q), load_pair(dn_ref, pair), hat, rstd, mask, load_pair(dx1_ref, pair))
        av_ref[0] += fold_lanes(total)
        av_ref[1] += fold_lanes(scaled)
        av_ref[2] += fold_lanes(grad)
        apatch_ref[...] += dot_nt(low, patches)
        return carry

    lax.fori_loop(0, pair_count(breadths), step, 0)


def call_embed_back(ext, row, patches, dq, dx1, rtop, rbot, nsel, kvt, pre, under, consts, wts, offset):
    whole, per = specs(WIDE)
    images = dq.shape[0]
    sums = [(DIM + 16, DIM), (DIM + 16, 2 * DIM), (DIM, PATCH_ROWS), (3, DIM, 128), (2 * DIM, 384)]
    return pl.pallas_call(
        functools.partial(embed_back_kernel, offset=offset),
        grid_spec=pltpu.PrefetchScalarGridSpec(
            num_scalar_prefetch=2, grid=(images // WIDE,),
            in_specs=[
                per(PATCH_ROWS, TOKENS), per(DIM, TOKENS), per(DIM, TOKENS), per(DIM, CANVAS_W), per(DIM, CANVAS_W),
                per(DIM, 384), per(2 * DIM, 384), key_lanes(2 * DIM, size=WIDE), key_lanes(2 * DIM, size=WIDE),
                whole(DIM, PATCH_ROWS), whole(DIM, 64), whole(DIM, 3 * DIM), whole(128, CANVAS_W)],
            out_specs=[whole(*s) for s in sums],
            scratch_shapes=[pltpu.VMEM((WIDE, DIM, TOKENS), F32)] * 2 + [pltpu.VMEM((3, DIM, 128), F32), pltpu.VMEM((2 * DIM, 384), F32)]),
        out_shape=[jax.ShapeDtypeStruct(s, F32) for s in sums],
        compiler_params=pltpu.CompilerParams(vmem_limit_bytes=VMEM_BYTES),
        cost_estimate=pl.CostEstimate(flops=images * 3_000_000_000, bytes_accessed=images * 3_000_000, transcendentals=0),
        name="embed_back",
    )(ext, row, patches, dq, dx1, rtop, rbot, nsel, kvt, pre, under, wts["wp"], wts["vec"], wts["wqkv"], consts["tap_t"])


def bit_count(size):
    return size.bit_length() - 1


def swap(value, axis, bit):
    size = lax.axis_size(axis)
    return lax.ppermute(value, axis, [(i, i ^ (1 << bit)) for i in range(size)])


def shifted(value, axis, step):
    size = lax.axis_size(axis)
    pairs = [(i, i + step) for i in range(size) if 0 <= i + step < size]
    return lax.ppermute(value, axis, pairs)


def summed(value, axis):
    for bit in range(bit_count(lax.axis_size(axis))):
        value = value + swap(value, axis, bit)
    return value


def scatter_step(value, axis, bit):
    half = value.shape[0] // 2
    return value[:half] + swap(value[half:].astype(BF16), axis, bit).astype(F32)


def together(*values):
    return lax.optimization_barrier(values)


def gather_params(value):
    dims = []
    for axis in ("img", "row"):
        index = lax.axis_index(axis)
        for bit in reversed(range(bit_count(lax.axis_size(axis)))):
            other = swap(value, axis, bit)
            mine_second = (index >> bit) & 1 == 1
            value = jnp.stack([jnp.where(mine_second, other, value), jnp.where(mine_second, value, other)])
            dims.append((axis, bit))
    dims = dims[::-1]
    wanted = [("img", b) for b in reversed(range(bit_count(lax.axis_size("img"))))]
    wanted += [("row", b) for b in reversed(range(bit_count(lax.axis_size("row"))))]
    order = [dims.index(d) for d in wanted]
    value = jnp.transpose(value, order + [value.ndim - 2, value.ndim - 1])
    return value.reshape(-1)


def sum_grads(flat, extra):
    rows, imgs = lax.axis_size("row"), lax.axis_size("img")
    bits = bit_count(rows)
    leaf = flat.shape[0] // (rows * imgs)
    value = flat.reshape((imgs,) + (2,) * bits + (leaf // 128, 128))
    index = lax.axis_index("row")
    for bit in range(bits):
        place = value.ndim - 3
        own = (index >> bit) & 1
        keep = lax.dynamic_index_in_dim(value, own, place, False)
        send = lax.dynamic_index_in_dim(value, 1 - own, place, False)
        value = keep + swap(send, "row", bit)
    value = jnp.concatenate([value.reshape(imgs * leaf // 128, 128), jnp.full((8, 128), extra)], axis=0)
    value = summed(value, "img")
    return value[:-8], value[-1, 0]


def segment_list(canvas_rows, canvas_cols):
    return [
        ("w_patch", (3 * PATCH * PATCH, DIM)),
        ("w_qkv", (DIM, 3 * DIM)),
        ("w_proj", (DIM, DIM)),
        ("w_fc1", (DIM, MLP)),
        ("w_fc2", (MLP, DIM)),
        ("w_head", (DIM, CLASSES)),
        ("rel_rows", (2 * canvas_rows - 8, DIM)),
        ("rel_cols", (2 * canvas_cols - 8, DIM)),
        ("small", (49, DIM)),
        ("b_head", (CLASSES,)),
    ]


def unpack(flat_vec, segments):
    pieces = {}
    position = 0
    for seg_name, seg_shape in segments:
        entries = int(np.prod(seg_shape))
        pieces[seg_name] = flat_vec[position : position + entries].reshape(seg_shape)
        position += entries
    return pieces


def patch_rows(weight):
    taps = jnp.pad(weight.reshape(PATCH, PATCH, 3, DIM), ((0, 1), (0, 0), (0, 1), (0, 0)))
    parts = []
    for piece in (taps[:, 3:7], jnp.pad(taps[:, 0:3], ((0, 0), (1, 0), (0, 0), (0, 0)))):
        parts.append(jnp.transpose(piece.reshape(2, 4, 4, 4, DIM), (0, 2, 1, 3, 4)).reshape(128, DIM))
    return jnp.concatenate(parts, axis=0)


def patch_rows_back(grad):
    taps = jnp.transpose(grad.T.reshape(2, 2, 4, 4, 4, DIM), (0, 1, 3, 2, 4, 5)).reshape(2, 8, 4, 4, DIM)
    return jnp.concatenate([taps[1, :PATCH, 1:, :3], taps[0, :PATCH, :, :3]], axis=1).reshape(3 * PATCH * PATCH, DIM)


def relative_windows(rel_rows, rel_cols, row_index, key_rows):
    offsets = jnp.flip(rel_cols.reshape(-1, 8, DIM), 0)
    offsets = jnp.transpose(jnp.pad(offsets, ((0, 1), (0, 0), (0, 0))), (1, 0, 2))
    blocks = rel_rows.reshape(2 * key_rows - 1, 8, DIM)
    rows = jnp.transpose(jnp.flip(lax.dynamic_slice_in_dim(blocks, row_index, key_rows, 0), 0), (1, 0, 2))
    rows = rows.reshape(8 * key_rows, DIM)
    windows = []
    for pair in range(PAIRS):
        cols = offsets[:, 24 - 8 * pair : 24 - 8 * pair + WIN].reshape(8 * WIN, DIM)
        windows.append(jnp.concatenate([cols, rows], axis=0))
    return jnp.stack(windows)


def relative_windows_back(grad, row_index, key_rows):
    cols = grad[:, : 8 * WIN].reshape(PAIRS, 8, WIN, DIM)
    total = 0.0
    for pair in range(PAIRS):
        start = 24 - 8 * pair
        total = total + jnp.pad(cols[pair], ((0, 0), (start, 64 - start - WIN), (0, 0)))
    rel_cols = jnp.flip(jnp.transpose(total[:, :63], (1, 0, 2)), 0).reshape(-1, DIM)
    rows = jnp.sum(grad[:, 8 * WIN :], axis=0).reshape(8, key_rows, DIM)
    rows = jnp.flip(jnp.transpose(rows, (1, 0, 2)), 0)
    blocks = lax.dynamic_update_slice_in_dim(jnp.zeros((2 * key_rows - 1, 8, DIM), F32), rows, row_index, 0)
    return blocks.reshape(-1, DIM), rel_cols


def tap_keep():
    keep = np.ones((3, 4, 32), np.float32)
    keep[:, 3] = 0.0
    keep[:, 0, 0] = 0.0
    return keep


def prepare(weights, row_index, key_rows):
    small = weights["small"]
    vec = jnp.pad(small.astype(F32).T, ((0, 0), (0, 15)))
    windows = relative_windows(weights["rel_rows"], weights["rel_cols"], row_index, key_rows)
    return {
        "vec": vec,
        "wp": patch_rows(weights["w_patch"]).T,
        "wqkv": weights["w_qkv"],
        "wqkv_t": weights["w_qkv"].T,
        "wproj": weights["w_proj"],
        "w1": weights["w_fc1"],
        "w2": weights["w_fc2"],
        "rw": windows,
        "rw_t": jnp.transpose(windows, (0, 2, 1)),
    }


def image_loss(pooled, head_w, head_b, log_teacher, labels, image_total):
    logits = jnp.dot(pooled, head_w, precision=HIGHEST_PREC) + head_b
    log_student = jax.nn.log_softmax(logits, axis=-1)
    onehot = (jnp.arange(CLASSES)[None, :] == labels[:, None]).astype(F32)
    per_image = jnp.sum(jnp.exp(log_teacher) * (log_teacher - log_student), axis=-1) - jnp.sum(onehot * log_student, axis=-1)
    return jnp.sum(per_image) / image_total


def body(flat_params, first_moment, second_moment, pixels, extents, labels, teacher):
    key_rows = lax.axis_size("row")
    row_index = lax.axis_index("row")
    row_lead = row_index == 0
    segments = segment_list(ROWS * key_rows, CANVAS_W)
    full_params = gather_params(flat_params.astype(BF16).reshape(-1, 128))
    weights = unpack(full_params, segments)
    wts = prepare(weights, row_index, key_rows)
    tap = tap_matrix()
    consts = {"perm": jnp.asarray(deinterleave_matrix(), BF16), "tap": jnp.asarray(tap, BF16), "tap_t": jnp.asarray(tap.T, BF16)}
    vectors = weights["small"][27:42].astype(F32)
    row = row_index.astype(jnp.int32).reshape(1)
    images = pixels.shape[0]
    parts = 1
    size = images // parts
    image_total = images * lax.axis_size("img") * 1.0
    head_w = weights["w_head"].astype(F32)
    head_b = weights["b_head"].astype(F32)

    ids = jnp.arange(images)
    widths = extents[:, 1]
    ahead = (widths[None, :] > widths[:, None]) | ((widths[None, :] == widths[:, None]) & (ids[None, :] < ids[:, None]))
    places = jnp.sum(ahead.astype(jnp.int32), axis=1)
    chosen = places[None, :] == ids[:, None]
    order = jnp.sum(jnp.where(chosen, ids[None, :], 0), axis=1)
    ext = jnp.sum(jnp.where(chosen[:, :, None], extents[None], 0), axis=1)

    log_teacher = jax.nn.log_softmax(teacher, axis=-1)
    pixel_view = jnp.transpose(pixels, (0, 2, 3, 1, 4))
    saved = []
    for part in range(parts):
        first, last, nsel, kvt, below, own = call_edge(ext, row, order, pixel_view, consts, wts, size, part * size)
        got = shifted(below, "row", 1)
        kv = lax.all_gather(call_pool_norm(own, got, wts["vec"]), "row", axis=0)
        top = shifted(last, "row", 1)
        bot = shifted(first, "row", -1)
        names = sorted(wts)
        after, log_teacher, *values = together(ext, log_teacher, *[wts[name] for name in names])
        wts = dict(zip(names, values))
        patches, x0, q = call_embed(after, row, order, pixel_view, consts, wts, size, part * size)
        saved.append(dict(patches=patches, x0=x0, q=q, top=top, bot=bot, nsel=nsel, kvt=kvt, own=own, got=got, kv=kv))
    for part in range(parts):
        s = saved[part]
        s["fwd"] = call_forward(ext, row, s["q"], s["top"], s["bot"], s["x0"], s["kv"], wts, part * size)
    total = {}

    def add(name, value):
        total[name] = total[name] + value if name in total else value

    sorted_local = jnp.sum(jnp.concatenate([s["fwd"][-1] for s in saved], axis=0), axis=-1)
    local = jnp.sum(jnp.where(chosen[:, :, None], sorted_local[:, None, :], 0.0), axis=0)
    everywhere = summed(local, "row")
    counts = (extents[:, 0] * extents[:, 1]).astype(F32)[:, None]
    pooled = (everywhere * vectors[13] + counts * vectors[14]) / counts

    def loss_of(pooled_now, w, b):
        return image_loss(pooled_now, w, b, log_teacher, labels, image_total)

    loss_value, loss_back = jax.vjp(loss_of, pooled, head_w, head_b)
    grad_pooled, total["w_head"], total["b_head"] = loss_back(jnp.ones_like(loss_value))
    gvec = grad_pooled / counts
    local_count = jnp.where(row_index * ROWS < extents[:, 0], ROWS * extents[:, 1], 0).astype(F32)[:, None]
    total["g_three"] = jnp.sum(gvec * local, axis=0)
    total["b_three"] = jnp.sum(gvec * local_count, axis=0)
    gvec = jnp.sum(jnp.where(chosen[:, :, None], gvec[None], 0.0), axis=1)[:, :, None]
    for part in range(parts):
        s = saved[part]
        s["bwd"] = call_backward(ext, row, s["fwd"][:-1], s["q"], s["top"], s["bot"], s["kv"], gvec[part * size : part * size + size], wts, part * size)
    for part in range(parts):
        s = saved[part]
        dx1, dq, up, down, dkv, *sums = s["bwd"]
        for bit in range(bit_count(key_rows)):
            if bit == 1:
                dkv, up, down = together(dkv, up, down)
                rtop = shifted(down, "row", 1)
                rbot = shifted(up, "row", -1)
            dkv = scatter_step(dkv, "row", bit)
            if bit == 1:
                dkv, *sums = together(dkv, *sums)
        for name, value in zip(("a2", "a1", "ap", "av", "ak", "ar"), sums):
            add(name, value)
        grad_kv = dkv[0]
        pre, pool_sums = call_pool_back(s["own"], s["got"], grad_kv, wts["vec"])
        add("pool_sums", pool_sums)
        under = shifted(pre.astype(BF16), "row", -1)
        aq, akv, apatch, av1, akt = call_embed_back(
            ext, row, s["patches"], dq, dx1, rtop, rbot, s["nsel"], s["kvt"], pre, under, consts, wts, part * size)
        for name, value in (("aq", aq), ("akv", akv), ("apatch", apatch), ("av1", av1), ("akt", akt)):
            add(name, value)

    t = total
    lead = jnp.where(row_lead, 1.0, 0.0)
    av, av1 = jnp.sum(t["av"], axis=-1), jnp.sum(t["av1"], axis=-1)
    pool_sums = jnp.sum(t["pool_sums"], axis=-1)
    rel_rows, rel_cols = relative_windows_back(t["ar"], row_index, key_rows)
    taps = jnp.sum((t["akt"].reshape(2, DIM, 3, 4, 32) * tap_keep())[:, :, :, :3], axis=-1)
    kernels = jnp.concatenate([jnp.sum(t["ak"], axis=-1), jnp.transpose(taps, (0, 2, 3, 1)).reshape(18, DIM)], axis=0)
    grad_vectors = jnp.stack([
        av1[0], av1[1], av1[2], av[2], av[3], pool_sums[0], pool_sums[1], pool_sums[2], pool_sums[3],
        t["ap"][DIM], av[0], av[1], t["a2"][MLP], t["g_three"], t["b_three"]])
    pieces = [
        patch_rows_back(t["apatch"]),
        jnp.concatenate([t["aq"][:DIM], t["akv"][:DIM]], axis=1),
        t["ap"][:DIM],
        t["a1"][:DIM],
        t["a2"][:MLP],
        t["w_head"] * lead,
        rel_rows,
        rel_cols,
        kernels,
        grad_vectors,
        t["aq"][DIM],
        t["akv"][DIM],
        t["a1"][DIM],
        t["b_head"] * lead,
    ]
    joined = jnp.concatenate([piece.reshape(-1) for piece in pieces])
    grad_flat = jnp.pad(joined, (0, full_params.shape[0] - joined.shape[0]))
    shares, loss_sum = sum_grads(grad_flat, loss_value)
    norm_sq = summed(jnp.sum(shares * shares), "row")
    lines = flat_params.shape[0] // 128
    grad_shard = lax.dynamic_slice_in_dim(shares, lax.axis_index("img") * lines, lines, 0).reshape(-1)
    grad_norm = jnp.sqrt(norm_sq)
    clip_factor = jnp.minimum(1.0, CLIP_NORM / (grad_norm + 1e-06))
    clipped = grad_shard * clip_factor
    moment_one = BETA_FIRST * first_moment + (1.0 - BETA_FIRST) * clipped
    moment_two = BETA_SECOND * second_moment + (1.0 - BETA_SECOND) * clipped * clipped
    fix_one = 1.0 - BETA_FIRST**STEP
    fix_two = 1.0 - BETA_SECOND**STEP
    update = moment_one / fix_one / (jnp.sqrt(moment_two / fix_two) + ADAM_EPS) + WEIGHT_DECAY * flat_params
    new_params = flat_params - LEARN_RATE * update
    return (new_params, moment_one, moment_two, grad_norm, loss_sum)


def solution(mesh):
    placed = (
        P(("img", "row")),
        P(("img", "row")),
        P(("img", "row")),
        P("img", "row", None, None, None),
        P("img", None),
        P("img"),
        P("img", None),
    )
    return jax.shard_map(
        body,
        mesh=mesh,
        in_specs=placed,
        out_specs=(P(("img", "row")), P(("img", "row")), P(("img", "row")), P(), P()),
        check_vma=False,
    )
```

```python
import functools

import jax
import jax.numpy as jnp
import numpy as np
from jax import lax
from jax.experimental import pallas as pl
from jax.experimental.pallas import tpu as pltpu
from jax.sharding import PartitionSpec as P

DIM = 96
MLP = 384
CLASSES = 1000
PATCH = 7
ROWS = 8
STEP = 7
CANVAS_W = 256

HIGHEST_PREC = lax.Precision.HIGHEST
CLIP_NORM = 0.02
LEARN_RATE = 0.05
WEIGHT_DECAY = 0.05
BETA_FIRST = 0.5
BETA_SECOND = 0.5
ADAM_EPS = 1e-08
NORM_EPS = 1e-06
NEG_FILL = -1e30

F32 = jnp.float32
BF16 = jnp.bfloat16
SCALE = DIM ** (-0.5)
EXP2_SCALE = SCALE * 1.4426950408889634

TOKENS = ROWS * CANVAS_W
PAIR = 512
PAIRS = TOKENS // PAIR
TILES = CANVAS_W // 32
GROUP = 2
WIDE = 4
PADDED = TOKENS + 512
WIN = 40
PATCH_ROWS = 256
VMEM_BYTES = 56 * 1024 * 1024


def deinterleave_matrix():
    out = np.zeros((4, 128, 4, 4, 32), np.float32)
    for row in range(4):
        for phase in range(4):
            for col in range(32):
                out[row, 4 * col + phase, phase, row, col] = 1.0
    return out.reshape(512, 512)


def tap_matrix():
    out = np.zeros((CANVAS_W, 128), np.float32)
    for tap in range(3):
        for key in range(32):
            col = 8 * key + tap - 1
            if col >= 0:
                out[col, tap * 32 + key] = 1.0
    return out


def dot(a, b):
    return jnp.dot(a, b, preferred_element_type=F32)


def dot_nt(a, b):
    return lax.dot_general(a, b, (((1,), (1,)), ((), ())), preferred_element_type=F32)


def normalized(x):
    mean = jnp.sum(x, axis=0, keepdims=True) * (1.0 / DIM)
    centered = x - mean
    var = jnp.sum(centered * centered, axis=0, keepdims=True) * (1.0 / DIM)
    rstd = lax.rsqrt(var + NORM_EPS)
    return centered * rstd, rstd


def norm_back(grad, hat, rstd, gain):
    inner = grad * gain
    mean_one = jnp.sum(inner, axis=0, keepdims=True) * (1.0 / DIM)
    mean_two = jnp.sum(inner * hat, axis=0, keepdims=True) * (1.0 / DIM)
    return rstd * (inner - mean_one - hat * mean_two)


def by_lanes(fn, *arrays):
    parts = [fn(k, *(a[:, 128 * k : 128 * k + 128] for a in arrays)) for k in range(arrays[0].shape[1] // 128)]
    return tuple(jnp.concatenate(column, axis=1) for column in zip(*parts))


def by_blocks(fn, height, *arrays):
    rows = []
    for top in range(0, arrays[0].shape[0], height):
        rows.append(by_lanes(lambda k, *block: fn(slice(top, top + height), *block), *(a[top : top + height] for a in arrays)))
    return tuple(jnp.concatenate(column, axis=0) for column in zip(*rows))


def fold_lanes(x):
    total = x[:, 0:128]
    for k in range(1, x.shape[1] // 128):
        total = total + x[:, 128 * k : 128 * k + 128]
    return total


def place_of(index):
    return index + 27 if index < 15 else index - 15 if index < 42 else index


def column(vec_ref, index):
    place = place_of(index)
    return vec_ref[:, place : place + 1]


def fill_wide(wide_ref, vec_ref, indices):
    for k, index in enumerate(indices):
        wide_ref[k] = jnp.broadcast_to(column(vec_ref, index), (DIM, 128))


def fill_taps(taps_ref, vec_ref):
    lane = lane_ids(128, DIM)
    for member in range(2):
        for r in range(3):
            block = jnp.zeros((DIM, 128), F32)
            for c in range(3):
                block = jnp.where((lane >> 5) == c, column(vec_ref, 24 + 9 * member + 3 * r + c), block)
            taps_ref[DIM * member : DIM * member + DIM, 128 * r : 128 * r + 128] = jnp.where(lane == 0, 0.0, block)


def fill_bias(bias_ref, vec_ref):
    for k in range(MLP // DIM):
        bias_ref[DIM * k : DIM * k + DIM] = jnp.broadcast_to(vec_ref[:, 45 + k : 46 + k], (DIM, 128))


def fill_transpose(dst_ref, src_ref):
    rows, cols = src_ref.shape
    value = src_ref[...].astype(F32)
    value = jnp.pad(value, ((0, -rows % 128), (0, -cols % 128)))
    dst_ref[...] = jnp.transpose(value)[:cols, :rows].astype(BF16)


def wide(wide_ref, k, width=PAIR):
    return jnp.concatenate([wide_ref[k]] * (width // 128), axis=1)


def lane_ids(width, rows=1):
    return lax.broadcasted_iota(jnp.int32, (rows, width), 1)


def pair_mask(pair, breadths, row_oks):
    lane = lane_ids(PAIR)
    col = pair * 64 + (lane >> 8) * 32 + (lane & 31)
    return jnp.concatenate([jnp.where((col < w) & ok, 1.0, 0.0).astype(F32) for w, ok in zip(breadths, row_oks)], axis=1)


def pair_lanes(pair, base=0):
    return pl.ds(pl.multiple_of(pair * PAIR + base, 128), PAIR)


def load_pair(ref, pair):
    lanes = pair_lanes(pair)
    return jnp.concatenate([ref[g, :, lanes] for g in range(ref.shape[0])], axis=1)


def store_pair(ref, pair, value, base=0):
    for g in range(value.shape[1] // PAIR):
        ref[g, :, pair_lanes(pair, base)] = value[:, PAIR * g : PAIR * g + PAIR]


def by_image(value):
    return [value[:, PAIR * g : PAIR * g + PAIR] for g in range(GROUP)]


def pair_count(breadths):
    widest = breadths[0]
    for breadth in breadths[1:]:
        widest = jnp.maximum(widest, breadth)
    return jnp.minimum((widest >> 6) + 1, PAIRS)


def group_extents(ext_ref, row_ref, offset, group=None, size=GROUP):
    group = pl.program_id(0) if group is None else group
    images = [group * size + g for g in range(size)]
    heights = [ext_ref[offset + image, 0] for image in images]
    breadths = [ext_ref[offset + image, 1] for image in images]
    return images, heights, breadths, [row_ref[0] * ROWS < height for height in heights]


def col_shifts(window, base):
    lane = lane_ids(128, window.shape[0])
    here = window[:, base : base + 128]
    before = window[:, base - 256 : base - 128]
    after = window[:, base + 256 : base + 384]
    left = jnp.where((lane & 31) == 0, pltpu.roll(before, 97, 1), pltpu.roll(here, 1, 1))
    right = jnp.where((lane & 31) == 31, pltpu.roll(after, 31, 1), pltpu.roll(here, 127, 1))
    return left.astype(F32), here.astype(F32), right.astype(F32)


def rows_down(first, second, entering):
    lane = lane_ids(128, first.shape[0])
    a, b = pltpu.roll(first, 32, 1), pltpu.roll(second, 32, 1)
    return jnp.where(lane < 32, entering, a), jnp.where(lane < 32, a, b), b


def rows_up(first, second, entering):
    lane = lane_ids(128, first.shape[0])
    a, b = pltpu.roll(first, 96, 1), pltpu.roll(second, 96, 1)
    return jnp.where(lane >= 96, b, a), jnp.where(lane >= 96, entering, b), a


def spread_halo(dst_ref, halo, target):
    for tile in range(TILES):
        block = halo[:, 128 * (tile // 4) : 128 * (tile // 4) + 128]
        shift = (target - 32 * (tile % 4)) % 128
        dst_ref[:, 128 * tile : 128 * tile + 128] = pltpu.roll(block, shift, 1) if shift else block


def store_lanes(dst_ref, value, image):
    place = image & 3
    lane = lane_ids(128, value.shape[0])
    dst_ref[...] = jnp.where((lane >> 5) == place, pltpu.roll(value, place * 32, 1), dst_ref[...])


def take_lanes(value, image, target):
    return pltpu.roll(value, (4 + target - (image & 3)) * 32 & 127, 1)


def gather_halo(src_ref, target):
    lane = lane_ids(128, DIM)
    blocks = []
    for half in range(2):
        total = None
        for k in range(4):
            tile = 4 * half + k
            block = src_ref[:, 128 * tile : 128 * tile + 128]
            shift = (32 * k - target) % 128
            block = pltpu.roll(block, shift, 1) if shift else block
            total = block if total is None else jnp.where((lane >> 5) == k, block, total)
        blocks.append(total)
    return jnp.concatenate(blocks, axis=1)


def reverse_bits(value, count):
    result = 0
    for bit in range(count.bit_length() - 1):
        result = result * 2 + ((value >> bit) & 1)
    return result


def key_tables(kv_ref, image, key_rows, height, breadth, ka_ref, kn_ref):
    lane = lane_ids(128, 2 * DIM)
    blocks = []
    for i in range(0, key_rows, 4):
        block = take_lanes(kv_ref[i].astype(F32), image, 0)
        for k in range(1, 4):
            block = jnp.where((lane >> 5) == k, take_lanes(kv_ref[i + k].astype(F32), image, k), block)
        blocks.append(block)
    both = jnp.concatenate(blocks, axis=1)
    total = key_rows * 32
    more = aug_rows(key_rows)
    rank = lax.broadcasted_iota(jnp.int32, (more, total), 0)
    key = lax.broadcasted_iota(jnp.int32, (more, total), 1)
    key_r, key_c = key >> 5, key & 31
    half = key_rows + 32
    low = rank >= half
    rank_in = jnp.where(low, rank - half, rank)
    hit = rank_in == jnp.where(rank_in < key_rows, key_r, key_c + key_rows)
    invalid = (key_r * ROWS >= height) | (key_c * ROWS >= breadth)
    table = jnp.where(rank < 2 * half, jnp.where(hit, 1.0, 0.0), 0.0)
    table = jnp.where((rank == 2 * half) & invalid, NEG_FILL, table)
    full = jnp.concatenate([both[:DIM], table, jnp.zeros((256 - DIM - more, total), F32)], axis=0)
    ka_ref[...] = full[: DIM + more].astype(BF16)
    kn_ref[...] = jnp.transpose(full).astype(BF16)
    return both[DIM:]


def aug_rows(key_rows):
    return 2 * key_rows + 64 + 16


def pixel_rows(pix_ref, s_ref):
    for a in range(4):
        for ch in range(3):
            block = pix_ref[0, a, ch].astype(F32)
            for tile in range(TILES):
                s_ref[tile, pl.ds(4 * a + ch, ROWS, stride=16), :] = block[:, 128 * tile : 128 * tile + 128]
    for a in range(3):
        for ch in range(3):
            block = pix_ref[0, 4 + a, ch].astype(F32)
            for tile in range(TILES):
                s_ref[tile, 128 + 4 * a + ch : 129 + 4 * a + ch, :] = block[ROWS - 1 : ROWS, 128 * tile : 128 * tile + 128]


def patch_blocks(s_ref, perm, shifted, sets):
    rows = [s_ref[tile] for tile in range(TILES)]
    if shifted:
        first = lane_ids(128, 144) < 4
        rolled = [pltpu.roll(block, 4, 1) for block in rows]
        rows = [jnp.where(first, rolled[tile - 1] if tile else 0.0, rolled[tile]) for tile in range(TILES)]
    rows = [block.astype(BF16) for block in rows]
    stack = []
    for chosen in sets:
        for tile in range(TILES):
            stack.append(jnp.concatenate([rows[tile][16 * r : 16 * r + 16] for r in chosen], axis=1))
    return dot(jnp.concatenate(stack, axis=0), perm).astype(BF16)


def edge_kernel(ext_ref, row_ref, order_ref, *refs, offset):
    pix_refs, refs = refs[:WIDE], refs[WIDE:]
    (perm_ref, tap_ref, wp_ref, wqkv_ref, vec_ref,
     first_ref, last_ref, nsel_ref, kvt_ref, below_ref, own_ref, s_ref, p_ref, wide_ref, kexp_ref) = refs
    images, heights, breadths, row_oks = group_extents(ext_ref, row_ref, offset, size=WIDE)

    @pl.when(pl.program_id(0) == 0)
    def _():
        s_ref[...] = jnp.zeros_like(s_ref)
        fill_wide(wide_ref, vec_ref, [0, 1, 2, 42, 43, 44])
        fill_taps(kexp_ref, vec_ref)

    lane = lane_ids(1024)
    masks = []
    for g in range(WIDE):
        pixel_rows(pix_refs[g], s_ref)
        for shifted in range(2):
            out = patch_blocks(s_ref, perm_ref[...], shifted, ((7, 0, 1, 1), (8, 1, 2, 2)))
            for half in range(2):
                for tile in range(TILES):
                    block = out[128 * half + 16 * tile : 128 * half + 16 * tile + 16]
                    for phase in range(4):
                        top = 128 * shifted + 64 * half + 16 * phase
                        p_ref[top : top + 16, 1024 * g + 128 * tile : 1024 * g + 128 * tile + 128] = block[:, 128 * phase : 128 * phase + 128]
        col = (lane >> 7) * 32 + (lane & 31)
        masks.append(jnp.where((col < breadths[g]) & row_oks[g], 1.0, 0.0).astype(F32))

    def first_norm(k, embed, mask):
        hat, _ = normalized((embed + wide_ref[0]) * mask)
        return ((hat * wide_ref[1] + wide_ref[2]).astype(BF16),)

    (normed,) = by_lanes(first_norm, dot(wp_ref[...], p_ref[...]), jnp.concatenate(masks, axis=1))
    rows = []
    for slot in range(3):
        rows.append(jnp.concatenate([gather_halo(normed[:, 1024 * g : 1024 * g + 1024], 32 * slot) for g in range(WIDE)], axis=1))
    edge = dot(wqkv_ref[0:DIM, :], jnp.concatenate(rows[:2], axis=1))
    (edge,) = by_lanes(lambda k, out: ((out + wide_ref[3]).astype(BF16),), edge)
    nsel = dot(jnp.concatenate([row[:, CANVAS_W * g : CANVAS_W * g + CANVAS_W] for g in range(WIDE) for row in rows], axis=0), tap_ref[...])
    nsel = jnp.concatenate([nsel[DIM * k : DIM * k + DIM] for k in range(3 * WIDE)], axis=1).astype(BF16)
    bias = jnp.concatenate([wide_ref[4], wide_ref[5]], axis=0)
    (taps,) = by_lanes(lambda k, out: ((out + bias).astype(BF16),), dot(wqkv_ref[DIM : 3 * DIM, :], nsel))
    for g in range(WIDE):
        last_ref[g] = edge[:, CANVAS_W * g : CANVAS_W * g + CANVAS_W]
        first_ref[g] = edge[:, CANVAS_W * (WIDE + g) : CANVAS_W * (WIDE + g) + CANVAS_W]
        nsel_ref[g] = nsel[:, 384 * g : 384 * g + 384]
        kvt_ref[g] = taps[:, 384 * g : 384 * g + 384]
        product = taps[:, 384 * g : 384 * g + 384].astype(F32) * kexp_ref[...]
        sums = []
        for k in range(3):
            part = product[:, 128 * k : 128 * k + 128]
            sums.append(part + pltpu.roll(part, 96, 1) + pltpu.roll(part, 64, 1))
        store_lanes(below_ref, sums[0], images[g])
        store_lanes(own_ref, sums[1] + sums[2], images[g])


def embed_kernel(ext_ref, row_ref, order_ref, *refs, offset):
    pix_refs, refs = refs[:WIDE], refs[WIDE:]
    perm_ref, wp_ref, wqkv_ref, vec_ref, patch_ref, x0_ref, q_ref, s_ref, wide_ref = refs
    images, heights, breadths, row_oks = group_extents(ext_ref, row_ref, offset, size=WIDE)

    @pl.when(pl.program_id(0) == 0)
    def _():
        s_ref[...] = jnp.zeros_like(s_ref)
        fill_wide(wide_ref, vec_ref, [0, 1, 2, 42])

    for g in range(WIDE):
        pixel_rows(pix_refs[g], s_ref)
        for shifted in range(2):
            out = patch_blocks(s_ref, perm_ref[...], shifted, ((0, 1, 2, 3), (4, 5, 6, 7), (1, 2, 3, 4), (5, 6, 7, 8)))
            for which in range(4):
                half, side = which // 2, which % 2
                for tile in range(TILES):
                    block = out[128 * which + 16 * tile : 128 * which + 16 * tile + 16]
                    for phase in range(4):
                        top = 128 * shifted + 64 * half + 16 * phase
                        patch_ref[g, top : top + 16, 256 * tile + 128 * side : 256 * tile + 128 * side + 128] = block[
                            :, 128 * phase : 128 * phase + 128]

    count = pair_count(breadths)

    def active(pair, carry):
        def first_norm(k, embed, mask):
            x0 = (embed + wide_ref[0]) * mask
            hat, _ = normalized(x0)
            return x0, (hat * wide_ref[1] + wide_ref[2]).astype(BF16)

        x0, normed = by_lanes(first_norm, dot(wp_ref[...], load_pair(patch_ref, pair)), pair_mask(pair, breadths, row_oks))
        store_pair(x0_ref, pair, x0)
        (query,) = by_lanes(lambda k, out: ((out + wide_ref[3]).astype(BF16),), dot(wqkv_ref[0:DIM, :], normed))
        store_pair(q_ref, pair, query, 256)
        return carry

    def idle(pair, carry):
        for g in range(WIDE):
            q_ref[g, :, pair_lanes(pair, 256)] = jnp.zeros((DIM, PAIR), BF16)
        return carry

    lax.fori_loop(0, count, active, 0)
    lax.fori_loop(count, PAIRS, idle, 0)
    for g in range(WIDE):
        q_ref[g, :, 0:256] = jnp.zeros((DIM, 256), BF16)
        q_ref[g, :, 256 + TOKENS : 512 + TOKENS] = jnp.zeros((DIM, 256), BF16)


def key_lanes(*lead, size=GROUP):
    return pl.BlockSpec(lead + (128,), lambda i, *_: (0,) * len(lead) + (i * size >> 2,))


def specs(size=GROUP):
    whole = lambda *shape: pl.BlockSpec(shape, lambda i, *_: (0,) * len(shape))
    per = lambda *shape: pl.BlockSpec((size,) + shape, lambda i, *_: (i,) + (0,) * len(shape))
    return whole, per


def pixel_specs(offset):
    return [pl.BlockSpec((1, PATCH, 3, ROWS, 1024), lambda i, ext, row, order, g=g: (order[offset + i * WIDE + g], 0, 0, 0, 0)) for g in range(WIDE)]


def call_edge(ext, row, order, pixels, consts, wts, images, offset):
    whole, per = specs(WIDE)
    shapes = [(DIM, CANVAS_W), (DIM, CANVAS_W), (DIM, 384), (2 * DIM, 384)]
    return pl.pallas_call(
        functools.partial(edge_kernel, offset=offset),
        grid_spec=pltpu.PrefetchScalarGridSpec(
            num_scalar_prefetch=3, grid=(images // WIDE,),
            in_specs=pixel_specs(offset) + [
                whole(512, 512), whole(CANVAS_W, 128), whole(DIM, PATCH_ROWS), whole(3 * DIM, DIM), whole(DIM, 64)],
            out_specs=[per(*s) for s in shapes] + [key_lanes(2 * DIM, size=WIDE)] * 2,
            scratch_shapes=[pltpu.VMEM((TILES, 144, 128), F32), pltpu.VMEM((PATCH_ROWS, 1024 * WIDE), BF16), pltpu.VMEM((6, DIM, 128), F32),
                            pltpu.VMEM((2 * DIM, 384), F32)]),
        out_shape=[jax.ShapeDtypeStruct((images,) + s, BF16) for s in shapes]
        + [jax.ShapeDtypeStruct((2 * DIM, 32 * images), F32)] * 2,
        compiler_params=pltpu.CompilerParams(vmem_limit_bytes=VMEM_BYTES),
        cost_estimate=pl.CostEstimate(flops=images * 1_000_000_000, bytes_accessed=images * 1_000_000, transcendentals=0),
        name="edge",
    )(ext, row, order, *[pixels] * WIDE, consts["perm"], consts["tap"], wts["wp"], wts["wqkv_t"], wts["vec"])


def call_embed(ext, row, order, pixels, consts, wts, images, offset):
    whole, per = specs(WIDE)
    shapes = [((PATCH_ROWS, TOKENS), BF16), ((DIM, TOKENS), F32), ((DIM, PADDED), BF16)]
    return pl.pallas_call(
        functools.partial(embed_kernel, offset=offset),
        grid_spec=pltpu.PrefetchScalarGridSpec(
            num_scalar_prefetch=3, grid=(images // WIDE,),
            in_specs=pixel_specs(offset) + [whole(512, 512), whole(DIM, PATCH_ROWS), whole(3 * DIM, DIM), whole(DIM, 64)],
            out_specs=[per(*s) for s, _ in shapes],
            scratch_shapes=[pltpu.VMEM((TILES, 144, 128), F32), pltpu.VMEM((4, DIM, 128), F32)]),
        out_shape=[jax.ShapeDtypeStruct((images,) + s, t) for s, t in shapes],
        compiler_params=pltpu.CompilerParams(vmem_limit_bytes=VMEM_BYTES),
        cost_estimate=pl.CostEstimate(flops=images * 2_000_000_000, bytes_accessed=images * 4_000_000, transcendentals=0),
        name="embed",
    )(ext, row, order, *[pixels] * WIDE, consts["perm"], wts["wp"], wts["wqkv_t"], wts["vec"])


def pool_norm_kernel(own_ref, got_ref, vec_ref, kv_ref):
    for member in range(2):
        part = slice(member * DIM, member * DIM + DIM)
        hat, _ = normalized(own_ref[part] + got_ref[part])
        kv_ref[part] = (hat * column(vec_ref, 5 + 2 * member) + column(vec_ref, 6 + 2 * member)).astype(BF16)


def call_pool_norm(own, got, vec):
    return pl.pallas_call(
        pool_norm_kernel, out_shape=jax.ShapeDtypeStruct(own.shape, BF16), name="pool_norm",
        cost_estimate=pl.CostEstimate(flops=own.size * 10, bytes_accessed=own.size * 10, transcendentals=0))(own, got, vec)


def pool_back_kernel(own_ref, got_ref, grad_ref, vec_ref, pre_ref, sums_ref):
    for member in range(2):
        part = slice(member * DIM, member * DIM + DIM)
        hat, rstd = normalized(own_ref[part] + got_ref[part])
        grad = grad_ref[part].astype(F32)
        pre_ref[part] = norm_back(grad, hat, rstd, column(vec_ref, 5 + 2 * member))
        sums_ref[2 * member] = fold_lanes(grad * hat)
        sums_ref[2 * member + 1] = fold_lanes(grad)


def call_pool_back(own, got, grad, vec):
    return pl.pallas_call(
        pool_back_kernel,
        out_shape=[jax.ShapeDtypeStruct(own.shape, F32), jax.ShapeDtypeStruct((4, DIM, 128), F32)], name="pool_back",
        cost_estimate=pl.CostEstimate(flops=own.size * 20, bytes_accessed=own.size * 16, transcendentals=0))(own, got, grad, vec)


def lane_bit(lane, bit):
    return (lane & bit) != 0


def relative_terms(block, products, key_rows):
    lane = lane_ids(128, WIN)
    parts = [products[WIN * s : WIN * s + WIN] for s in range(8)]
    for bit in (1, 2, 4):
        chosen = lane_bit(lane, bit)
        parts = [jnp.where(chosen, parts[2 * k + 1], parts[2 * k]) for k in range(len(parts) // 2)]
    by_col = parts[0]
    for bit, step in ((8, 1), (16, 2)):
        by_col = jnp.where(lane_bit(lane, bit), by_col, pltpu.roll(by_col, WIN - step, 0))
    by_col = by_col[0:32] if block & 2 else by_col[4:36]
    lane = lane_ids(128, key_rows)
    rows = products[8 * WIN :]
    parts = [rows[key_rows * r : key_rows * r + key_rows] for r in range(4 * (block & 1), 4 * (block & 1) + 4)]
    for bit in (32, 64):
        chosen = lane_bit(lane, bit)
        parts = [jnp.where(chosen, parts[2 * k + 1], parts[2 * k]) for k in range(len(parts) // 2)]
    return jnp.concatenate([parts[0], by_col], axis=0)


def relative_spread(block, grad_terms, key_rows):
    lane = lane_ids(128, WIN)
    by_row = grad_terms[:key_rows]
    if block & 2:
        pieces = [grad_terms[key_rows:], jnp.zeros((WIN - 32, 128), F32)]
    else:
        pieces = [jnp.zeros((4, 128), F32), grad_terms[key_rows:], jnp.zeros((WIN - 36, 128), F32)]
    by_col = jnp.concatenate(pieces, axis=0)
    for bit, step in ((8, 1), (16, 2)):
        by_col = jnp.where(lane_bit(lane, bit), by_col, pltpu.roll(by_col, step, 0))
    parts = [jnp.where((lane & 7) == s, by_col, 0.0) for s in range(8)]
    lane = lane_ids(128, key_rows)
    for r in range(8):
        hit = (lane >> 5) == r - 4 * (block & 1)
        parts.append(jnp.where(hit, by_row, 0.0) if r // 4 == block & 1 else jnp.zeros((key_rows, 128), F32))
    return jnp.concatenate(parts, axis=0).astype(BF16)


def gelu_parts(hidden):
    cumulative = 0.5 + 0.5 * lax.erf(hidden * 0.7071067811865476)
    slope = cumulative + hidden * (jnp.exp2(hidden * hidden * (-0.5 * 1.4426950408889634)) * 0.3989422804014327)
    return (hidden * cumulative).astype(BF16), slope.astype(BF16)


def forward_kernel(ext_ref, row_ref, q_ref, top_ref, bot_ref, x0_ref, kv_ref, vec_ref, rw_ref, wproj_ref, w1_ref, w2_ref,
                   hat_ref, query_ref, terms_ref, att_ref, act_ref, slope_ref, hat2_ref, hat3_ref, stat_ref, pool_ref, ka_ref, kn_ref, v_ref, ztop_ref, zbot_ref, pre_ref, wide_ref, wb1_ref, wprojt_ref, w1t_ref, w2t_ref,
                   *, offset, key_rows):
    images, heights, breadths, row_oks = group_extents(ext_ref, row_ref, offset)
    depth = DIM + aug_rows(key_rows)

    @pl.when(pl.program_id(0) == 0)
    def _():
        fill_wide(wide_ref, vec_ref, list(range(15, 24)) + [3, 4, 9, 10, 11, 12])
        fill_bias(wb1_ref, vec_ref)
        fill_transpose(wprojt_ref, wproj_ref)
        fill_transpose(w1t_ref, w1_ref)
        fill_transpose(w2t_ref, w2_ref)

    lane = lane_ids(CANVAS_W, DIM)
    for g in range(GROUP):
        v_ref[g] = key_tables(kv_ref, images[g], key_rows, heights[g], breadths[g], ka_ref, kn_ref.at[g]).astype(BF16)
        for halo_ref, dst_ref, tap_row, target in ((top_ref, ztop_ref, 0, 0), (bot_ref, zbot_ref, 2, 96)):
            halo = halo_ref[g].astype(F32)
            left = jnp.where(lane == 0, 0.0, pltpu.roll(halo, 1, 1))
            right = jnp.where(lane == CANVAS_W - 1, 0.0, pltpu.roll(halo, CANVAS_W - 1, 1))
            taps = [wide(wide_ref, 3 * tap_row + k, CANVAS_W) for k in range(3)]
            spread_halo(dst_ref.at[g], taps[0] * left + taps[1] * halo + taps[2] * right, target)
    pool_ref[...] = jnp.zeros_like(pool_ref)

    def step(pair, carry):
        for group in range(0, DIM, 16):
            part = slice(group, group + 16)
            taps = [wide_ref[k, part] for k in range(9)]
            for g in range(GROUP):
                window = q_ref[g, part, pl.ds(pl.multiple_of(pair * PAIR, 128), PAIR + 512)]
                for tile in range(2):
                    sums = []
                    for side in range(2):
                        shifts = col_shifts(window, 256 + 256 * tile + 128 * side)
                        sums.append([sum(taps[3 * r + c] * shifts[c] for c in range(3)) for r in range(3)])
                    halo = pl.ds(pl.multiple_of((2 * pair + tile) * 128, 128), 128)
                    down = rows_down(sums[0][0], sums[1][0], ztop_ref[g, part, halo])
                    up = rows_up(sums[0][2], sums[1][2], zbot_ref[g, part, halo])
                    for side in range(2):
                        base = PAIR * g + 256 * tile + 128 * side
                        pre_ref[part, base : base + 128] = sums[side][1] + down[side] + up[side]

        def query_of(k, pre):
            hat, rstd = normalized(pre)
            return hat.astype(BF16), (hat * wide_ref[9] + wide_ref[10]).astype(BF16), rstd

        hat, query, rstd = by_lanes(query_of, pre_ref[...])
        store_pair(hat_ref, pair, hat)
        store_pair(query_ref, pair, query)

        def extra_of(k, products):
            terms = relative_terms(k, products, key_rows) * (DIM**0.5)
            high = terms.astype(BF16).astype(F32)
            return (jnp.concatenate([high, terms - high, jnp.ones((16, 128), F32)], axis=0).astype(BF16),)

        (extra,) = by_lanes(extra_of, dot(rw_ref[pair], query))
        store_pair(terms_ref, pair, extra)

        def softmax(k, scores):
            peak = jnp.max(scores, axis=0, keepdims=True)
            weights = jnp.exp2((scores - peak) * EXP2_SCALE)
            inverse = 1.0 / jnp.sum(weights, axis=0, keepdims=True)
            return weights.astype(BF16), peak, inverse

        long_query = by_image(jnp.concatenate([query, extra], axis=0))
        scores = jnp.concatenate([dot(kn_ref[g, :, :depth], long_query[g]) for g in range(GROUP)], axis=1)
        probs, peak, inverse = by_lanes(softmax, scores)
        mixed = by_image(probs)
        mixed = jnp.concatenate([dot(v_ref[g], mixed[g]) for g in range(GROUP)], axis=1)
        attended = (mixed * inverse + query.astype(F32)).astype(BF16)
        store_pair(att_ref, pair, attended)

        def second_norm(k, x0, out):
            x1 = x0 + (out + wide_ref[11])
            hat, rstd = normalized(x1)
            return x1, (hat * wide_ref[12] + wide_ref[13]).astype(BF16), hat.astype(BF16), rstd

        x1, normed, hat_two, rstd_two = by_lanes(second_norm, load_pair(x0_ref, pair), dot(wprojt_ref[...], attended))
        store_pair(hat2_ref, pair, hat_two)
        act, slope = by_blocks(lambda part, hidden: gelu_parts(hidden + wb1_ref[part]), 64, dot(w1t_ref[...], normed))
        store_pair(act_ref, pair, act)
        store_pair(slope_ref, pair, slope)

        def third_norm(k, x1, out, mask):
            hat, rstd = normalized(x1 + (out + wide_ref[14]))
            return hat * mask, hat.astype(BF16), rstd

        kept, hat_three, rstd_three = by_lanes(third_norm, x1, dot(w2t_ref[...], act), pair_mask(pair, breadths, row_oks))
        store_pair(hat3_ref, pair, hat_three)
        stats = [peak, inverse, rstd, rstd_two, rstd_three, jnp.zeros((3, GROUP * PAIR), F32)]
        store_pair(stat_ref, pair, jnp.concatenate(stats, axis=0))
        for g, part in enumerate(by_image(kept)):
            pool_ref[g] += fold_lanes(part)
        return carry

    lax.fori_loop(0, pair_count(breadths), step, 0)


def call_forward(ext, row, q, top, bot, x0, kv, wts, offset):
    whole, per = specs()
    images, key_rows = q.shape[0], kv.shape[0]
    more = aug_rows(key_rows)
    shapes = [(rows, BF16) for rows in (DIM, DIM, more, DIM, MLP, MLP, DIM, DIM)]
    shapes = [((rows, TOKENS), kind) for rows, kind in shapes] + [((8, TOKENS), F32), ((DIM, 128), F32)]
    keys = key_rows * 32
    return pl.pallas_call(
        functools.partial(forward_kernel, offset=offset, key_rows=key_rows),
        grid_spec=pltpu.PrefetchScalarGridSpec(
            num_scalar_prefetch=2, grid=(images // GROUP,),
            in_specs=[
                per(DIM, PADDED), per(DIM, CANVAS_W), per(DIM, CANVAS_W), per(DIM, TOKENS),
                key_lanes(key_rows, 2 * DIM),
                whole(DIM, 64), whole(PAIRS, 8 * WIN + 8 * key_rows, DIM), whole(DIM, DIM), whole(DIM, MLP), whole(MLP, DIM)],
            out_specs=[per(*s) for s, _ in shapes],
            scratch_shapes=[
                pltpu.VMEM((DIM + more, keys), BF16), pltpu.VMEM((GROUP, keys, 256), BF16), pltpu.VMEM((GROUP, DIM, keys), BF16),
                pltpu.VMEM((GROUP, DIM, 1024), F32), pltpu.VMEM((GROUP, DIM, 1024), F32), pltpu.VMEM((DIM, GROUP * PAIR), F32),
                pltpu.VMEM((15, DIM, 128), F32), pltpu.VMEM((MLP, 128), F32),
                pltpu.VMEM((DIM, DIM), BF16), pltpu.VMEM((MLP, DIM), BF16), pltpu.VMEM((DIM, MLP), BF16)]),
        out_shape=[jax.ShapeDtypeStruct((images,) + s, t) for s, t in shapes],
        compiler_params=pltpu.CompilerParams(vmem_limit_bytes=VMEM_BYTES),
        cost_estimate=pl.CostEstimate(flops=images * 5_000_000_000, bytes_accessed=images * 4_000_000, transcendentals=0),
        name="forward",
    )(ext, row, q, top, bot, x0, kv, wts["vec"], wts["rw"], wts["wproj"], wts["w1"], wts["w2"])


def backward_kernel(ext_ref, row_ref, hat_ref, query_ref, terms_ref, att_ref, act_ref, slope_ref, hat2_ref, hat3_ref, stat_ref, q_ref, top_ref, bot_ref, kv_ref,
                    gvec_ref, vec_ref, rwt_ref, wproj_ref, w1_ref, w2_ref,
                    dx1_ref, dq_ref, up_ref, down_ref, dkv_ref, a2_ref, a1_ref, ap_ref, av_ref, ak_ref, ar_ref,
                    ka_ref, kn_ref, vn_ref, dp_ref, qtop_ref, qbot_ref, ru_ref, rd_ref, dk_ref, dv_ref, wide_ref, *, offset, key_rows):
    now = pl.program_id(0)
    steps = pl.num_programs(0) - 1
    images, heights, breadths, row_oks = group_extents(ext_ref, row_ref, offset, jnp.minimum(now, steps - 1))
    _, _, former, _ = group_extents(ext_ref, row_ref, offset, jnp.maximum(now - 1, 0))
    depth = DIM + aug_rows(key_rows)
    count = jnp.where(now < steps, pair_count(breadths), 0)
    former_count = pair_count(former)
    dp_now, dp_former = now & 1, (now & 1) ^ 1

    @pl.when(pl.program_id(0) == 0)
    def _():
        for ref in (a2_ref, a1_ref, ap_ref, av_ref, ak_ref, ar_ref, ru_ref, rd_ref):
            ref[...] = jnp.zeros_like(ref)
        fill_wide(wide_ref, vec_ref, list(range(15, 24)) + [3, 10, 11, 13])
        dp_ref[...] = jnp.zeros_like(dp_ref)

    for g in range(GROUP):
        values = key_tables(kv_ref, images[g], key_rows, heights[g], breadths[g], ka_ref.at[g], kn_ref.at[g])
        padded_values = jnp.concatenate([values, jnp.zeros((128 - DIM, values.shape[1]), F32)], axis=0)
        vn_ref[g] = jnp.transpose(padded_values).astype(BF16)
        spread_halo(qtop_ref.at[g], top_ref[g], 0)
        spread_halo(qbot_ref.at[g], bot_ref[g], 96)
    for ref in (dk_ref, dv_ref, dp_ref.at[dp_now]):
        ref[...] = jnp.zeros_like(ref)

    def step(pair, carry):
        ones = jnp.ones((16, GROUP * PAIR), BF16)
        stat = load_pair(stat_ref, pair)

        def third_back(k, hat, stat, mask):
            grad = norm_back(gvec_ref[k * 128 // PAIR] * mask, hat.astype(F32), stat[4:5], wide_ref[12])
            return grad, grad.astype(BF16)

        grad_x2, grad_mlp = by_lanes(third_back, load_pair(hat3_ref, pair), stat, pair_mask(pair, breadths, row_oks))
        act = load_pair(act_ref, pair)
        a2_ref[...] += dot_nt(jnp.concatenate([act, ones], axis=0), grad_mlp)
        (grad_hidden,) = by_blocks(
            lambda part, grad, slope: ((grad * slope.astype(F32)).astype(BF16),), 64, dot(w2_ref[...], grad_mlp), load_pair(slope_ref, pair))
        hat_two = load_pair(hat2_ref, pair)
        (normed,) = by_lanes(lambda k, hat: ((hat.astype(F32) * wide_ref[10] + wide_ref[11]).astype(BF16),), hat_two)
        a1_ref[...] += dot_nt(jnp.concatenate([normed, ones], axis=0), grad_hidden)

        def second_back(k, grad, hat, stat, grad_x2):
            hat = hat.astype(F32)
            total = grad_x2 + norm_back(grad, hat, stat[3:4], wide_ref[10])
            return total.astype(BF16), grad * hat

        grad_normed = dot(w1_ref[...], grad_hidden)
        grad_proj, scaled = by_lanes(second_back, grad_normed, hat_two, stat, grad_x2)
        av_ref[0] += fold_lanes(scaled)
        av_ref[1] += fold_lanes(grad_normed)
        store_pair(dx1_ref, pair, grad_proj)
        attended = load_pair(att_ref, pair)
        ap_ref[...] += dot_nt(jnp.concatenate([attended, ones], axis=0), grad_proj)
        grad_att = dot(wproj_ref[...], grad_proj)
        grad_att_low = grad_att.astype(BF16)
        hat = load_pair(hat_ref, pair)
        query = load_pair(query_ref, pair)
        long_query = by_image(jnp.concatenate([query, load_pair(terms_ref, pair)], axis=0))
        scores = jnp.concatenate([dot(kn_ref[g, :, :depth], long_query[g]) for g in range(GROUP)], axis=1)
        low = by_image(grad_att_low)
        grad_probs = jnp.concatenate([dot(vn_ref[g, :, :DIM], low[g]) for g in range(GROUP)], axis=1)

        def softmax_back(k, scores, grad_probs, stat):
            probs = jnp.exp2((scores - stat[0:1]) * EXP2_SCALE) * stat[1:2]
            inner = jnp.sum(probs * grad_probs, axis=0, keepdims=True)
            return probs.astype(BF16), (probs * (grad_probs - inner)).astype(BF16)

        probs, grad_scores = by_lanes(softmax_back, scores, grad_probs, stat)
        probs, grad_scores, queries = by_image(probs), by_image(grad_scores), by_image(query)
        back = []
        for g in range(GROUP):
            back.append(dot(ka_ref[g, : DIM + key_rows + 32, :], grad_scores[g]))
            dv_ref[g] += dot_nt(low[g], probs[g])
            dk_ref[g] += dot_nt(queries[g], grad_scores[g])
        back = jnp.concatenate(back, axis=1)
        (spread,) = by_lanes(lambda k, terms: (relative_spread(k, terms, key_rows),), back[DIM:])
        ar_ref[pair] += dot_nt(spread, query)

        def query_back(k, grad_att, back, far, hat, stat):
            grad = grad_att + back * SCALE + far
            hat = hat.astype(F32)
            return norm_back(grad, hat, stat[2:3], wide_ref[9]), grad * hat, grad

        grad_pre, scaled, grad = by_lanes(query_back, grad_att, back[:DIM], dot(rwt_ref[pair], spread), hat, stat)
        av_ref[2] += fold_lanes(scaled)
        av_ref[3] += fold_lanes(grad)
        store_pair(dp_ref.at[dp_now], pair, grad_pre.astype(BF16), 256)
        return carry

    def pool_step(pair, carry):
        for group in range(0, DIM, 16):
            part = slice(group, group + 16)
            taps = [wide_ref[k, part] for k in range(9)]
            grads = [None] * 9
            for g in range(GROUP):
                window = dp_ref[dp_former, g, part, pl.ds(pl.multiple_of(pair * PAIR, 128), PAIR + 512)]
                for tile in range(2):
                    base = pair * PAIR + 256 * tile
                    halo = pl.ds(pl.multiple_of((2 * pair + tile) * 128, 128), 128)
                    query = [q_ref[g, part, pl.ds(pl.multiple_of(base + 256 + 128 * side, 128), 128)] for side in range(2)]
                    above = rows_down(query[0], query[1], qtop_ref[g, part, halo])
                    under = rows_up(query[0], query[1], qbot_ref[g, part, halo])
                    sums = []
                    for side in range(2):
                        left, here, right = col_shifts(window, 256 + 256 * tile + 128 * side)
                        shifts = (right, here, left)
                        sums.append([sum(taps[3 * r + c] * shifts[c] for c in range(3)) for r in range(3)])
                        for r, rows in enumerate((above[side], query[side], under[side])):
                            rows = rows.astype(F32)
                            for c in range(3):
                                term = shifts[c] * rows
                                grads[3 * r + c] = term if grads[3 * r + c] is None else grads[3 * r + c] + term
                    zero = jnp.zeros((16, 128), F32)
                    up = rows_up(sums[0][0], sums[1][0], zero)
                    down = rows_down(sums[0][2], sums[1][2], zero)
                    for side in range(2):
                        lanes = pl.ds(pl.multiple_of(base + 128 * side, 128), 128)
                        dq_ref[g, part, lanes] = (sums[side][1] + up[side] + down[side]).astype(BF16)
                    ru_ref[g, part, halo] = up[2].astype(BF16)
                    rd_ref[g, part, halo] = down[2].astype(BF16)
            for k in range(9):
                ak_ref[k, part] += grads[k]
        return carry

    def pool_idle(pair, carry):
        for ref in (ru_ref, rd_ref):
            for g in range(GROUP):
                ref[g, :, pl.ds(pl.multiple_of(pair * 256, 128), 256)] = jnp.zeros((DIM, 256), BF16)
        store_pair(dq_ref, pair, jnp.zeros((DIM, GROUP * PAIR), BF16))
        return carry

    def idle(pair, carry):
        store_pair(dx1_ref, pair, jnp.zeros((DIM, GROUP * PAIR), BF16))
        return carry

    lax.fori_loop(0, count, lambda pair, carry: step(pair, pool_step(pair, carry)), 0)
    lax.fori_loop(count, former_count, pool_step, 0)
    lax.fori_loop(former_count, PAIRS, pool_idle, 0)
    lax.fori_loop(jnp.where(now < steps, count, PAIRS), PAIRS, idle, 0)

    @pl.when(now < steps)
    def _():
        lane = lane_ids(128, 2 * DIM)
        for g in range(GROUP):
            for i in range(key_rows):
                block = slice(128 * (i // 4), 128 * (i // 4) + 128)
                value = jnp.concatenate([dk_ref[g, :, block] * SCALE, dv_ref[g, :, block]], axis=0)
                value = pltpu.roll(value, (4 + (images[g] & 3) - i % 4) * 32 & 127, 1)
                slot = reverse_bits(jnp.bitwise_xor(row_ref[0], i), key_rows)
                dkv_ref[slot] = jnp.where((lane >> 5) == (images[g] & 3), value, dkv_ref[slot])

    for g in range(GROUP):
        up_ref[g] = gather_halo(ru_ref.at[g], 96)
        down_ref[g] = gather_halo(rd_ref.at[g], 0)


def call_backward(ext, row, saved, q, top, bot, kv, gvec, wts, offset):
    whole, _ = specs()
    images, key_rows = q.shape[0], kv.shape[0]
    more = aug_rows(key_rows)
    keys = key_rows * 32
    window = 8 * WIN + 8 * key_rows
    steps = images // GROUP
    now = lambda *shape: pl.BlockSpec((GROUP,) + shape, lambda i, *_: (jnp.minimum(i, steps - 1),) + (0,) * len(shape))
    former = lambda *shape: pl.BlockSpec((GROUP,) + shape, lambda i, *_: (jnp.maximum(i - 1, 0),) + (0,) * len(shape))
    heads = pl.BlockSpec((key_rows, 2 * DIM, 128), lambda i, *_: (0, 0, jnp.minimum(i, steps - 1) * GROUP >> 2))
    shapes = [(DIM, TOKENS), (DIM, TOKENS), (DIM, CANVAS_W), (DIM, CANVAS_W)]
    sums = [(MLP + 16, DIM), (DIM + 16, MLP), (DIM + 16, DIM), (4, DIM, 128), (9, DIM, 128), (PAIRS, window, DIM)]
    return pl.pallas_call(
        functools.partial(backward_kernel, offset=offset, key_rows=key_rows),
        grid_spec=pltpu.PrefetchScalarGridSpec(
            num_scalar_prefetch=2, grid=(steps + 1,),
            in_specs=[now(rows, TOKENS) for rows in (DIM, DIM, more, DIM, MLP, MLP, DIM, DIM, 8)] + [
                former(DIM, PADDED), former(DIM, CANVAS_W), former(DIM, CANVAS_W), heads, now(DIM, 1), whole(DIM, 64), whole(PAIRS, DIM, window),
                whole(DIM, DIM), whole(DIM, MLP), whole(MLP, DIM)],
            out_specs=[now(*shapes[0])] + [former(*s) for s in shapes[1:]] + [heads] + [whole(*s) for s in sums],
            scratch_shapes=[
                pltpu.VMEM((GROUP, DIM + more, keys), BF16), pltpu.VMEM((GROUP, keys, 256), BF16), pltpu.VMEM((GROUP, keys, 128), BF16),
                pltpu.VMEM((2, GROUP, DIM, PADDED), BF16)] + [pltpu.VMEM((GROUP, DIM, 1024), BF16)] * 4
            + [pltpu.VMEM((GROUP, DIM, keys), F32)] * 2 + [pltpu.VMEM((13, DIM, 128), F32)]),
        out_shape=[jax.ShapeDtypeStruct((images,) + s, BF16) for s in shapes]
        + [jax.ShapeDtypeStruct((key_rows, 2 * DIM, 32 * images), F32)] + [jax.ShapeDtypeStruct(s, F32) for s in sums],
        compiler_params=pltpu.CompilerParams(vmem_limit_bytes=VMEM_BYTES),
        cost_estimate=pl.CostEstimate(flops=images * 12_000_000_000, bytes_accessed=images * 6_000_000, transcendentals=0),
        name="backward",
    )(ext, row, *saved, q, top, bot, kv, gvec, wts["vec"], wts["rw_t"], wts["wproj"], wts["w1"], wts["w2"])


def embed_back_kernel(ext_ref, row_ref, patch_ref, dq_ref, dx1_ref, rtop_ref, rbot_ref, nsel_ref, kvt_ref, pre_ref, under_ref,
                      wp_ref, vec_ref, wqkv_ref, tapt_ref,
                      aq_ref, akv_ref, apatch_ref, av_ref, ak_ref, dn_ref, rim_ref, wide_ref, kexp_ref, *, offset):
    images, heights, breadths, row_oks = group_extents(ext_ref, row_ref, offset, size=WIDE)

    @pl.when(pl.program_id(0) == 0)
    def _():
        for ref in (aq_ref, akv_ref, apatch_ref, av_ref, ak_ref, dn_ref, rim_ref):
            ref[...] = jnp.zeros_like(ref)
        fill_wide(wide_ref, vec_ref, [0, 1, 2])
        fill_taps(kexp_ref, vec_ref)

    lane = lane_ids(128, 2 * DIM)

    def thrice(value, image):
        block = jnp.where((lane >> 5) == 1, take_lanes(value, image, 1), take_lanes(value, image, 0))
        block = jnp.where((lane >> 5) == 2, take_lanes(value, image, 2), block)
        return jnp.where((lane >> 5) == 3, 0.0, block)

    grad_taps = []
    for g in range(WIDE):
        own = thrice(pre_ref[...], images[g])
        spread = jnp.concatenate([thrice(under_ref[...].astype(F32), images[g]), own, own], axis=1)
        ak_ref[...] += kvt_ref[g].astype(F32) * spread
        grad_taps.append((spread * kexp_ref[...]).astype(BF16))
    grad_taps = jnp.concatenate(grad_taps, axis=1)
    nsel = jnp.concatenate([nsel_ref[g] for g in range(WIDE)], axis=1)
    akv_ref[...] += dot_nt(jnp.concatenate([nsel, jnp.ones((16, 384 * WIDE), BF16)], axis=0), grad_taps)
    grad_sel = dot(wqkv_ref[:, DIM : 3 * DIM], grad_taps)
    parts = [grad_sel.astype(BF16)[:, 128 * k : 128 * k + 128] for k in range(3 * WIDE)]
    lines = dot(jnp.concatenate(parts, axis=0), tapt_ref[...])
    for g in range(WIDE):
        for k, start in enumerate((224, 0, 32)):
            first = DIM * (3 * g + k)
            line = lines[first : first + DIM]
            for tile in range(TILES):
                dn_ref[g, :, 256 * tile + start : 256 * tile + start + 32] = line[:, 32 * tile : 32 * tile + 32]
        for halo_ref, start in ((rtop_ref, 0), (rbot_ref, 224)):
            line = halo_ref[g].astype(F32)
            for tile in range(TILES):
                rim_ref[g, :, 256 * tile + start : 256 * tile + start + 32] = line[:, 32 * tile : 32 * tile + 32]

    def step(pair, carry):
        mask = pair_mask(pair, breadths, row_oks)
        patches = load_pair(patch_ref, pair)

        def first_norm(k, embed, mask, grad, rim):
            hat, rstd = normalized((embed + wide_ref[0]) * mask)
            return hat, rstd, (hat * wide_ref[1] + wide_ref[2]).astype(BF16), (grad.astype(F32) + rim).astype(BF16)

        hat, rstd, normed, grad_q = by_lanes(first_norm, dot(wp_ref[...], patches), mask, load_pair(dq_ref, pair), load_pair(rim_ref, pair))
        aq_ref[...] += dot_nt(jnp.concatenate([normed, jnp.ones((16, WIDE * PAIR), BF16)], axis=0), grad_q)

        def first_back(k, out, extra, hat, rstd, mask, dx1):
            grad = out + extra
            total = (dx1.astype(F32) + norm_back(grad, hat, rstd, wide_ref[1])) * mask
            return total.astype(BF16), total, grad * hat, grad

        low, total, scaled, grad = by_lanes(
            first_back, dot(wqkv_ref[:, 0:DIM], grad_q), load_pair(dn_ref, pair), hat, rstd, mask, load_pair(dx1_ref, pair))
        av_ref[0] += fold_lanes(total)
        av_ref[1] += fold_lanes(scaled)
        av_ref[2] += fold_lanes(grad)
        apatch_ref[...] += dot_nt(low, patches)
        return carry

    lax.fori_loop(0, pair_count(breadths), step, 0)


def call_embed_back(ext, row, patches, dq, dx1, rtop, rbot, nsel, kvt, pre, under, consts, wts, offset):
    whole, per = specs(WIDE)
    images = dq.shape[0]
    sums = [(DIM + 16, DIM), (DIM + 16, 2 * DIM), (DIM, PATCH_ROWS), (3, DIM, 128), (2 * DIM, 384)]
    return pl.pallas_call(
        functools.partial(embed_back_kernel, offset=offset),
        grid_spec=pltpu.PrefetchScalarGridSpec(
            num_scalar_prefetch=2, grid=(images // WIDE,),
            in_specs=[
                per(PATCH_ROWS, TOKENS), per(DIM, TOKENS), per(DIM, TOKENS), per(DIM, CANVAS_W), per(DIM, CANVAS_W),
                per(DIM, 384), per(2 * DIM, 384), key_lanes(2 * DIM, size=WIDE), key_lanes(2 * DIM, size=WIDE),
                whole(DIM, PATCH_ROWS), whole(DIM, 64), whole(DIM, 3 * DIM), whole(128, CANVAS_W)],
            out_specs=[whole(*s) for s in sums],
            scratch_shapes=[pltpu.VMEM((WIDE, DIM, TOKENS), F32)] * 2 + [pltpu.VMEM((3, DIM, 128), F32), pltpu.VMEM((2 * DIM, 384), F32)]),
        out_shape=[jax.ShapeDtypeStruct(s, F32) for s in sums],
        compiler_params=pltpu.CompilerParams(vmem_limit_bytes=VMEM_BYTES),
        cost_estimate=pl.CostEstimate(flops=images * 3_000_000_000, bytes_accessed=images * 3_000_000, transcendentals=0),
        name="embed_back",
    )(ext, row, patches, dq, dx1, rtop, rbot, nsel, kvt, pre, under, wts["wp"], wts["vec"], wts["wqkv"], consts["tap_t"])


def bit_count(size):
    return size.bit_length() - 1


def swap(value, axis, bit):
    size = lax.axis_size(axis)
    return lax.ppermute(value, axis, [(i, i ^ (1 << bit)) for i in range(size)])


def shifted(value, axis, step):
    size = lax.axis_size(axis)
    pairs = [(i, i + step) for i in range(size) if 0 <= i + step < size]
    return lax.ppermute(value, axis, pairs)


def summed(value, axis):
    for bit in range(bit_count(lax.axis_size(axis))):
        value = value + swap(value, axis, bit)
    return value


def scatter_step(value, axis, bit):
    half = value.shape[0] // 2
    return value[:half] + swap(value[half:].astype(BF16), axis, bit).astype(F32)


def together(*values):
    return lax.optimization_barrier(values)


def gather_params(value):
    dims = []
    for axis in ("img", "row"):
        index = lax.axis_index(axis)
        for bit in reversed(range(bit_count(lax.axis_size(axis)))):
            other = swap(value, axis, bit)
            mine_second = (index >> bit) & 1 == 1
            value = jnp.stack([jnp.where(mine_second, other, value), jnp.where(mine_second, value, other)])
            dims.append((axis, bit))
    dims = dims[::-1]
    wanted = [("img", b) for b in reversed(range(bit_count(lax.axis_size("img"))))]
    wanted += [("row", b) for b in reversed(range(bit_count(lax.axis_size("row"))))]
    order = [dims.index(d) for d in wanted]
    value = jnp.transpose(value, order + [value.ndim - 2, value.ndim - 1])
    return value.reshape(-1)


def sum_grads(flat, extra):
    rows, imgs = lax.axis_size("row"), lax.axis_size("img")
    bits = bit_count(rows)
    leaf = flat.shape[0] // (rows * imgs)
    value = flat.reshape((imgs,) + (2,) * bits + (leaf // 128, 128))
    index = lax.axis_index("row")
    for bit in range(bits):
        place = value.ndim - 3
        own = (index >> bit) & 1
        keep = lax.dynamic_index_in_dim(value, own, place, False)
        send = lax.dynamic_index_in_dim(value, 1 - own, place, False)
        value = keep + swap(send, "row", bit)
    value = jnp.concatenate([value.reshape(imgs * leaf // 128, 128), jnp.full((8, 128), extra)], axis=0)
    value = summed(value, "img")
    return value[:-8], value[-1, 0]


def segment_list(canvas_rows, canvas_cols):
    return [
        ("w_patch", (3 * PATCH * PATCH, DIM)),
        ("w_qkv", (DIM, 3 * DIM)),
        ("w_proj", (DIM, DIM)),
        ("w_fc1", (DIM, MLP)),
        ("w_fc2", (MLP, DIM)),
        ("w_head", (DIM, CLASSES)),
        ("rel_rows", (2 * canvas_rows - 8, DIM)),
        ("rel_cols", (2 * canvas_cols - 8, DIM)),
        ("small", (49, DIM)),
        ("b_head", (CLASSES,)),
    ]


def unpack(flat_vec, segments):
    pieces = {}
    position = 0
    for seg_name, seg_shape in segments:
        entries = int(np.prod(seg_shape))
        pieces[seg_name] = flat_vec[position : position + entries].reshape(seg_shape)
        position += entries
    return pieces


def patch_rows(weight):
    taps = jnp.pad(weight.reshape(PATCH, PATCH, 3, DIM), ((0, 1), (0, 0), (0, 1), (0, 0)))
    parts = []
    for piece in (taps[:, 3:7], jnp.pad(taps[:, 0:3], ((0, 0), (1, 0), (0, 0), (0, 0)))):
        parts.append(jnp.transpose(piece.reshape(2, 4, 4, 4, DIM), (0, 2, 1, 3, 4)).reshape(128, DIM))
    return jnp.concatenate(parts, axis=0)


def patch_rows_back(grad):
    taps = jnp.transpose(grad.T.reshape(2, 2, 4, 4, 4, DIM), (0, 1, 3, 2, 4, 5)).reshape(2, 8, 4, 4, DIM)
    return jnp.concatenate([taps[1, :PATCH, 1:, :3], taps[0, :PATCH, :, :3]], axis=1).reshape(3 * PATCH * PATCH, DIM)


def relative_windows(rel_rows, rel_cols, row_index, key_rows):
    offsets = jnp.flip(rel_cols.reshape(-1, 8, DIM), 0)
    offsets = jnp.transpose(jnp.pad(offsets, ((0, 1), (0, 0), (0, 0))), (1, 0, 2))
    blocks = rel_rows.reshape(2 * key_rows - 1, 8, DIM)
    rows = jnp.transpose(jnp.flip(lax.dynamic_slice_in_dim(blocks, row_index, key_rows, 0), 0), (1, 0, 2))
    rows = rows.reshape(8 * key_rows, DIM)
    windows = []
    for pair in range(PAIRS):
        cols = offsets[:, 24 - 8 * pair : 24 - 8 * pair + WIN].reshape(8 * WIN, DIM)
        windows.append(jnp.concatenate([cols, rows], axis=0))
    return jnp.stack(windows)


def relative_windows_back(grad, row_index, key_rows):
    cols = grad[:, : 8 * WIN].reshape(PAIRS, 8, WIN, DIM)
    total = 0.0
    for pair in range(PAIRS):
        start = 24 - 8 * pair
        total = total + jnp.pad(cols[pair], ((0, 0), (start, 64 - start - WIN), (0, 0)))
    rel_cols = jnp.flip(jnp.transpose(total[:, :63], (1, 0, 2)), 0).reshape(-1, DIM)
    rows = jnp.sum(grad[:, 8 * WIN :], axis=0).reshape(8, key_rows, DIM)
    rows = jnp.flip(jnp.transpose(rows, (1, 0, 2)), 0)
    blocks = lax.dynamic_update_slice_in_dim(jnp.zeros((2 * key_rows - 1, 8, DIM), F32), rows, row_index, 0)
    return blocks.reshape(-1, DIM), rel_cols


def tap_keep():
    keep = np.ones((3, 4, 32), np.float32)
    keep[:, 3] = 0.0
    keep[:, 0, 0] = 0.0
    return keep


def prepare(weights, row_index, key_rows):
    small = weights["small"]
    vec = jnp.pad(small.astype(F32).T, ((0, 0), (0, 15)))
    windows = relative_windows(weights["rel_rows"], weights["rel_cols"], row_index, key_rows)
    return {
        "vec": vec,
        "wp": patch_rows(weights["w_patch"]).T,
        "wqkv": weights["w_qkv"],
        "wqkv_t": weights["w_qkv"].T,
        "wproj": weights["w_proj"],
        "w1": weights["w_fc1"],
        "w2": weights["w_fc2"],
        "rw": windows,
        "rw_t": jnp.transpose(windows, (0, 2, 1)),
    }


def image_loss(pooled, head_w, head_b, log_teacher, labels, image_total):
    logits = jnp.dot(pooled, head_w, precision=HIGHEST_PREC) + head_b
    log_student = jax.nn.log_softmax(logits, axis=-1)
    onehot = (jnp.arange(CLASSES)[None, :] == labels[:, None]).astype(F32)
    per_image = jnp.sum(jnp.exp(log_teacher) * (log_teacher - log_student), axis=-1) - jnp.sum(onehot * log_student, axis=-1)
    return jnp.sum(per_image) / image_total


def body(flat_params, first_moment, second_moment, pixels, extents, labels, teacher):
    key_rows = lax.axis_size("row")
    row_index = lax.axis_index("row")
    row_lead = row_index == 0
    segments = segment_list(ROWS * key_rows, CANVAS_W)
    full_params = gather_params(flat_params.astype(BF16).reshape(-1, 128))
    weights = unpack(full_params, segments)
    wts = prepare(weights, row_index, key_rows)
    tap = tap_matrix()
    consts = {"perm": jnp.asarray(deinterleave_matrix(), BF16), "tap": jnp.asarray(tap, BF16), "tap_t": jnp.asarray(tap.T, BF16)}
    vectors = weights["small"][27:42].astype(F32)
    row = row_index.astype(jnp.int32).reshape(1)
    images = pixels.shape[0]
    parts = 1
    size = images // parts
    image_total = images * lax.axis_size("img") * 1.0
    head_w = weights["w_head"].astype(F32)
    head_b = weights["b_head"].astype(F32)

    ids = jnp.arange(images)
    widths = extents[:, 1]
    ahead = (widths[None, :] > widths[:, None]) | ((widths[None, :] == widths[:, None]) & (ids[None, :] < ids[:, None]))
    places = jnp.sum(ahead.astype(jnp.int32), axis=1)
    chosen = places[None, :] == ids[:, None]
    order = jnp.sum(jnp.where(chosen, ids[None, :], 0), axis=1)
    ext = jnp.sum(jnp.where(chosen[:, :, None], extents[None], 0), axis=1)

    log_teacher = jax.nn.log_softmax(teacher, axis=-1)
    pixel_view = jnp.transpose(pixels, (0, 2, 3, 1, 4))
    saved = []
    for part in range(parts):
        first, last, nsel, kvt, below, own = call_edge(ext, row, order, pixel_view, consts, wts, size, part * size)
        got = shifted(below, "row", 1)
        kv = lax.all_gather(call_pool_norm(own, got, wts["vec"]), "row", axis=0)
        top = shifted(last, "row", 1)
        bot = shifted(first, "row", -1)
        names = sorted(wts)
        after, log_teacher, *values = together(ext, log_teacher, *[wts[name] for name in names])
        wts = dict(zip(names, values))
        patches, x0, q = call_embed(after, row, order, pixel_view, consts, wts, size, part * size)
        saved.append(dict(patches=patches, x0=x0, q=q, top=top, bot=bot, nsel=nsel, kvt=kvt, own=own, got=got, kv=kv))
    for part in range(parts):
        s = saved[part]
        s["fwd"] = call_forward(ext, row, s["q"], s["top"], s["bot"], s["x0"], s["kv"], wts, part * size)
    total = {}

    def add(name, value):
        total[name] = total[name] + value if name in total else value

    sorted_local = jnp.sum(jnp.concatenate([s["fwd"][-1] for s in saved], axis=0), axis=-1)
    local = jnp.sum(jnp.where(chosen[:, :, None], sorted_local[:, None, :], 0.0), axis=0)
    everywhere = summed(local, "row")
    counts = (extents[:, 0] * extents[:, 1]).astype(F32)[:, None]
    pooled = (everywhere * vectors[13] + counts * vectors[14]) / counts

    def loss_of(pooled_now, w, b):
        return image_loss(pooled_now, w, b, log_teacher, labels, image_total)

    loss_value, loss_back = jax.vjp(loss_of, pooled, head_w, head_b)
    grad_pooled, total["w_head"], total["b_head"] = loss_back(jnp.ones_like(loss_value))
    gvec = grad_pooled / counts
    local_count = jnp.where(row_index * ROWS < extents[:, 0], ROWS * extents[:, 1], 0).astype(F32)[:, None]
    total["g_three"] = jnp.sum(gvec * local, axis=0)
    total["b_three"] = jnp.sum(gvec * local_count, axis=0)
    gvec = jnp.sum(jnp.where(chosen[:, :, None], gvec[None], 0.0), axis=1)[:, :, None]
    for part in range(parts):
        s = saved[part]
        s["bwd"] = call_backward(ext, row, s["fwd"][:-1], s["q"], s["top"], s["bot"], s["kv"], gvec[part * size : part * size + size], wts, part * size)
    for part in range(parts):
        s = saved[part]
        dx1, dq, up, down, dkv, *sums = s["bwd"]
        for bit in range(bit_count(key_rows)):
            if bit == 1:
                dkv, up, down = together(dkv, up, down)
                rtop = shifted(down, "row", 1)
                rbot = shifted(up, "row", -1)
            dkv = scatter_step(dkv, "row", bit)
            if bit == 1:
                dkv, *sums = together(dkv, *sums)
        for name, value in zip(("a2", "a1", "ap", "av", "ak", "ar"), sums):
            add(name, value)
        grad_kv = dkv[0]
        pre, pool_sums = call_pool_back(s["own"], s["got"], grad_kv, wts["vec"])
        add("pool_sums", pool_sums)
        under = shifted(pre.astype(BF16), "row", -1)
        aq, akv, apatch, av1, akt = call_embed_back(
            ext, row, s["patches"], dq, dx1, rtop, rbot, s["nsel"], s["kvt"], pre, under, consts, wts, part * size)
        for name, value in (("aq", aq), ("akv", akv), ("apatch", apatch), ("av1", av1), ("akt", akt)):
            add(name, value)

    t = total
    lead = jnp.where(row_lead, 1.0, 0.0)
    av, av1 = jnp.sum(t["av"], axis=-1), jnp.sum(t["av1"], axis=-1)
    pool_sums = jnp.sum(t["pool_sums"], axis=-1)
    rel_rows, rel_cols = relative_windows_back(t["ar"], row_index, key_rows)
    taps = jnp.sum((t["akt"].reshape(2, DIM, 3, 4, 32) * tap_keep())[:, :, :, :3], axis=-1)
    kernels = jnp.concatenate([jnp.sum(t["ak"], axis=-1), jnp.transpose(taps, (0, 2, 3, 1)).reshape(18, DIM)], axis=0)
    grad_vectors = jnp.stack([
        av1[0], av1[1], av1[2], av[2], av[3], pool_sums[0], pool_sums[1], pool_sums[2], pool_sums[3],
        t["ap"][DIM], av[0], av[1], t["a2"][MLP], t["g_three"], t["b_three"]])
    pieces = [
        patch_rows_back(t["apatch"]),
        jnp.concatenate([t["aq"][:DIM], t["akv"][:DIM]], axis=1),
        t["ap"][:DIM],
        t["a1"][:DIM],
        t["a2"][:MLP],
        t["w_head"] * lead,
        rel_rows,
        rel_cols,
        kernels,
        grad_vectors,
        t["aq"][DIM],
        t["akv"][DIM],
        t["a1"][DIM],
        t["b_head"] * lead,
    ]
    joined = jnp.concatenate([piece.reshape(-1) for piece in pieces])
    grad_flat = jnp.pad(joined, (0, full_params.shape[0] - joined.shape[0]))
    shares, loss_sum = sum_grads(grad_flat, loss_value)
    norm_sq = summed(jnp.sum(shares * shares), "row")
    lines = flat_params.shape[0] // 128
    grad_shard = lax.dynamic_slice_in_dim(shares, lax.axis_index("img") * lines, lines, 0).reshape(-1)
    grad_norm = jnp.sqrt(norm_sq)
    clip_factor = jnp.minimum(1.0, CLIP_NORM / (grad_norm + 1e-06))
    clipped = grad_shard * clip_factor
    moment_one = BETA_FIRST * first_moment + (1.0 - BETA_FIRST) * clipped
    moment_two = BETA_SECOND * second_moment + (1.0 - BETA_SECOND) * clipped * clipped
    fix_one = 1.0 - BETA_FIRST**STEP
    fix_two = 1.0 - BETA_SECOND**STEP
    update = moment_one / fix_one / (jnp.sqrt(moment_two / fix_two) + ADAM_EPS) + WEIGHT_DECAY * flat_params
    new_params = flat_params - LEARN_RATE * update
    return (new_params, moment_one, moment_two, grad_norm, loss_sum)


def solution(mesh):
    placed = (
        P(("img", "row")),
        P(("img", "row")),
        P(("img", "row")),
        P("img", "row", None, None, None),
        P("img", None),
        P("img"),
        P("img", None),
    )
    return jax.shard_map(
        body,
        mesh=mesh,
        in_specs=placed,
        out_specs=(P(("img", "row")), P(("img", "row")), P(("img", "row")), P(), P()),
        check_vma=False,
    )
```
